32 devices in a mesh: section: 8 (over z, core), rep: 4 (over y, x).
Axes of the slice: x: 2, y: 2, z: 4, core: 2. Of those that a mesh axis runs over, the one named last changes fastest.
Arguments:
- features: bfloat16 [4096, 256], P(('section', 'rep')), may hold values from -6 to 6
- adj_tiles: bfloat16 [32, 4, 4, 128, 128], P('section', 'rep'), may hold values from -0.125 to 0.125
- adj_src: int32 [32, 4, 4], P('section', 'rep'), may hold values from 0 to 7
- cotangent: bfloat16 [4096, 256], P(('section', 'rep')), may hold values from -1 to 1
- weight: bfloat16 [256, 256], replicated, may hold values from -0.375 to 0.375
- destination: int32 [4096, 1], P(('section', 'rep')), may hold values from 0 to 7; in each aligned block of 128 rows (0 to 127, 128 to 255, ...) at most 32 rows name the same one
Outputs:
- relaid: bfloat16 [8, 4, 8, 32, 256], P('section', 'rep')
- weight_grad: float32 [256, 256], replicated
The draws below stay inside these ranges and needn't reach their ends.
Inputs may be any that keep to these rules, and one draw needn't show every extreme that they name: `destination`: from the rows of one device, at most 32 go to one section; some device sends exactly 32 to some section.
All inputs are finite; a program needn't handle non-finite values.
Results may differ from the reference program's by a relative error of at most 0.013.
Values may be sent and summed in bfloat16 or wider, within the bound.
No kernel may reach another device: no remote copies, remote signals or barrier semaphores. Data moves between devices by JAX's collectives and lax.ppermute only.
A program may use at most 64 MiB of HBM per device.

```python
import math
import jax
import jax.numpy as jnp
import numpy as np
from jax import lax

F = 256
TILE = 128
KT = 4
ROWS_DEV = 128
NB = 32
ROWS = 4096
CAP = 32
N_SECTION = 8
N_REP = 4
DEVICES = 32


def draw_cotangent(key, part):
    key = jax.random.fold_in(key, 7)
    first, second = jax.random.split(key)
    rows = jnp.arange(ROWS, dtype=jnp.float32)
    rise = jnp.exp(jnp.log(3.0) * rows / ROWS)[:, None]
    base = jax.random.normal(first, (ROWS, F), jnp.float32)
    base = jnp.clip(base, -5.0, 5.0)
    spread = jnp.exp(jax.random.uniform(second, (ROWS, 1), jnp.float32, 0.0, jnp.log(10.0)))
    scaled = base * spread * rise * (0.3 * ROWS ** (-0.5))
    return jnp.clip(scaled, -1.0, 1.0).astype(jnp.bfloat16)


def touch_ends(values, key, smallest, top_value):
    extent = values.shape
    place = [jax.random.randint(jax.random.fold_in(key, axis), (), 0, extent[axis]) for axis in range(len(extent))]
    values = values.at[tuple(place)].set(smallest)
    longest = extent.index(max(extent))
    place[longest] = (place[longest] + 1) % extent[longest]
    return values.at[tuple(place)].set(top_value)


def block_levels(own_key, dims, cuts, least, largest):
    level, own = 1.0, jax.random.fold_in(own_key, 6)
    for axis_at, blocks in cuts:
        heights = jnp.exp(jax.random.uniform(jax.random.fold_in(own, axis_at), (blocks,), jnp.float32, least / len(cuts), largest / len(cuts)))
        level = level * jnp.repeat(heights, dims[axis_at] // blocks).reshape([-1 if axis == axis_at else 1 for axis in range(len(dims))])
    return level


def shared_out(key, own, number, rows, count, top, limit, slope):
    order = jax.random.permutation(key, count)
    crowded, usual = shares(count, rows * top, limit, slope, True), shares(count, rows * top, limit, slope, False)
    places = jnp.arange(count)

    def named(lengths, offset_by):
        used = int((lengths > 0).sum())
        fixed = max(1, used // 4)
        shifted = fixed + (places - fixed + offset_by * (used - fixed)) % max(1, count - fixed)
        return jnp.zeros((count,), jnp.int32).at[order[jnp.where(places < fixed, places, shifted)]].set(jnp.asarray(lengths, jnp.int32))

    lengths = jnp.where(number % 4 == 0, named(crowded, number // 4), named(usual, number - number // 4 - 1))
    mixed = jax.random.permutation(jax.random.fold_in(own, 3), count)
    donor, receiver = mixed[0:count // 2 * 2:2], mixed[1:count // 2 * 2:2]
    room = jnp.minimum(lengths[donor] - 1, limit - lengths[receiver]) // 2
    room = jnp.where((donor == order[0]) | (receiver == order[0]) | (lengths[receiver] == 0), 0, jnp.maximum(room, 0))
    shifted = jax.random.randint(jax.random.fold_in(own, 4), (count // 2,), 0, 1 << 20) % (room + 1)
    lengths = lengths.at[donor].add(-shifted).at[receiver].add(shifted)
    labels = jnp.searchsorted(jnp.cumsum(lengths), jnp.arange(rows * top), side="right").astype(jnp.int32)
    grid = labels.reshape(top, rows).T
    grid = grid[jax.random.permutation(jax.random.fold_in(own, 1), rows)]
    offset_by = jax.random.randint(jax.random.fold_in(own, 2), (rows, 1), 0, top)
    return jnp.take_along_axis(grid, (jnp.arange(top)[None, :] + offset_by) % top, axis=1)


def shares(amount, total, bound, skew, full):
    portions = [(1 << 20) // math.isqrt(grade ** skew) + 1 for grade in range(1, amount + 1)]
    largest = bound if full else min(bound, max(-(-total // amount), total * portions[0] // sum(portions)))
    least = 1 if total - largest >= amount - 1 else 0
    counts, spare = [largest] + [least] * (amount - 1), total - largest - least * (amount - 1)
    while spare > 0:
        candidates = [i for i in range(1, amount) if counts[i] < largest] or [i for i in range(1, amount) if counts[i] < bound]
        mass, remaining = sum([portions[i] for i in candidates]), spare
        for i in candidates:
            addition = min(bound - counts[i], max(1, remaining * portions[i] // mass), spare)
            counts[i] = counts[i] + addition
            spare = spare - addition
    return np.array(counts)


def noise(rng, extent, deviation, most, cuts=(), kind=jnp.bfloat16):
    loudness = block_levels(rng, extent, cuts, -0.22, 0.18) if cuts else 1.0
    entries = jax.random.normal(rng, extent, jnp.float32) * deviation * loudness
    return jnp.minimum(jnp.maximum(entries, -most), most).astype(kind)


def setup_inputs(seed: int = 0) -> dict:
    key_list = jax.random.split(jax.random.key(seed), 7)
    features = noise(key_list[0], (ROWS, F), 1.0, 6.0, ((0, 32),))
    adj_tiles = noise(key_list[1], (NB, N_REP, KT, TILE, TILE), (TILE * KT * N_REP) ** -0.5, 0.125, ((0, 8), (1, 4)))
    adj_src = touch_ends(jax.random.randint(key_list[2], (NB, N_REP, KT), 0, N_SECTION), jax.random.fold_in(key_list[2], 1), 0, N_SECTION - 1).astype(jnp.int32)
    cotangent = draw_cotangent(jax.random.fold_in(key_list[6], 71), 0)
    weight = noise(key_list[4], (F, F), F ** -0.5, 0.375)
    destination_keys = jax.random.split(jax.random.fold_in(key_list[5], 1), ROWS // TILE)
    destination_turns = jax.random.permutation(jax.random.fold_in(key_list[5], 3), ROWS // TILE)
    destination = jax.vmap(lambda own, number: shared_out(jax.random.fold_in(key_list[5], 2), own, number, TILE, N_SECTION, 1, CAP, 2))(destination_keys, destination_turns).reshape((ROWS, 1))
    return dict(features=features, adj_tiles=adj_tiles, adj_src=adj_src, cotangent=cotangent, weight=weight, destination=destination)


def reference(features, adj_tiles, adj_src, cotangent, weight, destination):
    feature_blocks = features.reshape(NB, TILE, F)
    classes = jnp.arange(N_REP, dtype=jnp.int32)[None, :, None]
    columns = (adj_src * N_REP + classes).astype(jnp.int32)

    def one_block(pair):
        tiles, cols = pair
        picked = jnp.take(feature_blocks, cols.reshape(-1), axis=0).astype(jnp.float32)
        picked = picked.reshape(N_REP, KT, TILE, F)
        parts = jnp.einsum("rkab,rkbf->raf", tiles.astype(jnp.float32), picked)
        parts = lax.optimization_barrier(parts.astype(jnp.bfloat16))
        return jnp.sum(parts.astype(jnp.float32), axis=0)

    agg = lax.map(one_block, (adj_tiles, columns)).reshape(ROWS, F)
    agg_b = agg.astype(jnp.bfloat16)
    pre = jnp.dot(agg_b, weight, preferred_element_type=jnp.float32)
    sig = jax.nn.sigmoid(pre)
    output = (pre * sig).astype(jnp.bfloat16)
    factor = sig * (1.0 + pre * (1.0 - sig))
    grad_pre = (cotangent.astype(jnp.float32) * factor).astype(jnp.bfloat16)
    weight_grad = jnp.dot(agg_b.T, grad_pre, preferred_element_type=jnp.float32)
    target = destination[:, 0].reshape(DEVICES, ROWS_DEV)
    hits = (target[:, :, None] == jnp.arange(N_SECTION, dtype=jnp.int32)[None, None, :]).astype(jnp.int32)
    before = jnp.cumsum(hits, axis=1) - hits
    slot = jnp.sum(before * hits, axis=2).reshape(-1)
    device = (jnp.arange(ROWS, dtype=jnp.int32) // ROWS_DEV).astype(jnp.int32)
    relaid = jnp.zeros((N_SECTION, N_REP, N_SECTION, CAP, F), jnp.bfloat16)
    relaid = relaid.at[target.reshape(-1), device % N_REP, device // N_REP, slot].set(output)
    return relaid, weight_grad
```

```python
import functools

import jax
import jax.numpy as jnp
from jax import lax
from jax.experimental import pallas as pl
from jax.experimental.pallas import tpu as pltpu
from jax.sharding import PartitionSpec as P

VMEM = pl.BlockSpec(memory_space=pltpu.VMEM)
SMEM = pl.BlockSpec(memory_space=pltpu.SMEM)


def partials_kernel(src_ref, tiles_ref, blocks_ref, out_ref):
    many, depth = tiles_ref.shape[0], tiles_ref.shape[1]
    for g in range(many):
        left = jnp.concatenate([tiles_ref[g, k] for k in range(depth)], axis=1)
        right = jnp.concatenate([blocks_ref[src_ref[g, k]] for k in range(depth)], axis=0)
        out_ref[g] = jnp.dot(left, right, preferred_element_type=jnp.float32).astype(jnp.bfloat16)


def partials(sources, tiles, blocks):
    many, depth, tile, _ = tiles.shape
    width = blocks.shape[2]
    return pl.pallas_call(
        partials_kernel,
        out_shape=jax.ShapeDtypeStruct((many, tile, width), jnp.bfloat16),
        in_specs=[SMEM, VMEM, VMEM],
        out_specs=VMEM,
        compiler_params=pltpu.CompilerParams(vmem_limit_bytes=32 * 1024 * 1024),
        name="partials",
    )(sources, tiles, blocks)


def dense_kernel(slots, parts_ref, weight_ref, cot_ref, target_ref, packed_ref, grad_ref):
    rows = cot_ref.shape[0]
    places = packed_ref.shape[0]
    n_section = places // slots
    agg_b = jnp.sum(parts_ref[...].astype(jnp.float32), axis=0).astype(jnp.bfloat16)
    pre = jnp.dot(agg_b, weight_ref[...], preferred_element_type=jnp.float32)
    sig = jax.nn.sigmoid(pre)
    output = (pre * sig).astype(jnp.bfloat16)
    factor = sig * (1.0 + pre * (1.0 - sig))
    grad_pre = (cot_ref[...].astype(jnp.float32) * factor).astype(jnp.bfloat16)
    grad_ref[...] = lax.dot_general(
        agg_b, grad_pre, (((0,), (0,)), ((), ())), preferred_element_type=jnp.float32
    ).astype(grad_ref.dtype)
    target = target_ref[...]
    hits = lax.broadcasted_iota(jnp.int32, (n_section, rows), 0) == target
    hits_f = jnp.where(hits, 1.0, 0.0)
    earlier = lax.broadcasted_iota(jnp.int32, (rows, rows), 0) < lax.broadcasted_iota(
        jnp.int32, (rows, rows), 1
    )
    earlier = jnp.where(earlier, 1.0, 0.0).astype(jnp.bfloat16)
    before = jnp.dot(hits_f.astype(jnp.bfloat16), earlier, preferred_element_type=jnp.float32)
    slot = jnp.sum(before * hits_f, axis=0, keepdims=True).astype(jnp.int32)
    position = target * slots + slot
    placing = lax.broadcasted_iota(jnp.int32, (places, rows), 0) == position
    placing = jnp.where(placing, 1.0, 0.0).astype(jnp.bfloat16)
    packed_ref[...] = jnp.dot(placing, output, preferred_element_type=jnp.float32).astype(
        jnp.bfloat16
    )


def dense(parts, weight, cotangent, target, places, slots):
    width = weight.shape[0]
    return pl.pallas_call(
        functools.partial(dense_kernel, slots),
        out_shape=(
            jax.ShapeDtypeStruct((places, width), jnp.bfloat16),
            jax.ShapeDtypeStruct((width, width), jnp.float32),
        ),
        in_specs=[VMEM] * 4,
        out_specs=(VMEM, VMEM),
        compiler_params=pltpu.CompilerParams(vmem_limit_bytes=32 * 1024 * 1024),
        name="dense",
    )(parts, weight, cotangent, target)


def per_device(features, adj_tiles, adj_src, cotangent, weight, destination):
    n_section, n_rep = lax.axis_size("section"), lax.axis_size("rep")
    both = ("section", "rep")
    devices = n_section * n_rep
    rows_here, width = features.shape
    tile = adj_tiles.shape[3]
    gathered = lax.all_gather(features, "section", axis=0, tiled=True)
    blocks = gathered.reshape(-1, tile, width)
    part = partials(adj_src[:, 0], adj_tiles[:, 0], blocks)
    parts = part.reshape(n_rep, rows_here, width)
    parts = lax.all_to_all(parts, "rep", split_axis=0, concat_axis=0, tiled=True)
    slots = max(2, 2 * rows_here // n_section)
    target = destination.reshape(1, rows_here)
    packed, grad = dense(parts, weight, cotangent, target, n_section * slots, slots)
    packed = packed.reshape(n_section, slots, width)
    received = lax.all_to_all(packed, "section", split_axis=0, concat_axis=0, tiled=True)
    relaid = received.reshape(1, 1, n_section, slots, width)
    chunks = grad.reshape(devices, width * width // devices)
    if width % devices == 0:
        chunks = grad.reshape(devices, width // devices, width)
    terms = lax.all_to_all(chunks, both, split_axis=0, concat_axis=0, tiled=True)
    mine = jnp.sum(terms, axis=0, keepdims=True)
    spread = jnp.broadcast_to(mine, chunks.shape)
    weight_grad = lax.all_to_all(spread, both, split_axis=0, concat_axis=0, tiled=True)
    return (relaid, weight_grad.reshape(width, width))


def solution(mesh):
    placed = (
        P(("section", "rep"), None),
        P("section", "rep", None, None, None),
        P("section", "rep", None),
        P(("section", "rep"), None),
        P(),
        P(("section", "rep"), None),
    )
    return jax.shard_map(
        per_device,
        mesh=mesh,
        in_specs=placed,
        out_specs=(P("section", "rep", None, None, None), P()),
        check_vma=False,
    )
```

```python
import functools

import jax
import jax.numpy as jnp
from jax import lax
from jax.experimental import pallas as pl
from jax.experimental.pallas import tpu as pltpu
from jax.sharding import PartitionSpec as P

VMEM = pl.BlockSpec(memory_space=pltpu.VMEM)
SMEM = pl.BlockSpec(memory_space=pltpu.SMEM)


def partials_kernel(count, src_ref, tiles_ref, *refs):
    block_refs, out_refs, held = refs[:count], refs[count:-1], refs[-1]
    depth = tiles_ref.shape[1]
    section, rep = lax.axis_index("section"), lax.axis_index("rep")
    for j in range(count):
        held[j] = block_refs[j][...]
    for j, out_ref in enumerate(out_refs):
        g = rep ^ j
        left = jnp.concatenate([tiles_ref[g, k] for k in range(depth)], axis=1)
        right = jnp.concatenate([held[src_ref[g, k] ^ section] for k in range(depth)], axis=0)
        out_ref[...] = jnp.dot(left, right, preferred_element_type=jnp.float32).astype(jnp.bfloat16)


def partials(sources, tiles, blocks):
    many, tile = tiles.shape[0], tiles.shape[2]
    width = blocks[0].shape[1]
    return pl.pallas_call(
        functools.partial(partials_kernel, len(blocks)),
        out_shape=[jax.ShapeDtypeStruct((tile, width), jnp.bfloat16)] * many,
        in_specs=[SMEM] + [VMEM] * (1 + len(blocks)),
        out_specs=[VMEM] * many,
        scratch_shapes=[pltpu.VMEM((len(blocks), tile, width), jnp.bfloat16)],
        compiler_params=pltpu.CompilerParams(vmem_limit_bytes=32 * 1024 * 1024),
        name="partials",
    )(sources, tiles, *blocks)


def swap(value, axis, j):
    return lax.ppermute(value, axis, [(i, i ^ j) for i in range(lax.axis_size(axis))])


def gather_blocks(features, axis):
    n = lax.axis_size(axis)
    blocks = [None] * n
    blocks[0] = features
    for j in range(2, n, 2):
        blocks[j] = swap(features, axis, j)
    for j in range(0, n, 2):
        blocks[j + 1] = swap(blocks[j], axis, 1)
    return blocks


def dense_kernel(slots, weight_ref, cot_ref, target_ref, *refs):
    part_refs, (packed_ref, grad_ref) = refs[:-2], refs[-2:]
    rows = cot_ref.shape[0]
    places = packed_ref.shape[0]
    n_section = places // slots
    agg_b = sum(ref[...].astype(jnp.float32) for ref in part_refs).astype(jnp.bfloat16)
    pre = jnp.dot(agg_b, weight_ref[...], preferred_element_type=jnp.float32)
    sig = jax.nn.sigmoid(pre)
    output = (pre * sig).astype(jnp.bfloat16)
    factor = sig * (1.0 + pre * (1.0 - sig))
    grad_pre = (cot_ref[...].astype(jnp.float32) * factor).astype(jnp.bfloat16)
    grad_ref[...] = lax.dot_general(
        agg_b, grad_pre, (((0,), (0,)), ((), ())), preferred_element_type=jnp.float32
    ).astype(grad_ref.dtype)
    target = target_ref[...]
    hits = lax.broadcasted_iota(jnp.int32, (n_section, rows), 0) == target
    hits_f = jnp.where(hits, 1.0, 0.0)
    earlier = lax.broadcasted_iota(jnp.int32, (rows, rows), 0) < lax.broadcasted_iota(
        jnp.int32, (rows, rows), 1
    )
    earlier = jnp.where(earlier, 1.0, 0.0).astype(jnp.bfloat16)
    before = jnp.dot(hits_f.astype(jnp.bfloat16), earlier, preferred_element_type=jnp.float32)
    slot = jnp.sum(before * hits_f, axis=0, keepdims=True).astype(jnp.int32)
    position = target * slots + slot
    placing = lax.broadcasted_iota(jnp.int32, (places, rows), 0) == position
    placing = jnp.where(placing, 1.0, 0.0).astype(jnp.bfloat16)
    packed_ref[...] = jnp.dot(placing, output, preferred_element_type=jnp.float32).astype(
        jnp.bfloat16
    )


def dense(parts, weight, cotangent, target, places, slots):
    width = weight.shape[0]
    return pl.pallas_call(
        functools.partial(dense_kernel, slots),
        out_shape=(
            jax.ShapeDtypeStruct((places, width), jnp.bfloat16),
            jax.ShapeDtypeStruct((width, width), jnp.bfloat16),
        ),
        in_specs=[VMEM] * (3 + len(parts)),
        out_specs=(VMEM, VMEM),
        compiler_params=pltpu.CompilerParams(vmem_limit_bytes=32 * 1024 * 1024),
        name="dense",
    )(weight, cotangent, target, *parts)


def per_device(features, adj_tiles, adj_src, cotangent, weight, destination):
    n_section, n_rep = lax.axis_size("section"), lax.axis_size("rep")
    both = ("section", "rep")
    devices = n_section * n_rep
    rows_here, width = features.shape
    tile = adj_tiles.shape[3]
    blocks = gather_blocks(features.reshape(tile, width), "section")
    parts = partials(adj_src[:, 0], adj_tiles[:, 0], blocks)
    parts = [parts[0]] + [swap(parts[j], "rep", j) for j in range(1, n_rep)]
    slots = max(2, 2 * rows_here // n_section)
    target = destination.reshape(1, rows_here)
    packed, grad = dense(parts, weight, cotangent, target, n_section * slots, slots)
    packed = packed.reshape(n_section, slots, width)
    received = lax.all_to_all(packed, "section", split_axis=0, concat_axis=0, tiled=True)
    relaid = received.reshape(1, 1, n_section, slots, width)
    chunks = grad.reshape(devices, width * width // devices)
    if width % devices == 0:
        chunks = grad.reshape(devices, width // devices, width)
    terms = lax.all_to_all(chunks, both, split_axis=0, concat_axis=0, tiled=True)
    mine = jnp.sum(terms.astype(jnp.float32), axis=0, keepdims=True).astype(jnp.bfloat16)
    spread = jnp.broadcast_to(mine, chunks.shape)
    weight_grad = lax.all_to_all(spread, both, split_axis=0, concat_axis=0, tiled=True)
    return (relaid, weight_grad.reshape(width, width).astype(jnp.float32))


def solution(mesh):
    placed = (
        P(("section", "rep"), None),
        P("section", "rep", None, None, None),
        P("section", "rep", None),
        P(("section", "rep"), None),
        P(),
        P(("section", "rep"), None),
    )
    return jax.shard_map(
        per_device,
        mesh=mesh,
        in_specs=placed,
        out_specs=(P("section", "rep", None, None, None), P()),
        check_vma=False,
    )
```

```python
import functools

import jax
import jax.numpy as jnp
from jax import lax
from jax.experimental import pallas as pl
from jax.experimental.pallas import tpu as pltpu
from jax.sharding import PartitionSpec as P

VMEM = pl.BlockSpec(memory_space=pltpu.VMEM)
LIMIT = pltpu.CompilerParams(vmem_limit_bytes=32 * 1024 * 1024)
SMEM = pl.BlockSpec(memory_space=pltpu.SMEM)


def prepare_kernel(slots, tiles_ref, own_ref, target_ref, wide_ref, held_ref, placing_ref):
    many, depth = tiles_ref.shape[:2]
    for g in range(many):
        wide_ref[g] = jnp.concatenate([tiles_ref[g, k] for k in range(depth)], axis=1)
    held_ref[...] = own_ref[...]
    places, rows = placing_ref.shape
    n_section = places // slots
    target = target_ref[...]
    hits = lax.broadcasted_iota(jnp.int32, (n_section, rows), 0) == target
    hits = jnp.where(hits, 1.0, 0.0)
    earlier = lax.broadcasted_iota(jnp.int32, (rows, rows), 0) < lax.broadcasted_iota(
        jnp.int32, (rows, rows), 1
    )
    earlier = jnp.where(earlier, 1.0, 0.0).astype(jnp.bfloat16)
    before = jnp.dot(hits.astype(jnp.bfloat16), earlier, preferred_element_type=jnp.float32)
    slot = jnp.sum(before * hits, axis=0, keepdims=True).astype(jnp.int32)
    apart = target ^ lax.axis_index("section")
    position = ((apart & 1) * (n_section // 2) + (apart >> 1)) * slots + slot
    placing = lax.broadcasted_iota(jnp.int32, (places, rows), 0) == position
    placing_ref[...] = jnp.where(placing, 1.0, 0.0).astype(jnp.bfloat16)


def prepare(tiles, own, target, places, slots):
    many, depth, tile, _ = tiles.shape
    return pl.pallas_call(
        functools.partial(prepare_kernel, slots),
        out_shape=(
            jax.ShapeDtypeStruct((many, tile, depth * tile), jnp.bfloat16),
            jax.ShapeDtypeStruct(own.shape, jnp.bfloat16),
            jax.ShapeDtypeStruct((places, target.shape[1]), jnp.bfloat16),
        ),
        in_specs=[VMEM] * 3,
        out_specs=(VMEM,) * 3,
        compiler_params=LIMIT,
        cost_estimate=pl.CostEstimate(flops=0, bytes_accessed=2 * tiles.size * 2, transcendentals=0),
        name="prepare",
    )(tiles, own, target)


def partials_kernel(count, src_ref, wide_ref, *refs):
    block_refs, out_refs, held = refs[:count], refs[count:-1], refs[-1]
    depth = src_ref.shape[1]
    section, rep = lax.axis_index("section"), lax.axis_index("rep")
    for j in range(count):
        held[j] = block_refs[j][...]
    for j, out_ref in enumerate(out_refs):
        g = rep ^ j
        right = jnp.concatenate([held[src_ref[g, k] ^ section] for k in range(depth)], axis=0)
        out_ref[...] = jnp.dot(wide_ref[g], right, preferred_element_type=jnp.float32).astype(
            jnp.bfloat16
        )


def partials(sources, wide, blocks):
    many = wide.shape[0]
    tile, width = blocks[0].shape
    return pl.pallas_call(
        functools.partial(partials_kernel, len(blocks)),
        out_shape=[jax.ShapeDtypeStruct((tile, width), jnp.bfloat16)] * many,
        in_specs=[SMEM] + [VMEM] * (1 + len(blocks)),
        out_specs=[VMEM] * many,
        scratch_shapes=[pltpu.VMEM((len(blocks), tile, width), jnp.bfloat16)],
        compiler_params=LIMIT,
        name="partials",
    )(sources, wide, *blocks)


def swap(value, axis, j):
    return lax.ppermute(value, axis, [(i, i ^ j) for i in range(lax.axis_size(axis))])


def swaps_of(values, axis, steps):
    return [swap(value, axis, j) for value, j in zip(values, steps)]


def dense_kernel(n_part, weight_ref, cot_ref, placing_ref, *refs):
    part_refs, packed_ref, term_refs, term = refs[:n_part], refs[n_part], refs[n_part + 1 : -1], refs[-1]
    rep = lax.axis_index("rep")
    agg_b = sum(ref[...].astype(jnp.float32) for ref in part_refs).astype(jnp.bfloat16)
    pre = jnp.dot(agg_b, weight_ref[...], preferred_element_type=jnp.float32)
    sig = jax.nn.sigmoid(pre)
    factor = sig * (1.0 + pre * (1.0 - sig))
    grad_pre = (cot_ref[...].astype(jnp.float32) * factor).astype(jnp.bfloat16)
    whole = lax.dot_general(
        agg_b, grad_pre, (((0,), (0,)), ((), ())), preferred_element_type=jnp.float32
    )
    term[...] = whole.reshape(term.shape)
    for j, ref in enumerate(term_refs):
        ref[...] = term[rep ^ j].astype(jnp.bfloat16)
    output = (pre * sig).astype(jnp.bfloat16)
    packed_ref[...] = jnp.dot(placing_ref[...], output, preferred_element_type=jnp.float32).astype(
        jnp.bfloat16
    )


def dense(parts, weight, cotangent, placing):
    places, width = placing.shape[0], weight.shape[0]
    n_rep = len(parts)
    rows = width // n_rep
    return pl.pallas_call(
        functools.partial(dense_kernel, n_rep),
        out_shape=[jax.ShapeDtypeStruct((places, width), jnp.bfloat16)]
        + [jax.ShapeDtypeStruct((rows, width), jnp.bfloat16)] * n_rep,
        in_specs=[VMEM] * (3 + n_rep),
        out_specs=[VMEM] * (1 + n_rep),
        scratch_shapes=[pltpu.VMEM((n_rep, rows, width), jnp.float32)],
        compiler_params=LIMIT,
        name="dense",
    )(weight, cotangent, placing, *parts)


def add_kernel(*refs):
    total = sum(ref[...].astype(jnp.float32) for ref in refs[:-1])
    refs[-1][...] = total.astype(refs[-1].dtype)


def add(terms):
    return pl.pallas_call(
        add_kernel,
        out_shape=jax.ShapeDtypeStruct(terms[0].shape, jnp.bfloat16),
        in_specs=[VMEM] * len(terms),
        out_specs=VMEM,
        compiler_params=LIMIT,
        name="add",
    )(*terms)


def place_kernel(*refs):
    rep = lax.axis_index("rep")
    for j, ref in enumerate(refs[:-1]):
        refs[-1][rep ^ j] = ref[...].astype(jnp.float32)


def place(chunks):
    rows, width = chunks[0].shape
    return pl.pallas_call(
        place_kernel,
        out_shape=jax.ShapeDtypeStruct((len(chunks), rows, width), jnp.float32),
        in_specs=[VMEM] * len(chunks),
        out_specs=VMEM,
        compiler_params=LIMIT,
        name="place",
    )(*chunks)


def gather_blocks(features, axis, ready):
    n = lax.axis_size(axis)
    blocks = [None] * n
    blocks[0] = features
    for j in range(2, n, 2):
        blocks[j] = swap(features, axis, j)
    blocks[1] = swap(features, axis, 1)
    blocks[2::2], ready = lax.optimization_barrier((blocks[2::2], ready))
    for j in range(2, n, 2):
        blocks[j + 1] = swap(blocks[j], axis, 1)
    return blocks, ready


def pair_kernel(mine_ref, other_ref, *out_refs):
    for j, ref in enumerate(out_refs):
        ref[0] = mine_ref[j]
        ref[1] = other_ref[j]


def pair(mine, other):
    chips = mine.shape[0]
    return pl.pallas_call(
        pair_kernel,
        out_shape=[jax.ShapeDtypeStruct((2,) + mine.shape[1:], jnp.bfloat16)] * chips,
        in_specs=[VMEM] * 2,
        out_specs=[VMEM] * chips,
        compiler_params=LIMIT,
        name="pair",
    )(mine, other)


def unpack_kernel(*refs):
    section = lax.axis_index("section")
    for j, ref in enumerate(refs[:-1]):
        for i in range(2):
            refs[-1][section ^ (2 * j + i)] = ref[i]


def unpack(pairs):
    return pl.pallas_call(
        unpack_kernel,
        out_shape=jax.ShapeDtypeStruct((2 * len(pairs),) + pairs[0].shape[1:], jnp.bfloat16),
        in_specs=[VMEM] * len(pairs),
        out_specs=VMEM,
        compiler_params=LIMIT,
        name="unpack",
    )(*pairs)


def relay(packed, axis):
    chips = packed.shape[0] // 2
    pairs = list(pair(packed[:chips], swap(packed[chips:], axis, 1)))
    return unpack(pairs[:1] + [swap(pairs[j], axis, 2 * j) for j in range(1, chips)])


def per_device(features, adj_tiles, adj_src, cotangent, weight, destination):
    n_section, n_rep = lax.axis_size("section"), lax.axis_size("rep")
    rows_here, width = features.shape
    tile = adj_tiles.shape[3]
    slots = max(2, 2 * rows_here // n_section)
    target = destination.reshape(1, rows_here)
    wide, own, placing = prepare(adj_tiles[:, 0], features, target, n_section * slots, slots)
    blocks, (wide, own, placing) = gather_blocks(features, "section", (wide, own, placing))
    parts = list(partials(adj_src[:, 0], wide, [own] + blocks[1:]))
    across = range(1, n_rep)
    parts = parts[:1] + swaps_of(parts[1:], "rep", across)
    packed, *terms = dense(parts, weight, cotangent, placing)
    received = relay(packed.reshape(n_section, slots, width), "section")
    relaid = received.reshape(1, 1, n_section, slots, width)
    chunk = add(terms[:1] + swaps_of(terms[1:], "rep", across))
    chunk = add([chunk] + [swap(chunk, "section", j) for j in range(2, n_section, 2)])
    chunk = add([chunk, swap(chunk, "section", 1)])
    weight_grad = place([chunk] + [swap(chunk, "rep", j) for j in across])
    return (relaid, weight_grad.reshape(width, width))


def solution(mesh):
    placed = (
        P(("section", "rep"), None),
        P("section", "rep", None, None, None),
        P("section", "rep", None),
        P(("section", "rep"), None),
        P(),
        P(("section", "rep"), None),
    )
    return jax.shard_map(
        per_device,
        mesh=mesh,
        in_specs=placed,
        out_specs=(P("section", "rep", None, None, None), P()),
        check_vma=False,
    )
```

```python
import functools

import jax
import jax.numpy as jnp
from jax import lax
from jax.experimental import pallas as pl
from jax.experimental.pallas import tpu as pltpu
from jax.sharding import PartitionSpec as P

VMEM = pl.BlockSpec(memory_space=pltpu.VMEM)
LIMIT = pltpu.CompilerParams(vmem_limit_bytes=32 * 1024 * 1024)
SMEM = pl.BlockSpec(memory_space=pltpu.SMEM)


def across(n):
    return list(range(n - 1, 0, -1))


def prepare_kernel(slots, tiles_ref, own_ref, target_ref, wide_ref, held_ref, placing_ref):
    many, depth = tiles_ref.shape[:2]
    for g in range(many):
        wide_ref[g] = jnp.concatenate([tiles_ref[g, k] for k in range(depth)], axis=1)
    held_ref[...] = own_ref[...]
    places, rows = placing_ref.shape
    n_section = places // slots
    target = target_ref[...]
    hits = lax.broadcasted_iota(jnp.int32, (n_section, rows), 0) == target
    hits = jnp.where(hits, 1.0, 0.0)
    earlier = lax.broadcasted_iota(jnp.int32, (rows, rows), 0) < lax.broadcasted_iota(
        jnp.int32, (rows, rows), 1
    )
    earlier = jnp.where(earlier, 1.0, 0.0).astype(jnp.bfloat16)
    before = jnp.dot(hits.astype(jnp.bfloat16), earlier, preferred_element_type=jnp.float32)
    slot = jnp.sum(before * hits, axis=0, keepdims=True).astype(jnp.int32)
    apart = target ^ lax.axis_index("section")
    position = ((apart & 1) * (n_section // 2) + (apart >> 1)) * slots + slot
    placing = lax.broadcasted_iota(jnp.int32, (places, rows), 0) == position
    placing_ref[...] = jnp.where(placing, 1.0, 0.0).astype(jnp.bfloat16)


def prepare(tiles, own, target, places, slots):
    many, depth, tile, _ = tiles.shape
    return pl.pallas_call(
        functools.partial(prepare_kernel, slots),
        out_shape=(
            jax.ShapeDtypeStruct((many, tile, depth * tile), jnp.bfloat16),
            jax.ShapeDtypeStruct(own.shape, jnp.bfloat16),
            jax.ShapeDtypeStruct((places, target.shape[1]), jnp.bfloat16),
        ),
        in_specs=[VMEM] * 3,
        out_specs=(VMEM,) * 3,
        compiler_params=LIMIT,
        cost_estimate=pl.CostEstimate(flops=0, bytes_accessed=2 * tiles.size * 2, transcendentals=0),
        name="prepare",
    )(tiles, own, target)


def partials_kernel(count, src_ref, wide_ref, *refs):
    block_refs, out_refs, held = refs[:count], refs[count:-1], refs[-1]
    depth = src_ref.shape[1]
    section, rep = lax.axis_index("section"), lax.axis_index("rep")
    for j in range(count):
        held[j] = block_refs[j][...]
    for j, out_ref in zip([0] + across(len(out_refs)), out_refs):
        g = rep ^ j
        right = jnp.concatenate([held[src_ref[g, k] ^ section] for k in range(depth)], axis=0)
        out_ref[...] = jnp.dot(wide_ref[g], right, preferred_element_type=jnp.float32).astype(
            jnp.bfloat16
        )


def partials(sources, wide, blocks):
    many = wide.shape[0]
    tile, width = blocks[0].shape
    return pl.pallas_call(
        functools.partial(partials_kernel, len(blocks)),
        out_shape=[jax.ShapeDtypeStruct((tile, width), jnp.bfloat16)] * many,
        in_specs=[SMEM] + [VMEM] * (1 + len(blocks)),
        out_specs=[VMEM] * many,
        scratch_shapes=[pltpu.VMEM((len(blocks), tile, width), jnp.bfloat16)],
        compiler_params=LIMIT,
        name="partials",
    )(sources, wide, *blocks)


def swap(value, axis, j):
    return lax.ppermute(value, axis, [(i, i ^ j) for i in range(lax.axis_size(axis))])


def tree_sum(terms):
    while len(terms) > 1:
        terms = [terms[i] + terms[i + 1] for i in range(0, len(terms), 2)]
    return terms[0]


def dense_kernel(
    n_part, weight_ref, cot_ref, placing_ref, *refs
):
    part_refs, (same_ref, kept_ref, sent_ref, term) = refs[:n_part], refs[n_part:]
    core = lax.axis_index("section") & 1
    agg_b = tree_sum([ref[...].astype(jnp.float32) for ref in part_refs]).astype(jnp.bfloat16)
    pre = jnp.dot(agg_b, weight_ref[...], preferred_element_type=jnp.float32)
    sig = jax.nn.sigmoid(pre)
    factor = sig * (1.0 + pre * (1.0 - sig))
    grad_pre = (cot_ref[...].astype(jnp.float32) * factor).astype(jnp.bfloat16)
    whole = lax.dot_general(
        agg_b, grad_pre, (((0,), (0,)), ((), ())), preferred_element_type=jnp.float32
    )
    term[...] = whole.reshape(term.shape)
    kept_ref[...] = term[core]
    output = (pre * sig).astype(jnp.bfloat16)
    packed = jnp.dot(placing_ref[...], output, preferred_element_type=jnp.float32)
    half = packed.shape[0] // 2
    same_ref[...] = packed[:half].astype(jnp.bfloat16)
    sent_ref[:half] = packed[half:].astype(jnp.bfloat16)
    sent_ref[half:] = term[1 - core].astype(jnp.bfloat16)


def dense(parts, weight, cotangent, placing):
    places, width = placing.shape[0], weight.shape[0]
    return pl.pallas_call(
        functools.partial(dense_kernel, len(parts)),
        out_shape=(
            jax.ShapeDtypeStruct((places // 2, width), jnp.bfloat16),
            jax.ShapeDtypeStruct((width // 2, width), jnp.float32),
            jax.ShapeDtypeStruct((places // 2 + width // 2, width), jnp.bfloat16),
        ),
        in_specs=[VMEM] * (3 + len(parts)),
        out_specs=(VMEM,) * 3,
        scratch_shapes=[pltpu.VMEM((2, width // 2, width), jnp.float32)],
        compiler_params=LIMIT,
        name="dense",
    )(weight, cotangent, placing, *parts)


def split_kernel(kept_ref, came_ref, own_ref, *refs):
    out_refs, term = refs[:-1], refs[-1]
    rep = lax.axis_index("rep")
    half = kept_ref.shape[0]
    total = kept_ref[...] + came_ref[came_ref.shape[0] - half :].astype(jnp.float32)
    term[...] = total.reshape(term.shape)
    own_ref[...] = term[rep]
    for ref, j in zip(out_refs, across(len(out_refs) + 1)):
        ref[...] = term[rep ^ j].astype(jnp.bfloat16)


def split(kept, came, n_rep):
    half, width = kept.shape
    rows = half // n_rep
    return pl.pallas_call(
        split_kernel,
        out_shape=[jax.ShapeDtypeStruct((rows, width), jnp.float32)]
        + [jax.ShapeDtypeStruct((rows, width), jnp.bfloat16)] * (n_rep - 1),
        in_specs=[VMEM] * 2,
        out_specs=[VMEM] * n_rep,
        scratch_shapes=[pltpu.VMEM((n_rep, rows, width), jnp.float32)],
        compiler_params=LIMIT,
        name="split",
    )(kept, came)


def message_kernel(n_term, slots, same_ref, came_ref, *refs):
    term_refs, out_refs = refs[:n_term], refs[n_term:]
    chunk = sum(ref[...].astype(jnp.float32) for ref in term_refs).astype(jnp.bfloat16)
    for j, ref in zip([0] + across(len(out_refs)), out_refs):
        ref[:slots] = same_ref[j * slots : (j + 1) * slots]
        ref[slots : 2 * slots] = came_ref[j * slots : (j + 1) * slots]
        ref[2 * slots :] = chunk


def message(same, came, terms, slots):
    chips = same.shape[0] // slots
    rows, width = terms[0].shape
    return pl.pallas_call(
        functools.partial(message_kernel, len(terms), slots),
        out_shape=[jax.ShapeDtypeStruct((2 * slots + rows, width), jnp.bfloat16)] * chips,
        in_specs=[VMEM] * (2 + len(terms)),
        out_specs=[VMEM] * chips,
        compiler_params=LIMIT,
        name="message",
    )(same, came, *terms)


def chunk_kernel(start, *refs):
    by_xor = [refs[0]] + [None] * (len(refs) - 2)
    for ref, j in zip(refs[1:-1], across(len(by_xor))):
        by_xor[j] = ref
    total = tree_sum([ref[start:].astype(jnp.float32) for ref in by_xor])
    refs[-1][...] = total.astype(jnp.bfloat16)


def chunk_of(messages, start):
    rows, width = messages[0].shape
    return pl.pallas_call(
        functools.partial(chunk_kernel, start),
        out_shape=jax.ShapeDtypeStruct((rows - start, width), jnp.bfloat16),
        in_specs=[VMEM] * len(messages),
        out_specs=VMEM,
        compiler_params=LIMIT,
        name="chunk",
    )(*messages)


def unpack_kernel(slots, *refs):
    section = lax.axis_index("section")
    for j, ref in zip([0] + across(len(refs) - 1), refs[:-1]):
        refs[-1][section ^ (2 * j)] = ref[:slots]
        refs[-1][section ^ (2 * j + 1)] = ref[slots : 2 * slots]


def unpack(messages, slots):
    width = messages[0].shape[1]
    return pl.pallas_call(
        functools.partial(unpack_kernel, slots),
        out_shape=jax.ShapeDtypeStruct((2 * len(messages), slots, width), jnp.bfloat16),
        in_specs=[VMEM] * len(messages),
        out_specs=VMEM,
        compiler_params=LIMIT,
        name="unpack",
    )(*messages)


def place_kernel(*refs):
    rep = lax.axis_index("rep")
    for j, ref in zip([0] + across(len(refs) - 1), refs[:-1]):
        refs[-1][rep ^ j] = ref[...]


def place(chunks):
    rows, width = chunks[0].shape
    return pl.pallas_call(
        place_kernel,
        out_shape=jax.ShapeDtypeStruct((len(chunks), rows, width), jnp.bfloat16),
        in_specs=[VMEM] * len(chunks),
        out_specs=VMEM,
        compiler_params=LIMIT,
        name="place",
    )(*chunks)


def finish_kernel(own_ref, came_ref, out_ref):
    core = lax.axis_index("section") & 1
    out_ref[core] = own_ref[...].astype(jnp.float32)
    out_ref[1 - core] = came_ref[...].astype(jnp.float32)


def finish(own, came):
    return pl.pallas_call(
        finish_kernel,
        out_shape=jax.ShapeDtypeStruct((2,) + own.shape, jnp.float32),
        in_specs=[VMEM] * 2,
        out_specs=VMEM,
        compiler_params=LIMIT,
        name="finish",
    )(own, came)


def gather_blocks(features, axis, ready):
    n = lax.axis_size(axis)
    blocks = [None] * n
    blocks[0] = features
    for j in range(2, n, 2):
        blocks[j] = swap(features, axis, j)
    blocks[1] = swap(features, axis, 1)
    blocks[2::2], ready = lax.optimization_barrier((blocks[2::2], ready))
    for j in range(2, n, 2):
        blocks[j + 1] = swap(blocks[j], axis, 1)
    return blocks, ready


def per_device(features, adj_tiles, adj_src, cotangent, weight, destination):
    n_section, n_rep = lax.axis_size("section"), lax.axis_size("rep")
    rows_here, width = features.shape
    tile = adj_tiles.shape[3]
    slots = max(2, 2 * rows_here // n_section)
    target = destination.reshape(1, rows_here)
    wide, own, placing = prepare(adj_tiles[:, 0], features, target, n_section * slots, slots)
    blocks, (wide, own, placing) = gather_blocks(features, "section", (wide, own, placing))
    parts = list(partials(adj_src[:, 0], wide, [own] + blocks[1:]))
    others, chips = across(n_rep), across(n_section // 2)
    parts = [swap(part, "rep", j) if j else part for part, j in zip(parts, [0] + others)]
    parts = [parts[0]] + parts[:0:-1]
    same, kept, sent = dense(parts, weight, cotangent, placing)
    came = swap(sent, "section", 1)
    own, *terms = split(kept, came, n_rep)
    terms = [own] + [swap(term, "rep", j) for term, j in zip(terms, others)]
    messages = list(message(same, came, terms, slots))
    messages = messages[:1] + [swap(m, "section", 2 * j) for m, j in zip(messages[1:], chips)]
    chunk = chunk_of(messages, 2 * slots)
    relaid = unpack(messages, slots).reshape(1, 1, n_section, slots, width)
    half = place([chunk] + [swap(chunk, "rep", j) for j in others]).reshape(width // 2, width)
    weight_grad = finish(half, swap(half, "section", 1))
    return (relaid, weight_grad.reshape(width, width))


def solution(mesh):
    placed = (
        P(("section", "rep"), None),
        P("section", "rep", None, None, None),
        P("section", "rep", None),
        P(("section", "rep"), None),
        P(),
        P(("section", "rep"), None),
    )
    return jax.shard_map(
        per_device,
        mesh=mesh,
        in_specs=placed,
        out_specs=(P("section", "rep", None, None, None), P()),
        check_vma=False,
    )
```

```python
import functools

import jax
import jax.numpy as jnp
from jax import lax
from jax.experimental import pallas as pl
from jax.experimental.pallas import tpu as pltpu
from jax.sharding import PartitionSpec as P

VMEM = pl.BlockSpec(memory_space=pltpu.VMEM)
LIMIT = pltpu.CompilerParams(vmem_limit_bytes=32 * 1024 * 1024)
SMEM = pl.BlockSpec(memory_space=pltpu.SMEM)


def across(n):
    return list(range(n - 1, 0, -1))


def prepare_kernel(slots, tiles_ref, own_ref, target_ref, wide_ref, held_ref, placing_ref):
    many, depth = tiles_ref.shape[:2]
    for g in range(many):
        wide_ref[g] = jnp.concatenate([tiles_ref[g, k] for k in range(depth)], axis=1)
    held_ref[...] = own_ref[...]
    places, rows = placing_ref.shape
    n_section = places // slots
    target = target_ref[...]
    hits = lax.broadcasted_iota(jnp.int32, (n_section, rows), 0) == target
    hits = jnp.where(hits, 1.0, 0.0)
    earlier = lax.broadcasted_iota(jnp.int32, (rows, rows), 0) < lax.broadcasted_iota(
        jnp.int32, (rows, rows), 1
    )
    earlier = jnp.where(earlier, 1.0, 0.0).astype(jnp.bfloat16)
    before = jnp.dot(hits.astype(jnp.bfloat16), earlier, preferred_element_type=jnp.float32)
    slot = jnp.sum(before * hits, axis=0, keepdims=True).astype(jnp.int32)
    chip = lax.axis_index("section") & -2
    position = (target ^ chip) * slots + slot
    placing = lax.broadcasted_iota(jnp.int32, (places, rows), 0) == position
    placing_ref[...] = jnp.where(placing, 1.0, 0.0).astype(jnp.bfloat16)


def prepare(tiles, own, target, places, slots):
    many, depth, tile, _ = tiles.shape
    return pl.pallas_call(
        functools.partial(prepare_kernel, slots),
        out_shape=(
            jax.ShapeDtypeStruct((many, tile, depth * tile), jnp.bfloat16),
            jax.ShapeDtypeStruct(own.shape, jnp.bfloat16),
            jax.ShapeDtypeStruct((places, target.shape[1]), jnp.bfloat16),
        ),
        in_specs=[VMEM] * 3,
        out_specs=(VMEM,) * 3,
        compiler_params=LIMIT,
        cost_estimate=pl.CostEstimate(flops=0, bytes_accessed=2 * tiles.size * 2, transcendentals=0),
        name="prepare",
    )(tiles, own, target)


def partials_kernel(count, src_ref, wide_ref, *refs):
    block_refs, out_refs, held = refs[:count], refs[count:-1], refs[-1]
    depth = src_ref.shape[1]
    section, rep = lax.axis_index("section"), lax.axis_index("rep")
    for j in range(count):
        held[j] = block_refs[j][...]
    for j, out_ref in zip([0] + across(len(out_refs)), out_refs):
        g = rep ^ j
        right = jnp.concatenate([held[src_ref[g, k] ^ section] for k in range(depth)], axis=0)
        out_ref[...] = jnp.dot(wide_ref[g], right, preferred_element_type=jnp.float32).astype(
            jnp.bfloat16
        )


def partials(sources, wide, blocks):
    many = wide.shape[0]
    tile, width = blocks[0].shape
    return pl.pallas_call(
        functools.partial(partials_kernel, len(blocks)),
        out_shape=[jax.ShapeDtypeStruct((tile, width), jnp.bfloat16)] * many,
        in_specs=[SMEM] + [VMEM] * (1 + len(blocks)),
        out_specs=[VMEM] * many,
        scratch_shapes=[pltpu.VMEM((len(blocks), tile, width), jnp.bfloat16)],
        compiler_params=LIMIT,
        name="partials",
    )(sources, wide, *blocks)


def swap(value, axis, j):
    return lax.ppermute(value, axis, [(i, i ^ j) for i in range(lax.axis_size(axis))])


def tree_sum(terms):
    while len(terms) > 1:
        terms = [terms[i] + terms[i + 1] for i in range(0, len(terms), 2)]
    return terms[0]


def tree_sum(terms):
    while len(terms) > 1:
        terms = [terms[i] + terms[i + 1] for i in range(0, len(terms), 2)]
    return terms[0]


def dense_kernel(n_part, weight_ref, cot_ref, placing_ref, *refs):
    part_refs, (packed_ref, term_ref, sent_ref) = refs[:n_part], refs[n_part:]
    core = lax.axis_index("section") & 1
    agg_b = tree_sum([ref[...].astype(jnp.float32) for ref in part_refs]).astype(jnp.bfloat16)
    pre = jnp.dot(agg_b, weight_ref[...], preferred_element_type=jnp.float32)
    sig = jax.nn.sigmoid(pre)
    factor = sig * (1.0 + pre * (1.0 - sig))
    grad_pre = (cot_ref[...].astype(jnp.float32) * factor).astype(jnp.bfloat16)
    term = lax.dot_general(
        agg_b, grad_pre, (((0,), (0,)), ((), ())), preferred_element_type=jnp.float32
    )
    term_ref[...] = term
    output = (pre * sig).astype(jnp.bfloat16)
    packed = jnp.dot(placing_ref[...], output, preferred_element_type=jnp.float32)
    packed = packed.astype(jnp.bfloat16)
    packed_ref[...] = packed

    @pl.when(core == 0)
    def _():
        sent_ref[: term.shape[0]] = term.astype(jnp.bfloat16)

    @pl.when(core == 1)
    def _():
        sent_ref[: packed.shape[0]] = packed


def dense(parts, weight, cotangent, placing):
    places, width = placing.shape[0], weight.shape[0]
    return pl.pallas_call(
        functools.partial(dense_kernel, len(parts)),
        out_shape=(
            jax.ShapeDtypeStruct((places, width), jnp.bfloat16),
            jax.ShapeDtypeStruct((width, width), jnp.float32),
            jax.ShapeDtypeStruct((max(places, width), width), jnp.bfloat16),
        ),
        in_specs=[VMEM] * (3 + len(parts)),
        out_specs=(VMEM,) * 3,
        compiler_params=LIMIT,
        name="dense",
    )(weight, cotangent, placing, *parts)


def split_kernel(n_rep, packed_ref, term_ref, came_ref, own_ref, *refs):
    chunk_refs, message_refs, term = refs[: n_rep - 1], refs[n_rep - 1 : -1], refs[-1]
    rep = lax.axis_index("rep")
    width = term_ref.shape[0]
    total = term_ref[...] + came_ref[:width].astype(jnp.float32)
    term[...] = total.reshape(term.shape)
    own_ref[...] = term[rep]
    for ref, j in zip(chunk_refs, across(n_rep)):
        ref[...] = term[rep ^ j].astype(jnp.bfloat16)
    rows = packed_ref.shape[0] // len(message_refs)
    for ref, j in zip(message_refs, [0] + across(len(message_refs))):
        ref[:rows] = packed_ref[j * rows : (j + 1) * rows]
        ref[rows:] = came_ref[j * rows : (j + 1) * rows]


def split(packed, term, came, n_rep, chips):
    places, width = packed.shape
    chunk = (width // n_rep, width)
    return pl.pallas_call(
        functools.partial(split_kernel, n_rep),
        out_shape=[jax.ShapeDtypeStruct(chunk, jnp.float32)]
        + [jax.ShapeDtypeStruct(chunk, jnp.bfloat16)] * (n_rep - 1)
        + [jax.ShapeDtypeStruct((2 * places // chips, width), jnp.bfloat16)] * chips,
        in_specs=[VMEM] * 3,
        out_specs=[VMEM] * (n_rep + chips),
        scratch_shapes=[pltpu.VMEM((n_rep,) + chunk, jnp.float32)],
        compiler_params=LIMIT,
        name="split",
    )(packed, term, came)


def add_kernel(*refs):
    refs[-1][...] = tree_sum([ref[...].astype(jnp.float32) for ref in refs[:-1]]).astype(jnp.bfloat16)


def add(terms):
    return pl.pallas_call(
        add_kernel,
        out_shape=jax.ShapeDtypeStruct(terms[0].shape, jnp.bfloat16),
        in_specs=[VMEM] * len(terms),
        out_specs=VMEM,
        compiler_params=LIMIT,
        name="add",
    )(*terms)


def unpack_kernel(slots, *refs):
    message_refs, out_refs = refs[:-2], refs[-2:]
    chip = lax.axis_index("section") & -2
    for j, ref in zip([0] + across(len(message_refs)), message_refs):
        for source in range(2):
            for core in range(2):
                start = (2 * source + core) * slots
                out_refs[core][chip ^ (2 * j) | source] = ref[start : start + slots]


def unpack(messages, slots):
    width = messages[0].shape[1]
    n_section = 2 * len(messages)
    return pl.pallas_call(
        functools.partial(unpack_kernel, slots),
        out_shape=[jax.ShapeDtypeStruct((n_section, slots, width), jnp.bfloat16)] * 2,
        in_specs=[VMEM] * len(messages),
        out_specs=[VMEM] * 2,
        compiler_params=LIMIT,
        name="unpack",
    )(*messages)


def place_kernel(other_ref, *refs):
    chunk_refs, (whole_ref, sent_ref) = refs[:-2], refs[-2:]
    rep, core = lax.axis_index("rep"), lax.axis_index("section") & 1
    for j, ref in enumerate(chunk_refs):
        whole_ref[rep ^ j] = ref[...]

    @pl.when(core == 0)
    def _():
        sent_ref[: other_ref.shape[0]] = other_ref[...]

    @pl.when(core == 1)
    def _():
        n_rep, rows, _ = whole_ref.shape
        for r in range(n_rep):
            sent_ref[r * rows : (r + 1) * rows] = whole_ref[r]


def place(chunks, other):
    rows, width = chunks[0].shape
    return pl.pallas_call(
        place_kernel,
        out_shape=(
            jax.ShapeDtypeStruct((len(chunks), rows, width), jnp.bfloat16),
            jax.ShapeDtypeStruct((max(len(chunks) * rows, other.shape[0]), width), jnp.bfloat16),
        ),
        in_specs=[VMEM] * (1 + len(chunks)),
        out_specs=(VMEM,) * 2,
        compiler_params=LIMIT,
        name="place",
    )(other, *chunks)


def finish_kernel(whole_ref, mine_ref, came_ref, relaid_ref, grad_ref):
    core = lax.axis_index("section") & 1

    @pl.when(core == 0)
    def _():
        grad_ref[...] = came_ref[: grad_ref.shape[0]].astype(jnp.float32)
        relaid_ref[...] = mine_ref[...]

    @pl.when(core == 1)
    def _():
        grad_ref[...] = whole_ref[...].astype(jnp.float32)
        relaid_ref[...] = came_ref[: relaid_ref.shape[0]]


def finish(whole, mine, came):
    return pl.pallas_call(
        finish_kernel,
        out_shape=(
            jax.ShapeDtypeStruct(mine.shape, jnp.bfloat16),
            jax.ShapeDtypeStruct(whole.shape, jnp.float32),
        ),
        in_specs=[VMEM] * 3,
        out_specs=(VMEM,) * 2,
        compiler_params=LIMIT,
        name="finish",
    )(whole, mine, came)


def swap_on_core(value, core, section_xor, rep_xor):
    n_rep = lax.axis_size("rep")
    pairs = [
        (s * n_rep + r, (s ^ section_xor) * n_rep + (r ^ rep_xor))
        for s in range(core, lax.axis_size("section"), 2)
        for r in range(n_rep)
    ]
    return lax.ppermute(value, ("section", "rep"), pairs)


def gather_blocks(features, axis, ready):
    n = lax.axis_size(axis)
    blocks = [None] * n
    blocks[0] = features
    for j in range(2, n, 2):
        blocks[j] = swap(features, axis, j)
    blocks[1] = swap(features, axis, 1)
    blocks[2], ready = lax.optimization_barrier((blocks[2], ready))
    for j in range(2, n, 2):
        blocks[j + 1] = swap(blocks[j], axis, 1)
    return blocks, ready


def per_device(features, adj_tiles, adj_src, cotangent, weight, destination):
    n_section, n_rep = lax.axis_size("section"), lax.axis_size("rep")
    rows_here, width = features.shape
    tile = adj_tiles.shape[3]
    slots = max(2, 2 * rows_here // n_section)
    target = destination.reshape(1, rows_here)
    wide, own, placing = prepare(adj_tiles[:, 0], features, target, n_section * slots, slots)
    blocks, (wide, own, placing) = gather_blocks(features, "section", (wide, own, placing))
    parts = list(partials(adj_src[:, 0], wide, [own] + blocks[1:]))
    others = across(n_rep)
    parts = [swap(part, "rep", j) if j else part for part, j in zip(parts, [0] + others)]
    packed, term, sent = dense(parts, weight, cotangent, placing)
    came = swap(sent, "section", 1)
    chips = n_section // 2
    own, *rest = split(packed, term, came, n_rep, chips)
    terms, messages = rest[: n_rep - 1], rest[n_rep - 1 :]
    terms = [swap_on_core(t, 1, 0, j) for t, j in zip(terms, others)]
    chunk = add([own] + terms)
    others = across(chips)
    messages = messages[:1] + [swap_on_core(m, 0, 2 * j, 0) for m, j in zip(messages[1:], others)]
    chunk = add([chunk] + [swap_on_core(chunk, 1, 2 * j, 0) for j in range(1, chips)])
    mine, other = unpack(messages, slots)
    chunks = [chunk] + [swap_on_core(chunk, 1, 0, j) for j in range(1, n_rep)]
    whole, sent = place(chunks, other.reshape(n_section * slots, width))
    came = swap(sent, "section", 1)
    relaid, weight_grad = finish(
        whole.reshape(width, width), mine.reshape(n_section * slots, width), came
    )
    return (relaid.reshape(1, 1, n_section, slots, width), weight_grad)


def solution(mesh):
    placed = (
        P(("section", "rep"), None),
        P("section", "rep", None, None, None),
        P("section", "rep", None),
        P(("section", "rep"), None),
        P(),
        P(("section", "rep"), None),
    )
    return jax.shard_map(
        per_device,
        mesh=mesh,
        in_specs=placed,
        out_specs=(P("section", "rep", None, None, None), P()),
        check_vma=False,
    )
```

```python
import functools

import jax
import jax.numpy as jnp
from jax import lax
from jax.experimental import pallas as pl
from jax.experimental.pallas import tpu as pltpu
from jax.sharding import PartitionSpec as P

VMEM = pl.BlockSpec(memory_space=pltpu.VMEM)
LIMIT = pltpu.CompilerParams(vmem_limit_bytes=32 * 1024 * 1024)
SMEM = pl.BlockSpec(memory_space=pltpu.SMEM)


def across(n):
    return list(range(n - 1, 0, -1))


def prepare_kernel(slots, tiles_ref, own_ref, target_ref, wide_ref, held_ref, placing_ref):
    many, depth = tiles_ref.shape[:2]
    for g in range(many):
        wide_ref[g] = jnp.concatenate([tiles_ref[g, k] for k in range(depth)], axis=1)
    held_ref[...] = own_ref[...]
    places, rows = placing_ref.shape
    n_section = places // slots
    target = target_ref[...]
    hits = lax.broadcasted_iota(jnp.int32, (n_section, rows), 0) == target
    hits = jnp.where(hits, 1.0, 0.0)
    earlier = lax.broadcasted_iota(jnp.int32, (rows, rows), 0) < lax.broadcasted_iota(
        jnp.int32, (rows, rows), 1
    )
    earlier = jnp.where(earlier, 1.0, 0.0).astype(jnp.bfloat16)
    before = jnp.dot(hits.astype(jnp.bfloat16), earlier, preferred_element_type=jnp.float32)
    slot = jnp.sum(before * hits, axis=0, keepdims=True).astype(jnp.int32)
    chip = lax.axis_index("section") & -2
    position = (target ^ chip) * slots + slot
    placing = lax.broadcasted_iota(jnp.int32, (places, rows), 0) == position
    placing_ref[...] = jnp.where(placing, 1.0, 0.0).astype(jnp.bfloat16)


def prepare(tiles, own, target, places, slots):
    many, depth, tile, _ = tiles.shape
    return pl.pallas_call(
        functools.partial(prepare_kernel, slots),
        out_shape=(
            jax.ShapeDtypeStruct((many, tile, depth * tile), jnp.bfloat16),
            jax.ShapeDtypeStruct(own.shape, jnp.bfloat16),
            jax.ShapeDtypeStruct((places, target.shape[1]), jnp.bfloat16),
        ),
        in_specs=[VMEM] * 3,
        out_specs=(VMEM,) * 3,
        compiler_params=LIMIT,
        cost_estimate=pl.CostEstimate(flops=0, bytes_accessed=2 * tiles.size * 2, transcendentals=0),
        name="prepare",
    )(tiles, own, target)


def partials_kernel(count, src_ref, wide_ref, *refs):
    block_refs, out_refs, held = refs[:count], refs[count:-1], refs[-1]
    depth = src_ref.shape[1]
    section, rep = lax.axis_index("section"), lax.axis_index("rep")
    for j in range(count):
        held[j] = block_refs[j][...]
    for j, out_ref in zip([0] + across(len(out_refs)), out_refs):
        g = rep ^ j
        right = jnp.concatenate([held[src_ref[g, k] ^ section] for k in range(depth)], axis=0)
        out_ref[...] = jnp.dot(wide_ref[g], right, preferred_element_type=jnp.float32).astype(
            jnp.bfloat16
        )


def partials(sources, wide, blocks):
    many = wide.shape[0]
    tile, width = blocks[0].shape
    return pl.pallas_call(
        functools.partial(partials_kernel, len(blocks)),
        out_shape=[jax.ShapeDtypeStruct((tile, width), jnp.bfloat16)] * many,
        in_specs=[SMEM] + [VMEM] * (1 + len(blocks)),
        out_specs=[VMEM] * many,
        scratch_shapes=[pltpu.VMEM((len(blocks), tile, width), jnp.bfloat16)],
        compiler_params=LIMIT,
        name="partials",
    )(sources, wide, *blocks)


def swap(value, axis, j):
    return lax.ppermute(value, axis, [(i, i ^ j) for i in range(lax.axis_size(axis))])


def tree_sum(terms):
    while len(terms) > 1:
        terms = [terms[i] + terms[i + 1] for i in range(0, len(terms), 2)]
    return terms[0]


def tree_sum(terms):
    while len(terms) > 1:
        terms = [terms[i] + terms[i + 1] for i in range(0, len(terms), 2)]
    return terms[0]


def dense_kernel(n_part, weight_ref, cot_ref, placing_ref, *refs):
    part_refs, (packed_ref, term_ref, sent_ref) = refs[:n_part], refs[n_part:]
    core = lax.axis_index("section") & 1
    agg_b = tree_sum([ref[...].astype(jnp.float32) for ref in part_refs]).astype(jnp.bfloat16)
    pre = jnp.dot(agg_b, weight_ref[...], preferred_element_type=jnp.float32)
    sig = jax.nn.sigmoid(pre)
    factor = sig * (1.0 + pre * (1.0 - sig))
    grad_pre = (cot_ref[...].astype(jnp.float32) * factor).astype(jnp.bfloat16)
    term = lax.dot_general(
        agg_b, grad_pre, (((0,), (0,)), ((), ())), preferred_element_type=jnp.float32
    )
    term_ref[...] = term
    output = (pre * sig).astype(jnp.bfloat16)
    packed = jnp.dot(placing_ref[...], output, preferred_element_type=jnp.float32)
    packed = packed.astype(jnp.bfloat16)
    packed_ref[...] = packed

    @pl.when(core == 0)
    def _():
        sent_ref[: term.shape[0]] = term.astype(jnp.bfloat16)

    @pl.when(core == 1)
    def _():
        sent_ref[: packed.shape[0]] = packed


def dense(parts, weight, cotangent, placing):
    places, width = placing.shape[0], weight.shape[0]
    return pl.pallas_call(
        functools.partial(dense_kernel, len(parts)),
        out_shape=(
            jax.ShapeDtypeStruct((places, width), jnp.bfloat16),
            jax.ShapeDtypeStruct((width, width), jnp.float32),
            jax.ShapeDtypeStruct((max(places, width), width), jnp.bfloat16),
        ),
        in_specs=[VMEM] * (3 + len(parts)),
        out_specs=(VMEM,) * 3,
        compiler_params=LIMIT,
        name="dense",
    )(weight, cotangent, placing, *parts)


def split_kernel(packed_ref, term_ref, came_ref, own_ref, *refs):
    out_refs, term = refs[:-1], refs[-1]
    rep, core = lax.axis_index("rep"), lax.axis_index("section") & 1
    n_rep, chunk = term.shape[:2]
    total = term_ref[...] + came_ref[: n_rep * chunk].astype(jnp.float32)
    term[...] = total.reshape(term.shape)
    own_ref[...] = term[rep]
    rows = 2 * packed_ref.shape[0] // lax.axis_size("section")

    @pl.when(core == 1)
    def _():
        for ref, j in zip(out_refs, across(len(out_refs) + 1)):
            ref[:chunk] = term[rep ^ (j % n_rep)].astype(jnp.bfloat16)

    @pl.when(core == 0)
    def _():
        for ref, j in zip(out_refs, across(len(out_refs) + 1)):
            start = j * rows % packed_ref.shape[0]
            ref[:rows] = packed_ref[start : start + rows]


def split(packed, term, came, n_rep, chips):
    places, width = packed.shape
    chunk = width // n_rep
    out = jax.ShapeDtypeStruct((max(chunk, places // chips), width), jnp.bfloat16)
    many = max(n_rep, chips)
    return pl.pallas_call(
        split_kernel,
        out_shape=[jax.ShapeDtypeStruct((chunk, width), jnp.float32)] + [out] * (many - 1),
        in_specs=[VMEM] * 3,
        out_specs=[VMEM] * many,
        scratch_shapes=[pltpu.VMEM((n_rep, chunk, width), jnp.float32)],
        compiler_params=LIMIT,
        name="split",
    )(packed, term, came)


def second_kernel(n_rep, packed_ref, came_ref, own_ref, *refs):
    term_refs, chunk_ref, out_refs = refs[: n_rep - 1], refs[n_rep - 1], refs[n_rep:]
    core = lax.axis_index("section") & 1
    chunk = own_ref.shape[0]
    terms = [own_ref[...]] + [ref[:chunk].astype(jnp.float32) for ref in term_refs]
    total = tree_sum(terms).astype(jnp.bfloat16)
    chunk_ref[...] = total
    rows = packed_ref.shape[0] // (len(out_refs) + 1)

    @pl.when(core == 1)
    def _():
        for ref in out_refs:
            ref[:chunk] = total

    @pl.when(core == 0)
    def _():
        for ref, j in zip(out_refs, across(len(out_refs) + 1)):
            ref[:rows] = came_ref[j * rows : (j + 1) * rows]


def second(packed, came, own, terms, chips):
    places, width = packed.shape
    chunk = own.shape[0]
    out = jax.ShapeDtypeStruct((max(chunk, places // chips), width), jnp.bfloat16)
    return pl.pallas_call(
        functools.partial(second_kernel, len(terms) + 1),
        out_shape=[jax.ShapeDtypeStruct((chunk, width), jnp.bfloat16)] + [out] * (chips - 1),
        in_specs=[VMEM] * (3 + len(terms)),
        out_specs=[VMEM] * chips,
        compiler_params=LIMIT,
        name="second",
    )(packed, came, own, *terms)


def add_kernel(own_ref, *refs):
    chunk = own_ref.shape[0]
    by_xor = [own_ref] + list(refs[-2::-1])
    total = tree_sum([ref[:chunk].astype(jnp.float32) for ref in by_xor])
    refs[-1][...] = total.astype(jnp.bfloat16)


def add(own, others):
    return pl.pallas_call(
        add_kernel,
        out_shape=jax.ShapeDtypeStruct(own.shape, jnp.bfloat16),
        in_specs=[VMEM] * (1 + len(others)),
        out_specs=VMEM,
        compiler_params=LIMIT,
        name="add",
    )(own, *others)


def unpack_kernel(slots, chips, packed_ref, came_ref, *refs):
    out_refs = refs[-2:]
    chip = lax.axis_index("section") & -2
    sources = (
        [packed_ref] + list(refs[: chips - 1]),
        [came_ref] + list(refs[chips - 1 : -2]),
    )
    for source in range(2):
        for ref, j in zip(sources[source], [0] + across(chips)):
            for core in range(2):
                rows = ref[core * slots : (core + 1) * slots]
                out_refs[core][chip ^ (2 * j) | source] = rows


def unpack(packed, came, first, later, slots):
    width = packed.shape[1]
    chips = len(first) + 1
    return pl.pallas_call(
        functools.partial(unpack_kernel, slots, chips),
        out_shape=[jax.ShapeDtypeStruct((2 * chips, slots, width), jnp.bfloat16)] * 2,
        in_specs=[VMEM] * (2 * chips),
        out_specs=[VMEM] * 2,
        compiler_params=LIMIT,
        name="unpack",
    )(packed, came, *first, *later)


def place_kernel(other_ref, *refs):
    chunk_refs, (whole_ref, sent_ref) = refs[:-2], refs[-2:]
    rep, core = lax.axis_index("rep"), lax.axis_index("section") & 1
    for j, ref in enumerate(chunk_refs):
        whole_ref[rep ^ j] = ref[...]

    @pl.when(core == 0)
    def _():
        sent_ref[: other_ref.shape[0]] = other_ref[...]

    @pl.when(core == 1)
    def _():
        n_rep, rows, _ = whole_ref.shape
        for r in range(n_rep):
            sent_ref[r * rows : (r + 1) * rows] = whole_ref[r]


def place(chunks, other):
    rows, width = chunks[0].shape
    return pl.pallas_call(
        place_kernel,
        out_shape=(
            jax.ShapeDtypeStruct((len(chunks), rows, width), jnp.bfloat16),
            jax.ShapeDtypeStruct((max(len(chunks) * rows, other.shape[0]), width), jnp.bfloat16),
        ),
        in_specs=[VMEM] * (1 + len(chunks)),
        out_specs=(VMEM,) * 2,
        compiler_params=LIMIT,
        name="place",
    )(other, *chunks)


def finish_kernel(whole_ref, mine_ref, came_ref, relaid_ref, grad_ref):
    core = lax.axis_index("section") & 1

    @pl.when(core == 0)
    def _():
        grad_ref[...] = came_ref[: grad_ref.shape[0]].astype(jnp.float32)
        relaid_ref[...] = mine_ref[...]

    @pl.when(core == 1)
    def _():
        grad_ref[...] = whole_ref[...].astype(jnp.float32)
        relaid_ref[...] = came_ref[: relaid_ref.shape[0]]


def finish(whole, mine, came):
    return pl.pallas_call(
        finish_kernel,
        out_shape=(
            jax.ShapeDtypeStruct(mine.shape, jnp.bfloat16),
            jax.ShapeDtypeStruct(whole.shape, jnp.float32),
        ),
        in_specs=[VMEM] * 3,
        out_specs=(VMEM,) * 2,
        compiler_params=LIMIT,
        name="finish",
    )(whole, mine, came)


def swap_by_core(value, j):
    n_section, n_rep = lax.axis_size("section"), lax.axis_size("rep")
    along, side = 2 * j % n_section, j % n_rep
    pairs = [
        (s * n_rep + r, s * n_rep + (r ^ side) if s & 1 else (s ^ along) * n_rep + r)
        for s in range(n_section)
        for r in range(n_rep)
    ]
    return lax.ppermute(value, ("section", "rep"), pairs)


def gather_blocks(features, axis, ready):
    n = lax.axis_size(axis)
    blocks = [None] * n
    blocks[0] = features
    for j in range(2, n, 2):
        blocks[j] = swap(features, axis, j)
    blocks[1] = swap(features, axis, 1)
    blocks[2], ready = lax.optimization_barrier((blocks[2], ready))
    for j in range(2, n, 2):
        blocks[j + 1] = swap(blocks[j], axis, 1)
    return blocks, ready


def per_device(features, adj_tiles, adj_src, cotangent, weight, destination):
    n_section, n_rep = lax.axis_size("section"), lax.axis_size("rep")
    rows_here, width = features.shape
    tile = adj_tiles.shape[3]
    slots = max(2, 2 * rows_here // n_section)
    target = destination.reshape(1, rows_here)
    wide, own, placing = prepare(adj_tiles[:, 0], features, target, n_section * slots, slots)
    blocks, (wide, own, placing) = gather_blocks(features, "section", (wide, own, placing))
    parts = list(partials(adj_src[:, 0], wide, [own] + blocks[1:]))
    others = across(n_rep)
    parts = [swap(part, "rep", j) if j else part for part, j in zip(parts, [0] + others)]
    packed, term, sent = dense(parts, weight, cotangent, placing)
    came = swap(sent, "section", 1)
    chips = n_section // 2
    own, *first = split(packed, term, came, n_rep, chips)
    first = [swap_by_core(value, j) for value, j in zip(first, across(len(first) + 1))]
    chunk, *later = second(packed, came, own, first[1 - n_rep :], chips)
    later = [swap(value, "section", 2 * j) for value, j in zip(later, across(chips))]
    chunk = add(chunk, later)
    mine, other = unpack(packed, came, first[1 - chips :], later, slots)
    chunks = [chunk] + [swap(chunk, "rep", j) for j in range(1, n_rep)]
    whole, sent = place(chunks, other.reshape(n_section * slots, width))
    came = swap(sent, "section", 1)
    relaid, weight_grad = finish(
        whole.reshape(width, width), mine.reshape(n_section * slots, width), came
    )
    return (relaid.reshape(1, 1, n_section, slots, width), weight_grad)


def solution(mesh):
    placed = (
        P(("section", "rep"), None),
        P("section", "rep", None, None, None),
        P("section", "rep", None),
        P(("section", "rep"), None),
        P(),
        P(("section", "rep"), None),
    )
    return jax.shard_map(
        per_device,
        mesh=mesh,
        in_specs=placed,
        out_specs=(P("section", "rep", None, None, None), P()),
        check_vma=False,
    )
```

```python
import functools

import jax
import jax.numpy as jnp
from jax import lax
from jax.experimental import pallas as pl
from jax.experimental.pallas import tpu as pltpu
from jax.sharding import PartitionSpec as P

VMEM = pl.BlockSpec(memory_space=pltpu.VMEM)
LIMIT = pltpu.CompilerParams(vmem_limit_bytes=32 * 1024 * 1024)
SMEM = pl.BlockSpec(memory_space=pltpu.SMEM)


def across(n):
    return list(range(n - 1, 0, -1))


def prepare_kernel(slots, tiles_ref, own_ref, target_ref, wide_ref, held_ref, placing_ref):
    many, depth = tiles_ref.shape[:2]
    for g in range(many):
        wide_ref[g] = jnp.concatenate([tiles_ref[g, k] for k in range(depth)], axis=1)
    held_ref[...] = own_ref[...]
    places, rows = placing_ref.shape
    n_section = places // slots
    target = target_ref[...]
    hits = lax.broadcasted_iota(jnp.int32, (n_section, rows), 0) == target
    hits = jnp.where(hits, 1.0, 0.0)
    earlier = lax.broadcasted_iota(jnp.int32, (rows, rows), 0) < lax.broadcasted_iota(
        jnp.int32, (rows, rows), 1
    )
    earlier = jnp.where(earlier, 1.0, 0.0).astype(jnp.bfloat16)
    before = jnp.dot(hits.astype(jnp.bfloat16), earlier, preferred_element_type=jnp.float32)
    slot = jnp.sum(before * hits, axis=0, keepdims=True).astype(jnp.int32)
    chip = lax.axis_index("section") & -2
    position = (target ^ chip) * slots + slot
    placing = lax.broadcasted_iota(jnp.int32, (places, rows), 0) == position
    placing_ref[...] = jnp.where(placing, 1.0, 0.0).astype(jnp.bfloat16)


def prepare(tiles, own, target, places, slots):
    many, depth, tile, _ = tiles.shape
    return pl.pallas_call(
        functools.partial(prepare_kernel, slots),
        out_shape=(
            jax.ShapeDtypeStruct((many, tile, depth * tile), jnp.bfloat16),
            jax.ShapeDtypeStruct(own.shape, jnp.bfloat16),
            jax.ShapeDtypeStruct((places, target.shape[1]), jnp.bfloat16),
        ),
        in_specs=[VMEM] * 3,
        out_specs=(VMEM,) * 3,
        compiler_params=LIMIT,
        cost_estimate=pl.CostEstimate(flops=0, bytes_accessed=2 * tiles.size * 2, transcendentals=0),
        name="prepare",
    )(tiles, own, target)


def partials_kernel(count, src_ref, wide_ref, *refs):
    block_refs, out_refs, held = refs[:count], refs[count:-1], refs[-1]
    depth = src_ref.shape[1]
    section, rep = lax.axis_index("section"), lax.axis_index("rep")
    for j in range(count):
        held[j] = block_refs[j][...]
    for j, out_ref in zip([0] + across(len(out_refs)), out_refs):
        g = rep ^ j
        right = jnp.concatenate([held[src_ref[g, k] ^ section] for k in range(depth)], axis=0)
        out_ref[...] = jnp.dot(wide_ref[g], right, preferred_element_type=jnp.float32).astype(
            jnp.bfloat16
        )


def partials(sources, wide, blocks):
    many = wide.shape[0]
    tile, width = blocks[0].shape
    return pl.pallas_call(
        functools.partial(partials_kernel, len(blocks)),
        out_shape=[jax.ShapeDtypeStruct((tile, width), jnp.bfloat16)] * many,
        in_specs=[SMEM] + [VMEM] * (1 + len(blocks)),
        out_specs=[VMEM] * many,
        scratch_shapes=[pltpu.VMEM((len(blocks), tile, width), jnp.bfloat16)],
        compiler_params=LIMIT,
        name="partials",
    )(sources, wide, *blocks)


def swap(value, axis, j):
    return lax.ppermute(value, axis, [(i, i ^ j) for i in range(lax.axis_size(axis))])


def tree_sum(terms):
    while len(terms) > 1:
        terms = [terms[i] + terms[i + 1] for i in range(0, len(terms), 2)]
    return terms[0]


def tree_sum(terms):
    while len(terms) > 1:
        terms = [terms[i] + terms[i + 1] for i in range(0, len(terms), 2)]
    return terms[0]


def dense_kernel(n_part, weight_ref, cot_ref, placing_ref, *refs):
    part_refs, (packed_ref, term_ref, sent_ref) = refs[:n_part], refs[n_part:]
    core = lax.axis_index("section") & 1
    agg_b = tree_sum([ref[...].astype(jnp.float32) for ref in part_refs]).astype(jnp.bfloat16)
    pre = jnp.dot(agg_b, weight_ref[...], preferred_element_type=jnp.float32)
    sig = jax.nn.sigmoid(pre)
    factor = sig * (1.0 + pre * (1.0 - sig))
    grad_pre = (cot_ref[...].astype(jnp.float32) * factor).astype(jnp.bfloat16)
    term = lax.dot_general(
        agg_b, grad_pre, (((0,), (0,)), ((), ())), preferred_element_type=jnp.float32
    )
    term_ref[...] = term
    output = (pre * sig).astype(jnp.bfloat16)
    packed = jnp.dot(placing_ref[...], output, preferred_element_type=jnp.float32)
    packed = packed.astype(jnp.bfloat16)
    packed_ref[...] = packed

    @pl.when(core == 0)
    def _():
        sent_ref[: term.shape[0]] = term.astype(jnp.bfloat16)

    @pl.when(core == 1)
    def _():
        sent_ref[: packed.shape[0]] = packed


def dense(parts, weight, cotangent, placing):
    places, width = placing.shape[0], weight.shape[0]
    return pl.pallas_call(
        functools.partial(dense_kernel, len(parts)),
        out_shape=(
            jax.ShapeDtypeStruct((places, width), jnp.bfloat16),
            jax.ShapeDtypeStruct((width, width), jnp.float32),
            jax.ShapeDtypeStruct((max(places, width), width), jnp.bfloat16),
        ),
        in_specs=[VMEM] * (3 + len(parts)),
        out_specs=(VMEM,) * 3,
        compiler_params=LIMIT,
        name="dense",
    )(weight, cotangent, placing, *parts)


def split_kernel(packed_ref, term_ref, came_ref, own_ref, *refs):
    out_refs, term = refs[:-1], refs[-1]
    rep, core = lax.axis_index("rep"), lax.axis_index("section") & 1
    n_rep, chunk = term.shape[:2]
    total = term_ref[...] + came_ref[: n_rep * chunk].astype(jnp.float32)
    term[...] = total.reshape(term.shape)
    own_ref[...] = term[rep]
    rows = 2 * packed_ref.shape[0] // lax.axis_size("section")

    @pl.when(core == 1)
    def _():
        for ref, j in zip(out_refs, across(len(out_refs) + 1)):
            ref[:chunk] = term[rep ^ (j % n_rep)].astype(jnp.bfloat16)

    @pl.when(core == 0)
    def _():
        for ref, j in zip(out_refs, across(len(out_refs) + 1)):
            start = j * rows % packed_ref.shape[0]
            ref[:rows] = packed_ref[start : start + rows]


def split(packed, term, came, n_rep, chips):
    places, width = packed.shape
    chunk = width // n_rep
    out = jax.ShapeDtypeStruct((max(chunk, places // chips), width), jnp.bfloat16)
    many = max(n_rep, chips)
    return pl.pallas_call(
        split_kernel,
        out_shape=[jax.ShapeDtypeStruct((chunk, width), jnp.float32)] + [out] * (many - 1),
        in_specs=[VMEM] * 3,
        out_specs=[VMEM] * many,
        scratch_shapes=[pltpu.VMEM((n_rep, chunk, width), jnp.float32)],
        compiler_params=LIMIT,
        name="split",
    )(packed, term, came)


def second_kernel(n_rep, packed_ref, came_ref, own_ref, *refs):
    term_refs, chunk_ref, out_refs = refs[: n_rep - 1], refs[n_rep - 1], refs[n_rep:]
    core = lax.axis_index("section") & 1
    chunk = own_ref.shape[0]
    terms = [own_ref[...]] + [ref[:chunk].astype(jnp.float32) for ref in term_refs]
    total = tree_sum(terms).astype(jnp.bfloat16)
    chunk_ref[...] = total
    rows = packed_ref.shape[0] // (len(out_refs) + 1)

    @pl.when(core == 1)
    def _():
        for ref in out_refs:
            ref[:chunk] = total

    @pl.when(core == 0)
    def _():
        for ref, j in zip(out_refs, across(len(out_refs) + 1)):
            ref[:rows] = came_ref[j * rows : (j + 1) * rows]


def second(packed, came, own, terms, chips):
    places, width = packed.shape
    chunk = own.shape[0]
    out = jax.ShapeDtypeStruct((max(chunk, places // chips), width), jnp.bfloat16)
    return pl.pallas_call(
        functools.partial(second_kernel, len(terms) + 1),
        out_shape=[jax.ShapeDtypeStruct((chunk, width), jnp.bfloat16)] + [out] * (chips - 1),
        in_specs=[VMEM] * (3 + len(terms)),
        out_specs=[VMEM] * chips,
        compiler_params=LIMIT,
        name="second",
    )(packed, came, own, *terms)


def add_kernel(own_ref, *refs):
    chunk = own_ref.shape[0]
    by_xor = [own_ref] + list(refs[-2::-1])
    total = tree_sum([ref[:chunk].astype(jnp.float32) for ref in by_xor])
    refs[-1][...] = total.astype(jnp.bfloat16)


def add(own, others):
    return pl.pallas_call(
        add_kernel,
        out_shape=jax.ShapeDtypeStruct(own.shape, jnp.bfloat16),
        in_specs=[VMEM] * (1 + len(others)),
        out_specs=VMEM,
        compiler_params=LIMIT,
        name="add",
    )(own, *others)


def unpack_kernel(slots, chips, packed_ref, came_ref, *refs):
    out_refs = refs[-2:]
    chip = lax.axis_index("section") & -2
    sources = (
        [packed_ref] + list(refs[: chips - 1]),
        [came_ref] + list(refs[chips - 1 : -2]),
    )
    for source in range(2):
        for ref, j in zip(sources[source], [0] + across(chips)):
            for core in range(2):
                rows = ref[core * slots : (core + 1) * slots]
                out_refs[core][chip ^ (2 * j) | source] = rows


def unpack(packed, came, first, later, slots):
    width = packed.shape[1]
    chips = len(first) + 1
    return pl.pallas_call(
        functools.partial(unpack_kernel, slots, chips),
        out_shape=[jax.ShapeDtypeStruct((2 * chips, slots, width), jnp.bfloat16)] * 2,
        in_specs=[VMEM] * (2 * chips),
        out_specs=[VMEM] * 2,
        compiler_params=LIMIT,
        name="unpack",
    )(packed, came, *first, *later)


def place_kernel(other_ref, *refs):
    chunk_refs, (whole_ref, sent_ref) = refs[:-2], refs[-2:]
    rep, core = lax.axis_index("rep"), lax.axis_index("section") & 1
    for j, ref in enumerate(chunk_refs):
        whole_ref[rep ^ j] = ref[...]

    @pl.when(core == 0)
    def _():
        sent_ref[: other_ref.shape[0]] = other_ref[...]

    @pl.when(core == 1)
    def _():
        n_rep, rows, _ = whole_ref.shape
        for r in range(n_rep):
            sent_ref[r * rows : (r + 1) * rows] = whole_ref[r]


def place(chunks, other):
    rows, width = chunks[0].shape
    return pl.pallas_call(
        place_kernel,
        out_shape=(
            jax.ShapeDtypeStruct((len(chunks), rows, width), jnp.bfloat16),
            jax.ShapeDtypeStruct((max(len(chunks) * rows, other.shape[0]), width), jnp.bfloat16),
        ),
        in_specs=[VMEM] * (1 + len(chunks)),
        out_specs=(VMEM,) * 2,
        compiler_params=LIMIT,
        name="place",
    )(other, *chunks)


def finish_kernel(whole_ref, mine_ref, came_ref, relaid_ref, grad_ref):
    core = lax.axis_index("section") & 1

    @pl.when(core == 0)
    def _():
        grad_ref[...] = came_ref[: grad_ref.shape[0]].astype(jnp.float32)
        relaid_ref[...] = mine_ref[...]

    @pl.when(core == 1)
    def _():
        grad_ref[...] = whole_ref[...].astype(jnp.float32)
        relaid_ref[...] = came_ref[: relaid_ref.shape[0]]


def finish(whole, mine, came):
    return pl.pallas_call(
        finish_kernel,
        out_shape=(
            jax.ShapeDtypeStruct(mine.shape, jnp.bfloat16),
            jax.ShapeDtypeStruct(whole.shape, jnp.float32),
        ),
        in_specs=[VMEM] * 3,
        out_specs=(VMEM,) * 2,
        compiler_params=LIMIT,
        name="finish",
    )(whole, mine, came)


def swap_by_core(value, along, side):
    n_section, n_rep = lax.axis_size("section"), lax.axis_size("rep")
    along, side = 2 * along % n_section, side % n_rep
    pairs = [
        (s * n_rep + r, s * n_rep + (r ^ side) if s & 1 else (s ^ along) * n_rep + r)
        for s in range(n_section)
        for r in range(n_rep)
    ]
    return lax.ppermute(value, ("section", "rep"), pairs)


def gather_blocks(features, axis, ready):
    n = lax.axis_size(axis)
    blocks = [None] * n
    blocks[0] = features
    for j in range(2, n, 2):
        blocks[j] = swap(features, axis, j)
    blocks[1] = swap(features, axis, 1)
    blocks[2::2], ready = lax.optimization_barrier((blocks[2::2], ready))
    for j in range(2, n, 2):
        blocks[j + 1] = swap(blocks[j], axis, 1)
    return blocks, ready


def per_device(features, adj_tiles, adj_src, cotangent, weight, destination):
    n_section, n_rep = lax.axis_size("section"), lax.axis_size("rep")
    rows_here, width = features.shape
    tile = adj_tiles.shape[3]
    slots = max(2, 2 * rows_here // n_section)
    target = destination.reshape(1, rows_here)
    wide, own, placing = prepare(adj_tiles[:, 0], features, target, n_section * slots, slots)
    blocks, (wide, own, placing) = gather_blocks(features, "section", (wide, own, placing))
    parts = list(partials(adj_src[:, 0], wide, [own] + blocks[1:]))
    others = across(n_rep)
    parts = [swap(part, "rep", j) if j else part for part, j in zip(parts, [0] + others)]
    packed, term, sent = dense(parts, weight, cotangent, placing)
    came = swap(sent, "section", 1)
    chips = n_section // 2
    own, *first = split(packed, term, came, n_rep, chips)
    first = [swap_by_core(value, j, j) for value, j in zip(first, across(len(first) + 1))]
    chunk, *later = second(packed, came, own, first[1 - n_rep :], chips)
    later = [swap(value, "section", 2 * j) for value, j in zip(later, across(chips))]
    chunk = add(chunk, later)
    mine, other = unpack(packed, came, first[1 - chips :], later, slots)
    chunks = [chunk] + [swap_by_core(chunk, 0, j) for j in range(1, n_rep)]
    whole, sent = place(chunks, other.reshape(n_section * slots, width))
    came = swap(sent, "section", 1)
    relaid, weight_grad = finish(
        whole.reshape(width, width), mine.reshape(n_section * slots, width), came
    )
    return (relaid.reshape(1, 1, n_section, slots, width), weight_grad)


def solution(mesh):
    placed = (
        P(("section", "rep"), None),
        P("section", "rep", None, None, None),
        P("section", "rep", None),
        P(("section", "rep"), None),
        P(),
        P(("section", "rep"), None),
    )
    return jax.shard_map(
        per_device,
        mesh=mesh,
        in_specs=placed,
        out_specs=(P("section", "rep", None, None, None), P()),
        check_vma=False,
    )
```

```python
import functools

import jax
import jax.numpy as jnp
from jax import lax
from jax.experimental import pallas as pl
from jax.experimental.pallas import tpu as pltpu
from jax.sharding import PartitionSpec as P

VMEM = pl.BlockSpec(memory_space=pltpu.VMEM)
LIMIT = pltpu.CompilerParams(vmem_limit_bytes=32 * 1024 * 1024)
SMEM = pl.BlockSpec(memory_space=pltpu.SMEM)


def across(n):
    return list(range(n - 1, 0, -1))


def prepare_kernel(slots, tiles_ref, own_ref, target_ref, wide_ref, held_ref, placing_ref):
    many, depth = tiles_ref.shape[:2]
    for g in range(many):
        wide_ref[g] = jnp.concatenate([tiles_ref[g, k] for k in range(depth)], axis=1)
    held_ref[...] = own_ref[...]
    places, rows = placing_ref.shape
    n_section = places // slots
    target = target_ref[...]
    hits = lax.broadcasted_iota(jnp.int32, (n_section, rows), 0) == target
    hits = jnp.where(hits, 1.0, 0.0)
    earlier = lax.broadcasted_iota(jnp.int32, (rows, rows), 0) < lax.broadcasted_iota(
        jnp.int32, (rows, rows), 1
    )
    earlier = jnp.where(earlier, 1.0, 0.0).astype(jnp.bfloat16)
    before = jnp.dot(hits.astype(jnp.bfloat16), earlier, preferred_element_type=jnp.float32)
    slot = jnp.sum(before * hits, axis=0, keepdims=True).astype(jnp.int32)
    chip = lax.axis_index("section") & -2
    position = (target ^ chip) * slots + slot
    placing = lax.broadcasted_iota(jnp.int32, (places, rows), 0) == position
    placing_ref[...] = jnp.where(placing, 1.0, 0.0).astype(jnp.bfloat16)


def prepare(tiles, own, target, places, slots):
    many, depth, tile, _ = tiles.shape
    return pl.pallas_call(
        functools.partial(prepare_kernel, slots),
        out_shape=(
            jax.ShapeDtypeStruct((many, tile, depth * tile), jnp.bfloat16),
            jax.ShapeDtypeStruct(own.shape, jnp.bfloat16),
            jax.ShapeDtypeStruct((places, target.shape[1]), jnp.bfloat16),
        ),
        in_specs=[VMEM] * 3,
        out_specs=(VMEM,) * 3,
        compiler_params=LIMIT,
        cost_estimate=pl.CostEstimate(flops=0, bytes_accessed=2 * tiles.size * 2, transcendentals=0),
        name="prepare",
    )(tiles, own, target)


def partials_kernel(count, src_ref, wide_ref, *refs):
    block_refs, out_refs, held = refs[:count], refs[count:-1], refs[-1]
    depth = src_ref.shape[1]
    section, rep = lax.axis_index("section"), lax.axis_index("rep")
    for j in range(count):
        held[j] = block_refs[j][...]
    for j, out_ref in zip([0] + across(len(out_refs)), out_refs):
        g = rep ^ j
        right = jnp.concatenate([held[src_ref[g, k] ^ section] for k in range(depth)], axis=0)
        out_ref[...] = jnp.dot(wide_ref[g], right, preferred_element_type=jnp.float32).astype(
            jnp.bfloat16
        )


def partials(sources, wide, blocks):
    many = wide.shape[0]
    tile, width = blocks[0].shape
    return pl.pallas_call(
        functools.partial(partials_kernel, len(blocks)),
        out_shape=[jax.ShapeDtypeStruct((tile, width), jnp.bfloat16)] * many,
        in_specs=[SMEM] + [VMEM] * (1 + len(blocks)),
        out_specs=[VMEM] * many,
        scratch_shapes=[pltpu.VMEM((len(blocks), tile, width), jnp.bfloat16)],
        compiler_params=LIMIT,
        name="partials",
    )(sources, wide, *blocks)


def swap(value, axis, j):
    return lax.ppermute(value, axis, [(i, i ^ j) for i in range(lax.axis_size(axis))])


def tree_sum(terms):
    while len(terms) > 1:
        terms = [terms[i] + terms[i + 1] for i in range(0, len(terms), 2)]
    return terms[0]


def tree_sum(terms):
    while len(terms) > 1:
        terms = [terms[i] + terms[i + 1] for i in range(0, len(terms), 2)]
    return terms[0]


def dense_kernel(n_part, weight_ref, cot_ref, placing_ref, *refs):
    part_refs, (packed_ref, term_ref, sent_ref) = refs[:n_part], refs[n_part:]
    core = lax.axis_index("section") & 1
    agg_b = tree_sum([ref[...].astype(jnp.float32) for ref in part_refs]).astype(jnp.bfloat16)
    pre = jnp.dot(agg_b, weight_ref[...], preferred_element_type=jnp.float32)
    sig = jax.nn.sigmoid(pre)
    factor = sig * (1.0 + pre * (1.0 - sig))
    grad_pre = (cot_ref[...].astype(jnp.float32) * factor).astype(jnp.bfloat16)
    term = lax.dot_general(
        agg_b, grad_pre, (((0,), (0,)), ((), ())), preferred_element_type=jnp.float32
    )
    term_ref[...] = term
    output = (pre * sig).astype(jnp.bfloat16)
    packed = jnp.dot(placing_ref[...], output, preferred_element_type=jnp.float32)
    packed = packed.astype(jnp.bfloat16)
    packed_ref[...] = packed

    @pl.when(core == 0)
    def _():
        sent_ref[: term.shape[0]] = term.astype(jnp.bfloat16)

    @pl.when(core == 1)
    def _():
        sent_ref[: packed.shape[0]] = packed


def dense(parts, weight, cotangent, placing):
    places, width = placing.shape[0], weight.shape[0]
    return pl.pallas_call(
        functools.partial(dense_kernel, len(parts)),
        out_shape=(
            jax.ShapeDtypeStruct((places, width), jnp.bfloat16),
            jax.ShapeDtypeStruct((width, width), jnp.float32),
            jax.ShapeDtypeStruct((max(places, width), width), jnp.bfloat16),
        ),
        in_specs=[VMEM] * (3 + len(parts)),
        out_specs=(VMEM,) * 3,
        compiler_params=LIMIT,
        name="dense",
    )(weight, cotangent, placing, *parts)


def split_kernel(packed_ref, term_ref, came_ref, *out_refs):
    core = lax.axis_index("section") & 1
    width = term_ref.shape[0]
    rows = 2 * packed_ref.shape[0] // lax.axis_size("section")

    @pl.when(core == 1)
    def _():
        total = (term_ref[...] + came_ref[:width].astype(jnp.float32)).astype(jnp.bfloat16)
        for ref in out_refs:
            ref[:width] = total

    @pl.when(core == 0)
    def _():
        for ref, j in zip(out_refs, [0] + across(len(out_refs))):
            start = j * rows % packed_ref.shape[0]
            ref[:rows] = packed_ref[start : start + rows]
            ref[rows : 2 * rows] = came_ref[start : start + rows]


def split(packed, term, came, n_rep, chips):
    places, width = packed.shape
    many = max(n_rep, chips)
    return pl.pallas_call(
        split_kernel,
        out_shape=[jax.ShapeDtypeStruct((max(width, 2 * places // chips), width), jnp.bfloat16)] * many,
        in_specs=[VMEM] * 3,
        out_specs=[VMEM] * many,
        compiler_params=LIMIT,
        name="split",
    )(packed, term, came)


def middle_kernel(n_rep, slots, *refs):
    values, total_ref, out_refs = refs[:-3], refs[-3], refs[-2:]
    section = lax.axis_index("section")
    chips = lax.axis_size("section") // 2
    by_xor = [values[0]] + list(values[:0:-1])
    width = total_ref.shape[0]

    @pl.when(section & 1 == 1)
    def _():
        total = tree_sum([ref[:width].astype(jnp.float32) for ref in by_xor[:n_rep]])
        total_ref[...] = total.astype(jnp.bfloat16)

    @pl.when(section & 1 == 0)
    def _():
        total_ref[...] = jnp.zeros_like(total_ref)
        for j in range(chips):
            for source in range(2):
                for core in range(2):
                    start = (2 * source + core) * slots
                    out_refs[core][section ^ (2 * j + source)] = by_xor[j][start : start + slots]


def middle(values, n_rep, n_section, slots):
    width = values[0].shape[1]
    rows = jax.ShapeDtypeStruct((n_section, slots, width), jnp.bfloat16)
    return pl.pallas_call(
        functools.partial(middle_kernel, n_rep, slots),
        out_shape=(jax.ShapeDtypeStruct((width, width), jnp.bfloat16), rows, rows),
        in_specs=[VMEM] * len(values),
        out_specs=(VMEM,) * 3,
        compiler_params=LIMIT,
        name="middle",
    )(*values)


def place_kernel(other_ref, *refs):
    core = lax.axis_index("section") & 1

    @pl.when(core == 0)
    def _():
        refs[-1][: other_ref.shape[0]] = other_ref[...]

    @pl.when(core == 1)
    def _():
        total = tree_sum([ref[...].astype(jnp.float32) for ref in refs[:-1]])
        refs[-1][: total.shape[0]] = total.astype(jnp.bfloat16)


def place(other, terms):
    width = terms[0].shape[0]
    return pl.pallas_call(
        place_kernel,
        out_shape=jax.ShapeDtypeStruct((max(width, other.shape[0]), width), jnp.bfloat16),
        in_specs=[VMEM] * (1 + len(terms)),
        out_specs=VMEM,
        compiler_params=LIMIT,
        name="place",
    )(other, *terms)


def finish_kernel(whole_ref, mine_ref, came_ref, relaid_ref, grad_ref):
    core = lax.axis_index("section") & 1

    @pl.when(core == 0)
    def _():
        grad_ref[...] = came_ref[: grad_ref.shape[0]].astype(jnp.float32)
        relaid_ref[...] = mine_ref[...]

    @pl.when(core == 1)
    def _():
        grad_ref[...] = whole_ref[: grad_ref.shape[0]].astype(jnp.float32)
        relaid_ref[...] = came_ref[: relaid_ref.shape[0]]


def finish(whole, mine, came):
    return pl.pallas_call(
        finish_kernel,
        out_shape=(
            jax.ShapeDtypeStruct(mine.shape, jnp.bfloat16),
            jax.ShapeDtypeStruct((whole.shape[1],) * 2, jnp.float32),
        ),
        in_specs=[VMEM] * 3,
        out_specs=(VMEM,) * 2,
        compiler_params=LIMIT,
        name="finish",
    )(whole, mine, came)


def swap_by_core(value, first, second):
    n_section, n_rep = lax.axis_size("section"), lax.axis_size("rep")
    pairs = []
    for s in range(n_section):
        chip, rep = second if s & 1 else first
        for r in range(n_rep):
            pairs.append((s * n_rep + r, (s ^ 2 * chip % n_section) * n_rep + (r ^ rep % n_rep)))
    return lax.ppermute(value, ("section", "rep"), pairs)


def gather_blocks(features, axis, ready):
    n = lax.axis_size(axis)
    blocks = [None] * n
    blocks[0] = features
    for j in range(2, n, 2):
        blocks[j] = swap(features, axis, j)
    blocks[1] = swap(features, axis, 1)
    blocks[2::2], ready = lax.optimization_barrier((blocks[2::2], ready))
    for j in range(2, n, 2):
        blocks[j + 1] = swap(blocks[j], axis, 1)
    return blocks, ready


def per_device(features, adj_tiles, adj_src, cotangent, weight, destination):
    n_section, n_rep = lax.axis_size("section"), lax.axis_size("rep")
    rows_here, width = features.shape
    tile = adj_tiles.shape[3]
    slots = max(2, 2 * rows_here // n_section)
    target = destination.reshape(1, rows_here)
    wide, own, placing = prepare(adj_tiles[:, 0], features, target, n_section * slots, slots)
    blocks, (wide, own, placing) = gather_blocks(features, "section", (wide, own, placing))
    parts = list(partials(adj_src[:, 0], wide, [own] + blocks[1:]))
    others = across(n_rep)
    parts = [swap(part, "rep", j) if j else part for part, j in zip(parts, [0] + others)]
    packed, term, sent = dense(parts, weight, cotangent, placing)
    came = swap(sent, "section", 1)
    chips = n_section // 2
    own, *values = split(packed, term, came, n_rep, chips)
    steps = across(len(values) + 1)
    values = [own] + [swap_by_core(v, (j, 0), (0, j)) for v, j in zip(values, steps)]
    total, mine, other = middle(values, n_rep, n_section, slots)
    terms = [total] + [swap_by_core(total, (0, 1 + j % 2), (j, 0)) for j in range(1, chips)]
    sent = place(other.reshape(n_section * slots, width), terms)
    came = swap(sent, "section", 1)
    relaid, weight_grad = finish(sent, mine.reshape(n_section * slots, width), came)
    return (relaid.reshape(1, 1, n_section, slots, width), weight_grad)


def solution(mesh):
    placed = (
        P(("section", "rep"), None),
        P("section", "rep", None, None, None),
        P("section", "rep", None),
        P(("section", "rep"), None),
        P(),
        P(("section", "rep"), None),
    )
    return jax.shard_map(
        per_device,
        mesh=mesh,
        in_specs=placed,
        out_specs=(P("section", "rep", None, None, None), P()),
        check_vma=False,
    )
```

```python
import functools

import jax
import jax.numpy as jnp
from jax import lax
from jax.experimental import pallas as pl
from jax.experimental.pallas import tpu as pltpu
from jax.sharding import PartitionSpec as P

VMEM = pl.BlockSpec(memory_space=pltpu.VMEM)
LIMIT = pltpu.CompilerParams(vmem_limit_bytes=32 * 1024 * 1024)
SMEM = pl.BlockSpec(memory_space=pltpu.SMEM)


def across(n):
    return list(range(n - 1, 0, -1))


def prepare_kernel(slots, tiles_ref, own_ref, target_ref, wide_ref, held_ref, placing_ref):
    many, depth = tiles_ref.shape[:2]
    for g in range(many):
        wide_ref[g] = jnp.concatenate([tiles_ref[g, k] for k in range(depth)], axis=1)
    held_ref[...] = own_ref[...]
    places, rows = placing_ref.shape
    n_section = places // slots
    target = target_ref[...]
    hits = lax.broadcasted_iota(jnp.int32, (n_section, rows), 0) == target
    hits = jnp.where(hits, 1.0, 0.0)
    earlier = lax.broadcasted_iota(jnp.int32, (rows, rows), 0) < lax.broadcasted_iota(
        jnp.int32, (rows, rows), 1
    )
    earlier = jnp.where(earlier, 1.0, 0.0).astype(jnp.bfloat16)
    before = jnp.dot(hits.astype(jnp.bfloat16), earlier, preferred_element_type=jnp.float32)
    slot = jnp.sum(before * hits, axis=0, keepdims=True).astype(jnp.int32)
    apart = target ^ lax.axis_index("section")
    position = ((apart & 1) * (n_section // 2) + (apart >> 1)) * slots + slot
    placing = lax.broadcasted_iota(jnp.int32, (places, rows), 0) == position
    placing_ref[...] = jnp.where(placing, 1.0, 0.0).astype(jnp.bfloat16)


def prepare(tiles, own, target, places, slots):
    many, depth, tile, _ = tiles.shape
    return pl.pallas_call(
        functools.partial(prepare_kernel, slots),
        out_shape=(
            jax.ShapeDtypeStruct((many, tile, depth * tile), jnp.bfloat16),
            jax.ShapeDtypeStruct(own.shape, jnp.bfloat16),
            jax.ShapeDtypeStruct((places, target.shape[1]), jnp.bfloat16),
        ),
        in_specs=[VMEM] * 3,
        out_specs=(VMEM,) * 3,
        compiler_params=LIMIT,
        cost_estimate=pl.CostEstimate(flops=0, bytes_accessed=2 * tiles.size * 2, transcendentals=0),
        name="prepare",
    )(tiles, own, target)


def partials_kernel(count, src_ref, wide_ref, *refs):
    block_refs, out_refs, held = refs[:count], refs[count:-1], refs[-1]
    depth = src_ref.shape[1]
    section, rep = lax.axis_index("section"), lax.axis_index("rep")
    for j in range(count):
        held[j] = block_refs[j][...]
    for j, out_ref in zip([0] + across(len(out_refs)), out_refs):
        g = rep ^ j
        right = jnp.concatenate([held[src_ref[g, k] ^ section] for k in range(depth)], axis=0)
        out_ref[...] = jnp.dot(wide_ref[g], right, preferred_element_type=jnp.float32).astype(
            jnp.bfloat16
        )


def partials(sources, wide, blocks):
    many = wide.shape[0]
    tile, width = blocks[0].shape
    return pl.pallas_call(
        functools.partial(partials_kernel, len(blocks)),
        out_shape=[jax.ShapeDtypeStruct((tile, width), jnp.bfloat16)] * many,
        in_specs=[SMEM] + [VMEM] * (1 + len(blocks)),
        out_specs=[VMEM] * many,
        scratch_shapes=[pltpu.VMEM((len(blocks), tile, width), jnp.bfloat16)],
        compiler_params=LIMIT,
        name="partials",
    )(sources, wide, *blocks)


def swap(value, axis, j):
    return lax.ppermute(value, axis, [(i, i ^ j) for i in range(lax.axis_size(axis))])


def tree_sum(terms):
    while len(terms) > 1:
        terms = [terms[i] + terms[i + 1] for i in range(0, len(terms), 2)]
    return terms[0]


def dense_kernel(n_part, weight_ref, cot_ref, placing_ref, *refs):
    part_refs, (same_ref, kept_ref, sent_ref, term) = refs[:n_part], refs[n_part:]
    core = lax.axis_index("section") & 1
    agg_b = tree_sum([ref[...].astype(jnp.float32) for ref in part_refs]).astype(jnp.bfloat16)
    pre = jnp.dot(agg_b, weight_ref[...], preferred_element_type=jnp.float32)
    sig = jax.nn.sigmoid(pre)
    factor = sig * (1.0 + pre * (1.0 - sig))
    grad_pre = (cot_ref[...].astype(jnp.float32) * factor).astype(jnp.bfloat16)
    whole = lax.dot_general(
        agg_b, grad_pre, (((0,), (0,)), ((), ())), preferred_element_type=jnp.float32
    )
    term[...] = whole.reshape(term.shape)
    kept_ref[...] = term[core]
    output = (pre * sig).astype(jnp.bfloat16)
    packed = jnp.dot(placing_ref[...], output, preferred_element_type=jnp.float32)
    half = packed.shape[0] // 2
    same_ref[...] = packed[:half].astype(jnp.bfloat16)
    sent_ref[:half] = packed[half:].astype(jnp.bfloat16)
    sent_ref[half:] = term[1 - core].astype(jnp.bfloat16)


def dense(parts, weight, cotangent, placing):
    places, width = placing.shape[0], weight.shape[0]
    return pl.pallas_call(
        functools.partial(dense_kernel, len(parts)),
        out_shape=(
            jax.ShapeDtypeStruct((places // 2, width), jnp.bfloat16),
            jax.ShapeDtypeStruct((width // 2, width), jnp.float32),
            jax.ShapeDtypeStruct((places // 2 + width // 2, width), jnp.bfloat16),
        ),
        in_specs=[VMEM] * (3 + len(parts)),
        out_specs=(VMEM,) * 3,
        scratch_shapes=[pltpu.VMEM((2, width // 2, width), jnp.float32)],
        compiler_params=LIMIT,
        name="dense",
    )(weight, cotangent, placing, *parts)


def write_messages(slots, same_ref, came_ref, half, out_refs):
    for ref, j in zip(out_refs, across(len(out_refs) + 1)):
        start = j * slots % same_ref.shape[0]
        ref[:slots] = same_ref[start : start + slots]
        ref[slots : 2 * slots] = came_ref[start : start + slots]
        ref[2 * slots :] = half


def sum_halves(half_ref, slots, own_ref, message_refs, counts):
    by_xor = [own_ref[...].astype(jnp.float32)]
    by_xor += [ref[2 * slots :].astype(jnp.float32) for ref in message_refs[::-1]]
    for core in range(2):

        @pl.when(lax.axis_index("section") & 1 == core)
        def _():
            half_ref[...] = tree_sum(by_xor[: counts[core]]).astype(jnp.bfloat16)


def first_kernel(slots, same_ref, kept_ref, came_ref, half_ref, *out_refs):
    rows = kept_ref.shape[0]
    half = kept_ref[...] + came_ref[came_ref.shape[0] - rows :].astype(jnp.float32)
    half_ref[...] = half.astype(jnp.bfloat16)
    write_messages(slots, same_ref, came_ref, half_ref[...], out_refs)


def second_kernel(slots, counts, many, same_ref, came_ref, own_ref, *refs):
    message_refs, half_ref, out_refs = refs[:many], refs[many], refs[many + 1 :]
    sum_halves(half_ref, slots, own_ref, message_refs, counts)
    write_messages(slots, same_ref, came_ref, half_ref[...], out_refs)


def third_kernel(slots, counts, own_ref, *refs):
    sum_halves(refs[-1], slots, own_ref, refs[:-1], counts)


def call_halves(kernel, name, operands, half, slots, many):
    shapes = [jax.ShapeDtypeStruct(half, jnp.bfloat16)]
    shapes += [jax.ShapeDtypeStruct((2 * slots + half[0], half[1]), jnp.bfloat16)] * many
    return pl.pallas_call(
        kernel,
        out_shape=shapes,
        in_specs=[VMEM] * len(operands),
        out_specs=[VMEM] * len(shapes),
        compiler_params=LIMIT,
        name=name,
    )(*operands)


def unpack_kernel(slots, same_ref, came_ref, *refs):
    many = len(refs) // 2
    section = lax.axis_index("section")
    chips = lax.axis_size("section") // 2
    refs[-1][section] = same_ref[:slots]
    refs[-1][section ^ 1] = came_ref[:slots]
    for core in range(2):

        @pl.when(section & 1 == core)
        def _():
            for ref, j in zip(refs[core * many : (core + 1) * many], across(many + 1)):
                if j < chips:
                    refs[-1][section ^ (2 * j)] = ref[:slots]
                    refs[-1][section ^ (2 * j + 1)] = ref[slots : 2 * slots]


def unpack(same, came, first, second, n_section, slots):
    width = same.shape[1]
    return pl.pallas_call(
        functools.partial(unpack_kernel, slots),
        out_shape=jax.ShapeDtypeStruct((n_section, slots, width), jnp.bfloat16),
        in_specs=[VMEM] * (2 + len(first) + len(second)),
        out_specs=VMEM,
        compiler_params=LIMIT,
        name="unpack",
    )(same, came, *first, *second)


def finish_kernel(own_ref, came_ref, out_ref):
    core = lax.axis_index("section") & 1
    out_ref[core] = own_ref[...].astype(jnp.float32)
    out_ref[1 - core] = came_ref[...].astype(jnp.float32)


def finish(own, came):
    return pl.pallas_call(
        finish_kernel,
        out_shape=jax.ShapeDtypeStruct((2,) + own.shape, jnp.float32),
        in_specs=[VMEM] * 2,
        out_specs=VMEM,
        compiler_params=LIMIT,
        name="finish",
    )(own, came)


def swap_by_core(value, first, second):
    n_section, n_rep = lax.axis_size("section"), lax.axis_size("rep")
    pairs = []
    for s in range(n_section):
        chip, rep = second if s & 1 else first
        for r in range(n_rep):
            pairs.append((s * n_rep + r, (s ^ 2 * chip % n_section) * n_rep + (r ^ rep % n_rep)))
    return lax.ppermute(value, ("section", "rep"), pairs)


def gather_blocks(features, axis, ready):
    n = lax.axis_size(axis)
    blocks = [None] * n
    blocks[0] = features
    for j in range(2, n, 2):
        blocks[j] = swap(features, axis, j)
    blocks[1] = swap(features, axis, 1)
    blocks[2::2], ready = lax.optimization_barrier((blocks[2::2], ready))
    for j in range(2, n, 2):
        blocks[j + 1] = swap(blocks[j], axis, 1)
    return blocks, ready


def per_device(features, adj_tiles, adj_src, cotangent, weight, destination):
    n_section, n_rep = lax.axis_size("section"), lax.axis_size("rep")
    rows_here, width = features.shape
    tile = adj_tiles.shape[3]
    slots = max(2, 2 * rows_here // n_section)
    target = destination.reshape(1, rows_here)
    wide, own, placing = prepare(adj_tiles[:, 0], features, target, n_section * slots, slots)
    blocks, (wide, own, placing) = gather_blocks(features, "section", (wide, own, placing))
    parts = list(partials(adj_src[:, 0], wide, [own] + blocks[1:]))
    others = across(n_rep)
    parts = [swap(part, "rep", j) if j else part for part, j in zip(parts, [0] + others)]
    same, kept, sent = dense(parts, weight, cotangent, placing)
    came = swap(sent, "section", 1)
    chips = n_section // 2
    steps = across(max(n_rep, chips))
    half_shape = (width // 2, width)
    half, *first = call_halves(
        functools.partial(first_kernel, slots), "first", [same, kept, came], half_shape, slots, len(steps)
    )
    first = [swap_by_core(m, (j, 0), (0, j)) for m, j in zip(first, steps)]
    half, *second = call_halves(
        functools.partial(second_kernel, slots, (chips, n_rep), len(steps)),
        "second",
        [same, came, half, *first],
        half_shape,
        slots,
        len(steps),
    )
    second = [swap_by_core(m, (0, j), (j, 0)) for m, j in zip(second, steps)]
    (half,) = call_halves(
        functools.partial(third_kernel, slots, (n_rep, chips)), "third", [half, *second], half_shape, slots, 0
    )
    relaid = unpack(same, came, first, second, n_section, slots)
    weight_grad = finish(half, swap(half, "section", 1))
    return (relaid.reshape(1, 1, n_section, slots, width), weight_grad.reshape(width, width))


def solution(mesh):
    placed = (
        P(("section", "rep"), None),
        P("section", "rep", None, None, None),
        P("section", "rep", None),
        P(("section", "rep"), None),
        P(),
        P(("section", "rep"), None),
    )
    return jax.shard_map(
        per_device,
        mesh=mesh,
        in_specs=placed,
        out_specs=(P("section", "rep", None, None, None), P()),
        check_vma=False,
    )
```

```python
import functools

import jax
import jax.numpy as jnp
from jax import lax
from jax.experimental import pallas as pl
from jax.experimental.pallas import tpu as pltpu
from jax.sharding import PartitionSpec as P

VMEM = pl.BlockSpec(memory_space=pltpu.VMEM)
LIMIT = pltpu.CompilerParams(vmem_limit_bytes=32 * 1024 * 1024)
HBM = pl.BlockSpec(memory_space=pltpu.HBM)


def across(n):
    return list(range(n - 1, 0, -1))


def turned(n):
    first, *rest = across(n)
    return [first] + rest[::-1]


def prepare_kernel(slots, tiles_ref, own_ref, target_ref, wide_ref, held_ref, placing_ref):
    many, depth = tiles_ref.shape[:2]
    for g in range(many):
        wide_ref[g] = jnp.concatenate([tiles_ref[g, k] for k in range(depth)], axis=1)
    held_ref[...] = own_ref[...]
    places, rows = placing_ref.shape
    n_section = places // slots
    target = target_ref[...]
    hits = lax.broadcasted_iota(jnp.int32, (n_section, rows), 0) == target
    hits = jnp.where(hits, 1.0, 0.0)
    earlier = lax.broadcasted_iota(jnp.int32, (rows, rows), 0) < lax.broadcasted_iota(
        jnp.int32, (rows, rows), 1
    )
    earlier = jnp.where(earlier, 1.0, 0.0).astype(jnp.bfloat16)
    before = jnp.dot(hits.astype(jnp.bfloat16), earlier, preferred_element_type=jnp.float32)
    slot = jnp.sum(before * hits, axis=0, keepdims=True).astype(jnp.int32)
    apart = target ^ lax.axis_index("section")
    position = ((apart & 1) * (n_section // 2) + (apart >> 1)) * slots + slot
    placing = lax.broadcasted_iota(jnp.int32, (places, rows), 0) == position
    placing_ref[...] = jnp.where(placing, 1.0, 0.0).astype(jnp.bfloat16)


def prepare(tiles, own, target, places, slots):
    many, depth, tile, _ = tiles.shape
    return pl.pallas_call(
        functools.partial(prepare_kernel, slots),
        out_shape=(
            jax.ShapeDtypeStruct((many, tile, depth * tile), jnp.bfloat16),
            jax.ShapeDtypeStruct(own.shape, jnp.bfloat16),
            jax.ShapeDtypeStruct((places, target.shape[1]), jnp.bfloat16),
        ),
        in_specs=[VMEM] * 3,
        out_specs=(VMEM,) * 3,
        compiler_params=LIMIT,
        cost_estimate=pl.CostEstimate(flops=0, bytes_accessed=2 * tiles.size * 2, transcendentals=0),
        name="prepare",
    )(tiles, own, target)


def partials_kernel(count, src_ref, wide_ref, *refs):
    block_refs, out_refs, held = refs[:count], refs[count:-1], refs[-1]
    depth = src_ref.shape[1]
    section, rep = lax.axis_index("section"), lax.axis_index("rep")
    for j in range(count):
        held[j] = block_refs[j][...]
    steps = zip([0] + across(len(out_refs)), [0] + turned(len(out_refs)))
    for (j, j_turned), out_ref in zip(steps, out_refs):
        g = rep ^ jnp.where(section & 1 == 0, j, j_turned)
        right = jnp.concatenate([held[src_ref[g, k] ^ section] for k in range(depth)], axis=0)
        out_ref[...] = jnp.dot(wide_ref[g], right, preferred_element_type=jnp.float32).astype(
            jnp.bfloat16
        )


def partials(sources, wide, blocks):
    many = wide.shape[0]
    tile, width = blocks[0].shape
    return pl.pallas_call(
        functools.partial(partials_kernel, len(blocks)),
        out_shape=[jax.ShapeDtypeStruct((tile, width), jnp.bfloat16)] * many,
        in_specs=[VMEM] * (2 + len(blocks)),
        out_specs=[VMEM] * many,
        scratch_shapes=[pltpu.VMEM((len(blocks), tile, width), jnp.bfloat16)],
        compiler_params=LIMIT,
        name="partials",
    )(sources, wide, *blocks)


def swap(value, axis, j):
    return lax.ppermute(value, axis, [(i, i ^ j) for i in range(lax.axis_size(axis))])


def tree_sum(terms):
    while len(terms) > 1:
        terms = [terms[i] + terms[i + 1] for i in range(0, len(terms), 2)]
    return terms[0]


def dense_kernel(n_part, weight_ref, cot_ref, placing_ref, *refs):
    part_refs, (same_ref, kept_ref, sent_ref, term) = refs[:n_part], refs[n_part:]
    core = lax.axis_index("section") & 1
    agg_b = tree_sum([ref[...].astype(jnp.float32) for ref in part_refs]).astype(jnp.bfloat16)
    pre = jnp.dot(agg_b, weight_ref[...], preferred_element_type=jnp.float32)
    sig = jax.nn.sigmoid(pre)
    factor = sig * (1.0 + pre * (1.0 - sig))
    grad_pre = (cot_ref[...].astype(jnp.float32) * factor).astype(jnp.bfloat16)
    whole = lax.dot_general(
        agg_b, grad_pre, (((0,), (0,)), ((), ())), preferred_element_type=jnp.float32
    )
    term[...] = whole.reshape(term.shape)
    kept_ref[...] = term[core]
    output = (pre * sig).astype(jnp.bfloat16)
    packed = jnp.dot(placing_ref[...], output, preferred_element_type=jnp.float32)
    half = packed.shape[0] // 2
    same_ref[...] = packed[:half].astype(jnp.bfloat16)
    sent_ref[:half] = packed[half:].astype(jnp.bfloat16)
    sent_ref[half:] = term[1 - core].astype(jnp.bfloat16)


def dense(parts, weight, cotangent, placing):
    places, width = placing.shape[0], weight.shape[0]
    return pl.pallas_call(
        functools.partial(dense_kernel, len(parts)),
        out_shape=(
            jax.ShapeDtypeStruct((places // 2, width), jnp.bfloat16),
            jax.ShapeDtypeStruct((width // 2, width), jnp.float32),
            jax.ShapeDtypeStruct((places // 2 + width // 2, width), jnp.bfloat16),
        ),
        in_specs=[VMEM] * (3 + len(parts)),
        out_specs=(VMEM,) * 3,
        scratch_shapes=[pltpu.VMEM((2, width // 2, width), jnp.float32)],
        compiler_params=LIMIT,
        name="dense",
    )(weight, cotangent, placing, *parts)


def write_messages(slots, same_ref, came_ref, half, out_refs):
    for ref, j in zip(out_refs, across(len(out_refs) + 1)):
        start = j * slots % same_ref.shape[0]
        ref[:slots] = same_ref[start : start + slots]
        ref[slots : 2 * slots] = came_ref[start : start + slots]
        ref[2 * slots :] = half


def sum_halves(half_ref, slots, own_ref, message_refs, counts):
    by_xor = [own_ref[...].astype(jnp.float32)]
    by_xor += [ref[2 * slots :].astype(jnp.float32) for ref in message_refs[::-1]]
    for core in range(2):

        @pl.when(lax.axis_index("section") & 1 == core)
        def _():
            half_ref[...] = tree_sum(by_xor[: counts[core]]).astype(jnp.bfloat16)


def first_kernel(slots, same_ref, kept_ref, came_ref, half_ref, *out_refs):
    rows = kept_ref.shape[0]
    half = kept_ref[...] + came_ref[came_ref.shape[0] - rows :].astype(jnp.float32)
    half_ref[...] = half.astype(jnp.bfloat16)
    write_messages(slots, same_ref, came_ref, half_ref[...], out_refs)


def second_kernel(slots, counts, many, same_ref, came_ref, own_ref, *refs):
    message_refs, half_ref, out_refs = refs[:many], refs[many], refs[many + 1 :]
    sum_halves(half_ref, slots, own_ref, message_refs, counts)
    write_messages(slots, same_ref, came_ref, half_ref[...], out_refs)


def third_kernel(slots, counts, own_ref, *refs):
    sum_halves(refs[-1], slots, own_ref, refs[:-1], counts)


def call_halves(kernel, name, operands, half, slots, many):
    shapes = [jax.ShapeDtypeStruct(half, jnp.bfloat16)]
    shapes += [jax.ShapeDtypeStruct((2 * slots + half[0], half[1]), jnp.bfloat16)] * many
    return pl.pallas_call(
        kernel,
        out_shape=shapes,
        in_specs=[VMEM] * len(operands),
        out_specs=[VMEM] * len(shapes),
        compiler_params=LIMIT,
        name=name,
    )(*operands)


def store_kernel(core, slots, same_ref, came_ref, *refs):
    message_refs, (out_ref, rows, sem) = refs[:-3], refs[-3:]
    section = lax.axis_index("section")
    chips = lax.axis_size("section") // 2

    @pl.when(section & 1 == core)
    def _():
        rows[section] = same_ref[:slots]
        rows[section ^ 1] = came_ref[:slots]
        for ref, j in zip(message_refs, across(len(message_refs) + 1)):
            if j < chips:
                rows[section ^ (2 * j)] = ref[:slots]
                rows[section ^ (2 * j + 1)] = ref[slots : 2 * slots]
        copy = pltpu.make_async_copy(rows, out_ref, sem)
        copy.start()
        copy.wait()


def store(core, same, came, messages, n_section, slots, base=None):
    shape = (n_section, slots, same.shape[1])
    operands = [same, came, *messages]
    kernel, first, specs = functools.partial(store_kernel, core, slots), [], []
    if base is not None:
        kernel, first, specs = lambda _, *refs: store_kernel(core, slots, *refs), [base], [HBM]
    return pl.pallas_call(
        kernel,
        out_shape=jax.ShapeDtypeStruct(shape, jnp.bfloat16),
        in_specs=specs + [VMEM] * len(operands),
        out_specs=HBM,
        scratch_shapes=[pltpu.VMEM(shape, jnp.bfloat16), pltpu.SemaphoreType.DMA],
        input_output_aliases={0: 0} if first else {},
        compiler_params=LIMIT,
        name="store",
    )(*first, *operands)


def finish_kernel(own_ref, came_ref, out_ref):
    core = lax.axis_index("section") & 1
    out_ref[core] = own_ref[...].astype(jnp.float32)
    out_ref[1 - core] = came_ref[...].astype(jnp.float32)


def finish(own, came):
    return pl.pallas_call(
        finish_kernel,
        out_shape=jax.ShapeDtypeStruct((2,) + own.shape, jnp.float32),
        in_specs=[VMEM] * 2,
        out_specs=VMEM,
        compiler_params=LIMIT,
        name="finish",
    )(own, came)


def swap_by_core(value, first, second):
    n_section, n_rep = lax.axis_size("section"), lax.axis_size("rep")
    pairs = []
    for s in range(n_section):
        chip, rep = second if s & 1 else first
        for r in range(n_rep):
            pairs.append((s * n_rep + r, (s ^ 2 * chip % n_section) * n_rep + (r ^ rep % n_rep)))
    return lax.ppermute(value, ("section", "rep"), pairs)


def gather_blocks(features, axis, ready):
    n = lax.axis_size(axis)
    blocks = [None] * n
    blocks[0] = features
    for j in range(2, n, 2):
        blocks[j] = swap(features, axis, j)
    blocks[1] = swap(features, axis, 1)
    blocks[2::2], ready = lax.optimization_barrier((blocks[2::2], ready))
    for j in range(2, n, 2):
        blocks[j + 1] = swap(blocks[j], axis, 1)
    return blocks, ready


def per_device(features, adj_tiles, adj_src, cotangent, weight, destination):
    n_section, n_rep = lax.axis_size("section"), lax.axis_size("rep")
    rows_here, width = features.shape
    tile = adj_tiles.shape[3]
    slots = max(2, 2 * rows_here // n_section)
    target = destination.reshape(1, rows_here)
    wide, own, placing = prepare(adj_tiles[:, 0], features, target, n_section * slots, slots)
    blocks, (wide, own, placing) = gather_blocks(features, "section", (wide, own, placing))
    parts = list(partials(adj_src[:, 0], wide, [own] + blocks[1:]))
    others = across(n_rep)
    steps = zip(others, turned(n_rep))
    parts = parts[:1] + [swap_by_core(p, (0, j), (0, k)) for p, (j, k) in zip(parts[1:], steps)]
    same, kept, sent = dense(parts, weight, cotangent, placing)
    came = swap(sent, "section", 1)
    chips = n_section // 2
    steps = across(max(n_rep, chips))
    half_shape = (width // 2, width)
    half, *first = call_halves(
        functools.partial(first_kernel, slots), "first", [same, kept, came], half_shape, slots, len(steps)
    )
    first = [swap_by_core(m, (j, 0), (0, j)) for m, j in zip(first, steps)]
    relaid = store(0, same, came, first, n_section, slots)
    half, *second = call_halves(
        functools.partial(second_kernel, slots, (chips, n_rep), len(steps)),
        "second",
        [same, came, half, *first],
        half_shape,
        slots,
        len(steps),
    )
    second = [swap_by_core(m, (0, j), (j, 0)) for m, j in zip(second, steps)]
    (half,) = call_halves(
        functools.partial(third_kernel, slots, (n_rep, chips)), "third", [half, *second], half_shape, slots, 0
    )
    relaid = store(1, same, came, second, n_section, slots, relaid)
    half, relaid = lax.optimization_barrier((half, relaid))
    weight_grad = finish(half, swap(half, "section", 1))
    return (relaid.reshape(1, 1, n_section, slots, width), weight_grad.reshape(width, width))


def solution(mesh):
    placed = (
        P(("section", "rep"), None),
        P("section", "rep", None, None, None),
        P("section", "rep", None),
        P(("section", "rep"), None),
        P(),
        P(("section", "rep"), None),
    )
    return jax.shard_map(
        per_device,
        mesh=mesh,
        in_specs=placed,
        out_specs=(P("section", "rep", None, None, None), P()),
        check_vma=False,
    )
```

```python
import functools

import jax
import jax.numpy as jnp
from jax import lax
from jax.experimental import pallas as pl
from jax.experimental.pallas import tpu as pltpu
from jax.sharding import PartitionSpec as P

VMEM = pl.BlockSpec(memory_space=pltpu.VMEM)
LIMIT = pltpu.CompilerParams(vmem_limit_bytes=32 * 1024 * 1024)
HBM = pl.BlockSpec(memory_space=pltpu.HBM)


def across(n):
    return list(range(n - 1, 0, -1))


def turned(n):
    first, *rest = across(n)
    return [first] + rest[::-1]


def prepare_kernel(slots, tiles_ref, own_ref, target_ref, wide_ref, held_ref, placing_ref):
    many, depth = tiles_ref.shape[:2]
    for g in range(many):
        wide_ref[g] = jnp.concatenate([tiles_ref[g, k] for k in range(depth)], axis=1)
    held_ref[...] = own_ref[...]
    places, rows = placing_ref.shape
    n_section = places // slots
    target = target_ref[...]
    hits = lax.broadcasted_iota(jnp.int32, (n_section, rows), 0) == target
    hits = jnp.where(hits, 1.0, 0.0)
    earlier = lax.broadcasted_iota(jnp.int32, (rows, rows), 0) < lax.broadcasted_iota(
        jnp.int32, (rows, rows), 1
    )
    earlier = jnp.where(earlier, 1.0, 0.0).astype(jnp.bfloat16)
    before = jnp.dot(hits.astype(jnp.bfloat16), earlier, preferred_element_type=jnp.float32)
    slot = jnp.sum(before * hits, axis=0, keepdims=True).astype(jnp.int32)
    apart = target ^ lax.axis_index("section")
    position = ((apart & 1) * (n_section // 2) + (apart >> 1)) * slots + slot
    placing = lax.broadcasted_iota(jnp.int32, (places, rows), 0) == position
    placing_ref[...] = jnp.where(placing, 1.0, 0.0).astype(jnp.bfloat16)


def prepare(tiles, own, target, places, slots):
    many, depth, tile, _ = tiles.shape
    return pl.pallas_call(
        functools.partial(prepare_kernel, slots),
        out_shape=(
            jax.ShapeDtypeStruct((many, tile, depth * tile), jnp.bfloat16),
            jax.ShapeDtypeStruct(own.shape, jnp.bfloat16),
            jax.ShapeDtypeStruct((places, target.shape[1]), jnp.bfloat16),
        ),
        in_specs=[VMEM] * 3,
        out_specs=(VMEM,) * 3,
        compiler_params=LIMIT,
        cost_estimate=pl.CostEstimate(flops=0, bytes_accessed=2 * tiles.size * 2, transcendentals=0),
        name="prepare",
    )(tiles, own, target)


def partials_kernel(count, src_ref, wide_ref, *refs):
    block_refs, out_refs, held = refs[:count], refs[count:-1], refs[-1]
    depth = src_ref.shape[1]
    section, rep = lax.axis_index("section"), lax.axis_index("rep")
    for j in range(count):
        held[j] = block_refs[j][...]
    steps = zip([0] + across(len(out_refs)), [0] + turned(len(out_refs)))
    for (j, j_turned), out_ref in zip(steps, out_refs):
        g = rep ^ jnp.where(section & 1 == 0, j, j_turned)
        right = jnp.concatenate([held[src_ref[g, k] ^ section] for k in range(depth)], axis=0)
        out_ref[...] = jnp.dot(wide_ref[g], right, preferred_element_type=jnp.float32).astype(
            jnp.bfloat16
        )


def partials(sources, wide, blocks):
    many = wide.shape[0]
    tile, width = blocks[0].shape
    return pl.pallas_call(
        functools.partial(partials_kernel, len(blocks)),
        out_shape=[jax.ShapeDtypeStruct((tile, width), jnp.bfloat16)] * many,
        in_specs=[VMEM] * (2 + len(blocks)),
        out_specs=[VMEM] * many,
        scratch_shapes=[pltpu.VMEM((len(blocks), tile, width), jnp.bfloat16)],
        compiler_params=LIMIT,
        name="partials",
    )(sources, wide, *blocks)


def swap(value, axis, j):
    return lax.ppermute(value, axis, [(i, i ^ j) for i in range(lax.axis_size(axis))])


def tree_sum(terms):
    while len(terms) > 1:
        terms = [terms[i] + terms[i + 1] for i in range(0, len(terms), 2)]
    return terms[0]


def dense_kernel(n_part, weight_ref, cot_ref, placing_ref, *refs):
    part_refs, (same_ref, kept_ref, sent_ref, term) = refs[:n_part], refs[n_part:]
    core = lax.axis_index("section") & 1
    agg_b = tree_sum([ref[...].astype(jnp.float32) for ref in part_refs]).astype(jnp.bfloat16)
    pre = jnp.dot(agg_b, weight_ref[...], preferred_element_type=jnp.float32)
    sig = jax.nn.sigmoid(pre)
    factor = sig * (1.0 + pre * (1.0 - sig))
    grad_pre = (cot_ref[...].astype(jnp.float32) * factor).astype(jnp.bfloat16)
    whole = lax.dot_general(
        agg_b, grad_pre, (((0,), (0,)), ((), ())), preferred_element_type=jnp.float32
    )
    term[...] = whole.reshape(term.shape)
    kept_ref[...] = term[core]
    output = (pre * sig).astype(jnp.bfloat16)
    packed = jnp.dot(placing_ref[...], output, preferred_element_type=jnp.float32)
    half = packed.shape[0] // 2
    same_ref[...] = packed[:half].astype(jnp.bfloat16)
    sent_ref[:half] = packed[half:].astype(jnp.bfloat16)
    sent_ref[half:] = term[1 - core].astype(jnp.bfloat16)


def dense(parts, weight, cotangent, placing):
    places, width = placing.shape[0], weight.shape[0]
    return pl.pallas_call(
        functools.partial(dense_kernel, len(parts)),
        out_shape=(
            jax.ShapeDtypeStruct((places // 2, width), jnp.bfloat16),
            jax.ShapeDtypeStruct((width // 2, width), jnp.float32),
            jax.ShapeDtypeStruct((places // 2 + width // 2, width), jnp.bfloat16),
        ),
        in_specs=[VMEM] * (3 + len(parts)),
        out_specs=(VMEM,) * 3,
        scratch_shapes=[pltpu.VMEM((2, width // 2, width), jnp.float32)],
        compiler_params=LIMIT,
        name="dense",
    )(weight, cotangent, placing, *parts)


def write_messages(slots, same_ref, came_ref, half, out_refs):
    for ref, j in zip(out_refs, across(len(out_refs) + 1)):
        start = j * slots % same_ref.shape[0]
        ref[:slots] = same_ref[start : start + slots]
        ref[slots : 2 * slots] = came_ref[start : start + slots]
        ref[2 * slots :] = half


def sum_halves(half_ref, slots, own_ref, message_refs, counts):
    by_xor = [own_ref[...].astype(jnp.float32)]
    by_xor += [ref[2 * slots :].astype(jnp.float32) for ref in message_refs[::-1]]
    for core in range(2):

        @pl.when(lax.axis_index("section") & 1 == core)
        def _():
            half_ref[...] = tree_sum(by_xor[: counts[core]]).astype(jnp.bfloat16)


def first_kernel(slots, same_ref, kept_ref, came_ref, half_ref, *out_refs):
    rows = kept_ref.shape[0]
    half = kept_ref[...] + came_ref[came_ref.shape[0] - rows :].astype(jnp.float32)
    half_ref[...] = half.astype(jnp.bfloat16)
    write_messages(slots, same_ref, came_ref, half_ref[...], out_refs)


def second_kernel(slots, counts, many, same_ref, came_ref, own_ref, *refs):
    message_refs, half_ref, out_refs = refs[:many], refs[many], refs[many + 1 :]
    sum_halves(half_ref, slots, own_ref, message_refs, counts)
    write_messages(slots, same_ref, came_ref, half_ref[...], out_refs)


def third_kernel(slots, counts, own_ref, *refs):
    sum_halves(refs[-1], slots, own_ref, refs[:-1], counts)


def call_halves(kernel, name, operands, half, slots, many):
    shapes = [jax.ShapeDtypeStruct(half, jnp.bfloat16)]
    shapes += [jax.ShapeDtypeStruct((2 * slots + half[0], half[1]), jnp.bfloat16)] * many
    return pl.pallas_call(
        kernel,
        out_shape=shapes,
        in_specs=[VMEM] * len(operands),
        out_specs=[VMEM] * len(shapes),
        compiler_params=LIMIT,
        name=name,
    )(*operands)


def fill_rows(rows, slots, same_ref, came_ref, message_refs):
    section = lax.axis_index("section")
    chips = lax.axis_size("section") // 2
    rows[section] = same_ref[:slots]
    rows[section ^ 1] = came_ref[:slots]
    for ref, j in zip(message_refs, across(len(message_refs) + 1)):
        if j < chips:
            rows[section ^ (2 * j)] = ref[:slots]
            rows[section ^ (2 * j + 1)] = ref[slots : 2 * slots]


def store_kernel(slots, same_ref, came_ref, *refs):
    message_refs, (out_ref, rows, sem) = refs[:-3], refs[-3:]

    @pl.when(lax.axis_index("section") & 1 == 1)
    def _():
        fill_rows(rows, slots, same_ref, came_ref, message_refs)
        copy = pltpu.make_async_copy(rows, out_ref, sem)
        copy.start()
        copy.wait()


def store(same, came, messages, n_section, slots):
    shape = (n_section, slots, same.shape[1])
    operands = [same, came, *messages]
    return pl.pallas_call(
        functools.partial(store_kernel, slots),
        out_shape=jax.ShapeDtypeStruct(shape, jnp.bfloat16),
        in_specs=[VMEM] * len(operands),
        out_specs=HBM,
        scratch_shapes=[pltpu.VMEM(shape, jnp.bfloat16), pltpu.SemaphoreType.DMA],
        compiler_params=LIMIT,
        name="store",
    )(*operands)


def finish_kernel(slots, base_ref, own_ref, other_ref, same_ref, came_ref, *refs):
    message_refs, (relaid_ref, grad_ref, rows, sem) = refs[:-4], refs[-4:]
    core = lax.axis_index("section") & 1
    copy = pltpu.make_async_copy(rows, relaid_ref, sem)

    @pl.when(core == 0)
    def _():
        fill_rows(rows, slots, same_ref, came_ref, message_refs)
        copy.start()

    grad_ref[core] = own_ref[...].astype(jnp.float32)
    grad_ref[1 - core] = other_ref[...].astype(jnp.float32)

    @pl.when(core == 0)
    def _():
        copy.wait()


def finish(relaid, own, other, same, came, messages, slots):
    operands = [relaid, own, other, same, came, *messages]
    return pl.pallas_call(
        functools.partial(finish_kernel, slots),
        out_shape=(
            jax.ShapeDtypeStruct(relaid.shape, jnp.bfloat16),
            jax.ShapeDtypeStruct((2,) + own.shape, jnp.float32),
        ),
        in_specs=[HBM] + [VMEM] * (len(operands) - 1),
        out_specs=(HBM, VMEM),
        scratch_shapes=[pltpu.VMEM(relaid.shape, jnp.bfloat16), pltpu.SemaphoreType.DMA],
        input_output_aliases={0: 0},
        compiler_params=LIMIT,
        name="finish",
    )(*operands)


def swap_by_core(value, first, second):
    n_section, n_rep = lax.axis_size("section"), lax.axis_size("rep")
    pairs = []
    for s in range(n_section):
        chip, rep = second if s & 1 else first
        for r in range(n_rep):
            pairs.append((s * n_rep + r, (s ^ 2 * chip % n_section) * n_rep + (r ^ rep % n_rep)))
    return lax.ppermute(value, ("section", "rep"), pairs)


def gather_blocks(features, axis, ready):
    n = lax.axis_size(axis)
    blocks = [None] * n
    blocks[0] = features
    for j in range(2, n, 2):
        blocks[j] = swap(features, axis, j)
    blocks[1] = swap(features, axis, 1)
    blocks[2::2], ready = lax.optimization_barrier((blocks[2::2], ready))
    for j in range(2, n, 2):
        blocks[j + 1] = swap(blocks[j], axis, 1)
    return blocks, ready


def per_device(features, adj_tiles, adj_src, cotangent, weight, destination):
    n_section, n_rep = lax.axis_size("section"), lax.axis_size("rep")
    rows_here, width = features.shape
    tile = adj_tiles.shape[3]
    slots = max(2, 2 * rows_here // n_section)
    target = destination.reshape(1, rows_here)
    wide, own, placing = prepare(adj_tiles[:, 0], features, target, n_section * slots, slots)
    blocks, (wide, own, placing) = gather_blocks(features, "section", (wide, own, placing))
    parts = list(partials(adj_src[:, 0], wide, [own] + blocks[1:]))
    others = across(n_rep)
    steps = zip(others, turned(n_rep))
    parts = parts[:1] + [swap_by_core(p, (0, j), (0, k)) for p, (j, k) in zip(parts[1:], steps)]
    same, kept, sent = dense(parts, weight, cotangent, placing)
    came = swap(sent, "section", 1)
    chips = n_section // 2
    steps = across(max(n_rep, chips))
    half_shape = (width // 2, width)
    half, *first = call_halves(
        functools.partial(first_kernel, slots), "first", [same, kept, came], half_shape, slots, len(steps)
    )
    first = [swap_by_core(m, (0, j), (j, 0)) for m, j in zip(first, steps)]
    relaid = store(same, came, first, n_section, slots)
    half, *second = call_halves(
        functools.partial(second_kernel, slots, (n_rep, chips), len(steps)),
        "second",
        [same, came, half, *first],
        half_shape,
        slots,
        len(steps),
    )
    second = [swap_by_core(m, (j, 0), (0, j)) for m, j in zip(second, steps)]
    (half,) = call_halves(
        functools.partial(third_kernel, slots, (chips, n_rep)), "third", [half, *second], half_shape, slots, 0
    )
    other = swap(half, "section", 1)
    relaid, weight_grad = finish(relaid, half, other, same, came, second, slots)
    return (relaid.reshape(1, 1, n_section, slots, width), weight_grad.reshape(width, width))


def solution(mesh):
    placed = (
        P(("section", "rep"), None),
        P("section", "rep", None, None, None),
        P("section", "rep", None),
        P(("section", "rep"), None),
        P(),
        P(("section", "rep"), None),
    )
    return jax.shard_map(
        per_device,
        mesh=mesh,
        in_specs=placed,
        out_specs=(P("section", "rep", None, None, None), P()),
        check_vma=False,
    )
```

```python
import functools

import jax
import jax.numpy as jnp
from jax import lax
from jax.experimental import pallas as pl
from jax.experimental.pallas import tpu as pltpu
from jax.sharding import PartitionSpec as P

VMEM = pl.BlockSpec(memory_space=pltpu.VMEM)
LIMIT = pltpu.CompilerParams(vmem_limit_bytes=32 * 1024 * 1024)
HBM = pl.BlockSpec(memory_space=pltpu.HBM)


def across(n):
    return list(range(n - 1, 0, -1))


def prepare_kernel(slots, tiles_ref, own_ref, target_ref, wide_ref, held_ref, placing_ref):
    many, depth = tiles_ref.shape[:2]
    for g in range(many):
        wide_ref[g] = jnp.concatenate([tiles_ref[g, k] for k in range(depth)], axis=1)
    held_ref[...] = own_ref[...]
    places, rows = placing_ref.shape
    n_section = places // slots
    target = target_ref[...]
    hits = lax.broadcasted_iota(jnp.int32, (n_section, rows), 0) == target
    hits = jnp.where(hits, 1.0, 0.0)
    earlier = lax.broadcasted_iota(jnp.int32, (rows, rows), 0) < lax.broadcasted_iota(
        jnp.int32, (rows, rows), 1
    )
    earlier = jnp.where(earlier, 1.0, 0.0).astype(jnp.bfloat16)
    before = jnp.dot(hits.astype(jnp.bfloat16), earlier, preferred_element_type=jnp.float32)
    slot = jnp.sum(before * hits, axis=0, keepdims=True).astype(jnp.int32)
    apart = target ^ lax.axis_index("section")
    position = ((apart & 1) * (n_section // 2) + (apart >> 1)) * slots + slot
    placing = lax.broadcasted_iota(jnp.int32, (places, rows), 0) == position
    placing_ref[...] = jnp.where(placing, 1.0, 0.0).astype(jnp.bfloat16)


def prepare(tiles, own, target, places, slots):
    many, depth, tile, _ = tiles.shape
    return pl.pallas_call(
        functools.partial(prepare_kernel, slots),
        out_shape=(
            jax.ShapeDtypeStruct((many, tile, depth * tile), jnp.bfloat16),
            jax.ShapeDtypeStruct(own.shape, jnp.bfloat16),
            jax.ShapeDtypeStruct((places, target.shape[1]), jnp.bfloat16),
        ),
        in_specs=[VMEM] * 3,
        out_specs=(VMEM,) * 3,
        compiler_params=LIMIT,
        cost_estimate=pl.CostEstimate(flops=0, bytes_accessed=2 * tiles.size * 2, transcendentals=0),
        name="prepare",
    )(tiles, own, target)


def partials_kernel(count, src_ref, wide_ref, *refs):
    block_refs, out_refs, held = refs[:count], refs[count:-1], refs[-1]
    depth = src_ref.shape[1]
    section, rep = lax.axis_index("section"), lax.axis_index("rep")
    for j in range(count):
        held[j] = block_refs[j][...]
    for j, out_ref in zip([0] + across(len(out_refs)), out_refs):
        g = rep ^ j
        right = jnp.concatenate([held[src_ref[g, k] ^ section] for k in range(depth)], axis=0)
        out_ref[...] = jnp.dot(wide_ref[g], right, preferred_element_type=jnp.float32).astype(
            jnp.bfloat16
        )


def partials(sources, wide, blocks):
    many = wide.shape[0]
    tile, width = blocks[0].shape
    return pl.pallas_call(
        functools.partial(partials_kernel, len(blocks)),
        out_shape=[jax.ShapeDtypeStruct((tile, width), jnp.bfloat16)] * many,
        in_specs=[VMEM] * (2 + len(blocks)),
        out_specs=[VMEM] * many,
        scratch_shapes=[pltpu.VMEM((len(blocks), tile, width), jnp.bfloat16)],
        compiler_params=LIMIT,
        name="partials",
    )(sources, wide, *blocks)


def swap(value, axis, j):
    return lax.ppermute(value, axis, [(i, i ^ j) for i in range(lax.axis_size(axis))])


def tree_sum(terms):
    while len(terms) > 1:
        terms = [terms[i] + terms[i + 1] for i in range(0, len(terms), 2)]
    return terms[0]


def dense_kernel(n_part, weight_ref, cot_ref, placing_ref, *refs):
    part_refs, (same_ref, kept_ref, sent_ref, term) = refs[:n_part], refs[n_part:]
    core = lax.axis_index("section") & 1
    agg_b = tree_sum([ref[...].astype(jnp.float32) for ref in part_refs]).astype(jnp.bfloat16)
    pre = jnp.dot(agg_b, weight_ref[...], preferred_element_type=jnp.float32)
    sig = jax.nn.sigmoid(pre)
    factor = sig * (1.0 + pre * (1.0 - sig))
    grad_pre = (cot_ref[...].astype(jnp.float32) * factor).astype(jnp.bfloat16)
    whole = lax.dot_general(
        agg_b, grad_pre, (((0,), (0,)), ((), ())), preferred_element_type=jnp.float32
    )
    term[...] = whole.reshape(term.shape)
    kept_ref[...] = term[core]
    output = (pre * sig).astype(jnp.bfloat16)
    packed = jnp.dot(placing_ref[...], output, preferred_element_type=jnp.float32)
    half = packed.shape[0] // 2
    same_ref[...] = packed[:half].astype(jnp.bfloat16)
    sent_ref[:half] = packed[half:].astype(jnp.bfloat16)
    sent_ref[half:] = term[1 - core].astype(jnp.bfloat16)


def dense(parts, weight, cotangent, placing):
    places, width = placing.shape[0], weight.shape[0]
    return pl.pallas_call(
        functools.partial(dense_kernel, len(parts)),
        out_shape=(
            jax.ShapeDtypeStruct((places // 2, width), jnp.bfloat16),
            jax.ShapeDtypeStruct((width // 2, width), jnp.float32),
            jax.ShapeDtypeStruct((places // 2 + width // 2, width), jnp.bfloat16),
        ),
        in_specs=[VMEM] * (3 + len(parts)),
        out_specs=(VMEM,) * 3,
        scratch_shapes=[pltpu.VMEM((2, width // 2, width), jnp.float32)],
        compiler_params=LIMIT,
        name="dense",
    )(weight, cotangent, placing, *parts)


def write_messages(slots, same_ref, came_ref, half, out_refs):
    for ref, j in zip(out_refs, across(len(out_refs) + 1)):
        start = j * slots % same_ref.shape[0]
        ref[:slots] = same_ref[start : start + slots]
        ref[slots : 2 * slots] = came_ref[start : start + slots]
        ref[2 * slots :] = half


def sum_halves(half_ref, slots, own_ref, message_refs, counts):
    by_xor = [own_ref[...].astype(jnp.float32)]
    by_xor += [ref[2 * slots :].astype(jnp.float32) for ref in message_refs[::-1]]
    for core in range(2):

        @pl.when(lax.axis_index("section") & 1 == core)
        def _():
            half_ref[...] = tree_sum(by_xor[: counts[core]]).astype(jnp.bfloat16)


def first_kernel(slots, same_ref, kept_ref, came_ref, half_ref, *out_refs):
    rows = kept_ref.shape[0]
    half = kept_ref[...] + came_ref[came_ref.shape[0] - rows :].astype(jnp.float32)
    half_ref[...] = half.astype(jnp.bfloat16)
    write_messages(slots, same_ref, came_ref, half_ref[...], out_refs)


def second_kernel(slots, counts, many, same_ref, came_ref, own_ref, *refs):
    message_refs, half_ref, out_refs = refs[:many], refs[many], refs[many + 1 :]
    sum_halves(half_ref, slots, own_ref, message_refs, counts)
    write_messages(slots, same_ref, came_ref, half_ref[...], out_refs)


def third_kernel(slots, counts, own_ref, *refs):
    sum_halves(refs[-1], slots, own_ref, refs[:-1], counts)


def call_halves(kernel, name, operands, half, slots, many):
    shapes = [jax.ShapeDtypeStruct(half, jnp.bfloat16)]
    shapes += [jax.ShapeDtypeStruct((2 * slots + half[0], half[1]), jnp.bfloat16)] * many
    return pl.pallas_call(
        kernel,
        out_shape=shapes,
        in_specs=[VMEM] * len(operands),
        out_specs=[VMEM] * len(shapes),
        compiler_params=LIMIT,
        name=name,
    )(*operands)


def store_kernel(core, slots, same_ref, came_ref, *refs):
    message_refs, (out_ref, rows, sem) = refs[:-3], refs[-3:]
    section = lax.axis_index("section")
    chips = lax.axis_size("section") // 2

    @pl.when(section & 1 == core)
    def _():
        rows[section] = same_ref[:slots]
        rows[section ^ 1] = came_ref[:slots]
        for ref, j in zip(message_refs, across(len(message_refs) + 1)):
            if j < chips:
                rows[section ^ (2 * j)] = ref[:slots]
                rows[section ^ (2 * j + 1)] = ref[slots : 2 * slots]
        copy = pltpu.make_async_copy(rows, out_ref, sem)
        copy.start()
        copy.wait()


def store(core, same, came, messages, n_section, slots, base=None):
    shape = (n_section, slots, same.shape[1])
    operands = [same, came, *messages]
    kernel, first, specs = functools.partial(store_kernel, core, slots), [], []
    if base is not None:
        kernel, first, specs = lambda _, *refs: store_kernel(core, slots, *refs), [base], [HBM]
    return pl.pallas_call(
        kernel,
        out_shape=jax.ShapeDtypeStruct(shape, jnp.bfloat16),
        in_specs=specs + [VMEM] * len(operands),
        out_specs=HBM,
        scratch_shapes=[pltpu.VMEM(shape, jnp.bfloat16), pltpu.SemaphoreType.DMA],
        input_output_aliases={0: 0} if first else {},
        compiler_params=LIMIT,
        name="store",
    )(*first, *operands)


def finish_kernel(own_ref, came_ref, out_ref):
    core = lax.axis_index("section") & 1
    out_ref[core] = own_ref[...].astype(jnp.float32)
    out_ref[1 - core] = came_ref[...].astype(jnp.float32)


def finish(own, came):
    return pl.pallas_call(
        finish_kernel,
        out_shape=jax.ShapeDtypeStruct((2,) + own.shape, jnp.float32),
        in_specs=[VMEM] * 2,
        out_specs=VMEM,
        compiler_params=LIMIT,
        name="finish",
    )(own, came)


def swap_by_core(value, first, second):
    n_section, n_rep = lax.axis_size("section"), lax.axis_size("rep")
    pairs = []
    for s in range(n_section):
        chip, rep = second if s & 1 else first
        for r in range(n_rep):
            pairs.append((s * n_rep + r, (s ^ 2 * chip % n_section) * n_rep + (r ^ rep % n_rep)))
    return lax.ppermute(value, ("section", "rep"), pairs)


def gather_blocks(features, axis, ready):
    n = lax.axis_size(axis)
    blocks = [None] * n
    blocks[0] = features
    order = sorted(range(2, n, 2), key=lambda j: (j & 4, -(j & 2)))
    for j in order:
        blocks[j] = swap(features, axis, j)
    blocks[1] = swap(features, axis, 1)
    came, ready = lax.optimization_barrier(([blocks[j] for j in order], ready))
    for j, block in zip(order, came):
        blocks[j] = block
    for j in range(2, n, 2):
        blocks[j + 1] = swap(blocks[j], axis, 1)
    return blocks, ready


def per_device(features, adj_tiles, adj_src, cotangent, weight, destination):
    n_section, n_rep = lax.axis_size("section"), lax.axis_size("rep")
    rows_here, width = features.shape
    tile = adj_tiles.shape[3]
    slots = max(2, 2 * rows_here // n_section)
    target = destination.reshape(1, rows_here)
    wide, own, placing = prepare(adj_tiles[:, 0], features, target, n_section * slots, slots)
    blocks, (wide, own, placing) = gather_blocks(features, "section", (wide, own, placing))
    parts = list(partials(adj_src[:, 0], wide, [own] + blocks[1:]))
    others = across(n_rep)
    parts = parts[:1] + [swap(part, "rep", j) for part, j in zip(parts[1:], others)]
    same, kept, sent = dense(parts, weight, cotangent, placing)
    came = swap(sent, "section", 1)
    chips = n_section // 2
    steps = across(max(n_rep, chips))
    half_shape = (width // 2, width)
    half, *first = call_halves(
        functools.partial(first_kernel, slots), "first", [same, kept, came], half_shape, slots, len(steps)
    )
    first = [swap_by_core(m, (j, 0), (0, j)) for m, j in zip(first, steps)]
    relaid = store(0, same, came, first, n_section, slots)
    half, *second = call_halves(
        functools.partial(second_kernel, slots, (chips, n_rep), len(steps)),
        "second",
        [same, came, half, *first],
        half_shape,
        slots,
        len(steps),
    )
    second = [swap_by_core(m, (0, j), (j, 0)) for m, j in zip(second, steps)]
    (half,) = call_halves(
        functools.partial(third_kernel, slots, (n_rep, chips)), "third", [half, *second], half_shape, slots, 0
    )
    relaid = store(1, same, came, second, n_section, slots, relaid)
    half, relaid = lax.optimization_barrier((half, relaid))
    weight_grad = finish(half, swap(half, "section", 1))
    return (relaid.reshape(1, 1, n_section, slots, width), weight_grad.reshape(width, width))


def solution(mesh):
    placed = (
        P(("section", "rep"), None),
        P("section", "rep", None, None, None),
        P("section", "rep", None),
        P(("section", "rep"), None),
        P(),
        P(("section", "rep"), None),
    )
    return jax.shard_map(
        per_device,
        mesh=mesh,
        in_specs=placed,
        out_specs=(P("section", "rep", None, None, None), P()),
        check_vma=False,
    )
```

```python
import functools

import jax
import jax.numpy as jnp
from jax import lax
from jax.experimental import pallas as pl
from jax.experimental.pallas import tpu as pltpu
from jax.sharding import PartitionSpec as P

VMEM = pl.BlockSpec(memory_space=pltpu.VMEM)
LIMIT = pltpu.CompilerParams(vmem_limit_bytes=32 * 1024 * 1024)
HBM = pl.BlockSpec(memory_space=pltpu.HBM)


def across(n):
    return list(range(n - 1, 0, -1))


def place_of_chip():
    return lax.axis_index("section") >> 1, lax.axis_size("section") // 2


def prepare_kernel(slots, tiles_ref, own_ref, target_ref, wide_ref, held_ref, placing_ref):
    many, depth = tiles_ref.shape[:2]
    for g in range(many):
        wide_ref[g] = jnp.concatenate([tiles_ref[g, k] for k in range(depth)], axis=1)
    held_ref[...] = own_ref[...]
    places, rows = placing_ref.shape
    n_section = places // slots
    target = target_ref[...]
    hits = lax.broadcasted_iota(jnp.int32, (n_section, rows), 0) == target
    hits = jnp.where(hits, 1.0, 0.0)
    earlier = lax.broadcasted_iota(jnp.int32, (rows, rows), 0) < lax.broadcasted_iota(
        jnp.int32, (rows, rows), 1
    )
    earlier = jnp.where(earlier, 1.0, 0.0).astype(jnp.bfloat16)
    before = jnp.dot(hits.astype(jnp.bfloat16), earlier, preferred_element_type=jnp.float32)
    slot = jnp.sum(before * hits, axis=0, keepdims=True).astype(jnp.int32)
    chip, chips = place_of_chip()
    apart = (target >> 1) - chip
    apart = jnp.where(apart < 0, apart + chips, apart)
    other_core = (target ^ lax.axis_index("section")) & 1
    position = (other_core * chips + apart) * slots + slot
    placing = lax.broadcasted_iota(jnp.int32, (places, rows), 0) == position
    placing_ref[...] = jnp.where(placing, 1.0, 0.0).astype(jnp.bfloat16)


def prepare(tiles, own, target, places, slots):
    many, depth, tile, _ = tiles.shape
    return pl.pallas_call(
        functools.partial(prepare_kernel, slots),
        out_shape=(
            jax.ShapeDtypeStruct((many, tile, depth * tile), jnp.bfloat16),
            jax.ShapeDtypeStruct(own.shape, jnp.bfloat16),
            jax.ShapeDtypeStruct((places, target.shape[1]), jnp.bfloat16),
        ),
        in_specs=[VMEM] * 3,
        out_specs=(VMEM,) * 3,
        compiler_params=LIMIT,
        cost_estimate=pl.CostEstimate(flops=0, bytes_accessed=2 * tiles.size * 2, transcendentals=0),
        name="prepare",
    )(tiles, own, target)


def partials_kernel(count, src_ref, wide_ref, *refs):
    block_refs, out_refs, held = refs[:count], refs[count:-1], refs[-1]
    depth = src_ref.shape[1]
    section, rep = lax.axis_index("section"), lax.axis_index("rep")
    for j in range(count):
        held[j] = block_refs[j][...]
    for j, out_ref in zip([0] + across(len(out_refs)), out_refs):
        g = rep ^ j
        right = jnp.concatenate([held[src_ref[g, k] ^ section] for k in range(depth)], axis=0)
        out_ref[...] = jnp.dot(wide_ref[g], right, preferred_element_type=jnp.float32).astype(
            jnp.bfloat16
        )


def partials(sources, wide, blocks):
    many = wide.shape[0]
    tile, width = blocks[0].shape
    return pl.pallas_call(
        functools.partial(partials_kernel, len(blocks)),
        out_shape=[jax.ShapeDtypeStruct((tile, width), jnp.bfloat16)] * many,
        in_specs=[VMEM] * (2 + len(blocks)),
        out_specs=[VMEM] * many,
        scratch_shapes=[pltpu.VMEM((len(blocks), tile, width), jnp.bfloat16)],
        compiler_params=LIMIT,
        name="partials",
    )(sources, wide, *blocks)


def swap(value, axis, j):
    return lax.ppermute(value, axis, [(i, i ^ j) for i in range(lax.axis_size(axis))])


def tree_sum(terms):
    while len(terms) > 1:
        terms = [terms[i] + terms[i + 1] for i in range(0, len(terms), 2)]
    return terms[0]


def dense_kernel(n_part, weight_ref, cot_ref, placing_ref, *refs):
    part_refs, (same_ref, kept_ref, sent_ref, term) = refs[:n_part], refs[n_part:]
    core = lax.axis_index("section") & 1
    agg_b = tree_sum([ref[...].astype(jnp.float32) for ref in part_refs]).astype(jnp.bfloat16)
    pre = jnp.dot(agg_b, weight_ref[...], preferred_element_type=jnp.float32)
    sig = jax.nn.sigmoid(pre)
    factor = sig * (1.0 + pre * (1.0 - sig))
    grad_pre = (cot_ref[...].astype(jnp.float32) * factor).astype(jnp.bfloat16)
    whole = lax.dot_general(
        agg_b, grad_pre, (((0,), (0,)), ((), ())), preferred_element_type=jnp.float32
    )
    term[...] = whole.reshape(term.shape)
    kept_ref[...] = term[core]
    output = (pre * sig).astype(jnp.bfloat16)
    packed = jnp.dot(placing_ref[...], output, preferred_element_type=jnp.float32)
    half = packed.shape[0] // 2
    same_ref[...] = packed[:half].astype(jnp.bfloat16)
    sent_ref[:half] = packed[half:].astype(jnp.bfloat16)
    sent_ref[half:] = term[1 - core].astype(jnp.bfloat16)


def dense(parts, weight, cotangent, placing):
    places, width = placing.shape[0], weight.shape[0]
    return pl.pallas_call(
        functools.partial(dense_kernel, len(parts)),
        out_shape=(
            jax.ShapeDtypeStruct((places // 2, width), jnp.bfloat16),
            jax.ShapeDtypeStruct((width // 2, width), jnp.float32),
            jax.ShapeDtypeStruct((places // 2 + width // 2, width), jnp.bfloat16),
        ),
        in_specs=[VMEM] * (3 + len(parts)),
        out_specs=(VMEM,) * 3,
        scratch_shapes=[pltpu.VMEM((2, width // 2, width), jnp.float32)],
        compiler_params=LIMIT,
        name="dense",
    )(weight, cotangent, placing, *parts)


def write_messages(slots, same_ref, came_ref, half, out_refs):
    for i, ref in enumerate(out_refs):
        start = (i + 1) * slots % same_ref.shape[0]
        ref[:slots] = same_ref[start : start + slots]
        ref[slots : 2 * slots] = came_ref[start : start + slots]
        ref[2 * slots :] = half


def sum_halves(half_ref, held, slots, own_ref, message_refs, core_along, n_rep):
    chip, chips = place_of_chip()
    core = lax.axis_index("section") & 1

    @pl.when(core == core_along)
    def _():
        held[chip] = own_ref[...]
        for i, ref in enumerate(message_refs[: chips - 1]):
            held[(chip + chips - i - 1) % chips] = ref[2 * slots :]
        total = tree_sum([held[c].astype(jnp.float32) for c in range(chips)])
        half_ref[...] = total.astype(jnp.bfloat16)

    @pl.when(core != core_along)
    def _():
        by_xor = [own_ref[...].astype(jnp.float32)]
        by_xor += [ref[2 * slots :].astype(jnp.float32) for ref in message_refs[::-1]]
        half_ref[...] = tree_sum(by_xor[:n_rep]).astype(jnp.bfloat16)


def first_kernel(slots, same_ref, kept_ref, came_ref, half_ref, *out_refs):
    rows = kept_ref.shape[0]
    half = kept_ref[...] + came_ref[came_ref.shape[0] - rows :].astype(jnp.float32)
    half_ref[...] = half.astype(jnp.bfloat16)
    write_messages(slots, same_ref, came_ref, half_ref[...], out_refs)


def second_kernel(slots, n_rep, many, same_ref, came_ref, own_ref, *refs):
    message_refs, half_ref, out_refs, held = refs[:many], refs[many], refs[many + 1 : -1], refs[-1]
    sum_halves(half_ref, held, slots, own_ref, message_refs, 0, n_rep)
    write_messages(slots, same_ref, came_ref, half_ref[...], out_refs)


def third_kernel(slots, n_rep, own_ref, *refs):
    sum_halves(refs[-2], refs[-1], slots, own_ref, refs[:-2], 1, n_rep)


def call_halves(kernel, name, operands, half, slots, many, held=()):
    shapes = [jax.ShapeDtypeStruct(half, jnp.bfloat16)]
    shapes += [jax.ShapeDtypeStruct((2 * slots + half[0], half[1]), jnp.bfloat16)] * many
    return pl.pallas_call(
        kernel,
        out_shape=shapes,
        in_specs=[VMEM] * len(operands),
        out_specs=[VMEM] * len(shapes),
        scratch_shapes=[pltpu.VMEM(shape, jnp.bfloat16) for shape in held],
        compiler_params=LIMIT,
        name=name,
    )(*operands)


def store_kernel(core, slots, same_ref, came_ref, *refs):
    message_refs, (out_ref, rows, sem) = refs[:-3], refs[-3:]
    section = lax.axis_index("section")
    chip, chips = place_of_chip()

    @pl.when(section & 1 == core)
    def _():
        rows[section] = same_ref[:slots]
        rows[section ^ 1] = came_ref[:slots]
        for i, ref in enumerate(message_refs[: chips - 1]):
            source = 2 * ((chip + chips - i - 1) % chips)
            rows[source + core] = ref[:slots]
            rows[source + 1 - core] = ref[slots : 2 * slots]
        copy = pltpu.make_async_copy(rows, out_ref, sem)
        copy.start()
        copy.wait()


def store(core, same, came, messages, n_section, slots, base=None):
    shape = (n_section, slots, same.shape[1])
    operands = [same, came, *messages]
    kernel, first, specs = functools.partial(store_kernel, core, slots), [], []
    if base is not None:
        kernel, first, specs = lambda _, *refs: store_kernel(core, slots, *refs), [base], [HBM]
    return pl.pallas_call(
        kernel,
        out_shape=jax.ShapeDtypeStruct(shape, jnp.bfloat16),
        in_specs=specs + [VMEM] * len(operands),
        out_specs=HBM,
        scratch_shapes=[pltpu.VMEM(shape, jnp.bfloat16), pltpu.SemaphoreType.DMA],
        input_output_aliases={0: 0} if first else {},
        compiler_params=LIMIT,
        name="store",
    )(*first, *operands)


def finish_kernel(own_ref, came_ref, out_ref):
    core = lax.axis_index("section") & 1
    out_ref[core] = own_ref[...].astype(jnp.float32)
    out_ref[1 - core] = came_ref[...].astype(jnp.float32)


def finish(own, came):
    return pl.pallas_call(
        finish_kernel,
        out_shape=jax.ShapeDtypeStruct((2,) + own.shape, jnp.float32),
        in_specs=[VMEM] * 2,
        out_specs=VMEM,
        compiler_params=LIMIT,
        name="finish",
    )(own, came)


def exchange(value, core_along, shift, j):
    n_section, n_rep = lax.axis_size("section"), lax.axis_size("rep")
    pairs = []
    for s in range(n_section):
        along = s & 1 == core_along
        to = (s + 2 * shift) % n_section if along else s
        for r in range(n_rep):
            pairs.append((s * n_rep + r, to * n_rep + (r if along else r ^ j % n_rep)))
    return lax.ppermute(value, ("section", "rep"), pairs)


def gather_blocks(features, axis, ready):
    n = lax.axis_size(axis)
    blocks = [None] * n
    blocks[0] = features
    order = sorted(range(2, n, 2), key=lambda j: (j & 4, -(j & 2)))
    for j in order:
        blocks[j] = swap(features, axis, j)
    blocks[1] = swap(features, axis, 1)
    came, ready = lax.optimization_barrier(([blocks[j] for j in order], ready))
    for j, block in zip(order, came):
        blocks[j] = block
    for j in range(2, n, 2):
        blocks[j + 1] = swap(blocks[j], axis, 1)
    return blocks, ready


def per_device(features, adj_tiles, adj_src, cotangent, weight, destination):
    n_section, n_rep = lax.axis_size("section"), lax.axis_size("rep")
    rows_here, width = features.shape
    tile = adj_tiles.shape[3]
    slots = max(2, 2 * rows_here // n_section)
    target = destination.reshape(1, rows_here)
    wide, own, placing = prepare(adj_tiles[:, 0], features, target, n_section * slots, slots)
    blocks, (wide, own, placing) = gather_blocks(features, "section", (wide, own, placing))
    parts = list(partials(adj_src[:, 0], wide, [own] + blocks[1:]))
    others = across(n_rep)
    parts = parts[:1] + [swap(part, "rep", j) for part, j in zip(parts[1:], others)]
    same, kept, sent = dense(parts, weight, cotangent, placing)
    came = swap(sent, "section", 1)
    chips = n_section // 2
    steps = across(max(n_rep, chips))
    half_shape = (width // 2, width)
    held = [(chips,) + half_shape]
    half, *first = call_halves(
        functools.partial(first_kernel, slots), "first", [same, kept, came], half_shape, slots, len(steps)
    )
    first = [exchange(m, 0, i + 1, j) for i, (m, j) in enumerate(zip(first, steps))]
    relaid = store(0, same, came, first, n_section, slots)
    half, *second = call_halves(
        functools.partial(second_kernel, slots, n_rep, len(steps)),
        "second",
        [same, came, half, *first],
        half_shape,
        slots,
        len(steps),
        held,
    )
    second = [exchange(m, 1, i + 1, j) for i, (m, j) in enumerate(zip(second, steps))]
    (half,) = call_halves(
        functools.partial(third_kernel, slots, n_rep), "third", [half, *second], half_shape, slots, 0, held
    )
    relaid = store(1, same, came, second, n_section, slots, relaid)
    half, relaid = lax.optimization_barrier((half, relaid))
    weight_grad = finish(half, swap(half, "section", 1))
    return (relaid.reshape(1, 1, n_section, slots, width), weight_grad.reshape(width, width))


def solution(mesh):
    placed = (
        P(("section", "rep"), None),
        P("section", "rep", None, None, None),
        P("section", "rep", None),
        P(("section", "rep"), None),
        P(),
        P(("section", "rep"), None),
    )
    return jax.shard_map(
        per_device,
        mesh=mesh,
        in_specs=placed,
        out_specs=(P("section", "rep", None, None, None), P()),
        check_vma=False,
    )
```

```python
import functools

import jax
import jax.numpy as jnp
from jax import lax
from jax.experimental import pallas as pl
from jax.experimental.pallas import tpu as pltpu
from jax.sharding import PartitionSpec as P

VMEM = pl.BlockSpec(memory_space=pltpu.VMEM)
LIMIT = pltpu.CompilerParams(vmem_limit_bytes=32 * 1024 * 1024)
HBM = pl.BlockSpec(memory_space=pltpu.HBM)


def across(n):
    return list(range(n - 1, 0, -1))


def place_of_chip():
    return lax.axis_index("section") >> 1, lax.axis_size("section") // 2


def prepare_kernel(slots, tiles_ref, own_ref, target_ref, wide_ref, held_ref, placing_ref):
    many, depth = tiles_ref.shape[:2]
    for g in range(many):
        wide_ref[g] = jnp.concatenate([tiles_ref[g, k] for k in range(depth)], axis=1)
    held_ref[...] = own_ref[...]
    places, rows = placing_ref.shape
    n_section = places // slots
    target = target_ref[...]
    hits = lax.broadcasted_iota(jnp.int32, (n_section, rows), 0) == target
    hits = jnp.where(hits, 1.0, 0.0)
    earlier = lax.broadcasted_iota(jnp.int32, (rows, rows), 0) < lax.broadcasted_iota(
        jnp.int32, (rows, rows), 1
    )
    earlier = jnp.where(earlier, 1.0, 0.0).astype(jnp.bfloat16)
    before = jnp.dot(hits.astype(jnp.bfloat16), earlier, preferred_element_type=jnp.float32)
    slot = jnp.sum(before * hits, axis=0, keepdims=True).astype(jnp.int32)
    chip, chips = place_of_chip()
    apart = (target >> 1) - chip
    apart = jnp.where(apart < 0, apart + chips, apart)
    other_core = (target ^ lax.axis_index("section")) & 1
    position = (other_core * chips + apart) * slots + slot
    placing = lax.broadcasted_iota(jnp.int32, (places, rows), 0) == position
    placing_ref[...] = jnp.where(placing, 1.0, 0.0).astype(jnp.bfloat16)


def prepare(tiles, own, target, places, slots):
    many, depth, tile, _ = tiles.shape
    return pl.pallas_call(
        functools.partial(prepare_kernel, slots),
        out_shape=(
            jax.ShapeDtypeStruct((many, tile, depth * tile), jnp.bfloat16),
            jax.ShapeDtypeStruct(own.shape, jnp.bfloat16),
            jax.ShapeDtypeStruct((places, target.shape[1]), jnp.bfloat16),
        ),
        in_specs=[VMEM] * 3,
        out_specs=(VMEM,) * 3,
        compiler_params=LIMIT,
        cost_estimate=pl.CostEstimate(flops=0, bytes_accessed=2 * tiles.size * 2, transcendentals=0),
        name="prepare",
    )(tiles, own, target)


def partials_kernel(count, src_ref, wide_ref, *refs):
    block_refs, out_refs, held = refs[:count], refs[count:-1], refs[-1]
    depth = src_ref.shape[1]
    section, rep = lax.axis_index("section"), lax.axis_index("rep")
    for j in range(count):
        held[j] = block_refs[j][...]
    for j, out_ref in zip([0] + across(len(out_refs)), out_refs):
        g = rep ^ j
        right = jnp.concatenate([held[src_ref[g, k] ^ section] for k in range(depth)], axis=0)
        out_ref[...] = jnp.dot(wide_ref[g], right, preferred_element_type=jnp.float32).astype(
            jnp.bfloat16
        )


def partials(sources, wide, blocks):
    many = wide.shape[0]
    tile, width = blocks[0].shape
    return pl.pallas_call(
        functools.partial(partials_kernel, len(blocks)),
        out_shape=[jax.ShapeDtypeStruct((tile, width), jnp.bfloat16)] * many,
        in_specs=[VMEM] * (2 + len(blocks)),
        out_specs=[VMEM] * many,
        scratch_shapes=[pltpu.VMEM((len(blocks), tile, width), jnp.bfloat16)],
        compiler_params=LIMIT,
        name="partials",
    )(sources, wide, *blocks)


def swap(value, axis, j):
    return lax.ppermute(value, axis, [(i, i ^ j) for i in range(lax.axis_size(axis))])


def tree_sum(terms):
    while len(terms) > 1:
        terms = [terms[i] + terms[i + 1] for i in range(0, len(terms), 2)]
    return terms[0]


def dense_kernel(n_part, weight_ref, cot_ref, placing_ref, *refs):
    part_refs, (same_ref, kept_ref, sent_ref, term) = refs[:n_part], refs[n_part:]
    core = lax.axis_index("section") & 1
    agg_b = tree_sum([ref[...].astype(jnp.float32) for ref in part_refs]).astype(jnp.bfloat16)
    pre = jnp.dot(agg_b, weight_ref[...], preferred_element_type=jnp.float32)
    sig = jax.nn.sigmoid(pre)
    factor = sig * (1.0 + pre * (1.0 - sig))
    grad_pre = (cot_ref[...].astype(jnp.float32) * factor).astype(jnp.bfloat16)
    whole = lax.dot_general(
        agg_b, grad_pre, (((0,), (0,)), ((), ())), preferred_element_type=jnp.float32
    )
    term[...] = whole.reshape(term.shape)
    kept_ref[...] = term[core]
    output = (pre * sig).astype(jnp.bfloat16)
    packed = jnp.dot(placing_ref[...], output, preferred_element_type=jnp.float32)
    half = packed.shape[0] // 2
    same_ref[...] = packed[:half].astype(jnp.bfloat16)
    sent_ref[:half] = packed[half:].astype(jnp.bfloat16)
    sent_ref[half:] = term[1 - core].astype(jnp.bfloat16)


def dense(parts, weight, cotangent, placing):
    places, width = placing.shape[0], weight.shape[0]
    return pl.pallas_call(
        functools.partial(dense_kernel, len(parts)),
        out_shape=(
            jax.ShapeDtypeStruct((places // 2, width), jnp.bfloat16),
            jax.ShapeDtypeStruct((width // 2, width), jnp.float32),
            jax.ShapeDtypeStruct((places // 2 + width // 2, width), jnp.bfloat16),
        ),
        in_specs=[VMEM] * (3 + len(parts)),
        out_specs=(VMEM,) * 3,
        scratch_shapes=[pltpu.VMEM((2, width // 2, width), jnp.float32)],
        compiler_params=LIMIT,
        name="dense",
    )(weight, cotangent, placing, *parts)


def write_messages(slots, same_ref, came_ref, half, out_refs):
    for i, ref in enumerate(out_refs):
        start = (i + 1) * slots % same_ref.shape[0]
        ref[:slots] = same_ref[start : start + slots]
        ref[slots : 2 * slots] = came_ref[start : start + slots]
        ref[2 * slots :] = half


def first_kernel(slots, same_ref, kept_ref, came_ref, half_ref, *out_refs):
    rows = kept_ref.shape[0]
    half = kept_ref[...] + came_ref[came_ref.shape[0] - rows :].astype(jnp.float32)
    half_ref[...] = half.astype(jnp.bfloat16)
    write_messages(slots, same_ref, came_ref, half_ref[...], out_refs)


def second_kernel(slots, own_ref, *refs):
    message_refs, half_ref, held = refs[:-2], refs[-2], refs[-1]
    chip, chips = place_of_chip()
    held[chip] = own_ref[...]
    for i, ref in enumerate(message_refs):
        held[(chip + chips - i - 1) % chips] = ref[2 * slots :]
    total = tree_sum([held[c].astype(jnp.float32) for c in range(chips)])
    half_ref[...] = total.astype(jnp.bfloat16)


def third_kernel(*refs):
    refs[-1][...] = tree_sum([ref[...].astype(jnp.float32) for ref in refs[:-1]]).astype(jnp.bfloat16)


def call_halves(kernel, name, operands, half, slots, many, held=()):
    shapes = [jax.ShapeDtypeStruct(half, jnp.bfloat16)]
    shapes += [jax.ShapeDtypeStruct((2 * slots + half[0], half[1]), jnp.bfloat16)] * many
    return pl.pallas_call(
        kernel,
        out_shape=shapes,
        in_specs=[VMEM] * len(operands),
        out_specs=[VMEM] * len(shapes),
        scratch_shapes=[pltpu.VMEM(shape, jnp.bfloat16) for shape in held],
        compiler_params=LIMIT,
        name=name,
    )(*operands)


def store_kernel(slots, same_ref, came_ref, *refs):
    message_refs, (out_ref, rows, sem) = refs[:-3], refs[-3:]
    section = lax.axis_index("section")
    core = section & 1
    chip, chips = place_of_chip()
    rows[section] = same_ref[:slots]
    rows[section ^ 1] = came_ref[:slots]
    for i, ref in enumerate(message_refs):
        source = 2 * ((chip + chips - i - 1) % chips)
        rows[source + core] = ref[:slots]
        rows[source + 1 - core] = ref[slots : 2 * slots]
    copy = pltpu.make_async_copy(rows, out_ref, sem)
    copy.start()
    copy.wait()


def store(same, came, messages, n_section, slots):
    shape = (n_section, slots, same.shape[1])
    return pl.pallas_call(
        functools.partial(store_kernel, slots),
        out_shape=jax.ShapeDtypeStruct(shape, jnp.bfloat16),
        in_specs=[VMEM] * (2 + len(messages)),
        out_specs=HBM,
        scratch_shapes=[pltpu.VMEM(shape, jnp.bfloat16), pltpu.SemaphoreType.DMA],
        compiler_params=LIMIT,
        name="store",
    )(same, came, *messages)


def finish_kernel(own_ref, came_ref, out_ref):
    core = lax.axis_index("section") & 1
    out_ref[core] = own_ref[...].astype(jnp.float32)
    out_ref[1 - core] = came_ref[...].astype(jnp.float32)


def finish(own, came):
    return pl.pallas_call(
        finish_kernel,
        out_shape=jax.ShapeDtypeStruct((2,) + own.shape, jnp.float32),
        in_specs=[VMEM] * 2,
        out_specs=VMEM,
        compiler_params=LIMIT,
        name="finish",
    )(own, came)


def send_along(value, axis, shift):
    n = lax.axis_size(axis)
    return lax.ppermute(value, axis, [(s, (s + 2 * shift) % n) for s in range(n)])


def gather_blocks(features, axis, ready):
    n = lax.axis_size(axis)
    blocks = [None] * n
    blocks[0] = features
    order = sorted(range(2, n, 2), key=lambda j: (j & 4, -(j & 2)))
    for j in order:
        blocks[j] = swap(features, axis, j)
    blocks[1] = swap(features, axis, 1)
    came, ready = lax.optimization_barrier(([blocks[j] for j in order], ready))
    for j, block in zip(order, came):
        blocks[j] = block
    for j in range(2, n, 2):
        blocks[j + 1] = swap(blocks[j], axis, 1)
    return blocks, ready


def per_device(features, adj_tiles, adj_src, cotangent, weight, destination):
    n_section, n_rep = lax.axis_size("section"), lax.axis_size("rep")
    rows_here, width = features.shape
    tile = adj_tiles.shape[3]
    slots = max(2, 2 * rows_here // n_section)
    target = destination.reshape(1, rows_here)
    wide, own, placing = prepare(adj_tiles[:, 0], features, target, n_section * slots, slots)
    blocks, (wide, own, placing) = gather_blocks(features, "section", (wide, own, placing))
    parts = list(partials(adj_src[:, 0], wide, [own] + blocks[1:]))
    others = across(n_rep)
    parts = parts[:1] + [swap(part, "rep", j) for part, j in zip(parts[1:], others)]
    same, kept, sent = dense(parts, weight, cotangent, placing)
    came = swap(sent, "section", 1)
    chips = n_section // 2
    half_shape = (width // 2, width)
    half, *messages = call_halves(
        functools.partial(first_kernel, slots), "first", [same, kept, came], half_shape, slots, chips - 1
    )
    messages = [send_along(m, "section", i + 1) for i, m in enumerate(messages)]
    relaid = store(same, came, messages, n_section, slots)
    second = functools.partial(second_kernel, slots)
    held = [(chips,) + half_shape]
    (half,) = call_halves(second, "second", [half, *messages], half_shape, slots, 0, held)
    halves = [half] + [swap(half, "rep", j) for j in range(1, n_rep)]
    (half,) = call_halves(third_kernel, "third", halves, half_shape, slots, 0)
    half, relaid = lax.optimization_barrier((half, relaid))
    weight_grad = finish(half, swap(half, "section", 1))
    return (relaid.reshape(1, 1, n_section, slots, width), weight_grad.reshape(width, width))


def solution(mesh):
    placed = (
        P(("section", "rep"), None),
        P("section", "rep", None, None, None),
        P("section", "rep", None),
        P(("section", "rep"), None),
        P(),
        P(("section", "rep"), None),
    )
    return jax.shard_map(
        per_device,
        mesh=mesh,
        in_specs=placed,
        out_specs=(P("section", "rep", None, None, None), P()),
        check_vma=False,
    )
```

```python
import functools

import jax
import jax.numpy as jnp
from jax import lax
from jax.experimental import pallas as pl
from jax.experimental.pallas import tpu as pltpu
from jax.sharding import PartitionSpec as P

VMEM = pl.BlockSpec(memory_space=pltpu.VMEM)
LIMIT = pltpu.CompilerParams(vmem_limit_bytes=32 * 1024 * 1024)
HBM = pl.BlockSpec(memory_space=pltpu.HBM)


def across(n):
    return list(range(n - 1, 0, -1))


def place_of_chip():
    return lax.axis_index("section") >> 1, lax.axis_size("section") // 2


def prepare_kernel(slots, tiles_ref, own_ref, target_ref, wide_ref, held_ref, placing_ref):
    many, depth = tiles_ref.shape[:2]
    for g in range(many):
        wide_ref[g] = jnp.concatenate([tiles_ref[g, k] for k in range(depth)], axis=1)
    held_ref[...] = own_ref[...]
    places, rows = placing_ref.shape
    n_section = places // slots
    target = target_ref[...]
    hits = lax.broadcasted_iota(jnp.int32, (n_section, rows), 0) == target
    hits = jnp.where(hits, 1.0, 0.0)
    earlier = lax.broadcasted_iota(jnp.int32, (rows, rows), 0) < lax.broadcasted_iota(
        jnp.int32, (rows, rows), 1
    )
    earlier = jnp.where(earlier, 1.0, 0.0).astype(jnp.bfloat16)
    before = jnp.dot(hits.astype(jnp.bfloat16), earlier, preferred_element_type=jnp.float32)
    slot = jnp.sum(before * hits, axis=0, keepdims=True).astype(jnp.int32)
    chip, chips = place_of_chip()
    apart = (target >> 1) - chip
    apart = jnp.where(apart < 0, apart + chips, apart)
    other_core = (target ^ lax.axis_index("section")) & 1
    position = (other_core * chips + apart) * slots + slot
    placing = lax.broadcasted_iota(jnp.int32, (places, rows), 0) == position
    placing_ref[...] = jnp.where(placing, 1.0, 0.0).astype(jnp.bfloat16)


def prepare(tiles, own, target, places, slots):
    many, depth, tile, _ = tiles.shape
    return pl.pallas_call(
        functools.partial(prepare_kernel, slots),
        out_shape=(
            jax.ShapeDtypeStruct((many, tile, depth * tile), jnp.bfloat16),
            jax.ShapeDtypeStruct(own.shape, jnp.bfloat16),
            jax.ShapeDtypeStruct((places, target.shape[1]), jnp.bfloat16),
        ),
        in_specs=[VMEM] * 3,
        out_specs=(VMEM,) * 3,
        compiler_params=LIMIT,
        cost_estimate=pl.CostEstimate(flops=0, bytes_accessed=2 * tiles.size * 2, transcendentals=0),
        name="prepare",
    )(tiles, own, target)


def partials_kernel(count, src_ref, wide_ref, *refs):
    block_refs, out_refs, held = refs[:count], refs[count:-1], refs[-1]
    depth = src_ref.shape[1]
    section, rep = lax.axis_index("section"), lax.axis_index("rep")
    for j in range(count):
        held[j] = block_refs[j][...]
    for j, out_ref in zip([0] + across(len(out_refs)), out_refs):
        g = rep ^ j
        right = jnp.concatenate([held[src_ref[g, k] ^ section] for k in range(depth)], axis=0)
        out_ref[...] = jnp.dot(wide_ref[g], right, preferred_element_type=jnp.float32).astype(
            jnp.bfloat16
        )


def partials(sources, wide, blocks):
    many = wide.shape[0]
    tile, width = blocks[0].shape
    return pl.pallas_call(
        functools.partial(partials_kernel, len(blocks)),
        out_shape=[jax.ShapeDtypeStruct((tile, width), jnp.bfloat16)] * many,
        in_specs=[VMEM] * (2 + len(blocks)),
        out_specs=[VMEM] * many,
        scratch_shapes=[pltpu.VMEM((len(blocks), tile, width), jnp.bfloat16)],
        compiler_params=LIMIT,
        name="partials",
    )(sources, wide, *blocks)


def swap(value, axis, j):
    return lax.ppermute(value, axis, [(i, i ^ j) for i in range(lax.axis_size(axis))])


def tree_sum(terms):
    while len(terms) > 1:
        terms = [terms[i] + terms[i + 1] for i in range(0, len(terms), 2)]
    return terms[0]


def parts_of(width, slots):
    low = (width - 2 * slots) // 2 // 16 * 16
    return low, width - low


def dense_kernel(n_part, slots, weight_ref, cot_ref, placing_ref, *refs):
    part_refs, (same_ref, term_ref, sent_ref) = refs[:n_part], refs[n_part:]
    core = lax.axis_index("section") & 1
    agg_b = tree_sum([ref[...].astype(jnp.float32) for ref in part_refs]).astype(jnp.bfloat16)
    pre = jnp.dot(agg_b, weight_ref[...], preferred_element_type=jnp.float32)
    sig = jax.nn.sigmoid(pre)
    factor = sig * (1.0 + pre * (1.0 - sig))
    grad_pre = (cot_ref[...].astype(jnp.float32) * factor).astype(jnp.bfloat16)
    term = lax.dot_general(
        agg_b, grad_pre, (((0,), (0,)), ((), ())), preferred_element_type=jnp.float32
    )
    term_ref[...] = term
    output = (pre * sig).astype(jnp.bfloat16)
    packed = jnp.dot(placing_ref[...], output, preferred_element_type=jnp.float32)
    half = packed.shape[0] // 2
    same_ref[...] = packed[:half].astype(jnp.bfloat16)
    sent_ref[:half] = packed[half:].astype(jnp.bfloat16)
    low, high = parts_of(term.shape[0], slots)

    @pl.when(core == 0)
    def _():
        sent_ref[half:] = term[low:].astype(jnp.bfloat16)

    @pl.when(core == 1)
    def _():
        sent_ref[half : half + low] = term[:low].astype(jnp.bfloat16)


def dense(parts, weight, cotangent, placing, slots):
    places, width = placing.shape[0], weight.shape[0]
    return pl.pallas_call(
        functools.partial(dense_kernel, len(parts), slots),
        out_shape=(
            jax.ShapeDtypeStruct((places // 2, width), jnp.bfloat16),
            jax.ShapeDtypeStruct((width, width), jnp.float32),
            jax.ShapeDtypeStruct((places // 2 + parts_of(width, slots)[1], width), jnp.bfloat16),
        ),
        in_specs=[VMEM] * (3 + len(parts)),
        out_specs=(VMEM,) * 3,
        compiler_params=LIMIT,
        name="dense",
    )(weight, cotangent, placing, *parts)


def write_messages(core_along, slots, rows, same_ref, came_ref, half_ref, out_refs):
    core = lax.axis_index("section") & 1

    @pl.when(core == core_along)
    def _():
        for i, ref in enumerate(out_refs):
            start = (i + 1) * slots % same_ref.shape[0]
            ref[:slots] = same_ref[start : start + slots]
            ref[slots : 2 * slots] = came_ref[start : start + slots]
            ref[2 * slots : 2 * slots + rows[core_along]] = half_ref[: rows[core_along]]

    @pl.when(core != core_along)
    def _():
        for ref in out_refs:
            ref[: rows[1 - core_along]] = half_ref[: rows[1 - core_along]]


def sum_parts(core_along, slots, rows, half_ref, held, own_ref, message_refs, n_rep):
    chip, chips = place_of_chip()
    core = lax.axis_index("section") & 1

    @pl.when(core == core_along)
    def _():
        many = rows[core_along]
        held[chip, :many] = own_ref[:many]
        for i, ref in enumerate(message_refs[: chips - 1]):
            held[(chip + chips - i - 1) % chips, :many] = ref[2 * slots : 2 * slots + many]
        total = tree_sum([held[c, :many].astype(jnp.float32) for c in range(chips)])
        half_ref[:many] = total.astype(jnp.bfloat16)

    @pl.when(core != core_along)
    def _():
        many = rows[1 - core_along]
        by_xor = [ref[:many].astype(jnp.float32) for ref in [own_ref] + list(message_refs[::-1])]
        half_ref[:many] = tree_sum(by_xor[:n_rep]).astype(jnp.bfloat16)


def first_kernel(slots, rows, same_ref, term_ref, came_ref, half_ref, *out_refs):
    core = lax.axis_index("section") & 1
    start = same_ref.shape[0]

    @pl.when(core == 0)
    def _():
        other = came_ref[start : start + rows[0]].astype(jnp.float32)
        half_ref[: rows[0]] = (term_ref[: rows[0]] + other).astype(jnp.bfloat16)

    @pl.when(core == 1)
    def _():
        other = came_ref[start:].astype(jnp.float32)
        half_ref[...] = (term_ref[rows[0] :] + other).astype(jnp.bfloat16)

    write_messages(0, slots, rows, same_ref, came_ref, half_ref, out_refs)


def second_kernel(slots, rows, n_rep, many, same_ref, came_ref, own_ref, *refs):
    message_refs, half_ref, out_refs, held = refs[:many], refs[many], refs[many + 1 : -1], refs[-1]
    sum_parts(0, slots, rows, half_ref, held, own_ref, message_refs, n_rep)
    write_messages(1, slots, rows, same_ref, came_ref, half_ref, out_refs)


def third_kernel(slots, rows, n_rep, own_ref, *refs):
    sum_parts(1, slots, rows, refs[-2], refs[-1], own_ref, refs[:-2], n_rep)


def call_parts(kernel, name, operands, half, message, many, held=()):
    shapes = [jax.ShapeDtypeStruct(half, jnp.bfloat16)]
    shapes += [jax.ShapeDtypeStruct(message, jnp.bfloat16)] * many
    return pl.pallas_call(
        kernel,
        out_shape=shapes,
        in_specs=[VMEM] * len(operands),
        out_specs=[VMEM] * len(shapes),
        scratch_shapes=[pltpu.VMEM(shape, jnp.bfloat16) for shape in held],
        compiler_params=LIMIT,
        name=name,
    )(*operands)


def store_kernel(core, slots, same_ref, came_ref, *refs):
    message_refs, (out_ref, rows, sem) = refs[:-3], refs[-3:]
    section = lax.axis_index("section")
    chip, chips = place_of_chip()

    @pl.when(section & 1 == core)
    def _():
        rows[section] = same_ref[:slots]
        rows[section ^ 1] = came_ref[:slots]
        for i, ref in enumerate(message_refs[: chips - 1]):
            source = 2 * ((chip + chips - i - 1) % chips)
            rows[source + core] = ref[:slots]
            rows[source + 1 - core] = ref[slots : 2 * slots]
        copy = pltpu.make_async_copy(rows, out_ref, sem)
        copy.start()
        copy.wait()


def store(core, same, came, messages, n_section, slots, base=None):
    shape = (n_section, slots, same.shape[1])
    operands = [same, came, *messages]
    kernel, first, specs = functools.partial(store_kernel, core, slots), [], []
    if base is not None:
        kernel, first, specs = lambda _, *refs: store_kernel(core, slots, *refs), [base], [HBM]
    return pl.pallas_call(
        kernel,
        out_shape=jax.ShapeDtypeStruct(shape, jnp.bfloat16),
        in_specs=specs + [VMEM] * len(operands),
        out_specs=HBM,
        scratch_shapes=[pltpu.VMEM(shape, jnp.bfloat16), pltpu.SemaphoreType.DMA],
        input_output_aliases={0: 0} if first else {},
        compiler_params=LIMIT,
        name="store",
    )(*first, *operands)


def finish_kernel(rows, own_ref, came_ref, out_ref):
    core = lax.axis_index("section") & 1
    low, high = rows

    @pl.when(core == 0)
    def _():
        out_ref[:low] = own_ref[:low].astype(jnp.float32)
        out_ref[low:] = came_ref[...].astype(jnp.float32)

    @pl.when(core == 1)
    def _():
        out_ref[:low] = came_ref[:low].astype(jnp.float32)
        out_ref[low:] = own_ref[...].astype(jnp.float32)


def finish(own, came, rows):
    width = own.shape[1]
    return pl.pallas_call(
        functools.partial(finish_kernel, rows),
        out_shape=jax.ShapeDtypeStruct((width, width), jnp.float32),
        in_specs=[VMEM] * 2,
        out_specs=VMEM,
        compiler_params=LIMIT,
        name="finish",
    )(own, came)


def exchange(value, core_along, shift, j):
    n_section, n_rep = lax.axis_size("section"), lax.axis_size("rep")
    pairs = []
    for s in range(n_section):
        along = s & 1 == core_along
        to = (s + 2 * shift) % n_section if along else s
        for r in range(n_rep):
            pairs.append((s * n_rep + r, to * n_rep + (r if along else r ^ j % n_rep)))
    return lax.ppermute(value, ("section", "rep"), pairs)


def gather_blocks(features, axis, ready):
    n = lax.axis_size(axis)
    blocks = [None] * n
    blocks[0] = features
    order = sorted(range(2, n, 2), key=lambda j: (j & 4, -(j & 2)))
    for j in order:
        blocks[j] = swap(features, axis, j)
    blocks[1] = swap(features, axis, 1)
    came, ready = lax.optimization_barrier(([blocks[j] for j in order], ready))
    for j, block in zip(order, came):
        blocks[j] = block
    for j in range(2, n, 2):
        blocks[j + 1] = swap(blocks[j], axis, 1)
    return blocks, ready


def per_device(features, adj_tiles, adj_src, cotangent, weight, destination):
    n_section, n_rep = lax.axis_size("section"), lax.axis_size("rep")
    rows_here, width = features.shape
    tile = adj_tiles.shape[3]
    slots = max(2, 2 * rows_here // n_section)
    target = destination.reshape(1, rows_here)
    wide, own, placing = prepare(adj_tiles[:, 0], features, target, n_section * slots, slots)
    blocks, (wide, own, placing) = gather_blocks(features, "section", (wide, own, placing))
    parts = list(partials(adj_src[:, 0], wide, [own] + blocks[1:]))
    others = across(n_rep)
    parts = parts[:1] + [swap(part, "rep", j) for part, j in zip(parts[1:], others)]
    same, term, sent = dense(parts, weight, cotangent, placing, slots)
    came = swap(sent, "section", 1)
    chips = n_section // 2
    steps = across(max(n_rep, chips))
    many = len(steps)
    rows = parts_of(width, slots)
    part = (rows[1], width)
    held = [(chips,) + part]
    message = (max(rows[1], 2 * slots + rows[0]), width)
    operands = [same, term, came]
    half, *first = call_parts(
        functools.partial(first_kernel, slots, rows), "first", operands, part, message, many
    )
    first = [exchange(m, 0, i + 1, j) for i, (m, j) in enumerate(zip(first, steps))]
    relaid = store(0, same, came, first, n_section, slots)
    message = (2 * slots + rows[1], width)
    second = functools.partial(second_kernel, slots, rows, n_rep, many)
    operands = [same, came, half, *first]
    half, *second = call_parts(second, "second", operands, part, message, many, held)
    second = [exchange(m, 1, i + 1, j) for i, (m, j) in enumerate(zip(second, steps))]
    third = functools.partial(third_kernel, slots, rows, n_rep)
    (half,) = call_parts(third, "third", [half, *second], part, part, 0, held)
    relaid = store(1, same, came, second, n_section, slots, relaid)
    half, relaid = lax.optimization_barrier((half, relaid))
    weight_grad = finish(half, swap(half, "section", 1), rows)
    return (relaid.reshape(1, 1, n_section, slots, width), weight_grad)


def solution(mesh):
    placed = (
        P(("section", "rep"), None),
        P("section", "rep", None, None, None),
        P("section", "rep", None),
        P(("section", "rep"), None),
        P(),
        P(("section", "rep"), None),
    )
    return jax.shard_map(
        per_device,
        mesh=mesh,
        in_specs=placed,
        out_specs=(P("section", "rep", None, None, None), P()),
        check_vma=False,
    )
```

```python
import functools

import jax
import jax.numpy as jnp
from jax import lax
from jax.experimental import pallas as pl
from jax.experimental.pallas import tpu as pltpu
from jax.sharding import PartitionSpec as P

VMEM = pl.BlockSpec(memory_space=pltpu.VMEM)
LIMIT = pltpu.CompilerParams(vmem_limit_bytes=32 * 1024 * 1024)
HBM = pl.BlockSpec(memory_space=pltpu.HBM)


def across(n):
    return list(range(n - 1, 0, -1))


def place_of_chip():
    return lax.axis_index("section") >> 1, lax.axis_size("section") // 2


def prepare_kernel(slots, tiles_ref, own_ref, target_ref, wide_ref, held_ref, placing_ref):
    many, depth = tiles_ref.shape[:2]
    for g in range(many):
        wide_ref[g] = jnp.concatenate([tiles_ref[g, k] for k in range(depth)], axis=1)
    held_ref[...] = own_ref[...]
    places, rows = placing_ref.shape
    n_section = places // slots
    target = target_ref[...]
    hits = lax.broadcasted_iota(jnp.int32, (n_section, rows), 0) == target
    hits = jnp.where(hits, 1.0, 0.0)
    earlier = lax.broadcasted_iota(jnp.int32, (rows, rows), 0) < lax.broadcasted_iota(
        jnp.int32, (rows, rows), 1
    )
    earlier = jnp.where(earlier, 1.0, 0.0).astype(jnp.bfloat16)
    before = jnp.dot(hits.astype(jnp.bfloat16), earlier, preferred_element_type=jnp.float32)
    slot = jnp.sum(before * hits, axis=0, keepdims=True).astype(jnp.int32)
    chip, chips = place_of_chip()
    apart = (target >> 1) - chip
    apart = jnp.where(apart < 0, apart + chips, apart)
    other_core = (target ^ lax.axis_index("section")) & 1
    position = (other_core * chips + apart) * slots + slot
    placing = lax.broadcasted_iota(jnp.int32, (places, rows), 0) == position
    placing_ref[...] = jnp.where(placing, 1.0, 0.0).astype(jnp.bfloat16)


def prepare(tiles, own, target, places, slots):
    many, depth, tile, _ = tiles.shape
    return pl.pallas_call(
        functools.partial(prepare_kernel, slots),
        out_shape=(
            jax.ShapeDtypeStruct((many, tile, depth * tile), jnp.bfloat16),
            jax.ShapeDtypeStruct(own.shape, jnp.bfloat16),
            jax.ShapeDtypeStruct((places, target.shape[1]), jnp.bfloat16),
        ),
        in_specs=[VMEM] * 3,
        out_specs=(VMEM,) * 3,
        compiler_params=LIMIT,
        cost_estimate=pl.CostEstimate(flops=0, bytes_accessed=2 * tiles.size * 2, transcendentals=0),
        name="prepare",
    )(tiles, own, target)


def partials_kernel(count, src_ref, wide_ref, *refs):
    block_refs, out_refs, held = refs[:count], refs[count:-1], refs[-1]
    depth = src_ref.shape[1]
    section, rep = lax.axis_index("section"), lax.axis_index("rep")
    for j in range(count):
        held[j] = block_refs[j][...]
    for j, out_ref in zip([0] + across(len(out_refs)), out_refs):
        g = rep ^ j
        right = jnp.concatenate([held[src_ref[g, k] ^ section] for k in range(depth)], axis=0)
        out_ref[...] = jnp.dot(wide_ref[g], right, preferred_element_type=jnp.float32).astype(
            jnp.bfloat16
        )


def partials(sources, wide, blocks):
    many = wide.shape[0]
    tile, width = blocks[0].shape
    return pl.pallas_call(
        functools.partial(partials_kernel, len(blocks)),
        out_shape=[jax.ShapeDtypeStruct((tile, width), jnp.bfloat16)] * many,
        in_specs=[VMEM] * (2 + len(blocks)),
        out_specs=[VMEM] * many,
        scratch_shapes=[pltpu.VMEM((len(blocks), tile, width), jnp.bfloat16)],
        compiler_params=LIMIT,
        name="partials",
    )(sources, wide, *blocks)


def swap(value, axis, j):
    return lax.ppermute(value, axis, [(i, i ^ j) for i in range(lax.axis_size(axis))])


def tree_sum(terms):
    while len(terms) > 1:
        terms = [terms[i] + terms[i + 1] for i in range(0, len(terms), 2)]
    return terms[0]


def dense_kernel(n_part, weight_ref, cot_ref, placing_ref, *refs):
    part_refs, (same_ref, kept_ref, sent_ref, term) = refs[:n_part], refs[n_part:]
    core = lax.axis_index("section") & 1
    agg_b = tree_sum([ref[...].astype(jnp.float32) for ref in part_refs]).astype(jnp.bfloat16)
    pre = jnp.dot(agg_b, weight_ref[...], preferred_element_type=jnp.float32)
    sig = jax.nn.sigmoid(pre)
    factor = sig * (1.0 + pre * (1.0 - sig))
    grad_pre = (cot_ref[...].astype(jnp.float32) * factor).astype(jnp.bfloat16)
    whole = lax.dot_general(
        agg_b, grad_pre, (((0,), (0,)), ((), ())), preferred_element_type=jnp.float32
    )
    term[...] = whole.reshape(term.shape)
    kept_ref[...] = term[core]
    output = (pre * sig).astype(jnp.bfloat16)
    packed = jnp.dot(placing_ref[...], output, preferred_element_type=jnp.float32)
    half = packed.shape[0] // 2
    same_ref[...] = packed[:half].astype(jnp.bfloat16)
    sent_ref[:half] = packed[half:].astype(jnp.bfloat16)
    sent_ref[half:] = term[1 - core].astype(jnp.bfloat16)


def dense(parts, weight, cotangent, placing):
    places, width = placing.shape[0], weight.shape[0]
    return pl.pallas_call(
        functools.partial(dense_kernel, len(parts)),
        out_shape=(
            jax.ShapeDtypeStruct((places // 2, width), jnp.bfloat16),
            jax.ShapeDtypeStruct((width // 2, width), jnp.float32),
            jax.ShapeDtypeStruct((places // 2 + width // 2, width), jnp.bfloat16),
        ),
        in_specs=[VMEM] * (3 + len(parts)),
        out_specs=(VMEM,) * 3,
        scratch_shapes=[pltpu.VMEM((2, width // 2, width), jnp.float32)],
        compiler_params=LIMIT,
        name="dense",
    )(weight, cotangent, placing, *parts)


def write_messages(slots, same_ref, came_ref, half, out_refs):
    for i, ref in enumerate(out_refs):
        start = (i + 1) * slots % same_ref.shape[0]
        ref[:slots] = same_ref[start : start + slots]
        ref[slots : 2 * slots] = came_ref[start : start + slots]
        ref[2 * slots :] = half


def sum_halves(half_ref, held, slots, own_ref, message_refs, core_along, n_rep):
    chip, chips = place_of_chip()
    core = lax.axis_index("section") & 1

    @pl.when(core == core_along)
    def _():
        held[chip] = own_ref[...]
        for i, ref in enumerate(message_refs[: chips - 1]):
            held[(chip + chips - i - 1) % chips] = ref[2 * slots :]
        total = tree_sum([held[c].astype(jnp.float32) for c in range(chips)])
        half_ref[...] = total.astype(jnp.bfloat16)

    @pl.when(core != core_along)
    def _():
        by_xor = [own_ref[...].astype(jnp.float32)]
        by_xor += [ref[2 * slots :].astype(jnp.float32) for ref in message_refs[::-1]]
        half_ref[...] = tree_sum(by_xor[:n_rep]).astype(jnp.bfloat16)


def first_kernel(slots, same_ref, kept_ref, came_ref, half_ref, *out_refs):
    rows = kept_ref.shape[0]
    half = kept_ref[...] + came_ref[came_ref.shape[0] - rows :].astype(jnp.float32)
    half_ref[...] = half.astype(jnp.bfloat16)
    write_messages(slots, same_ref, came_ref, half_ref[...], out_refs)


def second_kernel(slots, n_rep, many, same_ref, came_ref, own_ref, *refs):
    message_refs, half_ref, out_refs, held = refs[:many], refs[many], refs[many + 1 : -1], refs[-1]
    sum_halves(half_ref, held, slots, own_ref, message_refs, 0, n_rep)
    write_messages(slots, same_ref, came_ref, half_ref[...], out_refs)


def third_kernel(slots, n_rep, own_ref, *refs):
    sum_halves(refs[-2], refs[-1], slots, own_ref, refs[:-2], 1, n_rep)


def call_halves(kernel, name, operands, half, slots, many, held=()):
    shapes = [jax.ShapeDtypeStruct(half, jnp.bfloat16)]
    shapes += [jax.ShapeDtypeStruct((2 * slots + half[0], half[1]), jnp.bfloat16)] * many
    return pl.pallas_call(
        kernel,
        out_shape=shapes,
        in_specs=[VMEM] * len(operands),
        out_specs=[VMEM] * len(shapes),
        scratch_shapes=[pltpu.VMEM(shape, jnp.bfloat16) for shape in held],
        compiler_params=LIMIT,
        name=name,
    )(*operands)


def store_kernel(core, slots, same_ref, came_ref, *refs):
    message_refs, (out_ref, rows, sem) = refs[:-3], refs[-3:]
    section = lax.axis_index("section")
    chip, chips = place_of_chip()

    @pl.when(section & 1 == core)
    def _():
        rows[section] = same_ref[:slots]
        rows[section ^ 1] = came_ref[:slots]
        for i, ref in enumerate(message_refs[: chips - 1]):
            source = 2 * ((chip + chips - i - 1) % chips)
            rows[source + core] = ref[:slots]
            rows[source + 1 - core] = ref[slots : 2 * slots]
        copy = pltpu.make_async_copy(rows, out_ref, sem)
        copy.start()
        copy.wait()


def store(core, same, came, messages, n_section, slots, base=None):
    shape = (n_section, slots, same.shape[1])
    operands = [same, came, *messages]
    kernel, first, specs = functools.partial(store_kernel, core, slots), [], []
    if base is not None:
        kernel, first, specs = lambda _, *refs: store_kernel(core, slots, *refs), [base], [HBM]
    return pl.pallas_call(
        kernel,
        out_shape=jax.ShapeDtypeStruct(shape, jnp.bfloat16),
        in_specs=specs + [VMEM] * len(operands),
        out_specs=HBM,
        scratch_shapes=[pltpu.VMEM(shape, jnp.bfloat16), pltpu.SemaphoreType.DMA],
        input_output_aliases={0: 0} if first else {},
        compiler_params=LIMIT,
        name="store",
    )(*first, *operands)


def half_kernel(mine, half_ref, *refs):
    out_ref, wide, sem = refs[-3:]
    core = lax.axis_index("section") & 1
    wide[...] = half_ref[...].astype(jnp.float32)
    copy = pltpu.make_async_copy(wide, out_ref.at[core if mine else 1 - core], sem)
    copy.start()
    copy.wait()


def store_half(mine, half, base=None):
    operands = [half] if base is None else [half, base]
    return pl.pallas_call(
        functools.partial(half_kernel, mine),
        out_shape=jax.ShapeDtypeStruct((2,) + half.shape, jnp.float32),
        in_specs=[VMEM, HBM][: len(operands)],
        out_specs=HBM,
        scratch_shapes=[pltpu.VMEM(half.shape, jnp.float32), pltpu.SemaphoreType.DMA],
        input_output_aliases={} if base is None else {1: 0},
        compiler_params=LIMIT,
        name="store_half",
    )(*operands)


def exchange(value, core_along, shift, j):
    n_section, n_rep = lax.axis_size("section"), lax.axis_size("rep")
    pairs = []
    for s in range(n_section):
        along = s & 1 == core_along
        to = (s + 2 * shift) % n_section if along else s
        for r in range(n_rep):
            pairs.append((s * n_rep + r, to * n_rep + (r if along else r ^ j % n_rep)))
    return lax.ppermute(value, ("section", "rep"), pairs)


def gather_blocks(features, axis, ready):
    n = lax.axis_size(axis)
    blocks = [None] * n
    blocks[0] = features
    far = n // 2 & -2
    for j in sorted(range(2, n, 2), key=lambda j: (j & 4, -(j & 2))):
        blocks[j] = swap(features, axis, j)
    blocks[1] = swap(features, axis, 1)
    blocks[far], ready = lax.optimization_barrier((blocks[far], ready))
    for j in sorted(range(2, n, 2), key=lambda j: -j):
        blocks[j + 1] = swap(blocks[j], axis, 1)
    return blocks, ready


def per_device(features, adj_tiles, adj_src, cotangent, weight, destination):
    n_section, n_rep = lax.axis_size("section"), lax.axis_size("rep")
    rows_here, width = features.shape
    tile = adj_tiles.shape[3]
    slots = max(2, 2 * rows_here // n_section)
    target = destination.reshape(1, rows_here)
    wide, own, placing = prepare(adj_tiles[:, 0], features, target, n_section * slots, slots)
    blocks, (wide, own, placing) = gather_blocks(features, "section", (wide, own, placing))
    parts = list(partials(adj_src[:, 0], wide, [own] + blocks[1:]))
    others = across(n_rep)
    parts = parts[:1] + [swap(part, "rep", j) for part, j in zip(parts[1:], others)]
    same, kept, sent = dense(parts, weight, cotangent, placing)
    came = swap(sent, "section", 1)
    chips = n_section // 2
    steps = across(max(n_rep, chips))
    half_shape = (width // 2, width)
    held = [(chips,) + half_shape]
    half, *first = call_halves(
        functools.partial(first_kernel, slots), "first", [same, kept, came], half_shape, slots, len(steps)
    )
    first = [exchange(m, 0, i + 1, j) for i, (m, j) in enumerate(zip(first, steps))]
    relaid = store(0, same, came, first, n_section, slots)
    half, *second = call_halves(
        functools.partial(second_kernel, slots, n_rep, len(steps)),
        "second",
        [same, came, half, *first],
        half_shape,
        slots,
        len(steps),
        held,
    )
    second = [exchange(m, 1, i + 1, j) for i, (m, j) in enumerate(zip(second, steps))]
    (half,) = call_halves(
        functools.partial(third_kernel, slots, n_rep), "third", [half, *second], half_shape, slots, 0, held
    )
    relaid = store(1, same, came, second, n_section, slots, relaid)
    half, relaid = lax.optimization_barrier((half, relaid))
    weight_grad = store_half(False, swap(half, "section", 1), store_half(True, half))
    return (relaid.reshape(1, 1, n_section, slots, width), weight_grad.reshape(width, width))


def solution(mesh):
    placed = (
        P(("section", "rep"), None),
        P("section", "rep", None, None, None),
        P("section", "rep", None),
        P(("section", "rep"), None),
        P(),
        P(("section", "rep"), None),
    )
    return jax.shard_map(
        per_device,
        mesh=mesh,
        in_specs=placed,
        out_specs=(P("section", "rep", None, None, None), P()),
        check_vma=False,
    )
```

```python
import functools

import jax
import jax.numpy as jnp
from jax import lax
from jax.experimental import pallas as pl
from jax.experimental.pallas import tpu as pltpu
from jax.sharding import PartitionSpec as P

VMEM = pl.BlockSpec(memory_space=pltpu.VMEM)
LIMIT = pltpu.CompilerParams(vmem_limit_bytes=32 * 1024 * 1024)
HBM = pl.BlockSpec(memory_space=pltpu.HBM)


def across(n):
    return list(range(n - 1, 0, -1))


def orders(n):
    near = list(range(1, n - 1))
    return list(zip([n - 1] + near, near + [n - 1]))


def place_of_chip():
    return lax.axis_index("section") >> 1, lax.axis_size("section") // 2


def prepare_kernel(slots, tiles_ref, own_ref, target_ref, wide_ref, held_ref, placing_ref):
    many, depth = tiles_ref.shape[:2]
    for g in range(many):
        wide_ref[g] = jnp.concatenate([tiles_ref[g, k] for k in range(depth)], axis=1)
    held_ref[...] = own_ref[...]
    places, rows = placing_ref.shape
    n_section = places // slots
    target = target_ref[...]
    hits = lax.broadcasted_iota(jnp.int32, (n_section, rows), 0) == target
    hits = jnp.where(hits, 1.0, 0.0)
    earlier = lax.broadcasted_iota(jnp.int32, (rows, rows), 0) < lax.broadcasted_iota(
        jnp.int32, (rows, rows), 1
    )
    earlier = jnp.where(earlier, 1.0, 0.0).astype(jnp.bfloat16)
    before = jnp.dot(hits.astype(jnp.bfloat16), earlier, preferred_element_type=jnp.float32)
    slot = jnp.sum(before * hits, axis=0, keepdims=True).astype(jnp.int32)
    chip, chips = place_of_chip()
    apart = (target >> 1) - chip
    apart = jnp.where(apart < 0, apart + chips, apart)
    other_core = (target ^ lax.axis_index("section")) & 1
    position = (other_core * chips + apart) * slots + slot
    placing = lax.broadcasted_iota(jnp.int32, (places, rows), 0) == position
    placing_ref[...] = jnp.where(placing, 1.0, 0.0).astype(jnp.bfloat16)


def prepare(tiles, own, target, places, slots):
    many, depth, tile, _ = tiles.shape
    return pl.pallas_call(
        functools.partial(prepare_kernel, slots),
        out_shape=(
            jax.ShapeDtypeStruct((many, tile, depth * tile), jnp.bfloat16),
            jax.ShapeDtypeStruct(own.shape, jnp.bfloat16),
            jax.ShapeDtypeStruct((places, target.shape[1]), jnp.bfloat16),
        ),
        in_specs=[VMEM] * 3,
        out_specs=(VMEM,) * 3,
        compiler_params=LIMIT,
        cost_estimate=pl.CostEstimate(flops=0, bytes_accessed=2 * tiles.size * 2, transcendentals=0),
        name="prepare",
    )(tiles, own, target)


def partials_kernel(count, src_ref, wide_ref, *refs):
    block_refs, out_refs, held = refs[:count], refs[count:-1], refs[-1]
    depth = src_ref.shape[1]
    section, rep = lax.axis_index("section"), lax.axis_index("rep")
    for j in range(count):
        held[j] = block_refs[j][...]
    for (j, k), out_ref in zip([(0, 0)] + orders(len(out_refs)), out_refs):
        g = rep ^ jnp.where(section & 1 == 0, j, k)
        right = jnp.concatenate([held[src_ref[g, k] ^ section] for k in range(depth)], axis=0)
        out_ref[...] = jnp.dot(wide_ref[g], right, preferred_element_type=jnp.float32).astype(
            jnp.bfloat16
        )


def partials(sources, wide, blocks):
    many = wide.shape[0]
    tile, width = blocks[0].shape
    return pl.pallas_call(
        functools.partial(partials_kernel, len(blocks)),
        out_shape=[jax.ShapeDtypeStruct((tile, width), jnp.bfloat16)] * many,
        in_specs=[VMEM] * (2 + len(blocks)),
        out_specs=[VMEM] * many,
        scratch_shapes=[pltpu.VMEM((len(blocks), tile, width), jnp.bfloat16)],
        compiler_params=LIMIT,
        name="partials",
    )(sources, wide, *blocks)


def swap(value, axis, j):
    return lax.ppermute(value, axis, [(i, i ^ j) for i in range(lax.axis_size(axis))])


def tree_sum(terms):
    while len(terms) > 1:
        terms = [terms[i] + terms[i + 1] for i in range(0, len(terms), 2)]
    return terms[0]


def dense_kernel(n_part, weight_ref, cot_ref, placing_ref, *refs):
    part_refs, (same_ref, kept_ref, sent_ref, term) = refs[:n_part], refs[n_part:]
    core = lax.axis_index("section") & 1
    agg_b = tree_sum([ref[...].astype(jnp.float32) for ref in part_refs]).astype(jnp.bfloat16)
    pre = jnp.dot(agg_b, weight_ref[...], preferred_element_type=jnp.float32)
    sig = jax.nn.sigmoid(pre)
    factor = sig * (1.0 + pre * (1.0 - sig))
    grad_pre = (cot_ref[...].astype(jnp.float32) * factor).astype(jnp.bfloat16)
    whole = lax.dot_general(
        agg_b, grad_pre, (((0,), (0,)), ((), ())), preferred_element_type=jnp.float32
    )
    term[...] = whole.reshape(term.shape)
    kept_ref[...] = term[core]
    output = (pre * sig).astype(jnp.bfloat16)
    packed = jnp.dot(placing_ref[...], output, preferred_element_type=jnp.float32)
    half = packed.shape[0] // 2
    same_ref[...] = packed[:half].astype(jnp.bfloat16)
    sent_ref[:half] = packed[half:].astype(jnp.bfloat16)
    sent_ref[half:] = term[1 - core].astype(jnp.bfloat16)


def dense(parts, weight, cotangent, placing):
    places, width = placing.shape[0], weight.shape[0]
    return pl.pallas_call(
        functools.partial(dense_kernel, len(parts)),
        out_shape=(
            jax.ShapeDtypeStruct((places // 2, width), jnp.bfloat16),
            jax.ShapeDtypeStruct((width // 2, width), jnp.float32),
            jax.ShapeDtypeStruct((places // 2 + width // 2, width), jnp.bfloat16),
        ),
        in_specs=[VMEM] * (3 + len(parts)),
        out_specs=(VMEM,) * 3,
        scratch_shapes=[pltpu.VMEM((2, width // 2, width), jnp.float32)],
        compiler_params=LIMIT,
        name="dense",
    )(weight, cotangent, placing, *parts)


def write_messages(slots, same_ref, came_ref, half, out_refs):
    for i, ref in enumerate(out_refs):
        start = (i + 1) * slots % same_ref.shape[0]
        ref[:slots] = same_ref[start : start + slots]
        ref[slots : 2 * slots] = came_ref[start : start + slots]
        ref[2 * slots :] = half


def sum_halves(half_ref, held, slots, own_ref, message_refs, core_along, n_rep):
    chip, chips = place_of_chip()
    core = lax.axis_index("section") & 1

    @pl.when(core == core_along)
    def _():
        held[chip] = own_ref[...]
        for i, ref in enumerate(message_refs[: chips - 1]):
            held[(chip + chips - i - 1) % chips] = ref[2 * slots :]
        total = tree_sum([held[c].astype(jnp.float32) for c in range(chips)])
        half_ref[...] = total.astype(jnp.bfloat16)

    @pl.when(core != core_along)
    def _():
        by_xor = [own_ref[...].astype(jnp.float32)]
        by_xor += [ref[2 * slots :].astype(jnp.float32) for ref in message_refs[::-1]]
        half_ref[...] = tree_sum(by_xor[:n_rep]).astype(jnp.bfloat16)


def first_kernel(slots, same_ref, kept_ref, came_ref, half_ref, *out_refs):
    rows = kept_ref.shape[0]
    half = kept_ref[...] + came_ref[came_ref.shape[0] - rows :].astype(jnp.float32)
    half_ref[...] = half.astype(jnp.bfloat16)
    write_messages(slots, same_ref, came_ref, half_ref[...], out_refs)


def second_kernel(slots, n_rep, many, same_ref, came_ref, own_ref, *refs):
    message_refs, half_ref, out_refs, held = refs[:many], refs[many], refs[many + 1 : -1], refs[-1]
    sum_halves(half_ref, held, slots, own_ref, message_refs, 0, n_rep)
    write_messages(slots, same_ref, came_ref, half_ref[...], out_refs)


def third_kernel(slots, n_rep, own_ref, *refs):
    sum_halves(refs[-2], refs[-1], slots, own_ref, refs[:-2], 1, n_rep)


def call_halves(kernel, name, operands, half, slots, many, held=()):
    shapes = [jax.ShapeDtypeStruct(half, jnp.bfloat16)]
    shapes += [jax.ShapeDtypeStruct((2 * slots + half[0], half[1]), jnp.bfloat16)] * many
    return pl.pallas_call(
        kernel,
        out_shape=shapes,
        in_specs=[VMEM] * len(operands),
        out_specs=[VMEM] * len(shapes),
        scratch_shapes=[pltpu.VMEM(shape, jnp.bfloat16) for shape in held],
        compiler_params=LIMIT,
        name=name,
    )(*operands)


def store_kernel(core, slots, same_ref, came_ref, *refs):
    message_refs, (out_ref, rows, sem) = refs[:-3], refs[-3:]
    section = lax.axis_index("section")
    chip, chips = place_of_chip()

    @pl.when(section & 1 == core)
    def _():
        rows[section] = same_ref[:slots]
        rows[section ^ 1] = came_ref[:slots]
        for i, ref in enumerate(message_refs[: chips - 1]):
            source = 2 * ((chip + chips - i - 1) % chips)
            rows[source + core] = ref[:slots]
            rows[source + 1 - core] = ref[slots : 2 * slots]
        copy = pltpu.make_async_copy(rows, out_ref, sem)
        copy.start()
        copy.wait()


def store(core, same, came, messages, n_section, slots, base=None):
    shape = (n_section, slots, same.shape[1])
    operands = [same, came, *messages]
    kernel, first, specs = functools.partial(store_kernel, core, slots), [], []
    if base is not None:
        kernel, first, specs = lambda _, *refs: store_kernel(core, slots, *refs), [base], [HBM]
    return pl.pallas_call(
        kernel,
        out_shape=jax.ShapeDtypeStruct(shape, jnp.bfloat16),
        in_specs=specs + [VMEM] * len(operands),
        out_specs=HBM,
        scratch_shapes=[pltpu.VMEM(shape, jnp.bfloat16), pltpu.SemaphoreType.DMA],
        input_output_aliases={0: 0} if first else {},
        compiler_params=LIMIT,
        name="store",
    )(*first, *operands)


def finish_kernel(own_ref, came_ref, out_ref):
    core = lax.axis_index("section") & 1
    out_ref[core] = own_ref[...].astype(jnp.float32)
    out_ref[1 - core] = came_ref[...].astype(jnp.float32)


def finish(own, came):
    return pl.pallas_call(
        finish_kernel,
        out_shape=jax.ShapeDtypeStruct((2,) + own.shape, jnp.float32),
        in_specs=[VMEM] * 2,
        out_specs=VMEM,
        compiler_params=LIMIT,
        name="finish",
    )(own, came)


def swap_rep(value, first, second):
    n_section, n_rep = lax.axis_size("section"), lax.axis_size("rep")
    pairs = []
    for s in range(n_section):
        j = second if s & 1 else first
        pairs += [(s * n_rep + r, s * n_rep + (r ^ j)) for r in range(n_rep)]
    return lax.ppermute(value, ("section", "rep"), pairs)


def exchange(value, core_along, shift, j):
    n_section, n_rep = lax.axis_size("section"), lax.axis_size("rep")
    pairs = []
    for s in range(n_section):
        along = s & 1 == core_along
        to = (s + 2 * shift) % n_section if along else s
        for r in range(n_rep):
            pairs.append((s * n_rep + r, to * n_rep + (r if along else r ^ j % n_rep)))
    return lax.ppermute(value, ("section", "rep"), pairs)


def gather_blocks(features, axis, ready):
    n = lax.axis_size(axis)
    blocks = [None] * n
    blocks[0] = features
    order = sorted(range(2, n, 2), key=lambda j: (j & 4, -(j & 2)))
    for j in order:
        blocks[j] = swap(features, axis, j)
    blocks[1] = swap(features, axis, 1)
    came, ready = lax.optimization_barrier(([blocks[j] for j in order], ready))
    for j, block in zip(order, came):
        blocks[j] = block
    for j in range(2, n, 2):
        blocks[j + 1] = swap(blocks[j], axis, 1)
    return blocks, ready


def per_device(features, adj_tiles, adj_src, cotangent, weight, destination):
    n_section, n_rep = lax.axis_size("section"), lax.axis_size("rep")
    rows_here, width = features.shape
    tile = adj_tiles.shape[3]
    slots = max(2, 2 * rows_here // n_section)
    target = destination.reshape(1, rows_here)
    wide, own, placing = prepare(adj_tiles[:, 0], features, target, n_section * slots, slots)
    blocks, (wide, own, placing) = gather_blocks(features, "section", (wide, own, placing))
    parts = list(partials(adj_src[:, 0], wide, [own] + blocks[1:]))
    parts = parts[:1] + [swap_rep(part, *step) for part, step in zip(parts[1:], orders(n_rep))]
    same, kept, sent = dense(parts, weight, cotangent, placing)
    came = swap(sent, "section", 1)
    chips = n_section // 2
    steps = across(max(n_rep, chips))
    half_shape = (width // 2, width)
    held = [(chips,) + half_shape]
    half, *first = call_halves(
        functools.partial(first_kernel, slots), "first", [same, kept, came], half_shape, slots, len(steps)
    )
    first = [exchange(m, 0, i + 1, j) for i, (m, j) in enumerate(zip(first, steps))]
    relaid = store(0, same, came, first, n_section, slots)
    half, *second = call_halves(
        functools.partial(second_kernel, slots, n_rep, len(steps)),
        "second",
        [same, came, half, *first],
        half_shape,
        slots,
        len(steps),
        held,
    )
    second = [exchange(m, 1, i + 1, j) for i, (m, j) in enumerate(zip(second, steps))]
    (half,) = call_halves(
        functools.partial(third_kernel, slots, n_rep), "third", [half, *second], half_shape, slots, 0, held
    )
    relaid = store(1, same, came, second, n_section, slots, relaid)
    half, relaid = lax.optimization_barrier((half, relaid))
    weight_grad = finish(half, swap(half, "section", 1))
    return (relaid.reshape(1, 1, n_section, slots, width), weight_grad.reshape(width, width))


def solution(mesh):
    placed = (
        P(("section", "rep"), None),
        P("section", "rep", None, None, None),
        P("section", "rep", None),
        P(("section", "rep"), None),
        P(),
        P(("section", "rep"), None),
    )
    return jax.shard_map(
        per_device,
        mesh=mesh,
        in_specs=placed,
        out_specs=(P("section", "rep", None, None, None), P()),
        check_vma=False,
    )
```

```python
import functools

import jax
import jax.numpy as jnp
from jax import lax
from jax.experimental import pallas as pl
from jax.experimental.pallas import tpu as pltpu
from jax.sharding import PartitionSpec as P

VMEM = pl.BlockSpec(memory_space=pltpu.VMEM)
LIMIT = pltpu.CompilerParams(vmem_limit_bytes=32 * 1024 * 1024)
HBM = pl.BlockSpec(memory_space=pltpu.HBM)


def across(n):
    return list(range(n - 1, 0, -1))


def place_of_chip():
    return lax.axis_index("section") >> 1, lax.axis_size("section") // 2


def prepare_kernel(slots, tiles_ref, own_ref, target_ref, wide_ref, held_ref, placing_ref):
    many, depth = tiles_ref.shape[:2]
    for g in range(many):
        wide_ref[g] = jnp.concatenate([tiles_ref[g, k] for k in range(depth)], axis=1)
    held_ref[...] = own_ref[...]
    places, rows = placing_ref.shape
    n_section = places // slots
    target = target_ref[...]
    hits = lax.broadcasted_iota(jnp.int32, (n_section, rows), 0) == target
    hits = jnp.where(hits, 1.0, 0.0)
    earlier = lax.broadcasted_iota(jnp.int32, (rows, rows), 0) < lax.broadcasted_iota(
        jnp.int32, (rows, rows), 1
    )
    earlier = jnp.where(earlier, 1.0, 0.0).astype(jnp.bfloat16)
    before = jnp.dot(hits.astype(jnp.bfloat16), earlier, preferred_element_type=jnp.float32)
    slot = jnp.sum(before * hits, axis=0, keepdims=True).astype(jnp.int32)
    chip, chips = place_of_chip()
    apart = (target >> 1) - chip
    apart = jnp.where(apart < 0, apart + chips, apart)
    other_core = (target ^ lax.axis_index("section")) & 1
    position = (other_core * chips + apart) * slots + slot
    placing = lax.broadcasted_iota(jnp.int32, (places, rows), 0) == position
    placing_ref[...] = jnp.where(placing, 1.0, 0.0).astype(jnp.bfloat16)


def prepare(tiles, own, target, places, slots):
    many, depth, tile, _ = tiles.shape
    return pl.pallas_call(
        functools.partial(prepare_kernel, slots),
        out_shape=(
            jax.ShapeDtypeStruct((many, tile, depth * tile), jnp.bfloat16),
            jax.ShapeDtypeStruct(own.shape, jnp.bfloat16),
            jax.ShapeDtypeStruct((places, target.shape[1]), jnp.bfloat16),
        ),
        in_specs=[VMEM] * 3,
        out_specs=(VMEM,) * 3,
        compiler_params=LIMIT,
        cost_estimate=pl.CostEstimate(flops=0, bytes_accessed=2 * tiles.size * 2, transcendentals=0),
        name="prepare",
    )(tiles, own, target)


def partials_kernel(count, src_ref, wide_ref, *refs):
    block_refs, out_refs, held = refs[:count], refs[count:-1], refs[-1]
    depth = src_ref.shape[1]
    section, rep = lax.axis_index("section"), lax.axis_index("rep")
    for j in range(count):
        held[j] = block_refs[j][...]
    for j, out_ref in zip([0] + across(len(out_refs)), out_refs):
        g = rep ^ j
        right = jnp.concatenate([held[src_ref[g, k] ^ section] for k in range(depth)], axis=0)
        out_ref[...] = jnp.dot(wide_ref[g], right, preferred_element_type=jnp.float32).astype(
            jnp.bfloat16
        )


def partials(sources, wide, blocks):
    many = wide.shape[0]
    tile, width = blocks[0].shape
    return pl.pallas_call(
        functools.partial(partials_kernel, len(blocks)),
        out_shape=[jax.ShapeDtypeStruct((tile, width), jnp.bfloat16)] * many,
        in_specs=[VMEM] * (2 + len(blocks)),
        out_specs=[VMEM] * many,
        scratch_shapes=[pltpu.VMEM((len(blocks), tile, width), jnp.bfloat16)],
        compiler_params=LIMIT,
        name="partials",
    )(sources, wide, *blocks)


def swap(value, axis, j):
    return lax.ppermute(value, axis, [(i, i ^ j) for i in range(lax.axis_size(axis))])


def tree_sum(terms):
    while len(terms) > 1:
        terms = [terms[i] + terms[i + 1] for i in range(0, len(terms), 2)]
    return terms[0]


def dense_kernel(n_part, weight_ref, cot_ref, placing_ref, *refs):
    part_refs, (same_ref, kept_ref, sent_ref, term) = refs[:n_part], refs[n_part:]
    core = lax.axis_index("section") & 1
    agg_b = tree_sum([ref[...].astype(jnp.float32) for ref in part_refs]).astype(jnp.bfloat16)
    pre = jnp.dot(agg_b, weight_ref[...], preferred_element_type=jnp.float32)
    sig = jax.nn.sigmoid(pre)
    factor = sig * (1.0 + pre * (1.0 - sig))
    grad_pre = (cot_ref[...].astype(jnp.float32) * factor).astype(jnp.bfloat16)
    whole = lax.dot_general(
        agg_b, grad_pre, (((0,), (0,)), ((), ())), preferred_element_type=jnp.float32
    )
    term[...] = whole.reshape(term.shape)
    kept_ref[...] = term[core]
    output = (pre * sig).astype(jnp.bfloat16)
    packed = jnp.dot(placing_ref[...], output, preferred_element_type=jnp.float32)
    half = packed.shape[0] // 2
    same_ref[...] = packed[:half].astype(jnp.bfloat16)
    sent_ref[:half] = packed[half:].astype(jnp.bfloat16)
    sent_ref[half:] = term[1 - core].astype(jnp.bfloat16)


def dense(parts, weight, cotangent, placing):
    places, width = placing.shape[0], weight.shape[0]
    return pl.pallas_call(
        functools.partial(dense_kernel, len(parts)),
        out_shape=(
            jax.ShapeDtypeStruct((places // 2, width), jnp.bfloat16),
            jax.ShapeDtypeStruct((width // 2, width), jnp.float32),
            jax.ShapeDtypeStruct((places // 2 + width // 2, width), jnp.bfloat16),
        ),
        in_specs=[VMEM] * (3 + len(parts)),
        out_specs=(VMEM,) * 3,
        scratch_shapes=[pltpu.VMEM((2, width // 2, width), jnp.float32)],
        compiler_params=LIMIT,
        name="dense",
    )(weight, cotangent, placing, *parts)


def write_messages(slots, same_ref, came_ref, half, out_refs):
    for i, ref in enumerate(out_refs):
        start = (i + 1) * slots % same_ref.shape[0]
        ref[:slots] = same_ref[start : start + slots]
        ref[slots : 2 * slots] = came_ref[start : start + slots]
        ref[2 * slots :] = half


def sum_halves(half_ref, held, slots, own_ref, message_refs, core_along, n_rep):
    chip, chips = place_of_chip()
    core = lax.axis_index("section") & 1

    @pl.when(core == core_along)
    def _():
        held[chip] = own_ref[...]
        for i, ref in enumerate(message_refs[: chips - 1]):
            held[(chip + chips - i - 1) % chips] = ref[2 * slots :]
        total = tree_sum([held[c].astype(jnp.float32) for c in range(chips)])
        half_ref[...] = total.astype(jnp.bfloat16)

    @pl.when(core != core_along)
    def _():
        by_xor = [own_ref[...].astype(jnp.float32)]
        by_xor += [ref[2 * slots :].astype(jnp.float32) for ref in message_refs[::-1]]
        half_ref[...] = tree_sum(by_xor[:n_rep]).astype(jnp.bfloat16)


def first_kernel(slots, same_ref, kept_ref, came_ref, half_ref, *out_refs):
    rows = kept_ref.shape[0]
    half = kept_ref[...] + came_ref[came_ref.shape[0] - rows :].astype(jnp.float32)
    half_ref[...] = half.astype(jnp.bfloat16)
    write_messages(slots, same_ref, came_ref, half_ref[...], out_refs)


def second_kernel(slots, n_rep, many, same_ref, came_ref, own_ref, *refs):
    message_refs, half_ref, out_refs, held = refs[:many], refs[many], refs[many + 1 : -1], refs[-1]
    sum_halves(half_ref, held, slots, own_ref, message_refs, 0, n_rep)
    write_messages(slots, same_ref, came_ref, half_ref[...], out_refs)


def third_kernel(slots, n_rep, own_ref, *refs):
    sum_halves(refs[-2], refs[-1], slots, own_ref, refs[:-2], 1, n_rep)


def call_halves(kernel, name, operands, half, slots, many, held=()):
    shapes = [jax.ShapeDtypeStruct(half, jnp.bfloat16)]
    shapes += [jax.ShapeDtypeStruct((2 * slots + half[0], half[1]), jnp.bfloat16)] * many
    return pl.pallas_call(
        kernel,
        out_shape=shapes,
        in_specs=[VMEM] * len(operands),
        out_specs=[VMEM] * len(shapes),
        scratch_shapes=[pltpu.VMEM(shape, jnp.bfloat16) for shape in held],
        compiler_params=LIMIT,
        name=name,
    )(*operands)


def store_kernel(core, slots, same_ref, came_ref, *refs):
    message_refs, (out_ref, rows, sem) = refs[:-3], refs[-3:]
    section = lax.axis_index("section")
    chip, chips = place_of_chip()

    @pl.when(section & 1 == core)
    def _():
        rows[section] = same_ref[:slots]
        rows[section ^ 1] = came_ref[:slots]
        for i, ref in enumerate(message_refs[: chips - 1]):
            source = 2 * ((chip + chips - i - 1) % chips)
            rows[source + core] = ref[:slots]
            rows[source + 1 - core] = ref[slots : 2 * slots]
        copy = pltpu.make_async_copy(rows, out_ref, sem)
        copy.start()
        copy.wait()


def store(core, same, came, messages, n_section, slots, base=None):
    shape = (n_section, slots, same.shape[1])
    operands = [same, came, *messages]
    kernel, first, specs = functools.partial(store_kernel, core, slots), [], []
    if base is not None:
        kernel, first, specs = lambda _, *refs: store_kernel(core, slots, *refs), [base], [HBM]
    return pl.pallas_call(
        kernel,
        out_shape=jax.ShapeDtypeStruct(shape, jnp.bfloat16),
        in_specs=specs + [VMEM] * len(operands),
        out_specs=HBM,
        scratch_shapes=[pltpu.VMEM(shape, jnp.bfloat16), pltpu.SemaphoreType.DMA],
        input_output_aliases={0: 0} if first else {},
        compiler_params=LIMIT,
        name="store",
    )(*first, *operands)


def finish_kernel(own_ref, came_ref, out_ref):
    core = lax.axis_index("section") & 1
    out_ref[core] = own_ref[...].astype(jnp.float32)
    out_ref[1 - core] = came_ref[...].astype(jnp.float32)


def finish(own, came):
    return pl.pallas_call(
        finish_kernel,
        out_shape=jax.ShapeDtypeStruct((2,) + own.shape, jnp.float32),
        in_specs=[VMEM] * 2,
        out_specs=VMEM,
        compiler_params=LIMIT,
        name="finish",
    )(own, came)


def exchange(value, core_along, shift, j):
    n_section, n_rep = lax.axis_size("section"), lax.axis_size("rep")
    pairs = []
    for s in range(n_section):
        along = s & 1 == core_along
        to = (s + 2 * shift) % n_section if along else s
        for r in range(n_rep):
            pairs.append((s * n_rep + r, to * n_rep + (r if along else r ^ j % n_rep)))
    return lax.ppermute(value, ("section", "rep"), pairs)


def gather_blocks(features, axis, ready):
    n = lax.axis_size(axis)
    blocks = [None] * n
    blocks[0] = features
    for j in range(2, n, 2):
        blocks[j] = swap(features, axis, j)
    blocks[1] = swap(features, axis, 1)
    blocks[2::2], ready = lax.optimization_barrier((blocks[2::2], ready))
    for j in range(2, n, 2):
        blocks[j + 1] = swap(blocks[j], axis, 1)
    return blocks, ready


def per_device(features, adj_tiles, adj_src, cotangent, weight, destination):
    n_section, n_rep = lax.axis_size("section"), lax.axis_size("rep")
    rows_here, width = features.shape
    tile = adj_tiles.shape[3]
    slots = max(2, 2 * rows_here // n_section)
    target = destination.reshape(1, rows_here)
    wide, own, placing = prepare(adj_tiles[:, 0], features, target, n_section * slots, slots)
    blocks, (wide, own, placing) = gather_blocks(features, "section", (wide, own, placing))
    parts = list(partials(adj_src[:, 0], wide, [own] + blocks[1:]))
    others = across(n_rep)
    parts = parts[:1] + [swap(part, "rep", j) for part, j in zip(parts[1:], others)]
    same, kept, sent = dense(parts, weight, cotangent, placing)
    came = swap(sent, "section", 1)
    chips = n_section // 2
    steps = across(max(n_rep, chips))
    half_shape = (width // 2, width)
    held = [(chips,) + half_shape]
    half, *first = call_halves(
        functools.partial(first_kernel, slots), "first", [same, kept, came], half_shape, slots, len(steps)
    )
    first = [exchange(m, 0, i + 1, j) for i, (m, j) in enumerate(zip(first, steps))]
    relaid = store(0, same, came, first, n_section, slots)
    half, *second = call_halves(
        functools.partial(second_kernel, slots, n_rep, len(steps)),
        "second",
        [same, came, half, *first],
        half_shape,
        slots,
        len(steps),
        held,
    )
    second = [exchange(m, 1, i + 1, j) for i, (m, j) in enumerate(zip(second, steps))]
    (half,) = call_halves(
        functools.partial(third_kernel, slots, n_rep), "third", [half, *second], half_shape, slots, 0, held
    )
    relaid = store(1, same, came, second, n_section, slots, relaid)
    half, relaid = lax.optimization_barrier((half, relaid))
    weight_grad = finish(half, swap(half, "section", 1))
    return (relaid.reshape(1, 1, n_section, slots, width), weight_grad.reshape(width, width))


def solution(mesh):
    placed = (
        P(("section", "rep"), None),
        P("section", "rep", None, None, None),
        P("section", "rep", None),
        P(("section", "rep"), None),
        P(),
        P(("section", "rep"), None),
    )
    return jax.shard_map(
        per_device,
        mesh=mesh,
        in_specs=placed,
        out_specs=(P("section", "rep", None, None, None), P()),
        check_vma=False,
    )
```

```python
import functools

import jax
import jax.numpy as jnp
from jax import lax
from jax.experimental import pallas as pl
from jax.experimental.pallas import tpu as pltpu
from jax.sharding import PartitionSpec as P

VMEM = pl.BlockSpec(memory_space=pltpu.VMEM)
LIMIT = pltpu.CompilerParams(vmem_limit_bytes=32 * 1024 * 1024)
HBM = pl.BlockSpec(memory_space=pltpu.HBM)


def across(n):
    return list(range(n - 1, 0, -1))


def place_of_chip():
    return lax.axis_index("section") >> 1, lax.axis_size("section") // 2


def prepare_kernel(slots, tiles_ref, own_ref, target_ref, wide_ref, held_ref, placing_ref):
    many, depth = tiles_ref.shape[:2]
    for g in range(many):
        wide_ref[g] = jnp.concatenate([tiles_ref[g, k] for k in range(depth)], axis=1)
    held_ref[...] = own_ref[...]
    places, rows = placing_ref.shape
    n_section = places // slots
    target = target_ref[...]
    hits = lax.broadcasted_iota(jnp.int32, (n_section, rows), 0) == target
    hits = jnp.where(hits, 1.0, 0.0)
    earlier = lax.broadcasted_iota(jnp.int32, (rows, rows), 0) < lax.broadcasted_iota(
        jnp.int32, (rows, rows), 1
    )
    earlier = jnp.where(earlier, 1.0, 0.0).astype(jnp.bfloat16)
    before = jnp.dot(hits.astype(jnp.bfloat16), earlier, preferred_element_type=jnp.float32)
    slot = jnp.sum(before * hits, axis=0, keepdims=True).astype(jnp.int32)
    chip, chips = place_of_chip()
    apart = (target >> 1) - chip
    apart = jnp.where(apart < 0, apart + chips, apart)
    other_core = (target ^ lax.axis_index("section")) & 1
    position = (other_core * chips + apart) * slots + slot
    placing = lax.broadcasted_iota(jnp.int32, (places, rows), 0) == position
    placing_ref[...] = jnp.where(placing, 1.0, 0.0).astype(jnp.bfloat16)


def prepare(tiles, own, target, places, slots):
    many, depth, tile, _ = tiles.shape
    return pl.pallas_call(
        functools.partial(prepare_kernel, slots),
        out_shape=(
            jax.ShapeDtypeStruct((many, tile, depth * tile), jnp.bfloat16),
            jax.ShapeDtypeStruct(own.shape, jnp.bfloat16),
            jax.ShapeDtypeStruct((places, target.shape[1]), jnp.bfloat16),
        ),
        in_specs=[VMEM] * 3,
        out_specs=(VMEM,) * 3,
        compiler_params=LIMIT,
        cost_estimate=pl.CostEstimate(flops=0, bytes_accessed=2 * tiles.size * 2, transcendentals=0),
        name="prepare",
    )(tiles, own, target)


def partials_kernel(count, src_ref, wide_ref, *refs):
    block_refs, out_refs, held = refs[:count], refs[count:-1], refs[-1]
    depth = src_ref.shape[1]
    section, rep = lax.axis_index("section"), lax.axis_index("rep")
    for j in range(count):
        held[j] = block_refs[j][...]
    for j, out_ref in zip([0] + across(len(out_refs)), out_refs):
        g = rep ^ j
        right = jnp.concatenate([held[src_ref[g, k] ^ section] for k in range(depth)], axis=0)
        out_ref[...] = jnp.dot(wide_ref[g], right, preferred_element_type=jnp.float32).astype(
            jnp.bfloat16
        )


def partials(sources, wide, blocks):
    many = wide.shape[0]
    tile, width = blocks[0].shape
    return pl.pallas_call(
        functools.partial(partials_kernel, len(blocks)),
        out_shape=[jax.ShapeDtypeStruct((tile, width), jnp.bfloat16)] * many,
        in_specs=[VMEM] * (2 + len(blocks)),
        out_specs=[VMEM] * many,
        scratch_shapes=[pltpu.VMEM((len(blocks), tile, width), jnp.bfloat16)],
        compiler_params=LIMIT,
        name="partials",
    )(sources, wide, *blocks)


def swap(value, axis, j):
    return lax.ppermute(value, axis, [(i, i ^ j) for i in range(lax.axis_size(axis))])


def tree_sum(terms):
    while len(terms) > 1:
        terms = [terms[i] + terms[i + 1] for i in range(0, len(terms), 2)]
    return terms[0]


def dense_kernel(n_part, weight_ref, cot_ref, placing_ref, *refs):
    part_refs, (same_ref, kept_ref, sent_ref, term) = refs[:n_part], refs[n_part:]
    core = lax.axis_index("section") & 1
    agg_b = tree_sum([ref[...].astype(jnp.float32) for ref in part_refs]).astype(jnp.bfloat16)
    pre = jnp.dot(agg_b, weight_ref[...], preferred_element_type=jnp.float32)
    sig = jax.nn.sigmoid(pre)
    factor = sig * (1.0 + pre * (1.0 - sig))
    grad_pre = (cot_ref[...].astype(jnp.float32) * factor).astype(jnp.bfloat16)
    whole = lax.dot_general(
        agg_b, grad_pre, (((0,), (0,)), ((), ())), preferred_element_type=jnp.float32
    )
    term[...] = whole.reshape(term.shape)
    kept_ref[...] = term[core]
    output = (pre * sig).astype(jnp.bfloat16)
    packed = jnp.dot(placing_ref[...], output, preferred_element_type=jnp.float32)
    half = packed.shape[0] // 2
    same_ref[...] = packed[:half].astype(jnp.bfloat16)
    sent_ref[:half] = packed[half:].astype(jnp.bfloat16)
    sent_ref[half:] = term[1 - core].astype(jnp.bfloat16)


def dense(parts, weight, cotangent, placing):
    places, width = placing.shape[0], weight.shape[0]
    return pl.pallas_call(
        functools.partial(dense_kernel, len(parts)),
        out_shape=(
            jax.ShapeDtypeStruct((places // 2, width), jnp.bfloat16),
            jax.ShapeDtypeStruct((width // 2, width), jnp.float32),
            jax.ShapeDtypeStruct((places // 2 + width // 2, width), jnp.bfloat16),
        ),
        in_specs=[VMEM] * (3 + len(parts)),
        out_specs=(VMEM,) * 3,
        scratch_shapes=[pltpu.VMEM((2, width // 2, width), jnp.float32)],
        compiler_params=LIMIT,
        name="dense",
    )(weight, cotangent, placing, *parts)


def write_messages(slots, same_ref, came_ref, half, out_refs):
    for i, ref in enumerate(out_refs):
        start = (i + 1) * slots % same_ref.shape[0]
        ref[:slots] = same_ref[start : start + slots]
        ref[slots : 2 * slots] = came_ref[start : start + slots]
        ref[2 * slots :] = half


def sum_halves(half_ref, held, slots, own_ref, message_refs, core_along, n_rep):
    chip, chips = place_of_chip()
    core = lax.axis_index("section") & 1

    @pl.when(core == core_along)
    def _():
        held[chip] = own_ref[...]
        for i, ref in enumerate(message_refs[: chips - 1]):
            held[(chip + chips - i - 1) % chips] = ref[2 * slots :]
        total = tree_sum([held[c].astype(jnp.float32) for c in range(chips)])
        half_ref[...] = total.astype(jnp.bfloat16)

    @pl.when(core != core_along)
    def _():
        by_xor = [own_ref[...].astype(jnp.float32)]
        by_xor += [ref[2 * slots :].astype(jnp.float32) for ref in message_refs[::-1]]
        half_ref[...] = tree_sum(by_xor[:n_rep]).astype(jnp.bfloat16)


def first_kernel(slots, same_ref, kept_ref, came_ref, half_ref, *out_refs):
    rows = kept_ref.shape[0]
    half = kept_ref[...] + came_ref[came_ref.shape[0] - rows :].astype(jnp.float32)
    half_ref[...] = half.astype(jnp.bfloat16)
    write_messages(slots, same_ref, came_ref, half_ref[...], out_refs)


def second_kernel(slots, n_rep, many, same_ref, came_ref, own_ref, *refs):
    message_refs, half_ref, out_refs, held = refs[:many], refs[many], refs[many + 1 : -1], refs[-1]
    sum_halves(half_ref, held, slots, own_ref, message_refs, 0, n_rep)
    write_messages(slots, same_ref, came_ref, half_ref[...], out_refs)


def third_kernel(slots, n_rep, own_ref, *refs):
    sum_halves(refs[-2], refs[-1], slots, own_ref, refs[:-2], 1, n_rep)


def call_halves(kernel, name, operands, half, slots, many, held=()):
    shapes = [jax.ShapeDtypeStruct(half, jnp.bfloat16)]
    shapes += [jax.ShapeDtypeStruct((2 * slots + half[0], half[1]), jnp.bfloat16)] * many
    return pl.pallas_call(
        kernel,
        out_shape=shapes,
        in_specs=[VMEM] * len(operands),
        out_specs=[VMEM] * len(shapes),
        scratch_shapes=[pltpu.VMEM(shape, jnp.bfloat16) for shape in held],
        compiler_params=LIMIT,
        name=name,
    )(*operands)


def store_kernel(core, slots, same_ref, came_ref, *refs):
    message_refs, (out_ref, rows, sem) = refs[:-3], refs[-3:]
    section = lax.axis_index("section")
    chip, chips = place_of_chip()

    @pl.when(section & 1 == core)
    def _():
        rows[section] = same_ref[:slots]
        rows[section ^ 1] = came_ref[:slots]
        for i, ref in enumerate(message_refs[: chips - 1]):
            source = 2 * ((chip + chips - i - 1) % chips)
            rows[source + core] = ref[:slots]
            rows[source + 1 - core] = ref[slots : 2 * slots]
        copy = pltpu.make_async_copy(rows, out_ref, sem)
        copy.start()
        copy.wait()


def store(core, same, came, messages, n_section, slots, base=None):
    shape = (n_section, slots, same.shape[1])
    operands = [same, came, *messages]
    kernel, first, specs = functools.partial(store_kernel, core, slots), [], []
    if base is not None:
        kernel, first, specs = lambda _, *refs: store_kernel(core, slots, *refs), [base], [HBM]
    return pl.pallas_call(
        kernel,
        out_shape=jax.ShapeDtypeStruct(shape, jnp.bfloat16),
        in_specs=specs + [VMEM] * len(operands),
        out_specs=HBM,
        scratch_shapes=[pltpu.VMEM(shape, jnp.bfloat16), pltpu.SemaphoreType.DMA],
        input_output_aliases={0: 0} if first else {},
        compiler_params=LIMIT,
        name="store",
    )(*first, *operands)


def finish_kernel(own_ref, came_ref, out_ref):
    core = lax.axis_index("section") & 1
    out_ref[core] = own_ref[...].astype(jnp.float32)
    out_ref[1 - core] = came_ref[...].astype(jnp.float32)


def finish(own, came):
    return pl.pallas_call(
        finish_kernel,
        out_shape=jax.ShapeDtypeStruct((2,) + own.shape, jnp.float32),
        in_specs=[VMEM] * 2,
        out_specs=VMEM,
        compiler_params=LIMIT,
        name="finish",
    )(own, came)


def exchange(value, core_along, shift, j):
    n_section, n_rep = lax.axis_size("section"), lax.axis_size("rep")
    pairs = []
    for s in range(n_section):
        along = s & 1 == core_along
        to = (s + 2 * shift) % n_section if along else s
        for r in range(n_rep):
            pairs.append((s * n_rep + r, to * n_rep + (r if along else r ^ j % n_rep)))
    return lax.ppermute(value, ("section", "rep"), pairs)


def gather_blocks(features, axis, ready):
    n = lax.axis_size(axis)
    blocks = [None] * n
    blocks[0] = features
    order = sorted(range(2, n, 2), key=lambda j: (j & 4, -(j & 2)))
    for j in order:
        blocks[j] = swap(features, axis, j)
    blocks[1] = swap(features, axis, 1)
    blocks[3] = swap(features, axis, 3)
    came, ready = lax.optimization_barrier(([blocks[j] for j in [3] + order], ready))
    for j, block in zip([3] + order, came):
        blocks[j] = block
    for j in range(4, n, 2):
        blocks[j + 1] = swap(blocks[j], axis, 1)
    return blocks, ready


def per_device(features, adj_tiles, adj_src, cotangent, weight, destination):
    n_section, n_rep = lax.axis_size("section"), lax.axis_size("rep")
    rows_here, width = features.shape
    tile = adj_tiles.shape[3]
    slots = max(2, 2 * rows_here // n_section)
    target = destination.reshape(1, rows_here)
    wide, own, placing = prepare(adj_tiles[:, 0], features, target, n_section * slots, slots)
    blocks, (wide, own, placing) = gather_blocks(features, "section", (wide, own, placing))
    parts = list(partials(adj_src[:, 0], wide, [own] + blocks[1:]))
    others = across(n_rep)
    parts = parts[:1] + [swap(part, "rep", j) for part, j in zip(parts[1:], others)]
    same, kept, sent = dense(parts, weight, cotangent, placing)
    came = swap(sent, "section", 1)
    chips = n_section // 2
    steps = across(max(n_rep, chips))
    half_shape = (width // 2, width)
    held = [(chips,) + half_shape]
    half, *first = call_halves(
        functools.partial(first_kernel, slots), "first", [same, kept, came], half_shape, slots, len(steps)
    )
    first = [exchange(m, 0, i + 1, j) for i, (m, j) in enumerate(zip(first, steps))]
    relaid = store(0, same, came, first, n_section, slots)
    half, *second = call_halves(
        functools.partial(second_kernel, slots, n_rep, len(steps)),
        "second",
        [same, came, half, *first],
        half_shape,
        slots,
        len(steps),
        held,
    )
    second = [exchange(m, 1, i + 1, j) for i, (m, j) in enumerate(zip(second, steps))]
    (half,) = call_halves(
        functools.partial(third_kernel, slots, n_rep), "third", [half, *second], half_shape, slots, 0, held
    )
    relaid = store(1, same, came, second, n_section, slots, relaid)
    half, relaid = lax.optimization_barrier((half, relaid))
    weight_grad = finish(half, swap(half, "section", 1))
    return (relaid.reshape(1, 1, n_section, slots, width), weight_grad.reshape(width, width))


def solution(mesh):
    placed = (
        P(("section", "rep"), None),
        P("section", "rep", None, None, None),
        P("section", "rep", None),
        P(("section", "rep"), None),
        P(),
        P(("section", "rep"), None),
    )
    return jax.shard_map(
        per_device,
        mesh=mesh,
        in_specs=placed,
        out_specs=(P("section", "rep", None, None, None), P()),
        check_vma=False,
    )
```

```python
import functools

import jax
import jax.numpy as jnp
from jax import lax
from jax.experimental import pallas as pl
from jax.experimental.pallas import tpu as pltpu
from jax.sharding import PartitionSpec as P

VMEM = pl.BlockSpec(memory_space=pltpu.VMEM)
LIMIT = pltpu.CompilerParams(vmem_limit_bytes=32 * 1024 * 1024)
HBM = pl.BlockSpec(memory_space=pltpu.HBM)


def across(n):
    return list(range(n - 1, 0, -1))


def place_of_chip():
    return lax.axis_index("section") >> 1, lax.axis_size("section") // 2


def prepare_kernel(slots, tiles_ref, own_ref, target_ref, wide_ref, held_ref, placing_ref):
    many, depth = tiles_ref.shape[:2]
    for g in range(many):
        wide_ref[g] = jnp.concatenate([tiles_ref[g, k] for k in range(depth)], axis=1)
    held_ref[...] = own_ref[...]
    places, rows = placing_ref.shape
    n_section = places // slots
    target = target_ref[...]
    hits = lax.broadcasted_iota(jnp.int32, (n_section, rows), 0) == target
    hits = jnp.where(hits, 1.0, 0.0)
    earlier = lax.broadcasted_iota(jnp.int32, (rows, rows), 0) < lax.broadcasted_iota(
        jnp.int32, (rows, rows), 1
    )
    earlier = jnp.where(earlier, 1.0, 0.0).astype(jnp.bfloat16)
    before = jnp.dot(hits.astype(jnp.bfloat16), earlier, preferred_element_type=jnp.float32)
    slot = jnp.sum(before * hits, axis=0, keepdims=True).astype(jnp.int32)
    chip, chips = place_of_chip()
    apart = (target >> 1) - chip
    apart = jnp.where(apart < 0, apart + chips, apart)
    other_core = (target ^ lax.axis_index("section")) & 1
    position = (other_core * chips + apart) * slots + slot
    placing = lax.broadcasted_iota(jnp.int32, (places, rows), 0) == position
    placing_ref[...] = jnp.where(placing, 1.0, 0.0).astype(jnp.bfloat16)


def prepare(tiles, own, target, places, slots):
    many, depth, tile, _ = tiles.shape
    return pl.pallas_call(
        functools.partial(prepare_kernel, slots),
        out_shape=(
            jax.ShapeDtypeStruct((many, tile, depth * tile), jnp.bfloat16),
            jax.ShapeDtypeStruct(own.shape, jnp.bfloat16),
            jax.ShapeDtypeStruct((places, target.shape[1]), jnp.bfloat16),
        ),
        in_specs=[VMEM] * 3,
        out_specs=(VMEM,) * 3,
        compiler_params=LIMIT,
        cost_estimate=pl.CostEstimate(flops=0, bytes_accessed=2 * tiles.size * 2, transcendentals=0),
        name="prepare",
    )(tiles, own, target)


def partials_kernel(count, src_ref, wide_ref, *refs):
    block_refs, out_refs, held = refs[:count], refs[count:-1], refs[-1]
    depth = src_ref.shape[1]
    section, rep = lax.axis_index("section"), lax.axis_index("rep")
    for j in range(count):
        held[j] = block_refs[j][...]
    for j, out_ref in zip([0] + across(len(out_refs)), out_refs):
        g = rep ^ j
        right = jnp.concatenate([held[src_ref[g, k] ^ section] for k in range(depth)], axis=0)
        out_ref[...] = jnp.dot(wide_ref[g], right, preferred_element_type=jnp.float32).astype(
            jnp.bfloat16
        )


def partials(sources, wide, blocks):
    many = wide.shape[0]
    tile, width = blocks[0].shape
    return pl.pallas_call(
        functools.partial(partials_kernel, len(blocks)),
        out_shape=[jax.ShapeDtypeStruct((tile, width), jnp.bfloat16)] * many,
        in_specs=[VMEM] * (2 + len(blocks)),
        out_specs=[VMEM] * many,
        scratch_shapes=[pltpu.VMEM((len(blocks), tile, width), jnp.bfloat16)],
        compiler_params=LIMIT,
        name="partials",
    )(sources, wide, *blocks)


def swap(value, axis, j):
    return lax.ppermute(value, axis, [(i, i ^ j) for i in range(lax.axis_size(axis))])


def tree_sum(terms):
    while len(terms) > 1:
        terms = [terms[i] + terms[i + 1] for i in range(0, len(terms), 2)]
    return terms[0]


def dense_kernel(n_part, weight_ref, cot_ref, placing_ref, *refs):
    part_refs, (same_ref, kept_ref, sent_ref, term) = refs[:n_part], refs[n_part:]
    core = lax.axis_index("section") & 1
    agg_b = tree_sum([ref[...].astype(jnp.float32) for ref in part_refs]).astype(jnp.bfloat16)
    pre = jnp.dot(agg_b, weight_ref[...], preferred_element_type=jnp.float32)
    sig = jax.nn.sigmoid(pre)
    factor = sig * (1.0 + pre * (1.0 - sig))
    grad_pre = (cot_ref[...].astype(jnp.float32) * factor).astype(jnp.bfloat16)
    whole = lax.dot_general(
        agg_b, grad_pre, (((0,), (0,)), ((), ())), preferred_element_type=jnp.float32
    )
    term[...] = whole.reshape(term.shape)
    kept_ref[...] = term[core]
    output = (pre * sig).astype(jnp.bfloat16)
    packed = jnp.dot(placing_ref[...], output, preferred_element_type=jnp.float32)
    half = packed.shape[0] // 2
    same_ref[...] = packed[:half].astype(jnp.bfloat16)
    sent_ref[:half] = packed[half:].astype(jnp.bfloat16)
    sent_ref[half:] = term[1 - core].astype(jnp.bfloat16)


def dense(parts, weight, cotangent, placing):
    places, width = placing.shape[0], weight.shape[0]
    return pl.pallas_call(
        functools.partial(dense_kernel, len(parts)),
        out_shape=(
            jax.ShapeDtypeStruct((places // 2, width), jnp.bfloat16),
            jax.ShapeDtypeStruct((width // 2, width), jnp.float32),
            jax.ShapeDtypeStruct((places // 2 + width // 2, width), jnp.bfloat16),
        ),
        in_specs=[VMEM] * (3 + len(parts)),
        out_specs=(VMEM,) * 3,
        scratch_shapes=[pltpu.VMEM((2, width // 2, width), jnp.float32)],
        compiler_params=LIMIT,
        name="dense",
    )(weight, cotangent, placing, *parts)


def write_messages(slots, same_ref, came_ref, half, out_refs):
    for i, ref in enumerate(out_refs):
        start = (i + 1) * slots % same_ref.shape[0]
        ref[:slots] = same_ref[start : start + slots]
        ref[slots : 2 * slots] = came_ref[start : start + slots]
        ref[2 * slots :] = half


def sum_halves(half_ref, held, slots, own_ref, message_refs, core_along, n_rep):
    chip, chips = place_of_chip()
    core = lax.axis_index("section") & 1

    @pl.when(core == core_along)
    def _():
        held[chip] = own_ref[...]
        for i, ref in enumerate(message_refs[: chips - 1]):
            held[(chip + chips - i - 1) % chips] = ref[2 * slots :]
        total = tree_sum([held[c].astype(jnp.float32) for c in range(chips)])
        half_ref[...] = total.astype(jnp.bfloat16)

    @pl.when(core != core_along)
    def _():
        by_xor = [own_ref[...].astype(jnp.float32)]
        by_xor += [ref[2 * slots :].astype(jnp.float32) for ref in message_refs[::-1]]
        half_ref[...] = tree_sum(by_xor[:n_rep]).astype(jnp.bfloat16)


def first_kernel(slots, same_ref, kept_ref, came_ref, half_ref, *out_refs):
    rows = kept_ref.shape[0]
    half = kept_ref[...] + came_ref[came_ref.shape[0] - rows :].astype(jnp.float32)
    half_ref[...] = half.astype(jnp.bfloat16)
    write_messages(slots, same_ref, came_ref, half_ref[...], out_refs)


def second_kernel(slots, n_rep, many, same_ref, came_ref, own_ref, *refs):
    message_refs, half_ref, out_refs, held = refs[:many], refs[many], refs[many + 1 : -1], refs[-1]
    sum_halves(half_ref, held, slots, own_ref, message_refs, 0, n_rep)
    write_messages(slots, same_ref, came_ref, half_ref[...], out_refs)


def third_kernel(slots, n_rep, own_ref, *refs):
    sum_halves(refs[-2], refs[-1], slots, own_ref, refs[:-2], 1, n_rep)


def call_halves(kernel, name, operands, half, slots, many, held=()):
    shapes = [jax.ShapeDtypeStruct(half, jnp.bfloat16)]
    shapes += [jax.ShapeDtypeStruct((2 * slots + half[0], half[1]), jnp.bfloat16)] * many
    return pl.pallas_call(
        kernel,
        out_shape=shapes,
        in_specs=[VMEM] * len(operands),
        out_specs=[VMEM] * len(shapes),
        scratch_shapes=[pltpu.VMEM(shape, jnp.bfloat16) for shape in held],
        compiler_params=LIMIT,
        name=name,
    )(*operands)


def store_kernel(core, slots, same_ref, came_ref, *refs):
    message_refs, (out_ref, rows, sem) = refs[:-3], refs[-3:]
    section = lax.axis_index("section")
    chip, chips = place_of_chip()

    @pl.when(section & 1 == core)
    def _():
        rows[section] = same_ref[:slots]
        rows[section ^ 1] = came_ref[:slots]
        for i, ref in enumerate(message_refs[: chips - 1]):
            source = 2 * ((chip + chips - i - 1) % chips)
            rows[source + core] = ref[:slots]
            rows[source + 1 - core] = ref[slots : 2 * slots]
        copy = pltpu.make_async_copy(rows, out_ref, sem)
        copy.start()
        copy.wait()


def store(core, same, came, messages, n_section, slots, base=None):
    shape = (n_section, slots, same.shape[1])
    operands = [same, came, *messages]
    kernel, first, specs = functools.partial(store_kernel, core, slots), [], []
    if base is not None:
        kernel, first, specs = lambda _, *refs: store_kernel(core, slots, *refs), [base], [HBM]
    return pl.pallas_call(
        kernel,
        out_shape=jax.ShapeDtypeStruct(shape, jnp.bfloat16),
        in_specs=specs + [VMEM] * len(operands),
        out_specs=HBM,
        scratch_shapes=[pltpu.VMEM(shape, jnp.bfloat16), pltpu.SemaphoreType.DMA],
        input_output_aliases={0: 0} if first else {},
        compiler_params=LIMIT,
        name="store",
    )(*first, *operands)


def finish_kernel(own_ref, came_ref, out_ref):
    core = lax.axis_index("section") & 1
    out_ref[core] = own_ref[...].astype(jnp.float32)
    out_ref[1 - core] = came_ref[...].astype(jnp.float32)


def finish(own, came):
    return pl.pallas_call(
        finish_kernel,
        out_shape=jax.ShapeDtypeStruct((2,) + own.shape, jnp.float32),
        in_specs=[VMEM] * 2,
        out_specs=VMEM,
        compiler_params=LIMIT,
        name="finish",
    )(own, came)


def exchange(value, core_along, shift, j):
    n_section, n_rep = lax.axis_size("section"), lax.axis_size("rep")
    pairs = []
    for s in range(n_section):
        along = s & 1 == core_along
        to = (s + 2 * shift) % n_section if along else s
        for r in range(n_rep):
            pairs.append((s * n_rep + r, to * n_rep + (r if along else r ^ j % n_rep)))
    return lax.ppermute(value, ("section", "rep"), pairs)


def gather_blocks(features, axis, ready):
    n = lax.axis_size(axis)
    blocks = [None] * n
    blocks[0] = features
    first, *rest = [n // 2 & -2] + [j for j in range(2, n, 2) if j != n // 2 & -2]
    for j in rest + [first]:
        blocks[j] = swap(features, axis, j)
    blocks[1] = swap(features, axis, 1)
    blocks[first], ready = lax.optimization_barrier((blocks[first], ready))
    blocks[first + 1] = swap(blocks[first], axis, 1)
    tied = lax.optimization_barrier([blocks[j] for j in rest + [first + 1]])
    for j, block in zip(rest + [first + 1], tied):
        blocks[j] = block
    for j in rest:
        blocks[j + 1] = swap(blocks[j], axis, 1)
    return blocks, ready


def per_device(features, adj_tiles, adj_src, cotangent, weight, destination):
    n_section, n_rep = lax.axis_size("section"), lax.axis_size("rep")
    rows_here, width = features.shape
    tile = adj_tiles.shape[3]
    slots = max(2, 2 * rows_here // n_section)
    target = destination.reshape(1, rows_here)
    wide, own, placing = prepare(adj_tiles[:, 0], features, target, n_section * slots, slots)
    blocks, (wide, own, placing) = gather_blocks(features, "section", (wide, own, placing))
    parts = list(partials(adj_src[:, 0], wide, [own] + blocks[1:]))
    others = across(n_rep)
    parts = parts[:1] + [swap(part, "rep", j) for part, j in zip(parts[1:], others)]
    same, kept, sent = dense(parts, weight, cotangent, placing)
    came = swap(sent, "section", 1)
    chips = n_section // 2
    steps = across(max(n_rep, chips))
    half_shape = (width // 2, width)
    held = [(chips,) + half_shape]
    half, *first = call_halves(
        functools.partial(first_kernel, slots), "first", [same, kept, came], half_shape, slots, len(steps)
    )
    first = [exchange(m, 0, i + 1, j) for i, (m, j) in enumerate(zip(first, steps))]
    relaid = store(0, same, came, first, n_section, slots)
    half, *second = call_halves(
        functools.partial(second_kernel, slots, n_rep, len(steps)),
        "second",
        [same, came, half, *first],
        half_shape,
        slots,
        len(steps),
        held,
    )
    second = [exchange(m, 1, i + 1, j) for i, (m, j) in enumerate(zip(second, steps))]
    (half,) = call_halves(
        functools.partial(third_kernel, slots, n_rep), "third", [half, *second], half_shape, slots, 0, held
    )
    relaid = store(1, same, came, second, n_section, slots, relaid)
    half, relaid = lax.optimization_barrier((half, relaid))
    weight_grad = finish(half, swap(half, "section", 1))
    return (relaid.reshape(1, 1, n_section, slots, width), weight_grad.reshape(width, width))


def solution(mesh):
    placed = (
        P(("section", "rep"), None),
        P("section", "rep", None, None, None),
        P("section", "rep", None),
        P(("section", "rep"), None),
        P(),
        P(("section", "rep"), None),
    )
    return jax.shard_map(
        per_device,
        mesh=mesh,
        in_specs=placed,
        out_specs=(P("section", "rep", None, None, None), P()),
        check_vma=False,
    )
```

```python
import functools

import jax
import jax.numpy as jnp
from jax import lax
from jax.experimental import pallas as pl
from jax.experimental.pallas import tpu as pltpu
from jax.sharding import PartitionSpec as P

VMEM = pl.BlockSpec(memory_space=pltpu.VMEM)
LIMIT = pltpu.CompilerParams(vmem_limit_bytes=32 * 1024 * 1024)
HBM = pl.BlockSpec(memory_space=pltpu.HBM)


def across(n):
    return list(range(n - 1, 0, -1))


def place_of_chip():
    return lax.axis_index("section") >> 1, lax.axis_size("section") // 2


def prepare_kernel(slots, tiles_ref, own_ref, target_ref, wide_ref, held_ref, placing_ref):
    many, depth = tiles_ref.shape[:2]
    for g in range(many):
        wide_ref[g] = jnp.concatenate([tiles_ref[g, k] for k in range(depth)], axis=1)
    held_ref[...] = own_ref[...]
    places, rows = placing_ref.shape
    n_section = places // slots
    target = target_ref[...]
    hits = lax.broadcasted_iota(jnp.int32, (n_section, rows), 0) == target
    hits = jnp.where(hits, 1.0, 0.0)
    earlier = lax.broadcasted_iota(jnp.int32, (rows, rows), 0) < lax.broadcasted_iota(
        jnp.int32, (rows, rows), 1
    )
    earlier = jnp.where(earlier, 1.0, 0.0).astype(jnp.bfloat16)
    before = jnp.dot(hits.astype(jnp.bfloat16), earlier, preferred_element_type=jnp.float32)
    slot = jnp.sum(before * hits, axis=0, keepdims=True).astype(jnp.int32)
    chip, chips = place_of_chip()
    apart = (target >> 1) - chip
    apart = jnp.where(apart < 0, apart + chips, apart)
    other_core = (target ^ lax.axis_index("section")) & 1
    position = (other_core * chips + apart) * slots + slot
    placing = lax.broadcasted_iota(jnp.int32, (places, rows), 0) == position
    placing_ref[...] = jnp.where(placing, 1.0, 0.0).astype(jnp.bfloat16)


def prepare(tiles, own, target, places, slots):
    many, depth, tile, _ = tiles.shape
    return pl.pallas_call(
        functools.partial(prepare_kernel, slots),
        out_shape=(
            jax.ShapeDtypeStruct((many, tile, depth * tile), jnp.bfloat16),
            jax.ShapeDtypeStruct(own.shape, jnp.bfloat16),
            jax.ShapeDtypeStruct((places, target.shape[1]), jnp.bfloat16),
        ),
        in_specs=[VMEM] * 3,
        out_specs=(VMEM,) * 3,
        compiler_params=LIMIT,
        cost_estimate=pl.CostEstimate(flops=0, bytes_accessed=2 * tiles.size * 2, transcendentals=0),
        name="prepare",
    )(tiles, own, target)


def partials_kernel(count, src_ref, wide_ref, *refs):
    block_refs, out_refs, held = refs[:count], refs[count:-1], refs[-1]
    depth = src_ref.shape[1]
    section, rep = lax.axis_index("section"), lax.axis_index("rep")
    chip, chips = place_of_chip()
    for i, ref in enumerate(block_refs):
        held[2 * ((chip + chips - i % chips) % chips) + ((section + i // chips) & 1)] = ref[...]
    for j, out_ref in zip([0] + across(len(out_refs)), out_refs):
        g = rep ^ j
        right = jnp.concatenate([held[src_ref[g, k]] for k in range(depth)], axis=0)
        out_ref[...] = jnp.dot(wide_ref[g], right, preferred_element_type=jnp.float32).astype(
            jnp.bfloat16
        )


def partials(sources, wide, blocks):
    many = wide.shape[0]
    tile, width = blocks[0].shape
    return pl.pallas_call(
        functools.partial(partials_kernel, len(blocks)),
        out_shape=[jax.ShapeDtypeStruct((tile, width), jnp.bfloat16)] * many,
        in_specs=[VMEM] * (2 + len(blocks)),
        out_specs=[VMEM] * many,
        scratch_shapes=[pltpu.VMEM((len(blocks), tile, width), jnp.bfloat16)],
        compiler_params=LIMIT,
        name="partials",
    )(sources, wide, *blocks)


def swap(value, axis, j):
    return lax.ppermute(value, axis, [(i, i ^ j) for i in range(lax.axis_size(axis))])


def tree_sum(terms):
    while len(terms) > 1:
        terms = [terms[i] + terms[i + 1] for i in range(0, len(terms), 2)]
    return terms[0]


def dense_kernel(n_part, weight_ref, cot_ref, placing_ref, *refs):
    part_refs, (same_ref, kept_ref, sent_ref, term) = refs[:n_part], refs[n_part:]
    core = lax.axis_index("section") & 1
    agg_b = tree_sum([ref[...].astype(jnp.float32) for ref in part_refs]).astype(jnp.bfloat16)
    pre = jnp.dot(agg_b, weight_ref[...], preferred_element_type=jnp.float32)
    sig = jax.nn.sigmoid(pre)
    factor = sig * (1.0 + pre * (1.0 - sig))
    grad_pre = (cot_ref[...].astype(jnp.float32) * factor).astype(jnp.bfloat16)
    whole = lax.dot_general(
        agg_b, grad_pre, (((0,), (0,)), ((), ())), preferred_element_type=jnp.float32
    )
    term[...] = whole.reshape(term.shape)
    kept_ref[...] = term[core]
    output = (pre * sig).astype(jnp.bfloat16)
    packed = jnp.dot(placing_ref[...], output, preferred_element_type=jnp.float32)
    half = packed.shape[0] // 2
    same_ref[...] = packed[:half].astype(jnp.bfloat16)
    sent_ref[:half] = packed[half:].astype(jnp.bfloat16)
    sent_ref[half:] = term[1 - core].astype(jnp.bfloat16)


def dense(parts, weight, cotangent, placing):
    places, width = placing.shape[0], weight.shape[0]
    return pl.pallas_call(
        functools.partial(dense_kernel, len(parts)),
        out_shape=(
            jax.ShapeDtypeStruct((places // 2, width), jnp.bfloat16),
            jax.ShapeDtypeStruct((width // 2, width), jnp.float32),
            jax.ShapeDtypeStruct((places // 2 + width // 2, width), jnp.bfloat16),
        ),
        in_specs=[VMEM] * (3 + len(parts)),
        out_specs=(VMEM,) * 3,
        scratch_shapes=[pltpu.VMEM((2, width // 2, width), jnp.float32)],
        compiler_params=LIMIT,
        name="dense",
    )(weight, cotangent, placing, *parts)


def write_messages(slots, same_ref, came_ref, half, out_refs):
    for i, ref in enumerate(out_refs):
        start = (i + 1) * slots % same_ref.shape[0]
        ref[:slots] = same_ref[start : start + slots]
        ref[slots : 2 * slots] = came_ref[start : start + slots]
        ref[2 * slots :] = half


def sum_halves(half_ref, held, slots, own_ref, message_refs, core_along, n_rep):
    chip, chips = place_of_chip()
    core = lax.axis_index("section") & 1

    @pl.when(core == core_along)
    def _():
        held[chip] = own_ref[...]
        for i, ref in enumerate(message_refs[: chips - 1]):
            held[(chip + chips - i - 1) % chips] = ref[2 * slots :]
        total = tree_sum([held[c].astype(jnp.float32) for c in range(chips)])
        half_ref[...] = total.astype(jnp.bfloat16)

    @pl.when(core != core_along)
    def _():
        by_xor = [own_ref[...].astype(jnp.float32)]
        by_xor += [ref[2 * slots :].astype(jnp.float32) for ref in message_refs[::-1]]
        half_ref[...] = tree_sum(by_xor[:n_rep]).astype(jnp.bfloat16)


def first_kernel(slots, same_ref, kept_ref, came_ref, half_ref, *out_refs):
    rows = kept_ref.shape[0]
    half = kept_ref[...] + came_ref[came_ref.shape[0] - rows :].astype(jnp.float32)
    half_ref[...] = half.astype(jnp.bfloat16)
    write_messages(slots, same_ref, came_ref, half_ref[...], out_refs)


def second_kernel(slots, n_rep, many, same_ref, came_ref, own_ref, *refs):
    message_refs, half_ref, out_refs, held = refs[:many], refs[many], refs[many + 1 : -1], refs[-1]
    sum_halves(half_ref, held, slots, own_ref, message_refs, 0, n_rep)
    write_messages(slots, same_ref, came_ref, half_ref[...], out_refs)


def third_kernel(slots, n_rep, own_ref, *refs):
    sum_halves(refs[-2], refs[-1], slots, own_ref, refs[:-2], 1, n_rep)


def call_halves(kernel, name, operands, half, slots, many, held=()):
    shapes = [jax.ShapeDtypeStruct(half, jnp.bfloat16)]
    shapes += [jax.ShapeDtypeStruct((2 * slots + half[0], half[1]), jnp.bfloat16)] * many
    return pl.pallas_call(
        kernel,
        out_shape=shapes,
        in_specs=[VMEM] * len(operands),
        out_specs=[VMEM] * len(shapes),
        scratch_shapes=[pltpu.VMEM(shape, jnp.bfloat16) for shape in held],
        compiler_params=LIMIT,
        name=name,
    )(*operands)


def store_kernel(core, slots, same_ref, came_ref, *refs):
    message_refs, (out_ref, rows, sem) = refs[:-3], refs[-3:]
    section = lax.axis_index("section")
    chip, chips = place_of_chip()

    @pl.when(section & 1 == core)
    def _():
        rows[section] = same_ref[:slots]
        rows[section ^ 1] = came_ref[:slots]
        for i, ref in enumerate(message_refs[: chips - 1]):
            source = 2 * ((chip + chips - i - 1) % chips)
            rows[source + core] = ref[:slots]
            rows[source + 1 - core] = ref[slots : 2 * slots]
        copy = pltpu.make_async_copy(rows, out_ref, sem)
        copy.start()
        copy.wait()


def store(core, same, came, messages, n_section, slots, base=None):
    shape = (n_section, slots, same.shape[1])
    operands = [same, came, *messages]
    kernel, first, specs = functools.partial(store_kernel, core, slots), [], []
    if base is not None:
        kernel, first, specs = lambda _, *refs: store_kernel(core, slots, *refs), [base], [HBM]
    return pl.pallas_call(
        kernel,
        out_shape=jax.ShapeDtypeStruct(shape, jnp.bfloat16),
        in_specs=specs + [VMEM] * len(operands),
        out_specs=HBM,
        scratch_shapes=[pltpu.VMEM(shape, jnp.bfloat16), pltpu.SemaphoreType.DMA],
        input_output_aliases={0: 0} if first else {},
        compiler_params=LIMIT,
        name="store",
    )(*first, *operands)


def finish_kernel(own_ref, came_ref, out_ref):
    core = lax.axis_index("section") & 1
    out_ref[core] = own_ref[...].astype(jnp.float32)
    out_ref[1 - core] = came_ref[...].astype(jnp.float32)


def finish(own, came):
    return pl.pallas_call(
        finish_kernel,
        out_shape=jax.ShapeDtypeStruct((2,) + own.shape, jnp.float32),
        in_specs=[VMEM] * 2,
        out_specs=VMEM,
        compiler_params=LIMIT,
        name="finish",
    )(own, came)


def exchange(value, core_along, shift, j):
    n_section, n_rep = lax.axis_size("section"), lax.axis_size("rep")
    pairs = []
    for s in range(n_section):
        along = s & 1 == core_along
        to = (s + 2 * shift) % n_section if along else s
        for r in range(n_rep):
            pairs.append((s * n_rep + r, to * n_rep + (r if along else r ^ j % n_rep)))
    return lax.ppermute(value, ("section", "rep"), pairs)


def send_along(value, axis, shift):
    n = lax.axis_size(axis)
    return lax.ppermute(value, axis, [(s, (s + 2 * shift) % n) for s in range(n)])


def gather_blocks(features, axis, ready):
    chips = lax.axis_size(axis) // 2
    near = [features] + [send_along(features, axis, i) for i in range(1, chips)]
    beside = swap(features, axis, 1)
    came, ready = lax.optimization_barrier((near[:0:-1], ready))
    near[1:] = came[::-1]
    return near, [beside] + [swap(block, axis, 1) for block in near[1:]], ready


def per_device(features, adj_tiles, adj_src, cotangent, weight, destination):
    n_section, n_rep = lax.axis_size("section"), lax.axis_size("rep")
    rows_here, width = features.shape
    tile = adj_tiles.shape[3]
    slots = max(2, 2 * rows_here // n_section)
    target = destination.reshape(1, rows_here)
    wide, own, placing = prepare(adj_tiles[:, 0], features, target, n_section * slots, slots)
    near, beside, (wide, own, placing) = gather_blocks(features, "section", (wide, own, placing))
    parts = list(partials(adj_src[:, 0], wide, [own] + near[1:] + beside))
    others = across(n_rep)
    parts = parts[:1] + [swap(part, "rep", j) for part, j in zip(parts[1:], others)]
    same, kept, sent = dense(parts, weight, cotangent, placing)
    came = swap(sent, "section", 1)
    chips = n_section // 2
    steps = across(max(n_rep, chips))
    half_shape = (width // 2, width)
    held = [(chips,) + half_shape]
    half, *first = call_halves(
        functools.partial(first_kernel, slots), "first", [same, kept, came], half_shape, slots, len(steps)
    )
    first = [exchange(m, 0, i + 1, j) for i, (m, j) in enumerate(zip(first, steps))]
    relaid = store(0, same, came, first, n_section, slots)
    half, *second = call_halves(
        functools.partial(second_kernel, slots, n_rep, len(steps)),
        "second",
        [same, came, half, *first],
        half_shape,
        slots,
        len(steps),
        held,
    )
    second = [exchange(m, 1, i + 1, j) for i, (m, j) in enumerate(zip(second, steps))]
    (half,) = call_halves(
        functools.partial(third_kernel, slots, n_rep), "third", [half, *second], half_shape, slots, 0, held
    )
    relaid = store(1, same, came, second, n_section, slots, relaid)
    half, relaid = lax.optimization_barrier((half, relaid))
    weight_grad = finish(half, swap(half, "section", 1))
    return (relaid.reshape(1, 1, n_section, slots, width), weight_grad.reshape(width, width))


def solution(mesh):
    placed = (
        P(("section", "rep"), None),
        P("section", "rep", None, None, None),
        P("section", "rep", None),
        P(("section", "rep"), None),
        P(),
        P(("section", "rep"), None),
    )
    return jax.shard_map(
        per_device,
        mesh=mesh,
        in_specs=placed,
        out_specs=(P("section", "rep", None, None, None), P()),
        check_vma=False,
    )
```

```python
import functools

import jax
import jax.numpy as jnp
from jax import lax
from jax.experimental import pallas as pl
from jax.experimental.pallas import tpu as pltpu
from jax.sharding import PartitionSpec as P

VMEM = pl.BlockSpec(memory_space=pltpu.VMEM)
LIMIT = pltpu.CompilerParams(vmem_limit_bytes=32 * 1024 * 1024)
HBM = pl.BlockSpec(memory_space=pltpu.HBM)


def across(n):
    return list(range(n - 1, 0, -1))


def place_of_chip():
    return lax.axis_index("section") >> 1, lax.axis_size("section") // 2


def prepare_kernel(slots, tiles_ref, own_ref, target_ref, wide_ref, held_ref, placing_ref):
    many, depth = tiles_ref.shape[:2]
    for g in range(many):
        wide_ref[g] = jnp.concatenate([tiles_ref[g, k] for k in range(depth)], axis=1)
    held_ref[...] = own_ref[...]
    places, rows = placing_ref.shape
    n_section = places // slots
    target = target_ref[...]
    hits = lax.broadcasted_iota(jnp.int32, (n_section, rows), 0) == target
    hits = jnp.where(hits, 1.0, 0.0)
    earlier = lax.broadcasted_iota(jnp.int32, (rows, rows), 0) < lax.broadcasted_iota(
        jnp.int32, (rows, rows), 1
    )
    earlier = jnp.where(earlier, 1.0, 0.0).astype(jnp.bfloat16)
    before = jnp.dot(hits.astype(jnp.bfloat16), earlier, preferred_element_type=jnp.float32)
    slot = jnp.sum(before * hits, axis=0, keepdims=True).astype(jnp.int32)
    chip, chips = place_of_chip()
    apart = (target >> 1) - chip
    apart = jnp.where(apart < 0, apart + chips, apart)
    other_core = (target ^ lax.axis_index("section")) & 1
    position = (other_core * chips + apart) * slots + slot
    placing = lax.broadcasted_iota(jnp.int32, (places, rows), 0) == position
    placing_ref[...] = jnp.where(placing, 1.0, 0.0).astype(jnp.bfloat16)


def prepare(tiles, own, target, places, slots):
    many, depth, tile, _ = tiles.shape
    return pl.pallas_call(
        functools.partial(prepare_kernel, slots),
        out_shape=(
            jax.ShapeDtypeStruct((many, tile, depth * tile), jnp.bfloat16),
            jax.ShapeDtypeStruct(own.shape, jnp.bfloat16),
            jax.ShapeDtypeStruct((places, target.shape[1]), jnp.bfloat16),
        ),
        in_specs=[VMEM] * 3,
        out_specs=(VMEM,) * 3,
        compiler_params=LIMIT,
        cost_estimate=pl.CostEstimate(flops=0, bytes_accessed=2 * tiles.size * 2, transcendentals=0),
        name="prepare",
    )(tiles, own, target)


def partials_kernel(count, src_ref, wide_ref, *refs):
    block_refs, out_refs, held = refs[:count], refs[count:-1], refs[-1]
    depth = src_ref.shape[1]
    section, rep = lax.axis_index("section"), lax.axis_index("rep")
    chip, chips = place_of_chip()
    sources = [chip]
    for route in routes(chips):
        source = jnp.int32(0)
        for c, to in enumerate(route):
            source = jnp.where(chip == to, c, source)
        sources.append(source)
    for i, ref in enumerate(block_refs):
        held[2 * sources[i % chips] + ((section + i // chips) & 1)] = ref[...]
    for j, out_ref in zip([0] + across(len(out_refs)), out_refs):
        g = rep ^ j
        right = jnp.concatenate([held[src_ref[g, k]] for k in range(depth)], axis=0)
        out_ref[...] = jnp.dot(wide_ref[g], right, preferred_element_type=jnp.float32).astype(
            jnp.bfloat16
        )


def partials(sources, wide, blocks):
    many = wide.shape[0]
    tile, width = blocks[0].shape
    return pl.pallas_call(
        functools.partial(partials_kernel, len(blocks)),
        out_shape=[jax.ShapeDtypeStruct((tile, width), jnp.bfloat16)] * many,
        in_specs=[VMEM] * (2 + len(blocks)),
        out_specs=[VMEM] * many,
        scratch_shapes=[pltpu.VMEM((len(blocks), tile, width), jnp.bfloat16)],
        compiler_params=LIMIT,
        name="partials",
    )(sources, wide, *blocks)


def swap(value, axis, j):
    return lax.ppermute(value, axis, [(i, i ^ j) for i in range(lax.axis_size(axis))])


def tree_sum(terms):
    while len(terms) > 1:
        terms = [terms[i] + terms[i + 1] for i in range(0, len(terms), 2)]
    return terms[0]


def dense_kernel(n_part, weight_ref, cot_ref, placing_ref, *refs):
    part_refs, (same_ref, kept_ref, sent_ref, term) = refs[:n_part], refs[n_part:]
    core = lax.axis_index("section") & 1
    agg_b = tree_sum([ref[...].astype(jnp.float32) for ref in part_refs]).astype(jnp.bfloat16)
    pre = jnp.dot(agg_b, weight_ref[...], preferred_element_type=jnp.float32)
    sig = jax.nn.sigmoid(pre)
    factor = sig * (1.0 + pre * (1.0 - sig))
    grad_pre = (cot_ref[...].astype(jnp.float32) * factor).astype(jnp.bfloat16)
    whole = lax.dot_general(
        agg_b, grad_pre, (((0,), (0,)), ((), ())), preferred_element_type=jnp.float32
    )
    term[...] = whole.reshape(term.shape)
    kept_ref[...] = term[core]
    output = (pre * sig).astype(jnp.bfloat16)
    packed = jnp.dot(placing_ref[...], output, preferred_element_type=jnp.float32)
    half = packed.shape[0] // 2
    same_ref[...] = packed[:half].astype(jnp.bfloat16)
    sent_ref[:half] = packed[half:].astype(jnp.bfloat16)
    sent_ref[half:] = term[1 - core].astype(jnp.bfloat16)


def dense(parts, weight, cotangent, placing):
    places, width = placing.shape[0], weight.shape[0]
    return pl.pallas_call(
        functools.partial(dense_kernel, len(parts)),
        out_shape=(
            jax.ShapeDtypeStruct((places // 2, width), jnp.bfloat16),
            jax.ShapeDtypeStruct((width // 2, width), jnp.float32),
            jax.ShapeDtypeStruct((places // 2 + width // 2, width), jnp.bfloat16),
        ),
        in_specs=[VMEM] * (3 + len(parts)),
        out_specs=(VMEM,) * 3,
        scratch_shapes=[pltpu.VMEM((2, width // 2, width), jnp.float32)],
        compiler_params=LIMIT,
        name="dense",
    )(weight, cotangent, placing, *parts)


def write_messages(slots, same_ref, came_ref, half, out_refs):
    for i, ref in enumerate(out_refs):
        start = (i + 1) * slots % same_ref.shape[0]
        ref[:slots] = same_ref[start : start + slots]
        ref[slots : 2 * slots] = came_ref[start : start + slots]
        ref[2 * slots :] = half


def sum_halves(half_ref, held, slots, own_ref, message_refs, core_along, n_rep):
    chip, chips = place_of_chip()
    core = lax.axis_index("section") & 1

    @pl.when(core == core_along)
    def _():
        held[chip] = own_ref[...]
        for i, ref in enumerate(message_refs[: chips - 1]):
            held[(chip + chips - i - 1) % chips] = ref[2 * slots :]
        total = tree_sum([held[c].astype(jnp.float32) for c in range(chips)])
        half_ref[...] = total.astype(jnp.bfloat16)

    @pl.when(core != core_along)
    def _():
        by_xor = [own_ref[...].astype(jnp.float32)]
        by_xor += [ref[2 * slots :].astype(jnp.float32) for ref in message_refs[::-1]]
        half_ref[...] = tree_sum(by_xor[:n_rep]).astype(jnp.bfloat16)


def first_kernel(slots, same_ref, kept_ref, came_ref, half_ref, *out_refs):
    rows = kept_ref.shape[0]
    half = kept_ref[...] + came_ref[came_ref.shape[0] - rows :].astype(jnp.float32)
    half_ref[...] = half.astype(jnp.bfloat16)
    write_messages(slots, same_ref, came_ref, half_ref[...], out_refs)


def second_kernel(slots, n_rep, many, same_ref, came_ref, own_ref, *refs):
    message_refs, half_ref, out_refs, held = refs[:many], refs[many], refs[many + 1 : -1], refs[-1]
    sum_halves(half_ref, held, slots, own_ref, message_refs, 0, n_rep)
    write_messages(slots, same_ref, came_ref, half_ref[...], out_refs)


def third_kernel(slots, n_rep, own_ref, *refs):
    sum_halves(refs[-2], refs[-1], slots, own_ref, refs[:-2], 1, n_rep)


def call_halves(kernel, name, operands, half, slots, many, held=()):
    shapes = [jax.ShapeDtypeStruct(half, jnp.bfloat16)]
    shapes += [jax.ShapeDtypeStruct((2 * slots + half[0], half[1]), jnp.bfloat16)] * many
    return pl.pallas_call(
        kernel,
        out_shape=shapes,
        in_specs=[VMEM] * len(operands),
        out_specs=[VMEM] * len(shapes),
        scratch_shapes=[pltpu.VMEM(shape, jnp.bfloat16) for shape in held],
        compiler_params=LIMIT,
        name=name,
    )(*operands)


def store_kernel(core, slots, same_ref, came_ref, *refs):
    message_refs, (out_ref, rows, sem) = refs[:-3], refs[-3:]
    section = lax.axis_index("section")
    chip, chips = place_of_chip()

    @pl.when(section & 1 == core)
    def _():
        rows[section] = same_ref[:slots]
        rows[section ^ 1] = came_ref[:slots]
        for i, ref in enumerate(message_refs[: chips - 1]):
            source = 2 * ((chip + chips - i - 1) % chips)
            rows[source + core] = ref[:slots]
            rows[source + 1 - core] = ref[slots : 2 * slots]
        copy = pltpu.make_async_copy(rows, out_ref, sem)
        copy.start()
        copy.wait()


def store(core, same, came, messages, n_section, slots, base=None):
    shape = (n_section, slots, same.shape[1])
    operands = [same, came, *messages]
    kernel, first, specs = functools.partial(store_kernel, core, slots), [], []
    if base is not None:
        kernel, first, specs = lambda _, *refs: store_kernel(core, slots, *refs), [base], [HBM]
    return pl.pallas_call(
        kernel,
        out_shape=jax.ShapeDtypeStruct(shape, jnp.bfloat16),
        in_specs=specs + [VMEM] * len(operands),
        out_specs=HBM,
        scratch_shapes=[pltpu.VMEM(shape, jnp.bfloat16), pltpu.SemaphoreType.DMA],
        input_output_aliases={0: 0} if first else {},
        compiler_params=LIMIT,
        name="store",
    )(*first, *operands)


def finish_kernel(own_ref, came_ref, out_ref):
    core = lax.axis_index("section") & 1
    out_ref[core] = own_ref[...].astype(jnp.float32)
    out_ref[1 - core] = came_ref[...].astype(jnp.float32)


def finish(own, came):
    return pl.pallas_call(
        finish_kernel,
        out_shape=jax.ShapeDtypeStruct((2,) + own.shape, jnp.float32),
        in_specs=[VMEM] * 2,
        out_specs=VMEM,
        compiler_params=LIMIT,
        name="finish",
    )(own, came)


def exchange(value, core_along, shift, j):
    n_section, n_rep = lax.axis_size("section"), lax.axis_size("rep")
    pairs = []
    for s in range(n_section):
        along = s & 1 == core_along
        to = (s + 2 * shift) % n_section if along else s
        for r in range(n_rep):
            pairs.append((s * n_rep + r, to * n_rep + (r if along else r ^ j % n_rep)))
    return lax.ppermute(value, ("section", "rep"), pairs)


def routes(chips):
    if chips == 4:
        return [(1, 3, 0, 2), (3, 2, 1, 0), (2, 0, 3, 1)]
    return [tuple((c + i) % chips for c in range(chips)) for i in range(1, chips)]


def send_along(value, axis, route):
    pairs = [(s, 2 * route[s // 2] + s % 2) for s in range(lax.axis_size(axis))]
    return lax.ppermute(value, axis, pairs)


def gather_blocks(features, axis, ready):
    chips = lax.axis_size(axis) // 2
    near = [features] + [send_along(features, axis, route) for route in routes(chips)]
    beside = swap(features, axis, 1)
    came, ready = lax.optimization_barrier((near[:0:-1], ready))
    near[1:] = came[::-1]
    return near, [beside] + [swap(block, axis, 1) for block in near[1:]], ready


def per_device(features, adj_tiles, adj_src, cotangent, weight, destination):
    n_section, n_rep = lax.axis_size("section"), lax.axis_size("rep")
    rows_here, width = features.shape
    tile = adj_tiles.shape[3]
    slots = max(2, 2 * rows_here // n_section)
    target = destination.reshape(1, rows_here)
    wide, own, placing = prepare(adj_tiles[:, 0], features, target, n_section * slots, slots)
    near, beside, (wide, own, placing) = gather_blocks(features, "section", (wide, own, placing))
    parts = list(partials(adj_src[:, 0], wide, [own] + near[1:] + beside))
    others = across(n_rep)
    parts = parts[:1] + [swap(part, "rep", j) for part, j in zip(parts[1:], others)]
    same, kept, sent = dense(parts, weight, cotangent, placing)
    came = swap(sent, "section", 1)
    chips = n_section // 2
    steps = across(max(n_rep, chips))
    half_shape = (width // 2, width)
    held = [(chips,) + half_shape]
    half, *first = call_halves(
        functools.partial(first_kernel, slots), "first", [same, kept, came], half_shape, slots, len(steps)
    )
    first = [exchange(m, 0, i + 1, j) for i, (m, j) in enumerate(zip(first, steps))]
    relaid = store(0, same, came, first, n_section, slots)
    half, *second = call_halves(
        functools.partial(second_kernel, slots, n_rep, len(steps)),
        "second",
        [same, came, half, *first],
        half_shape,
        slots,
        len(steps),
        held,
    )
    second = [exchange(m, 1, i + 1, j) for i, (m, j) in enumerate(zip(second, steps))]
    (half,) = call_halves(
        functools.partial(third_kernel, slots, n_rep), "third", [half, *second], half_shape, slots, 0, held
    )
    relaid = store(1, same, came, second, n_section, slots, relaid)
    half, relaid = lax.optimization_barrier((half, relaid))
    weight_grad = finish(half, swap(half, "section", 1))
    return (relaid.reshape(1, 1, n_section, slots, width), weight_grad.reshape(width, width))


def solution(mesh):
    placed = (
        P(("section", "rep"), None),
        P("section", "rep", None, None, None),
        P("section", "rep", None),
        P(("section", "rep"), None),
        P(),
        P(("section", "rep"), None),
    )
    return jax.shard_map(
        per_device,
        mesh=mesh,
        in_specs=placed,
        out_specs=(P("section", "rep", None, None, None), P()),
        check_vma=False,
    )
```

```python
import functools

import jax
import jax.numpy as jnp
from jax import lax
from jax.experimental import pallas as pl
from jax.experimental.pallas import tpu as pltpu
from jax.sharding import PartitionSpec as P

VMEM = pl.BlockSpec(memory_space=pltpu.VMEM)
LIMIT = pltpu.CompilerParams(vmem_limit_bytes=32 * 1024 * 1024)
HBM = pl.BlockSpec(memory_space=pltpu.HBM)


def across(n):
    return list(range(n - 1, 0, -1))


def place_of_chip():
    return lax.axis_index("section") >> 1, lax.axis_size("section") // 2


def prepare_kernel(slots, tiles_ref, own_ref, target_ref, wide_ref, held_ref, placing_ref):
    many, depth = tiles_ref.shape[:2]
    for g in range(many):
        wide_ref[g] = jnp.concatenate([tiles_ref[g, k] for k in range(depth)], axis=1)
    held_ref[...] = own_ref[...]
    places, rows = placing_ref.shape
    n_section = places // slots
    target = target_ref[...]
    hits = lax.broadcasted_iota(jnp.int32, (n_section, rows), 0) == target
    hits = jnp.where(hits, 1.0, 0.0)
    earlier = lax.broadcasted_iota(jnp.int32, (rows, rows), 0) < lax.broadcasted_iota(
        jnp.int32, (rows, rows), 1
    )
    earlier = jnp.where(earlier, 1.0, 0.0).astype(jnp.bfloat16)
    before = jnp.dot(hits.astype(jnp.bfloat16), earlier, preferred_element_type=jnp.float32)
    slot = jnp.sum(before * hits, axis=0, keepdims=True).astype(jnp.int32)
    chip, chips = place_of_chip()
    apart = (target >> 1) - chip
    apart = jnp.where(apart < 0, apart + chips, apart)
    other_core = (target ^ lax.axis_index("section")) & 1
    position = (other_core * chips + apart) * slots + slot
    placing = lax.broadcasted_iota(jnp.int32, (places, rows), 0) == position
    placing_ref[...] = jnp.where(placing, 1.0, 0.0).astype(jnp.bfloat16)


def prepare(tiles, own, target, places, slots):
    many, depth, tile, _ = tiles.shape
    return pl.pallas_call(
        functools.partial(prepare_kernel, slots),
        out_shape=(
            jax.ShapeDtypeStruct((many, tile, depth * tile), jnp.bfloat16),
            jax.ShapeDtypeStruct(own.shape, jnp.bfloat16),
            jax.ShapeDtypeStruct((places, target.shape[1]), jnp.bfloat16),
        ),
        in_specs=[VMEM] * 3,
        out_specs=(VMEM,) * 3,
        compiler_params=LIMIT,
        cost_estimate=pl.CostEstimate(flops=0, bytes_accessed=2 * tiles.size * 2, transcendentals=0),
        name="prepare",
    )(tiles, own, target)


def partials_kernel(count, src_ref, wide_ref, *refs):
    block_refs, out_refs, held = refs[:count], refs[count:-1], refs[-1]
    depth = src_ref.shape[1]
    section, rep = lax.axis_index("section"), lax.axis_index("rep")
    chip, chips = place_of_chip()
    sources = [chip] + [source_of(route, chip) for route in routes(chips)]
    for i, ref in enumerate(block_refs):
        held[2 * sources[i % chips] + ((section + i // chips) & 1)] = ref[...]
    for j, out_ref in zip([0] + across(len(out_refs)), out_refs):
        g = rep ^ j
        right = jnp.concatenate([held[src_ref[g, k]] for k in range(depth)], axis=0)
        out_ref[...] = jnp.dot(wide_ref[g], right, preferred_element_type=jnp.float32).astype(
            jnp.bfloat16
        )


def partials(sources, wide, blocks):
    many = wide.shape[0]
    tile, width = blocks[0].shape
    return pl.pallas_call(
        functools.partial(partials_kernel, len(blocks)),
        out_shape=[jax.ShapeDtypeStruct((tile, width), jnp.bfloat16)] * many,
        in_specs=[VMEM] * (2 + len(blocks)),
        out_specs=[VMEM] * many,
        scratch_shapes=[pltpu.VMEM((len(blocks), tile, width), jnp.bfloat16)],
        compiler_params=LIMIT,
        name="partials",
    )(sources, wide, *blocks)


def swap(value, axis, j):
    return lax.ppermute(value, axis, [(i, i ^ j) for i in range(lax.axis_size(axis))])


def tree_sum(terms):
    while len(terms) > 1:
        terms = [terms[i] + terms[i + 1] for i in range(0, len(terms), 2)]
    return terms[0]


def dense_kernel(n_part, weight_ref, cot_ref, placing_ref, *refs):
    part_refs, (same_ref, kept_ref, sent_ref, term) = refs[:n_part], refs[n_part:]
    core = lax.axis_index("section") & 1
    agg_b = tree_sum([ref[...].astype(jnp.float32) for ref in part_refs]).astype(jnp.bfloat16)
    pre = jnp.dot(agg_b, weight_ref[...], preferred_element_type=jnp.float32)
    sig = jax.nn.sigmoid(pre)
    factor = sig * (1.0 + pre * (1.0 - sig))
    grad_pre = (cot_ref[...].astype(jnp.float32) * factor).astype(jnp.bfloat16)
    whole = lax.dot_general(
        agg_b, grad_pre, (((0,), (0,)), ((), ())), preferred_element_type=jnp.float32
    )
    term[...] = whole.reshape(term.shape)
    kept_ref[...] = term[core]
    output = (pre * sig).astype(jnp.bfloat16)
    packed = jnp.dot(placing_ref[...], output, preferred_element_type=jnp.float32)
    half = packed.shape[0] // 2
    same_ref[...] = packed[:half].astype(jnp.bfloat16)
    sent_ref[:half] = packed[half:].astype(jnp.bfloat16)
    sent_ref[half:] = term[1 - core].astype(jnp.bfloat16)


def dense(parts, weight, cotangent, placing):
    places, width = placing.shape[0], weight.shape[0]
    return pl.pallas_call(
        functools.partial(dense_kernel, len(parts)),
        out_shape=(
            jax.ShapeDtypeStruct((places // 2, width), jnp.bfloat16),
            jax.ShapeDtypeStruct((width // 2, width), jnp.float32),
            jax.ShapeDtypeStruct((places // 2 + width // 2, width), jnp.bfloat16),
        ),
        in_specs=[VMEM] * (3 + len(parts)),
        out_specs=(VMEM,) * 3,
        scratch_shapes=[pltpu.VMEM((2, width // 2, width), jnp.float32)],
        compiler_params=LIMIT,
        name="dense",
    )(weight, cotangent, placing, *parts)


def write_messages(slots, same_ref, came_ref, half, out_refs):
    for i, ref in enumerate(out_refs):
        start = (i + 1) * slots % same_ref.shape[0]
        ref[:slots] = same_ref[start : start + slots]
        ref[slots : 2 * slots] = came_ref[start : start + slots]
        ref[2 * slots :] = half


def sum_halves(half_ref, held, slots, own_ref, message_refs, core_along, n_rep):
    chip, chips = place_of_chip()
    core = lax.axis_index("section") & 1

    @pl.when(core == core_along)
    def _():
        held[chip] = own_ref[...]
        for i, ref in enumerate(message_refs[: chips - 1]):
            held[(chip + chips - i - 1) % chips] = ref[2 * slots :]
        total = tree_sum([held[c].astype(jnp.float32) for c in range(chips)])
        half_ref[...] = total.astype(jnp.bfloat16)

    @pl.when(core != core_along)
    def _():
        rep = lax.axis_index("rep")
        held[rep] = own_ref[...]
        for route, ref in zip(rep_routes(n_rep, 1 + core_along), message_refs):
            held[source_of(route, rep)] = ref[2 * slots :]
        total = tree_sum([held[r].astype(jnp.float32) for r in range(n_rep)])
        half_ref[...] = total.astype(jnp.bfloat16)


def first_kernel(slots, same_ref, kept_ref, came_ref, half_ref, *out_refs):
    rows = kept_ref.shape[0]
    half = kept_ref[...] + came_ref[came_ref.shape[0] - rows :].astype(jnp.float32)
    half_ref[...] = half.astype(jnp.bfloat16)
    write_messages(slots, same_ref, came_ref, half_ref[...], out_refs)


def second_kernel(slots, n_rep, many, same_ref, came_ref, own_ref, *refs):
    message_refs, half_ref, out_refs, held = refs[:many], refs[many], refs[many + 1 : -1], refs[-1]
    sum_halves(half_ref, held, slots, own_ref, message_refs, 0, n_rep)
    write_messages(slots, same_ref, came_ref, half_ref[...], out_refs)


def third_kernel(slots, n_rep, own_ref, *refs):
    sum_halves(refs[-2], refs[-1], slots, own_ref, refs[:-2], 1, n_rep)


def call_halves(kernel, name, operands, half, slots, many, held=()):
    shapes = [jax.ShapeDtypeStruct(half, jnp.bfloat16)]
    shapes += [jax.ShapeDtypeStruct((2 * slots + half[0], half[1]), jnp.bfloat16)] * many
    return pl.pallas_call(
        kernel,
        out_shape=shapes,
        in_specs=[VMEM] * len(operands),
        out_specs=[VMEM] * len(shapes),
        scratch_shapes=[pltpu.VMEM(shape, jnp.bfloat16) for shape in held],
        compiler_params=LIMIT,
        name=name,
    )(*operands)


def store_kernel(core, slots, same_ref, came_ref, *refs):
    message_refs, (out_ref, rows, sem) = refs[:-3], refs[-3:]
    section = lax.axis_index("section")
    chip, chips = place_of_chip()

    @pl.when(section & 1 == core)
    def _():
        rows[section] = same_ref[:slots]
        rows[section ^ 1] = came_ref[:slots]
        for i, ref in enumerate(message_refs[: chips - 1]):
            source = 2 * ((chip + chips - i - 1) % chips)
            rows[source + core] = ref[:slots]
            rows[source + 1 - core] = ref[slots : 2 * slots]
        copy = pltpu.make_async_copy(rows, out_ref, sem)
        copy.start()
        copy.wait()


def store(core, same, came, messages, n_section, slots, base=None):
    shape = (n_section, slots, same.shape[1])
    operands = [same, came, *messages]
    kernel, first, specs = functools.partial(store_kernel, core, slots), [], []
    if base is not None:
        kernel, first, specs = lambda _, *refs: store_kernel(core, slots, *refs), [base], [HBM]
    return pl.pallas_call(
        kernel,
        out_shape=jax.ShapeDtypeStruct(shape, jnp.bfloat16),
        in_specs=specs + [VMEM] * len(operands),
        out_specs=HBM,
        scratch_shapes=[pltpu.VMEM(shape, jnp.bfloat16), pltpu.SemaphoreType.DMA],
        input_output_aliases={0: 0} if first else {},
        compiler_params=LIMIT,
        name="store",
    )(*first, *operands)


def finish_kernel(own_ref, came_ref, out_ref):
    core = lax.axis_index("section") & 1
    out_ref[core] = own_ref[...].astype(jnp.float32)
    out_ref[1 - core] = came_ref[...].astype(jnp.float32)


def finish(own, came):
    return pl.pallas_call(
        finish_kernel,
        out_shape=jax.ShapeDtypeStruct((2,) + own.shape, jnp.float32),
        in_specs=[VMEM] * 2,
        out_specs=VMEM,
        compiler_params=LIMIT,
        name="finish",
    )(own, came)


def exchange(value, core_along, shift):
    n_section, n_rep = lax.axis_size("section"), lax.axis_size("rep")
    over = rep_routes(n_rep, 1 + core_along)[(shift - 1) % (n_rep - 1)]
    pairs = []
    for s in range(n_section):
        along = s & 1 == core_along
        to = (s + 2 * shift) % n_section if along else s
        for r in range(n_rep):
            pairs.append((s * n_rep + r, to * n_rep + (r if along else over[r])))
    return lax.ppermute(value, ("section", "rep"), pairs)


def routes(chips):
    if chips == 4:
        return [(1, 3, 0, 2), (3, 2, 1, 0), (2, 0, 3, 1)]
    return [tuple((c + i) % chips for c in range(chips)) for i in range(1, chips)]


def rep_routes(n, phase):
    if n == 4 and phase == 2:
        return [(1, 0, 3, 2), (2, 3, 1, 0), (3, 2, 0, 1)]
    return [tuple(r ^ j for r in range(n)) for j in across(n)]


def source_of(route, place):
    source = jnp.int32(0)
    for c, to in enumerate(route):
        source = jnp.where(place == to, c, source)
    return source


def send_along(value, axis, route):
    pairs = [(s, 2 * route[s // 2] + s % 2) for s in range(lax.axis_size(axis))]
    return lax.ppermute(value, axis, pairs)


def gather_blocks(features, axis, ready):
    chips = lax.axis_size(axis) // 2
    near = [features] + [send_along(features, axis, route) for route in routes(chips)]
    beside = swap(features, axis, 1)
    near[1], ready = lax.optimization_barrier((near[1], ready))
    return near, [beside] + [swap(block, axis, 1) for block in near[1:]], ready


def per_device(features, adj_tiles, adj_src, cotangent, weight, destination):
    n_section, n_rep = lax.axis_size("section"), lax.axis_size("rep")
    rows_here, width = features.shape
    tile = adj_tiles.shape[3]
    slots = max(2, 2 * rows_here // n_section)
    target = destination.reshape(1, rows_here)
    wide, own, placing = prepare(adj_tiles[:, 0], features, target, n_section * slots, slots)
    near, beside, (wide, own, placing) = gather_blocks(features, "section", (wide, own, placing))
    parts = list(partials(adj_src[:, 0], wide, [own] + near[1:] + beside))
    others = across(n_rep)
    parts = parts[:1] + [swap(part, "rep", j) for part, j in zip(parts[1:], others)]
    same, kept, sent = dense(parts, weight, cotangent, placing)
    came = swap(sent, "section", 1)
    chips = n_section // 2
    steps = across(max(n_rep, chips))
    half_shape = (width // 2, width)
    held = [(max(n_rep, chips),) + half_shape]
    half, *first = call_halves(
        functools.partial(first_kernel, slots), "first", [same, kept, came], half_shape, slots, len(steps)
    )
    first = [exchange(m, 0, i + 1) for i, m in enumerate(first)]
    relaid = store(0, same, came, first, n_section, slots)
    half, *second = call_halves(
        functools.partial(second_kernel, slots, n_rep, len(steps)),
        "second",
        [same, came, half, *first],
        half_shape,
        slots,
        len(steps),
        held,
    )
    second = [exchange(m, 1, i + 1) for i, m in enumerate(second)]
    (half,) = call_halves(
        functools.partial(third_kernel, slots, n_rep), "third", [half, *second], half_shape, slots, 0, held
    )
    relaid = store(1, same, came, second, n_section, slots, relaid)
    half, relaid = lax.optimization_barrier((half, relaid))
    weight_grad = finish(half, swap(half, "section", 1))
    return (relaid.reshape(1, 1, n_section, slots, width), weight_grad.reshape(width, width))


def solution(mesh):
    placed = (
        P(("section", "rep"), None),
        P("section", "rep", None, None, None),
        P("section", "rep", None),
        P(("section", "rep"), None),
        P(),
        P(("section", "rep"), None),
    )
    return jax.shard_map(
        per_device,
        mesh=mesh,
        in_specs=placed,
        out_specs=(P("section", "rep", None, None, None), P()),
        check_vma=False,
    )
```

```python
import functools

import jax
import jax.numpy as jnp
from jax import lax
from jax.experimental import pallas as pl
from jax.experimental.pallas import tpu as pltpu
from jax.sharding import PartitionSpec as P

VMEM = pl.BlockSpec(memory_space=pltpu.VMEM)
LIMIT = pltpu.CompilerParams(vmem_limit_bytes=32 * 1024 * 1024)
HBM = pl.BlockSpec(memory_space=pltpu.HBM)


def across(n):
    return list(range(n - 1, 0, -1))


def place_of_chip():
    return lax.axis_index("section") >> 1, lax.axis_size("section") // 2


def prepare_kernel(slots, tiles_ref, own_ref, target_ref, wide_ref, held_ref, placing_ref):
    many, depth = tiles_ref.shape[:2]
    for g in range(many):
        wide_ref[g] = jnp.concatenate([tiles_ref[g, k] for k in range(depth)], axis=1)
    held_ref[...] = own_ref[...]
    places, rows = placing_ref.shape
    n_section = places // slots
    target = target_ref[...]
    hits = lax.broadcasted_iota(jnp.int32, (n_section, rows), 0) == target
    hits = jnp.where(hits, 1.0, 0.0)
    earlier = lax.broadcasted_iota(jnp.int32, (rows, rows), 0) < lax.broadcasted_iota(
        jnp.int32, (rows, rows), 1
    )
    earlier = jnp.where(earlier, 1.0, 0.0).astype(jnp.bfloat16)
    before = jnp.dot(hits.astype(jnp.bfloat16), earlier, preferred_element_type=jnp.float32)
    slot = jnp.sum(before * hits, axis=0, keepdims=True).astype(jnp.int32)
    chip, chips = place_of_chip()
    apart = (target >> 1) - chip
    apart = jnp.where(apart < 0, apart + chips, apart)
    other_core = (target ^ lax.axis_index("section")) & 1
    position = (other_core * chips + apart) * slots + slot
    placing = lax.broadcasted_iota(jnp.int32, (places, rows), 0) == position
    placing_ref[...] = jnp.where(placing, 1.0, 0.0).astype(jnp.bfloat16)


def prepare(tiles, own, target, places, slots):
    many, depth, tile, _ = tiles.shape
    return pl.pallas_call(
        functools.partial(prepare_kernel, slots),
        out_shape=(
            jax.ShapeDtypeStruct((many, tile, depth * tile), jnp.bfloat16),
            jax.ShapeDtypeStruct(own.shape, jnp.bfloat16),
            jax.ShapeDtypeStruct((places, target.shape[1]), jnp.bfloat16),
        ),
        in_specs=[VMEM] * 3,
        out_specs=(VMEM,) * 3,
        compiler_params=LIMIT,
        cost_estimate=pl.CostEstimate(flops=0, bytes_accessed=2 * tiles.size * 2, transcendentals=0),
        name="prepare",
    )(tiles, own, target)


def partials_kernel(count, src_ref, wide_ref, *refs):
    block_refs, out_refs, held = refs[:count], refs[count:-1], refs[-1]
    depth = src_ref.shape[1]
    section, rep = lax.axis_index("section"), lax.axis_index("rep")
    chip, chips = place_of_chip()
    sources = [chip] + [source_of(route, chip) for route in routes(chips)]
    for i, ref in enumerate(block_refs):
        held[2 * sources[i % chips] + ((section + i // chips) & 1)] = ref[...]
    for j, out_ref in zip([0] + across(len(out_refs)), out_refs):
        g = rep ^ j
        right = jnp.concatenate([held[src_ref[g, k]] for k in range(depth)], axis=0)
        out_ref[...] = jnp.dot(wide_ref[g], right, preferred_element_type=jnp.float32).astype(
            jnp.bfloat16
        )


def partials(sources, wide, blocks):
    many = wide.shape[0]
    tile, width = blocks[0].shape
    return pl.pallas_call(
        functools.partial(partials_kernel, len(blocks)),
        out_shape=[jax.ShapeDtypeStruct((tile, width), jnp.bfloat16)] * many,
        in_specs=[VMEM] * (2 + len(blocks)),
        out_specs=[VMEM] * many,
        scratch_shapes=[pltpu.VMEM((len(blocks), tile, width), jnp.bfloat16)],
        compiler_params=LIMIT,
        name="partials",
    )(sources, wide, *blocks)


def swap(value, axis, j):
    return lax.ppermute(value, axis, [(i, i ^ j) for i in range(lax.axis_size(axis))])


def tree_sum(terms):
    while len(terms) > 1:
        terms = [terms[i] + terms[i + 1] for i in range(0, len(terms), 2)]
    return terms[0]


def dense_kernel(n_part, weight_ref, cot_ref, placing_ref, *refs):
    part_refs, (same_ref, kept_ref, sent_ref, term) = refs[:n_part], refs[n_part:]
    core = lax.axis_index("section") & 1
    agg_b = tree_sum([ref[...].astype(jnp.float32) for ref in part_refs]).astype(jnp.bfloat16)
    pre = jnp.dot(agg_b, weight_ref[...], preferred_element_type=jnp.float32)
    sig = jax.nn.sigmoid(pre)
    factor = sig * (1.0 + pre * (1.0 - sig))
    grad_pre = (cot_ref[...].astype(jnp.float32) * factor).astype(jnp.bfloat16)
    whole = lax.dot_general(
        agg_b, grad_pre, (((0,), (0,)), ((), ())), preferred_element_type=jnp.float32
    )
    term[...] = whole.reshape(term.shape)
    kept_ref[...] = term[core]
    output = (pre * sig).astype(jnp.bfloat16)
    packed = jnp.dot(placing_ref[...], output, preferred_element_type=jnp.float32)
    half = packed.shape[0] // 2
    same_ref[...] = packed[:half].astype(jnp.bfloat16)
    sent_ref[:half] = packed[half:].astype(jnp.bfloat16)
    sent_ref[half:] = term[1 - core].astype(jnp.bfloat16)


def dense(parts, weight, cotangent, placing):
    places, width = placing.shape[0], weight.shape[0]
    return pl.pallas_call(
        functools.partial(dense_kernel, len(parts)),
        out_shape=(
            jax.ShapeDtypeStruct((places // 2, width), jnp.bfloat16),
            jax.ShapeDtypeStruct((width // 2, width), jnp.float32),
            jax.ShapeDtypeStruct((places // 2 + width // 2, width), jnp.bfloat16),
        ),
        in_specs=[VMEM] * (3 + len(parts)),
        out_specs=(VMEM,) * 3,
        scratch_shapes=[pltpu.VMEM((2, width // 2, width), jnp.float32)],
        compiler_params=LIMIT,
        name="dense",
    )(weight, cotangent, placing, *parts)


def write_messages(slots, same_ref, came_ref, half, out_refs):
    for i, ref in enumerate(out_refs):
        start = (i + 1) * slots % same_ref.shape[0]
        ref[:slots] = same_ref[start : start + slots]
        ref[slots : 2 * slots] = came_ref[start : start + slots]
        ref[2 * slots :] = half


def sum_halves(half_ref, held, slots, own_ref, message_refs, core_along, n_rep):
    chip, chips = place_of_chip()
    core = lax.axis_index("section") & 1

    @pl.when(core == core_along)
    def _():
        held[chip] = own_ref[...]
        for i, ref in enumerate(message_refs[: chips - 1]):
            held[(chip + chips - i - 1) % chips] = ref[2 * slots :]
        total = tree_sum([held[c].astype(jnp.float32) for c in range(chips)])
        half_ref[...] = total.astype(jnp.bfloat16)

    @pl.when(core != core_along)
    def _():
        rep = lax.axis_index("rep")
        held[rep] = own_ref[...]
        for route, ref in zip(rep_routes(n_rep), message_refs):
            held[source_of(route, rep)] = ref[2 * slots :]
        total = tree_sum([held[r].astype(jnp.float32) for r in range(n_rep)])
        half_ref[...] = total.astype(jnp.bfloat16)


def first_kernel(slots, same_ref, kept_ref, came_ref, half_ref, *out_refs):
    rows = kept_ref.shape[0]
    half = kept_ref[...] + came_ref[came_ref.shape[0] - rows :].astype(jnp.float32)
    half_ref[...] = half.astype(jnp.bfloat16)
    write_messages(slots, same_ref, came_ref, half_ref[...], out_refs)


def second_kernel(slots, n_rep, many, same_ref, came_ref, own_ref, *refs):
    message_refs, half_ref, out_refs, held = refs[:many], refs[many], refs[many + 1 : -1], refs[-1]
    sum_halves(half_ref, held, slots, own_ref, message_refs, 0, n_rep)
    write_messages(slots, same_ref, came_ref, half_ref[...], out_refs)


def third_kernel(slots, n_rep, own_ref, *refs):
    sum_halves(refs[-2], refs[-1], slots, own_ref, refs[:-2], 1, n_rep)


def call_halves(kernel, name, operands, half, slots, many, held=()):
    shapes = [jax.ShapeDtypeStruct(half, jnp.bfloat16)]
    shapes += [jax.ShapeDtypeStruct((2 * slots + half[0], half[1]), jnp.bfloat16)] * many
    return pl.pallas_call(
        kernel,
        out_shape=shapes,
        in_specs=[VMEM] * len(operands),
        out_specs=[VMEM] * len(shapes),
        scratch_shapes=[pltpu.VMEM(shape, jnp.bfloat16) for shape in held],
        compiler_params=LIMIT,
        name=name,
    )(*operands)


def store_kernel(core, slots, same_ref, came_ref, *refs):
    message_refs, (out_ref, rows, sem) = refs[:-3], refs[-3:]
    section = lax.axis_index("section")
    chip, chips = place_of_chip()

    @pl.when(section & 1 == core)
    def _():
        rows[section] = same_ref[:slots]
        rows[section ^ 1] = came_ref[:slots]
        for i, ref in enumerate(message_refs[: chips - 1]):
            source = 2 * ((chip + chips - i - 1) % chips)
            rows[source + core] = ref[:slots]
            rows[source + 1 - core] = ref[slots : 2 * slots]
        copy = pltpu.make_async_copy(rows, out_ref, sem)
        copy.start()
        copy.wait()


def store(core, same, came, messages, n_section, slots, base=None):
    shape = (n_section, slots, same.shape[1])
    operands = [same, came, *messages]
    kernel, first, specs = functools.partial(store_kernel, core, slots), [], []
    if base is not None:
        kernel, first, specs = lambda _, *refs: store_kernel(core, slots, *refs), [base], [HBM]
    return pl.pallas_call(
        kernel,
        out_shape=jax.ShapeDtypeStruct(shape, jnp.bfloat16),
        in_specs=specs + [VMEM] * len(operands),
        out_specs=HBM,
        scratch_shapes=[pltpu.VMEM(shape, jnp.bfloat16), pltpu.SemaphoreType.DMA],
        input_output_aliases={0: 0} if first else {},
        compiler_params=LIMIT,
        name="store",
    )(*first, *operands)


def finish_kernel(own_ref, came_ref, out_ref):
    core = lax.axis_index("section") & 1
    out_ref[core] = own_ref[...].astype(jnp.float32)
    out_ref[1 - core] = came_ref[...].astype(jnp.float32)


def finish(own, came):
    return pl.pallas_call(
        finish_kernel,
        out_shape=jax.ShapeDtypeStruct((2,) + own.shape, jnp.float32),
        in_specs=[VMEM] * 2,
        out_specs=VMEM,
        compiler_params=LIMIT,
        name="finish",
    )(own, came)


def exchange(value, core_along, shift):
    n_section, n_rep = lax.axis_size("section"), lax.axis_size("rep")
    over = rep_routes(n_rep)[(shift - 1) % (n_rep - 1)]
    pairs = []
    for s in range(n_section):
        along = s & 1 == core_along
        to = (s + 2 * shift) % n_section if along else s
        for r in range(n_rep):
            pairs.append((s * n_rep + r, to * n_rep + (r if along else over[r])))
    return lax.ppermute(value, ("section", "rep"), pairs)


def routes(chips):
    if chips == 4:
        return [(1, 3, 0, 2), (3, 2, 1, 0), (2, 0, 3, 1)]
    return [tuple((c + i) % chips for c in range(chips)) for i in range(1, chips)]


def rep_routes(n):
    return [tuple(r ^ j for r in range(n)) for j in across(n)]


def source_of(route, place):
    source = jnp.int32(0)
    for c, to in enumerate(route):
        source = jnp.where(place == to, c, source)
    return source


def send_along(value, axis, route):
    pairs = [(s, 2 * route[s // 2] + s % 2) for s in range(lax.axis_size(axis))]
    return lax.ppermute(value, axis, pairs)


def gather_blocks(features, axis, ready):
    chips = lax.axis_size(axis) // 2
    near = [features] + [send_along(features, axis, route) for route in routes(chips)]
    beside = swap(features, axis, 1)
    near[1], ready = lax.optimization_barrier((near[1], ready))
    return near, [beside] + [swap(block, axis, 1) for block in near[1:]], ready


def per_device(features, adj_tiles, adj_src, cotangent, weight, destination):
    n_section, n_rep = lax.axis_size("section"), lax.axis_size("rep")
    rows_here, width = features.shape
    tile = adj_tiles.shape[3]
    slots = max(2, 2 * rows_here // n_section)
    target = destination.reshape(1, rows_here)
    wide, own, placing = prepare(adj_tiles[:, 0], features, target, n_section * slots, slots)
    near, beside, (wide, own, placing) = gather_blocks(features, "section", (wide, own, placing))
    parts = list(partials(adj_src[:, 0], wide, [own] + near[1:] + beside))
    others = across(n_rep)
    parts = parts[:1] + [swap(part, "rep", j) for part, j in zip(parts[1:], others)]
    same, kept, sent = dense(parts, weight, cotangent, placing)
    came = swap(sent, "section", 1)
    chips = n_section // 2
    steps = across(max(n_rep, chips))
    half_shape = (width // 2, width)
    held = [(max(n_rep, chips),) + half_shape]
    half, *first = call_halves(
        functools.partial(first_kernel, slots), "first", [same, kept, came], half_shape, slots, len(steps)
    )
    first = [exchange(m, 0, i + 1) for i, m in enumerate(first)]
    relaid = store(0, same, came, first, n_section, slots)
    half, *second = call_halves(
        functools.partial(second_kernel, slots, n_rep, len(steps)),
        "second",
        [same, came, half, *first],
        half_shape,
        slots,
        len(steps),
        held,
    )
    second = [exchange(m, 1, i + 1) for i, m in enumerate(second)]
    (half,) = call_halves(
        functools.partial(third_kernel, slots, n_rep), "third", [half, *second], half_shape, slots, 0, held
    )
    relaid = store(1, same, came, second, n_section, slots, relaid)
    half, relaid = lax.optimization_barrier((half, relaid))
    weight_grad = finish(half, swap(half, "section", 1))
    return (relaid.reshape(1, 1, n_section, slots, width), weight_grad.reshape(width, width))


def solution(mesh):
    placed = (
        P(("section", "rep"), None),
        P("section", "rep", None, None, None),
        P("section", "rep", None),
        P(("section", "rep"), None),
        P(),
        P(("section", "rep"), None),
    )
    return jax.shard_map(
        per_device,
        mesh=mesh,
        in_specs=placed,
        out_specs=(P("section", "rep", None, None, None), P()),
        check_vma=False,
    )
```

```python
import functools

import jax
import jax.numpy as jnp
from jax import lax
from jax.experimental import pallas as pl
from jax.experimental.pallas import tpu as pltpu
from jax.sharding import PartitionSpec as P

VMEM = pl.BlockSpec(memory_space=pltpu.VMEM)
LIMIT = pltpu.CompilerParams(vmem_limit_bytes=32 * 1024 * 1024)
HBM = pl.BlockSpec(memory_space=pltpu.HBM)


def across(n):
    return list(range(n - 1, 0, -1))


def place_of_chip():
    return lax.axis_index("section") >> 1, lax.axis_size("section") // 2


def prepare_kernel(slots, tiles_ref, own_ref, target_ref, wide_ref, held_ref, placing_ref):
    many, depth = tiles_ref.shape[:2]
    for g in range(many):
        wide_ref[g] = jnp.concatenate([tiles_ref[g, k] for k in range(depth)], axis=1)
    held_ref[...] = own_ref[...]
    places, rows = placing_ref.shape
    n_section = places // slots
    target = target_ref[...]
    hits = lax.broadcasted_iota(jnp.int32, (n_section, rows), 0) == target
    hits = jnp.where(hits, 1.0, 0.0)
    earlier = lax.broadcasted_iota(jnp.int32, (rows, rows), 0) < lax.broadcasted_iota(
        jnp.int32, (rows, rows), 1
    )
    earlier = jnp.where(earlier, 1.0, 0.0).astype(jnp.bfloat16)
    before = jnp.dot(hits.astype(jnp.bfloat16), earlier, preferred_element_type=jnp.float32)
    slot = jnp.sum(before * hits, axis=0, keepdims=True).astype(jnp.int32)
    chip, chips = place_of_chip()
    apart = (target >> 1) - chip
    apart = jnp.where(apart < 0, apart + chips, apart)
    other_core = (target ^ lax.axis_index("section")) & 1
    position = (other_core * chips + apart) * slots + slot
    placing = lax.broadcasted_iota(jnp.int32, (places, rows), 0) == position
    placing_ref[...] = jnp.where(placing, 1.0, 0.0).astype(jnp.bfloat16)


def prepare(tiles, own, target, places, slots):
    many, depth, tile, _ = tiles.shape
    return pl.pallas_call(
        functools.partial(prepare_kernel, slots),
        out_shape=(
            jax.ShapeDtypeStruct((many, tile, depth * tile), jnp.bfloat16),
            jax.ShapeDtypeStruct(own.shape, jnp.bfloat16),
            jax.ShapeDtypeStruct((places, target.shape[1]), jnp.bfloat16),
        ),
        in_specs=[VMEM] * 3,
        out_specs=(VMEM,) * 3,
        compiler_params=LIMIT,
        cost_estimate=pl.CostEstimate(flops=0, bytes_accessed=2 * tiles.size * 2, transcendentals=0),
        name="prepare",
    )(tiles, own, target)


def partials_kernel(count, src_ref, wide_ref, *refs):
    block_refs, out_refs, held = refs[:count], refs[count:-1], refs[-1]
    depth = src_ref.shape[1]
    section, rep = lax.axis_index("section"), lax.axis_index("rep")
    chip, chips = place_of_chip()
    sources = [chip] + [source_of(route, chip) for route in routes(chips)]
    for i, ref in enumerate(block_refs):
        held[2 * sources[i % chips] + ((section + i // chips) & 1)] = ref[...]
    for j, out_ref in zip([0] + across(len(out_refs)), out_refs):
        g = rep ^ j
        right = jnp.concatenate([held[src_ref[g, k]] for k in range(depth)], axis=0)
        out_ref[...] = jnp.dot(wide_ref[g], right, preferred_element_type=jnp.float32).astype(
            jnp.bfloat16
        )


def partials(sources, wide, blocks):
    many = wide.shape[0]
    tile, width = blocks[0].shape
    return pl.pallas_call(
        functools.partial(partials_kernel, len(blocks)),
        out_shape=[jax.ShapeDtypeStruct((tile, width), jnp.bfloat16)] * many,
        in_specs=[VMEM] * (2 + len(blocks)),
        out_specs=[VMEM] * many,
        scratch_shapes=[pltpu.VMEM((len(blocks), tile, width), jnp.bfloat16)],
        compiler_params=LIMIT,
        name="partials",
    )(sources, wide, *blocks)


def swap(value, axis, j):
    return lax.ppermute(value, axis, [(i, i ^ j) for i in range(lax.axis_size(axis))])


def tree_sum(terms):
    while len(terms) > 1:
        terms = [terms[i] + terms[i + 1] for i in range(0, len(terms), 2)]
    return terms[0]


def parts_of(width, slots):
    low = (width - 2 * slots) // 2 // 16 * 16
    return low, width - low


def dense_kernel(n_part, slots, weight_ref, cot_ref, placing_ref, *refs):
    part_refs, (same_ref, term_ref, sent_ref) = refs[:n_part], refs[n_part:]
    core = lax.axis_index("section") & 1
    agg_b = tree_sum([ref[...].astype(jnp.float32) for ref in part_refs]).astype(jnp.bfloat16)
    pre = jnp.dot(agg_b, weight_ref[...], preferred_element_type=jnp.float32)
    sig = jax.nn.sigmoid(pre)
    factor = sig * (1.0 + pre * (1.0 - sig))
    grad_pre = (cot_ref[...].astype(jnp.float32) * factor).astype(jnp.bfloat16)
    term = lax.dot_general(
        agg_b, grad_pre, (((0,), (0,)), ((), ())), preferred_element_type=jnp.float32
    )
    term_ref[...] = term
    output = (pre * sig).astype(jnp.bfloat16)
    packed = jnp.dot(placing_ref[...], output, preferred_element_type=jnp.float32)
    half = packed.shape[0] // 2
    same_ref[...] = packed[:half].astype(jnp.bfloat16)
    sent_ref[:half] = packed[half:].astype(jnp.bfloat16)
    low, high = parts_of(term.shape[0], slots)

    @pl.when(core == 0)
    def _():
        sent_ref[half:] = term[low:].astype(jnp.bfloat16)

    @pl.when(core == 1)
    def _():
        sent_ref[half : half + low] = term[:low].astype(jnp.bfloat16)


def dense(parts, weight, cotangent, placing, slots):
    places, width = placing.shape[0], weight.shape[0]
    return pl.pallas_call(
        functools.partial(dense_kernel, len(parts), slots),
        out_shape=(
            jax.ShapeDtypeStruct((places // 2, width), jnp.bfloat16),
            jax.ShapeDtypeStruct((width, width), jnp.float32),
            jax.ShapeDtypeStruct((places // 2 + parts_of(width, slots)[1], width), jnp.bfloat16),
        ),
        in_specs=[VMEM] * (3 + len(parts)),
        out_specs=(VMEM,) * 3,
        compiler_params=LIMIT,
        name="dense",
    )(weight, cotangent, placing, *parts)


def write_messages(core_along, slots, rows, same_ref, came_ref, half_ref, out_refs):
    core = lax.axis_index("section") & 1

    @pl.when(core == core_along)
    def _():
        for i, ref in enumerate(out_refs):
            start = (i + 1) * slots % same_ref.shape[0]
            ref[:slots] = same_ref[start : start + slots]
            ref[slots : 2 * slots] = came_ref[start : start + slots]
            ref[2 * slots : 2 * slots + rows[core_along]] = half_ref[: rows[core_along]]

    @pl.when(core != core_along)
    def _():
        for ref in out_refs:
            ref[: rows[1 - core_along]] = half_ref[: rows[1 - core_along]]


def sum_parts(core_along, slots, rows, half_ref, held, own_ref, message_refs, n_rep):
    chip, chips = place_of_chip()
    core = lax.axis_index("section") & 1

    @pl.when(core == core_along)
    def _():
        many = rows[core_along]
        held[chip, :many] = own_ref[:many]
        for i, ref in enumerate(message_refs[: chips - 1]):
            held[(chip + chips - i - 1) % chips, :many] = ref[2 * slots : 2 * slots + many]
        total = tree_sum([held[c, :many].astype(jnp.float32) for c in range(chips)])
        half_ref[:many] = total.astype(jnp.bfloat16)

    @pl.when(core != core_along)
    def _():
        many = rows[1 - core_along]
        by_xor = [ref[:many].astype(jnp.float32) for ref in [own_ref] + list(message_refs[::-1])]
        half_ref[:many] = tree_sum(by_xor[:n_rep]).astype(jnp.bfloat16)


def first_kernel(slots, rows, same_ref, term_ref, came_ref, half_ref, *out_refs):
    core = lax.axis_index("section") & 1
    start = same_ref.shape[0]

    @pl.when(core == 0)
    def _():
        other = came_ref[start : start + rows[0]].astype(jnp.float32)
        half_ref[: rows[0]] = (term_ref[: rows[0]] + other).astype(jnp.bfloat16)

    @pl.when(core == 1)
    def _():
        other = came_ref[start:].astype(jnp.float32)
        half_ref[...] = (term_ref[rows[0] :] + other).astype(jnp.bfloat16)

    write_messages(0, slots, rows, same_ref, came_ref, half_ref, out_refs)


def second_kernel(slots, rows, n_rep, many, same_ref, came_ref, own_ref, *refs):
    message_refs, half_ref, out_refs, held = refs[:many], refs[many], refs[many + 1 : -1], refs[-1]
    sum_parts(0, slots, rows, half_ref, held, own_ref, message_refs, n_rep)
    write_messages(1, slots, rows, same_ref, came_ref, half_ref, out_refs)


def third_kernel(slots, rows, n_rep, own_ref, *refs):
    sum_parts(1, slots, rows, refs[-2], refs[-1], own_ref, refs[:-2], n_rep)


def call_parts(kernel, name, operands, half, message, many, held=()):
    shapes = [jax.ShapeDtypeStruct(half, jnp.bfloat16)]
    shapes += [jax.ShapeDtypeStruct(message, jnp.bfloat16)] * many
    return pl.pallas_call(
        kernel,
        out_shape=shapes,
        in_specs=[VMEM] * len(operands),
        out_specs=[VMEM] * len(shapes),
        scratch_shapes=[pltpu.VMEM(shape, jnp.bfloat16) for shape in held],
        compiler_params=LIMIT,
        name=name,
    )(*operands)


def store_kernel(core, slots, same_ref, came_ref, *refs):
    message_refs, (out_ref, rows, sem) = refs[:-3], refs[-3:]
    section = lax.axis_index("section")
    chip, chips = place_of_chip()

    @pl.when(section & 1 == core)
    def _():
        rows[section] = same_ref[:slots]
        rows[section ^ 1] = came_ref[:slots]
        for i, ref in enumerate(message_refs[: chips - 1]):
            source = 2 * ((chip + chips - i - 1) % chips)
            rows[source + core] = ref[:slots]
            rows[source + 1 - core] = ref[slots : 2 * slots]
        copy = pltpu.make_async_copy(rows, out_ref, sem)
        copy.start()
        copy.wait()


def store(core, same, came, messages, n_section, slots, base=None):
    shape = (n_section, slots, same.shape[1])
    operands = [same, came, *messages]
    kernel, first, specs = functools.partial(store_kernel, core, slots), [], []
    if base is not None:
        kernel, first, specs = lambda _, *refs: store_kernel(core, slots, *refs), [base], [HBM]
    return pl.pallas_call(
        kernel,
        out_shape=jax.ShapeDtypeStruct(shape, jnp.bfloat16),
        in_specs=specs + [VMEM] * len(operands),
        out_specs=HBM,
        scratch_shapes=[pltpu.VMEM(shape, jnp.bfloat16), pltpu.SemaphoreType.DMA],
        input_output_aliases={0: 0} if first else {},
        compiler_params=LIMIT,
        name="store",
    )(*first, *operands)


def finish_kernel(rows, own_ref, came_ref, out_ref):
    core = lax.axis_index("section") & 1
    low, high = rows

    @pl.when(core == 0)
    def _():
        out_ref[:low] = own_ref[:low].astype(jnp.float32)
        out_ref[low:] = came_ref[...].astype(jnp.float32)

    @pl.when(core == 1)
    def _():
        out_ref[:low] = came_ref[:low].astype(jnp.float32)
        out_ref[low:] = own_ref[...].astype(jnp.float32)


def finish(own, came, rows):
    width = own.shape[1]
    return pl.pallas_call(
        functools.partial(finish_kernel, rows),
        out_shape=jax.ShapeDtypeStruct((width, width), jnp.float32),
        in_specs=[VMEM] * 2,
        out_specs=VMEM,
        compiler_params=LIMIT,
        name="finish",
    )(own, came)


def exchange(value, core_along, shift, j):
    n_section, n_rep = lax.axis_size("section"), lax.axis_size("rep")
    pairs = []
    for s in range(n_section):
        along = s & 1 == core_along
        to = (s + 2 * shift) % n_section if along else s
        for r in range(n_rep):
            pairs.append((s * n_rep + r, to * n_rep + (r if along else r ^ j % n_rep)))
    return lax.ppermute(value, ("section", "rep"), pairs)


def routes(chips):
    if chips == 4:
        return [(1, 3, 0, 2), (3, 2, 1, 0), (2, 0, 3, 1)]
    return [tuple((c + i) % chips for c in range(chips)) for i in range(1, chips)]


def source_of(route, place):
    source = jnp.int32(0)
    for c, to in enumerate(route):
        source = jnp.where(place == to, c, source)
    return source


def send_along(value, axis, route):
    pairs = [(s, 2 * route[s // 2] + s % 2) for s in range(lax.axis_size(axis))]
    return lax.ppermute(value, axis, pairs)


def gather_blocks(features, axis, ready):
    chips = lax.axis_size(axis) // 2
    near = [features] + [send_along(features, axis, route) for route in routes(chips)]
    beside = swap(features, axis, 1)
    near[1], ready = lax.optimization_barrier((near[1], ready))
    return near, [beside] + [swap(block, axis, 1) for block in near[1:]], ready


def per_device(features, adj_tiles, adj_src, cotangent, weight, destination):
    n_section, n_rep = lax.axis_size("section"), lax.axis_size("rep")
    rows_here, width = features.shape
    tile = adj_tiles.shape[3]
    slots = max(2, 2 * rows_here // n_section)
    target = destination.reshape(1, rows_here)
    wide, own, placing = prepare(adj_tiles[:, 0], features, target, n_section * slots, slots)
    near, beside, (wide, own, placing) = gather_blocks(features, "section", (wide, own, placing))
    parts = list(partials(adj_src[:, 0], wide, [own] + near[1:] + beside))
    others = across(n_rep)
    parts = parts[:1] + [swap(part, "rep", j) for part, j in zip(parts[1:], others)]
    same, term, sent = dense(parts, weight, cotangent, placing, slots)
    came = swap(sent, "section", 1)
    chips = n_section // 2
    steps = across(max(n_rep, chips))
    many = len(steps)
    rows = parts_of(width, slots)
    part = (rows[1], width)
    held = [(chips,) + part]
    message = (max(rows[1], 2 * slots + rows[0]), width)
    operands = [same, term, came]
    half, *first = call_parts(
        functools.partial(first_kernel, slots, rows), "first", operands, part, message, many
    )
    first = [exchange(m, 0, i + 1, j) for i, (m, j) in enumerate(zip(first, steps))]
    relaid = store(0, same, came, first, n_section, slots)
    message = (2 * slots + rows[1], width)
    second = functools.partial(second_kernel, slots, rows, n_rep, many)
    operands = [same, came, half, *first]
    half, *second = call_parts(second, "second", operands, part, message, many, held)
    second = [exchange(m, 1, i + 1, j) for i, (m, j) in enumerate(zip(second, steps))]
    third = functools.partial(third_kernel, slots, rows, n_rep)
    (half,) = call_parts(third, "third", [half, *second], part, part, 0, held)
    relaid = store(1, same, came, second, n_section, slots, relaid)
    half, relaid = lax.optimization_barrier((half, relaid))
    weight_grad = finish(half, swap(half, "section", 1), rows)
    return (relaid.reshape(1, 1, n_section, slots, width), weight_grad)


def solution(mesh):
    placed = (
        P(("section", "rep"), None),
        P("section", "rep", None, None, None),
        P("section", "rep", None),
        P(("section", "rep"), None),
        P(),
        P(("section", "rep"), None),
    )
    return jax.shard_map(
        per_device,
        mesh=mesh,
        in_specs=placed,
        out_specs=(P("section", "rep", None, None, None), P()),
        check_vma=False,
    )
```

```python
import functools

import jax
import jax.numpy as jnp
from jax import lax
from jax.experimental import pallas as pl
from jax.experimental.pallas import tpu as pltpu
from jax.sharding import PartitionSpec as P

VMEM = pl.BlockSpec(memory_space=pltpu.VMEM)
LIMIT = pltpu.CompilerParams(vmem_limit_bytes=32 * 1024 * 1024)
HBM = pl.BlockSpec(memory_space=pltpu.HBM)


def across(n):
    return list(range(n - 1, 0, -1))


def place_of_chip():
    return lax.axis_index("section") >> 1, lax.axis_size("section") // 2


def prepare_kernel(slots, tiles_ref, own_ref, target_ref, wide_ref, held_ref, placing_ref):
    many, depth = tiles_ref.shape[:2]
    for g in range(many):
        wide_ref[g] = jnp.concatenate([tiles_ref[g, k] for k in range(depth)], axis=1)
    held_ref[...] = own_ref[...]
    places, rows = placing_ref.shape
    n_section = places // slots
    target = target_ref[...]
    hits = lax.broadcasted_iota(jnp.int32, (n_section, rows), 0) == target
    hits = jnp.where(hits, 1.0, 0.0)
    earlier = lax.broadcasted_iota(jnp.int32, (rows, rows), 0) < lax.broadcasted_iota(
        jnp.int32, (rows, rows), 1
    )
    earlier = jnp.where(earlier, 1.0, 0.0).astype(jnp.bfloat16)
    before = jnp.dot(hits.astype(jnp.bfloat16), earlier, preferred_element_type=jnp.float32)
    slot = jnp.sum(before * hits, axis=0, keepdims=True).astype(jnp.int32)
    chip, chips = place_of_chip()
    apart = (target >> 1) - chip
    apart = jnp.where(apart < 0, apart + chips, apart)
    other_core = (target ^ lax.axis_index("section")) & 1
    position = (other_core * chips + apart) * slots + slot
    placing = lax.broadcasted_iota(jnp.int32, (places, rows), 0) == position
    placing_ref[...] = jnp.where(placing, 1.0, 0.0).astype(jnp.bfloat16)


def prepare(tiles, own, target, places, slots):
    many, depth, tile, _ = tiles.shape
    return pl.pallas_call(
        functools.partial(prepare_kernel, slots),
        out_shape=(
            jax.ShapeDtypeStruct((many, tile, depth * tile), jnp.bfloat16),
            jax.ShapeDtypeStruct(own.shape, jnp.bfloat16),
            jax.ShapeDtypeStruct((places, target.shape[1]), jnp.bfloat16),
        ),
        in_specs=[VMEM] * 3,
        out_specs=(VMEM,) * 3,
        compiler_params=LIMIT,
        cost_estimate=pl.CostEstimate(flops=0, bytes_accessed=2 * tiles.size * 2, transcendentals=0),
        name="prepare",
    )(tiles, own, target)


def partials_kernel(count, src_ref, wide_ref, *refs):
    block_refs, out_refs, held = refs[:count], refs[count:-1], refs[-1]
    depth = src_ref.shape[1]
    section, rep = lax.axis_index("section"), lax.axis_index("rep")
    for j in range(count):
        held[j] = block_refs[j][...]
    for j, out_ref in zip([0] + across(len(out_refs)), out_refs):
        g = rep ^ j
        right = jnp.concatenate([held[src_ref[g, k] ^ section] for k in range(depth)], axis=0)
        out_ref[...] = jnp.dot(wide_ref[g], right, preferred_element_type=jnp.float32).astype(
            jnp.bfloat16
        )


def partials(sources, wide, blocks):
    many = wide.shape[0]
    tile, width = blocks[0].shape
    return pl.pallas_call(
        functools.partial(partials_kernel, len(blocks)),
        out_shape=[jax.ShapeDtypeStruct((tile, width), jnp.bfloat16)] * many,
        in_specs=[VMEM] * (2 + len(blocks)),
        out_specs=[VMEM] * many,
        scratch_shapes=[pltpu.VMEM((len(blocks), tile, width), jnp.bfloat16)],
        compiler_params=LIMIT,
        name="partials",
    )(sources, wide, *blocks)


def swap(value, axis, j):
    return lax.ppermute(value, axis, [(i, i ^ j) for i in range(lax.axis_size(axis))])


def tree_sum(terms):
    while len(terms) > 1:
        terms = [terms[i] + terms[i + 1] for i in range(0, len(terms), 2)]
    return terms[0]


def parts_of(width, slots):
    low = (width - 2 * slots) // 2 // 16 * 16
    return low, width - low


def dense_kernel(n_part, slots, weight_ref, cot_ref, placing_ref, *refs):
    part_refs, (same_ref, term_ref, sent_ref) = refs[:n_part], refs[n_part:]
    core = lax.axis_index("section") & 1
    agg_b = tree_sum([ref[...].astype(jnp.float32) for ref in part_refs]).astype(jnp.bfloat16)
    pre = jnp.dot(agg_b, weight_ref[...], preferred_element_type=jnp.float32)
    sig = jax.nn.sigmoid(pre)
    factor = sig * (1.0 + pre * (1.0 - sig))
    grad_pre = (cot_ref[...].astype(jnp.float32) * factor).astype(jnp.bfloat16)
    term = lax.dot_general(
        agg_b, grad_pre, (((0,), (0,)), ((), ())), preferred_element_type=jnp.float32
    )
    term_ref[...] = term
    output = (pre * sig).astype(jnp.bfloat16)
    packed = jnp.dot(placing_ref[...], output, preferred_element_type=jnp.float32)
    half = packed.shape[0] // 2
    same_ref[...] = packed[:half].astype(jnp.bfloat16)
    sent_ref[:half] = packed[half:].astype(jnp.bfloat16)
    low, high = parts_of(term.shape[0], slots)

    @pl.when(core == 0)
    def _():
        sent_ref[half:] = term[low:].astype(jnp.bfloat16)

    @pl.when(core == 1)
    def _():
        sent_ref[half : half + low] = term[:low].astype(jnp.bfloat16)


def dense(parts, weight, cotangent, placing, slots):
    places, width = placing.shape[0], weight.shape[0]
    return pl.pallas_call(
        functools.partial(dense_kernel, len(parts), slots),
        out_shape=(
            jax.ShapeDtypeStruct((places // 2, width), jnp.bfloat16),
            jax.ShapeDtypeStruct((width, width), jnp.float32),
            jax.ShapeDtypeStruct((places // 2 + parts_of(width, slots)[1], width), jnp.bfloat16),
        ),
        in_specs=[VMEM] * (3 + len(parts)),
        out_specs=(VMEM,) * 3,
        compiler_params=LIMIT,
        name="dense",
    )(weight, cotangent, placing, *parts)


def write_messages(core_along, slots, rows, same_ref, came_ref, half_ref, out_refs):
    core = lax.axis_index("section") & 1

    @pl.when(core == core_along)
    def _():
        for i, ref in enumerate(out_refs):
            start = (i + 1) * slots % same_ref.shape[0]
            ref[:slots] = same_ref[start : start + slots]
            ref[slots : 2 * slots] = came_ref[start : start + slots]
            ref[2 * slots : 2 * slots + rows[core_along]] = half_ref[: rows[core_along]]

    @pl.when(core != core_along)
    def _():
        for ref in out_refs:
            ref[: rows[1 - core_along]] = half_ref[: rows[1 - core_along]]


def sum_parts(core_along, slots, rows, half_ref, held, own_ref, message_refs, n_rep):
    chip, chips = place_of_chip()
    core = lax.axis_index("section") & 1

    @pl.when(core == core_along)
    def _():
        many = rows[core_along]
        held[chip, :many] = own_ref[:many]
        for i, ref in enumerate(message_refs[: chips - 1]):
            held[(chip + chips - i - 1) % chips, :many] = ref[2 * slots : 2 * slots + many]
        total = tree_sum([held[c, :many].astype(jnp.float32) for c in range(chips)])
        half_ref[:many] = total.astype(jnp.bfloat16)

    @pl.when(core != core_along)
    def _():
        many = rows[1 - core_along]
        by_xor = [ref[:many].astype(jnp.float32) for ref in [own_ref] + list(message_refs[::-1])]
        half_ref[:many] = tree_sum(by_xor[:n_rep]).astype(jnp.bfloat16)


def first_kernel(slots, rows, same_ref, term_ref, came_ref, half_ref, *out_refs):
    core = lax.axis_index("section") & 1
    start = same_ref.shape[0]

    @pl.when(core == 0)
    def _():
        other = came_ref[start : start + rows[0]].astype(jnp.float32)
        half_ref[: rows[0]] = (term_ref[: rows[0]] + other).astype(jnp.bfloat16)

    @pl.when(core == 1)
    def _():
        other = came_ref[start:].astype(jnp.float32)
        half_ref[...] = (term_ref[rows[0] :] + other).astype(jnp.bfloat16)

    write_messages(0, slots, rows, same_ref, came_ref, half_ref, out_refs)


def second_kernel(slots, rows, n_rep, many, same_ref, came_ref, own_ref, *refs):
    message_refs, half_ref, out_refs, held = refs[:many], refs[many], refs[many + 1 : -1], refs[-1]
    sum_parts(0, slots, rows, half_ref, held, own_ref, message_refs, n_rep)
    write_messages(1, slots, rows, same_ref, came_ref, half_ref, out_refs)


def third_kernel(slots, rows, n_rep, own_ref, *refs):
    sum_parts(1, slots, rows, refs[-2], refs[-1], own_ref, refs[:-2], n_rep)


def call_parts(kernel, name, operands, half, message, many, held=()):
    shapes = [jax.ShapeDtypeStruct(half, jnp.bfloat16)]
    shapes += [jax.ShapeDtypeStruct(message, jnp.bfloat16)] * many
    return pl.pallas_call(
        kernel,
        out_shape=shapes,
        in_specs=[VMEM] * len(operands),
        out_specs=[VMEM] * len(shapes),
        scratch_shapes=[pltpu.VMEM(shape, jnp.bfloat16) for shape in held],
        compiler_params=LIMIT,
        name=name,
    )(*operands)


def store_kernel(core, slots, same_ref, came_ref, *refs):
    message_refs, (out_ref, rows, sem) = refs[:-3], refs[-3:]
    section = lax.axis_index("section")
    chip, chips = place_of_chip()

    @pl.when(section & 1 == core)
    def _():
        rows[section] = same_ref[:slots]
        rows[section ^ 1] = came_ref[:slots]
        for i, ref in enumerate(message_refs[: chips - 1]):
            source = 2 * ((chip + chips - i - 1) % chips)
            rows[source + core] = ref[:slots]
            rows[source + 1 - core] = ref[slots : 2 * slots]
        copy = pltpu.make_async_copy(rows, out_ref, sem)
        copy.start()
        copy.wait()


def store(core, same, came, messages, n_section, slots, base=None):
    shape = (n_section, slots, same.shape[1])
    operands = [same, came, *messages]
    kernel, first, specs = functools.partial(store_kernel, core, slots), [], []
    if base is not None:
        kernel, first, specs = lambda _, *refs: store_kernel(core, slots, *refs), [base], [HBM]
    return pl.pallas_call(
        kernel,
        out_shape=jax.ShapeDtypeStruct(shape, jnp.bfloat16),
        in_specs=specs + [VMEM] * len(operands),
        out_specs=HBM,
        scratch_shapes=[pltpu.VMEM(shape, jnp.bfloat16), pltpu.SemaphoreType.DMA],
        input_output_aliases={0: 0} if first else {},
        compiler_params=LIMIT,
        name="store",
    )(*first, *operands)


def finish_kernel(rows, own_ref, came_ref, out_ref):
    core = lax.axis_index("section") & 1
    low, high = rows

    @pl.when(core == 0)
    def _():
        out_ref[:low] = own_ref[:low].astype(jnp.float32)
        out_ref[low:] = came_ref[...].astype(jnp.float32)

    @pl.when(core == 1)
    def _():
        out_ref[:low] = came_ref[:low].astype(jnp.float32)
        out_ref[low:] = own_ref[...].astype(jnp.float32)


def finish(own, came, rows):
    width = own.shape[1]
    return pl.pallas_call(
        functools.partial(finish_kernel, rows),
        out_shape=jax.ShapeDtypeStruct((width, width), jnp.float32),
        in_specs=[VMEM] * 2,
        out_specs=VMEM,
        compiler_params=LIMIT,
        name="finish",
    )(own, came)


def exchange(value, core_along, shift, j):
    n_section, n_rep = lax.axis_size("section"), lax.axis_size("rep")
    pairs = []
    for s in range(n_section):
        along = s & 1 == core_along
        to = (s + 2 * shift) % n_section if along else s
        for r in range(n_rep):
            pairs.append((s * n_rep + r, to * n_rep + (r if along else r ^ j % n_rep)))
    return lax.ppermute(value, ("section", "rep"), pairs)


def gather_blocks(features, axis, ready):
    n = lax.axis_size(axis)
    blocks = [None] * n
    blocks[0] = features
    far = n // 2 & -2
    for j in sorted(range(2, n, 2), key=lambda j: (j & 4, -(j & 2))):
        blocks[j] = swap(features, axis, j)
    blocks[1] = swap(features, axis, 1)
    blocks[far], ready = lax.optimization_barrier((blocks[far], ready))
    for j in sorted(range(2, n, 2), key=lambda j: -j):
        blocks[j + 1] = swap(blocks[j], axis, 1)
    return blocks, ready


def per_device(features, adj_tiles, adj_src, cotangent, weight, destination):
    n_section, n_rep = lax.axis_size("section"), lax.axis_size("rep")
    rows_here, width = features.shape
    tile = adj_tiles.shape[3]
    slots = max(2, 2 * rows_here // n_section)
    target = destination.reshape(1, rows_here)
    wide, own, placing = prepare(adj_tiles[:, 0], features, target, n_section * slots, slots)
    blocks, (wide, own, placing) = gather_blocks(features, "section", (wide, own, placing))
    parts = list(partials(adj_src[:, 0], wide, [own] + blocks[1:]))
    others = across(n_rep)
    parts = parts[:1] + [swap(part, "rep", j) for part, j in zip(parts[1:], others)]
    same, term, sent = dense(parts, weight, cotangent, placing, slots)
    came = swap(sent, "section", 1)
    chips = n_section // 2
    steps = across(max(n_rep, chips))
    many = len(steps)
    rows = parts_of(width, slots)
    part = (rows[1], width)
    held = [(chips,) + part]
    message = (max(rows[1], 2 * slots + rows[0]), width)
    operands = [same, term, came]
    half, *first = call_parts(
        functools.partial(first_kernel, slots, rows), "first", operands, part, message, many
    )
    first = [exchange(m, 0, i + 1, j) for i, (m, j) in enumerate(zip(first, steps))]
    relaid = store(0, same, came, first, n_section, slots)
    message = (2 * slots + rows[1], width)
    second = functools.partial(second_kernel, slots, rows, n_rep, many)
    operands = [same, came, half, *first]
    half, *second = call_parts(second, "second", operands, part, message, many, held)
    second = [exchange(m, 1, i + 1, j) for i, (m, j) in enumerate(zip(second, steps))]
    third = functools.partial(third_kernel, slots, rows, n_rep)
    (half,) = call_parts(third, "third", [half, *second], part, part, 0, held)
    relaid = store(1, same, came, second, n_section, slots, relaid)
    half, relaid = lax.optimization_barrier((half, relaid))
    weight_grad = finish(half, swap(half, "section", 1), rows)
    return (relaid.reshape(1, 1, n_section, slots, width), weight_grad)


def solution(mesh):
    placed = (
        P(("section", "rep"), None),
        P("section", "rep", None, None, None),
        P("section", "rep", None),
        P(("section", "rep"), None),
        P(),
        P(("section", "rep"), None),
    )
    return jax.shard_map(
        per_device,
        mesh=mesh,
        in_specs=placed,
        out_specs=(P("section", "rep", None, None, None), P()),
        check_vma=False,
    )
```

```python
import functools

import jax
import jax.numpy as jnp
from jax import lax
from jax.experimental import pallas as pl
from jax.experimental.pallas import tpu as pltpu
from jax.sharding import PartitionSpec as P

VMEM = pl.BlockSpec(memory_space=pltpu.VMEM)
LIMIT = pltpu.CompilerParams(vmem_limit_bytes=32 * 1024 * 1024)
HBM = pl.BlockSpec(memory_space=pltpu.HBM)


def across(n):
    return [n - 1] + list(range(1, n - 1))


def place_of_chip():
    return lax.axis_index("section") >> 1, lax.axis_size("section") // 2


def prepare_kernel(slots, tiles_ref, own_ref, target_ref, wide_ref, held_ref, placing_ref):
    many, depth = tiles_ref.shape[:2]
    for g in range(many):
        wide_ref[g] = jnp.concatenate([tiles_ref[g, k] for k in range(depth)], axis=1)
    held_ref[...] = own_ref[...]
    places, rows = placing_ref.shape
    n_section = places // slots
    target = target_ref[...]
    hits = lax.broadcasted_iota(jnp.int32, (n_section, rows), 0) == target
    hits = jnp.where(hits, 1.0, 0.0)
    earlier = lax.broadcasted_iota(jnp.int32, (rows, rows), 0) < lax.broadcasted_iota(
        jnp.int32, (rows, rows), 1
    )
    earlier = jnp.where(earlier, 1.0, 0.0).astype(jnp.bfloat16)
    before = jnp.dot(hits.astype(jnp.bfloat16), earlier, preferred_element_type=jnp.float32)
    slot = jnp.sum(before * hits, axis=0, keepdims=True).astype(jnp.int32)
    chip, chips = place_of_chip()
    apart = (target >> 1) - chip
    apart = jnp.where(apart < 0, apart + chips, apart)
    other_core = (target ^ lax.axis_index("section")) & 1
    position = (other_core * chips + apart) * slots + slot
    placing = lax.broadcasted_iota(jnp.int32, (places, rows), 0) == position
    placing_ref[...] = jnp.where(placing, 1.0, 0.0).astype(jnp.bfloat16)


def prepare(tiles, own, target, places, slots):
    many, depth, tile, _ = tiles.shape
    return pl.pallas_call(
        functools.partial(prepare_kernel, slots),
        out_shape=(
            jax.ShapeDtypeStruct((many, tile, depth * tile), jnp.bfloat16),
            jax.ShapeDtypeStruct(own.shape, jnp.bfloat16),
            jax.ShapeDtypeStruct((places, target.shape[1]), jnp.bfloat16),
        ),
        in_specs=[VMEM] * 3,
        out_specs=(VMEM,) * 3,
        compiler_params=LIMIT,
        cost_estimate=pl.CostEstimate(flops=0, bytes_accessed=2 * tiles.size * 2, transcendentals=0),
        name="prepare",
    )(tiles, own, target)


def partials_kernel(count, src_ref, wide_ref, *refs):
    block_refs, out_refs, held = refs[:count], refs[count:-1], refs[-1]
    depth = src_ref.shape[1]
    section, rep = lax.axis_index("section"), lax.axis_index("rep")
    for j in range(count):
        held[j] = block_refs[j][...]
    for j, out_ref in zip([0] + across(len(out_refs)), out_refs):
        g = rep ^ j
        right = jnp.concatenate([held[src_ref[g, k] ^ section] for k in range(depth)], axis=0)
        out_ref[...] = jnp.dot(wide_ref[g], right, preferred_element_type=jnp.float32).astype(
            jnp.bfloat16
        )


def partials(sources, wide, blocks):
    many = wide.shape[0]
    tile, width = blocks[0].shape
    return pl.pallas_call(
        functools.partial(partials_kernel, len(blocks)),
        out_shape=[jax.ShapeDtypeStruct((tile, width), jnp.bfloat16)] * many,
        in_specs=[VMEM] * (2 + len(blocks)),
        out_specs=[VMEM] * many,
        scratch_shapes=[pltpu.VMEM((len(blocks), tile, width), jnp.bfloat16)],
        compiler_params=LIMIT,
        name="partials",
    )(sources, wide, *blocks)


def swap(value, axis, j):
    return lax.ppermute(value, axis, [(i, i ^ j) for i in range(lax.axis_size(axis))])


def tree_sum(terms):
    while len(terms) > 1:
        terms = [terms[i] + terms[i + 1] for i in range(0, len(terms), 2)]
    return terms[0]


def parts_of(width, slots):
    low = (width - 2 * slots) // 2 // 16 * 16
    return low, width - low


def dense_kernel(n_part, slots, weight_ref, cot_ref, placing_ref, *refs):
    part_refs, (same_ref, term_ref, sent_ref) = refs[:n_part], refs[n_part:]
    core = lax.axis_index("section") & 1
    agg_b = tree_sum([ref[...].astype(jnp.float32) for ref in part_refs]).astype(jnp.bfloat16)
    pre = jnp.dot(agg_b, weight_ref[...], preferred_element_type=jnp.float32)
    sig = jax.nn.sigmoid(pre)
    factor = sig * (1.0 + pre * (1.0 - sig))
    grad_pre = (cot_ref[...].astype(jnp.float32) * factor).astype(jnp.bfloat16)
    term = lax.dot_general(
        agg_b, grad_pre, (((0,), (0,)), ((), ())), preferred_element_type=jnp.float32
    )
    term_ref[...] = term
    output = (pre * sig).astype(jnp.bfloat16)
    packed = jnp.dot(placing_ref[...], output, preferred_element_type=jnp.float32)
    half = packed.shape[0] // 2
    same_ref[...] = packed[:half].astype(jnp.bfloat16)
    sent_ref[:half] = packed[half:].astype(jnp.bfloat16)
    low, high = parts_of(term.shape[0], slots)

    @pl.when(core == 0)
    def _():
        sent_ref[half:] = term[low:].astype(jnp.bfloat16)

    @pl.when(core == 1)
    def _():
        sent_ref[half : half + low] = term[:low].astype(jnp.bfloat16)


def dense(parts, weight, cotangent, placing, slots):
    places, width = placing.shape[0], weight.shape[0]
    return pl.pallas_call(
        functools.partial(dense_kernel, len(parts), slots),
        out_shape=(
            jax.ShapeDtypeStruct((places // 2, width), jnp.bfloat16),
            jax.ShapeDtypeStruct((width, width), jnp.float32),
            jax.ShapeDtypeStruct((places // 2 + parts_of(width, slots)[1], width), jnp.bfloat16),
        ),
        in_specs=[VMEM] * (3 + len(parts)),
        out_specs=(VMEM,) * 3,
        compiler_params=LIMIT,
        name="dense",
    )(weight, cotangent, placing, *parts)


def write_messages(core_along, slots, rows, same_ref, came_ref, half_ref, out_refs):
    core = lax.axis_index("section") & 1

    @pl.when(core == core_along)
    def _():
        for i, ref in enumerate(out_refs):
            start = (i + 1) * slots % same_ref.shape[0]
            ref[:slots] = same_ref[start : start + slots]
            ref[slots : 2 * slots] = came_ref[start : start + slots]
            ref[2 * slots : 2 * slots + rows[core_along]] = half_ref[: rows[core_along]]

    @pl.when(core != core_along)
    def _():
        for ref in out_refs:
            ref[: rows[1 - core_along]] = half_ref[: rows[1 - core_along]]


def sum_parts(core_along, slots, rows, half_ref, held, own_ref, message_refs, n_rep):
    chip, chips = place_of_chip()
    core = lax.axis_index("section") & 1

    @pl.when(core == core_along)
    def _():
        many = rows[core_along]
        held[chip, :many] = own_ref[:many]
        for i, ref in enumerate(message_refs[: chips - 1]):
            held[(chip + chips - i - 1) % chips, :many] = ref[2 * slots : 2 * slots + many]
        total = tree_sum([held[c, :many].astype(jnp.float32) for c in range(chips)])
        half_ref[:many] = total.astype(jnp.bfloat16)

    @pl.when(core != core_along)
    def _():
        many = rows[1 - core_along]
        refs = dict(zip(across(len(message_refs) + 1), message_refs))
        refs = [own_ref] + [refs[j] for j in sorted(refs)]
        by_xor = [ref[:many].astype(jnp.float32) for ref in refs]
        half_ref[:many] = tree_sum(by_xor[:n_rep]).astype(jnp.bfloat16)


def first_kernel(slots, rows, same_ref, term_ref, came_ref, half_ref, *out_refs):
    core = lax.axis_index("section") & 1
    start = same_ref.shape[0]

    @pl.when(core == 0)
    def _():
        other = came_ref[start : start + rows[0]].astype(jnp.float32)
        half_ref[: rows[0]] = (term_ref[: rows[0]] + other).astype(jnp.bfloat16)

    @pl.when(core == 1)
    def _():
        other = came_ref[start:].astype(jnp.float32)
        half_ref[...] = (term_ref[rows[0] :] + other).astype(jnp.bfloat16)

    write_messages(0, slots, rows, same_ref, came_ref, half_ref, out_refs)


def second_kernel(slots, rows, n_rep, many, same_ref, came_ref, own_ref, *refs):
    message_refs, half_ref, out_refs, held = refs[:many], refs[many], refs[many + 1 : -1], refs[-1]
    sum_parts(0, slots, rows, half_ref, held, own_ref, message_refs, n_rep)
    write_messages(1, slots, rows, same_ref, came_ref, half_ref, out_refs)


def third_kernel(slots, rows, n_rep, own_ref, *refs):
    sum_parts(1, slots, rows, refs[-2], refs[-1], own_ref, refs[:-2], n_rep)


def call_parts(kernel, name, operands, half, message, many, held=()):
    shapes = [jax.ShapeDtypeStruct(half, jnp.bfloat16)]
    shapes += [jax.ShapeDtypeStruct(message, jnp.bfloat16)] * many
    return pl.pallas_call(
        kernel,
        out_shape=shapes,
        in_specs=[VMEM] * len(operands),
        out_specs=[VMEM] * len(shapes),
        scratch_shapes=[pltpu.VMEM(shape, jnp.bfloat16) for shape in held],
        compiler_params=LIMIT,
        name=name,
    )(*operands)


def store_kernel(core, slots, same_ref, came_ref, *refs):
    message_refs, (out_ref, rows, sem) = refs[:-3], refs[-3:]
    section = lax.axis_index("section")
    chip, chips = place_of_chip()

    @pl.when(section & 1 == core)
    def _():
        rows[section] = same_ref[:slots]
        rows[section ^ 1] = came_ref[:slots]
        for i, ref in enumerate(message_refs[: chips - 1]):
            source = 2 * ((chip + chips - i - 1) % chips)
            rows[source + core] = ref[:slots]
            rows[source + 1 - core] = ref[slots : 2 * slots]
        copy = pltpu.make_async_copy(rows, out_ref, sem)
        copy.start()
        copy.wait()


def store(core, same, came, messages, n_section, slots, base=None):
    shape = (n_section, slots, same.shape[1])
    operands = [same, came, *messages]
    kernel, first, specs = functools.partial(store_kernel, core, slots), [], []
    if base is not None:
        kernel, first, specs = lambda _, *refs: store_kernel(core, slots, *refs), [base], [HBM]
    return pl.pallas_call(
        kernel,
        out_shape=jax.ShapeDtypeStruct(shape, jnp.bfloat16),
        in_specs=specs + [VMEM] * len(operands),
        out_specs=HBM,
        scratch_shapes=[pltpu.VMEM(shape, jnp.bfloat16), pltpu.SemaphoreType.DMA],
        input_output_aliases={0: 0} if first else {},
        compiler_params=LIMIT,
        name="store",
    )(*first, *operands)


def finish_kernel(rows, own_ref, came_ref, out_ref):
    core = lax.axis_index("section") & 1
    low, high = rows

    @pl.when(core == 0)
    def _():
        out_ref[:low] = own_ref[:low].astype(jnp.float32)
        out_ref[low:] = came_ref[...].astype(jnp.float32)

    @pl.when(core == 1)
    def _():
        out_ref[:low] = came_ref[:low].astype(jnp.float32)
        out_ref[low:] = own_ref[...].astype(jnp.float32)


def finish(own, came, rows):
    width = own.shape[1]
    return pl.pallas_call(
        functools.partial(finish_kernel, rows),
        out_shape=jax.ShapeDtypeStruct((width, width), jnp.float32),
        in_specs=[VMEM] * 2,
        out_specs=VMEM,
        compiler_params=LIMIT,
        name="finish",
    )(own, came)


def exchange(value, core_along, shift, j):
    n_section, n_rep = lax.axis_size("section"), lax.axis_size("rep")
    pairs = []
    for s in range(n_section):
        along = s & 1 == core_along
        to = (s + 2 * shift) % n_section if along else s
        for r in range(n_rep):
            pairs.append((s * n_rep + r, to * n_rep + (r if along else r ^ j % n_rep)))
    return lax.ppermute(value, ("section", "rep"), pairs)


def gather_blocks(features, axis, ready):
    n = lax.axis_size(axis)
    blocks = [None] * n
    blocks[0] = features
    far = n // 2 & -2
    for j in sorted(range(2, n, 2), key=lambda j: (j & 4, -(j & 2))):
        blocks[j] = swap(features, axis, j)
    blocks[1] = swap(features, axis, 1)
    blocks[far], ready = lax.optimization_barrier((blocks[far], ready))
    for j in sorted(range(2, n, 2), key=lambda j: -j):
        blocks[j + 1] = swap(blocks[j], axis, 1)
    return blocks, ready


def per_device(features, adj_tiles, adj_src, cotangent, weight, destination):
    n_section, n_rep = lax.axis_size("section"), lax.axis_size("rep")
    rows_here, width = features.shape
    tile = adj_tiles.shape[3]
    slots = max(2, 2 * rows_here // n_section)
    target = destination.reshape(1, rows_here)
    wide, own, placing = prepare(adj_tiles[:, 0], features, target, n_section * slots, slots)
    blocks, (wide, own, placing) = gather_blocks(features, "section", (wide, own, placing))
    parts = list(partials(adj_src[:, 0], wide, [own] + blocks[1:]))
    others = across(n_rep)
    parts = parts[:1] + [swap(part, "rep", j) for part, j in zip(parts[1:], others)]
    same, term, sent = dense(parts, weight, cotangent, placing, slots)
    came = swap(sent, "section", 1)
    chips = n_section // 2
    steps = across(max(n_rep, chips))
    many = len(steps)
    rows = parts_of(width, slots)
    part = (rows[1], width)
    held = [(chips,) + part]
    message = (max(rows[1], 2 * slots + rows[0]), width)
    operands = [same, term, came]
    half, *first = call_parts(
        functools.partial(first_kernel, slots, rows), "first", operands, part, message, many
    )
    first = [exchange(m, 0, i + 1, j) for i, (m, j) in enumerate(zip(first, steps))]
    relaid = store(0, same, came, first, n_section, slots)
    message = (2 * slots + rows[1], width)
    second = functools.partial(second_kernel, slots, rows, n_rep, many)
    operands = [same, came, half, *first]
    half, *second = call_parts(second, "second", operands, part, message, many, held)
    second = [exchange(m, 1, i + 1, j) for i, (m, j) in enumerate(zip(second, steps))]
    third = functools.partial(third_kernel, slots, rows, n_rep)
    (half,) = call_parts(third, "third", [half, *second], part, part, 0, held)
    relaid = store(1, same, came, second, n_section, slots, relaid)
    half, relaid = lax.optimization_barrier((half, relaid))
    weight_grad = finish(half, swap(half, "section", 1), rows)
    return (relaid.reshape(1, 1, n_section, slots, width), weight_grad)


def solution(mesh):
    placed = (
        P(("section", "rep"), None),
        P("section", "rep", None, None, None),
        P("section", "rep", None),
        P(("section", "rep"), None),
        P(),
        P(("section", "rep"), None),
    )
    return jax.shard_map(
        per_device,
        mesh=mesh,
        in_specs=placed,
        out_specs=(P("section", "rep", None, None, None), P()),
        check_vma=False,
    )
```

```python
import functools

import jax
import jax.numpy as jnp
from jax import lax
from jax.experimental import pallas as pl
from jax.experimental.pallas import tpu as pltpu
from jax.sharding import PartitionSpec as P

VMEM = pl.BlockSpec(memory_space=pltpu.VMEM)
LIMIT = pltpu.CompilerParams(vmem_limit_bytes=32 * 1024 * 1024)
HBM = pl.BlockSpec(memory_space=pltpu.HBM)


def across(n):
    return list(range(n - 1, 0, -1))


def place_of_chip():
    return lax.axis_index("section") >> 1, lax.axis_size("section") // 2


def prepare_kernel(slots, tiles_ref, own_ref, target_ref, wide_ref, held_ref, placing_ref):
    many, depth = tiles_ref.shape[:2]
    for g in range(many):
        wide_ref[g] = jnp.concatenate([tiles_ref[g, k] for k in range(depth)], axis=1)
    held_ref[...] = own_ref[...]
    places, rows = placing_ref.shape
    n_section = places // slots
    target = target_ref[...]
    hits = lax.broadcasted_iota(jnp.int32, (n_section, rows), 0) == target
    hits = jnp.where(hits, 1.0, 0.0)
    earlier = lax.broadcasted_iota(jnp.int32, (rows, rows), 0) < lax.broadcasted_iota(
        jnp.int32, (rows, rows), 1
    )
    earlier = jnp.where(earlier, 1.0, 0.0).astype(jnp.bfloat16)
    before = jnp.dot(hits.astype(jnp.bfloat16), earlier, preferred_element_type=jnp.float32)
    slot = jnp.sum(before * hits, axis=0, keepdims=True).astype(jnp.int32)
    chip, chips = place_of_chip()
    apart = (target >> 1) - chip
    apart = jnp.where(apart < 0, apart + chips, apart)
    other_core = (target ^ lax.axis_index("section")) & 1
    position = (other_core * chips + apart) * slots + slot
    placing = lax.broadcasted_iota(jnp.int32, (places, rows), 0) == position
    placing_ref[...] = jnp.where(placing, 1.0, 0.0).astype(jnp.bfloat16)


def prepare(tiles, own, target, places, slots):
    many, depth, tile, _ = tiles.shape
    return pl.pallas_call(
        functools.partial(prepare_kernel, slots),
        out_shape=(
            jax.ShapeDtypeStruct((many, tile, depth * tile), jnp.bfloat16),
            jax.ShapeDtypeStruct(own.shape, jnp.bfloat16),
            jax.ShapeDtypeStruct((places, target.shape[1]), jnp.bfloat16),
        ),
        in_specs=[VMEM] * 3,
        out_specs=(VMEM,) * 3,
        compiler_params=LIMIT,
        cost_estimate=pl.CostEstimate(flops=0, bytes_accessed=2 * tiles.size * 2, transcendentals=0),
        name="prepare",
    )(tiles, own, target)


def partials_kernel(count, src_ref, wide_ref, *refs):
    block_refs, out_refs, held = refs[:count], refs[count:-1], refs[-1]
    depth = src_ref.shape[1]
    section, rep = lax.axis_index("section"), lax.axis_index("rep")
    for j in range(count):
        held[j] = block_refs[j][...]
    for j, out_ref in zip([0] + across(len(out_refs)), out_refs):
        g = rep ^ j
        right = jnp.concatenate([held[src_ref[g, k] ^ section] for k in range(depth)], axis=0)
        out_ref[...] = jnp.dot(wide_ref[g], right, preferred_element_type=jnp.float32).astype(
            jnp.bfloat16
        )


def partials(sources, wide, blocks):
    many = wide.shape[0]
    tile, width = blocks[0].shape
    return pl.pallas_call(
        functools.partial(partials_kernel, len(blocks)),
        out_shape=[jax.ShapeDtypeStruct((tile, width), jnp.bfloat16)] * many,
        in_specs=[VMEM] * (2 + len(blocks)),
        out_specs=[VMEM] * many,
        scratch_shapes=[pltpu.VMEM((len(blocks), tile, width), jnp.bfloat16)],
        compiler_params=LIMIT,
        name="partials",
    )(sources, wide, *blocks)


def swap(value, axis, j):
    return lax.ppermute(value, axis, [(i, i ^ j) for i in range(lax.axis_size(axis))])


def tree_sum(terms):
    while len(terms) > 1:
        terms = [terms[i] + terms[i + 1] for i in range(0, len(terms), 2)]
    return terms[0]


def parts_of(width, slots):
    low = (width - slots) // 2 // 16 * 16
    return low, width - low


def dense_kernel(n_part, slots, weight_ref, cot_ref, placing_ref, *refs):
    part_refs, (same_ref, term_ref, sent_ref) = refs[:n_part], refs[n_part:]
    core = lax.axis_index("section") & 1
    agg_b = tree_sum([ref[...].astype(jnp.float32) for ref in part_refs]).astype(jnp.bfloat16)
    pre = jnp.dot(agg_b, weight_ref[...], preferred_element_type=jnp.float32)
    sig = jax.nn.sigmoid(pre)
    factor = sig * (1.0 + pre * (1.0 - sig))
    grad_pre = (cot_ref[...].astype(jnp.float32) * factor).astype(jnp.bfloat16)
    term = lax.dot_general(
        agg_b, grad_pre, (((0,), (0,)), ((), ())), preferred_element_type=jnp.float32
    )
    term_ref[...] = term
    output = (pre * sig).astype(jnp.bfloat16)
    packed = jnp.dot(placing_ref[...], output, preferred_element_type=jnp.float32)
    half = packed.shape[0] // 2
    same_ref[...] = packed[:half].astype(jnp.bfloat16)
    sent_ref[:half] = packed[half:].astype(jnp.bfloat16)
    low, high = parts_of(term.shape[0], slots)

    @pl.when(core == 0)
    def _():
        sent_ref[half:] = term[low:].astype(jnp.bfloat16)

    @pl.when(core == 1)
    def _():
        sent_ref[half : half + low] = term[:low].astype(jnp.bfloat16)


def dense(parts, weight, cotangent, placing, slots):
    places, width = placing.shape[0], weight.shape[0]
    return pl.pallas_call(
        functools.partial(dense_kernel, len(parts), slots),
        out_shape=(
            jax.ShapeDtypeStruct((places // 2, width), jnp.bfloat16),
            jax.ShapeDtypeStruct((width, width), jnp.float32),
            jax.ShapeDtypeStruct((places // 2 + parts_of(width, slots)[1], width), jnp.bfloat16),
        ),
        in_specs=[VMEM] * (3 + len(parts)),
        out_specs=(VMEM,) * 3,
        compiler_params=LIMIT,
        name="dense",
    )(weight, cotangent, placing, *parts)


def write_messages(core_along, slots, rows, same_ref, came_ref, half_ref, out_refs):
    core = lax.axis_index("section") & 1

    @pl.when(core == core_along)
    def _():
        for i, ref in enumerate(out_refs):
            start = (i + 1) * slots % same_ref.shape[0]
            ref[:slots] = same_ref[start : start + slots]
            ref[slots : 2 * slots] = came_ref[start : start + slots]
            ref[2 * slots : 2 * slots + rows[core_along]] = half_ref[: rows[core_along]]

    @pl.when(core != core_along)
    def _():
        for ref in out_refs:
            ref[: rows[1 - core_along]] = half_ref[: rows[1 - core_along]]


def sum_parts(core_along, slots, rows, half_ref, held, own_ref, message_refs, n_rep):
    chip, chips = place_of_chip()
    core = lax.axis_index("section") & 1

    @pl.when(core == core_along)
    def _():
        many = rows[core_along]
        held[chip, :many] = own_ref[:many]
        for i, ref in enumerate(message_refs[: chips - 1]):
            held[(chip + chips - i - 1) % chips, :many] = ref[2 * slots : 2 * slots + many]
        total = tree_sum([held[c, :many].astype(jnp.float32) for c in range(chips)])
        half_ref[:many] = total.astype(jnp.bfloat16)

    @pl.when(core != core_along)
    def _():
        many = rows[1 - core_along]
        by_xor = [ref[:many].astype(jnp.float32) for ref in [own_ref] + list(message_refs[::-1])]
        half_ref[:many] = tree_sum(by_xor[:n_rep]).astype(jnp.bfloat16)


def first_kernel(slots, rows, same_ref, term_ref, came_ref, half_ref, *out_refs):
    core = lax.axis_index("section") & 1
    start = same_ref.shape[0]

    @pl.when(core == 0)
    def _():
        other = came_ref[start : start + rows[0]].astype(jnp.float32)
        half_ref[: rows[0]] = (term_ref[: rows[0]] + other).astype(jnp.bfloat16)

    @pl.when(core == 1)
    def _():
        other = came_ref[start:].astype(jnp.float32)
        half_ref[...] = (term_ref[rows[0] :] + other).astype(jnp.bfloat16)

    write_messages(0, slots, rows, same_ref, came_ref, half_ref, out_refs)


def second_kernel(slots, rows, n_rep, many, same_ref, came_ref, own_ref, *refs):
    message_refs, half_ref, out_refs, held = refs[:many], refs[many], refs[many + 1 : -1], refs[-1]
    sum_parts(0, slots, rows, half_ref, held, own_ref, message_refs, n_rep)
    write_messages(1, slots, rows, same_ref, came_ref, half_ref, out_refs)


def third_kernel(slots, rows, n_rep, own_ref, *refs):
    sum_parts(1, slots, rows, refs[-2], refs[-1], own_ref, refs[:-2], n_rep)


def call_parts(kernel, name, operands, half, message, many, held=()):
    shapes = [jax.ShapeDtypeStruct(half, jnp.bfloat16)]
    shapes += [jax.ShapeDtypeStruct(message, jnp.bfloat16)] * many
    return pl.pallas_call(
        kernel,
        out_shape=shapes,
        in_specs=[VMEM] * len(operands),
        out_specs=[VMEM] * len(shapes),
        scratch_shapes=[pltpu.VMEM(shape, jnp.bfloat16) for shape in held],
        compiler_params=LIMIT,
        name=name,
    )(*operands)


def store_kernel(core, slots, same_ref, came_ref, *refs):
    message_refs, (out_ref, rows, sem) = refs[:-3], refs[-3:]
    section = lax.axis_index("section")
    chip, chips = place_of_chip()

    @pl.when(section & 1 == core)
    def _():
        rows[section] = same_ref[:slots]
        rows[section ^ 1] = came_ref[:slots]
        for i, ref in enumerate(message_refs[: chips - 1]):
            source = 2 * ((chip + chips - i - 1) % chips)
            rows[source + core] = ref[:slots]
            rows[source + 1 - core] = ref[slots : 2 * slots]
        copy = pltpu.make_async_copy(rows, out_ref, sem)
        copy.start()
        copy.wait()


def store(core, same, came, messages, n_section, slots, base=None):
    shape = (n_section, slots, same.shape[1])
    operands = [same, came, *messages]
    kernel, first, specs = functools.partial(store_kernel, core, slots), [], []
    if base is not None:
        kernel, first, specs = lambda _, *refs: store_kernel(core, slots, *refs), [base], [HBM]
    return pl.pallas_call(
        kernel,
        out_shape=jax.ShapeDtypeStruct(shape, jnp.bfloat16),
        in_specs=specs + [VMEM] * len(operands),
        out_specs=HBM,
        scratch_shapes=[pltpu.VMEM(shape, jnp.bfloat16), pltpu.SemaphoreType.DMA],
        input_output_aliases={0: 0} if first else {},
        compiler_params=LIMIT,
        name="store",
    )(*first, *operands)


def finish_kernel(rows, own_ref, came_ref, out_ref):
    core = lax.axis_index("section") & 1
    low, high = rows

    @pl.when(core == 0)
    def _():
        out_ref[:low] = own_ref[:low].astype(jnp.float32)
        out_ref[low:] = came_ref[...].astype(jnp.float32)

    @pl.when(core == 1)
    def _():
        out_ref[:low] = came_ref[:low].astype(jnp.float32)
        out_ref[low:] = own_ref[...].astype(jnp.float32)


def finish(own, came, rows):
    width = own.shape[1]
    return pl.pallas_call(
        functools.partial(finish_kernel, rows),
        out_shape=jax.ShapeDtypeStruct((width, width), jnp.float32),
        in_specs=[VMEM] * 2,
        out_specs=VMEM,
        compiler_params=LIMIT,
        name="finish",
    )(own, came)


def exchange(value, core_along, shift, j):
    n_section, n_rep = lax.axis_size("section"), lax.axis_size("rep")
    pairs = []
    for s in range(n_section):
        along = s & 1 == core_along
        to = (s + 2 * shift) % n_section if along else s
        for r in range(n_rep):
            pairs.append((s * n_rep + r, to * n_rep + (r if along else r ^ j % n_rep)))
    return lax.ppermute(value, ("section", "rep"), pairs)


def gather_blocks(features, axis, ready):
    n = lax.axis_size(axis)
    blocks = [None] * n
    blocks[0] = features
    far = n // 2 & -2
    for j in sorted(range(2, n, 2), key=lambda j: (j & 4, -(j & 2))):
        blocks[j] = swap(features, axis, j)
    blocks[1] = swap(features, axis, 1)
    blocks[far], ready = lax.optimization_barrier((blocks[far], ready))
    for j in sorted(range(2, n, 2), key=lambda j: -j):
        blocks[j + 1] = swap(blocks[j], axis, 1)
    return blocks, ready


def per_device(features, adj_tiles, adj_src, cotangent, weight, destination):
    n_section, n_rep = lax.axis_size("section"), lax.axis_size("rep")
    rows_here, width = features.shape
    tile = adj_tiles.shape[3]
    slots = max(2, 2 * rows_here // n_section)
    target = destination.reshape(1, rows_here)
    wide, own, placing = prepare(adj_tiles[:, 0], features, target, n_section * slots, slots)
    blocks, (wide, own, placing) = gather_blocks(features, "section", (wide, own, placing))
    parts = list(partials(adj_src[:, 0], wide, [own] + blocks[1:]))
    others = across(n_rep)
    parts = parts[:1] + [swap(part, "rep", j) for part, j in zip(parts[1:], others)]
    same, term, sent = dense(parts, weight, cotangent, placing, slots)
    came = swap(sent, "section", 1)
    chips = n_section // 2
    steps = across(max(n_rep, chips))
    many = len(steps)
    rows = parts_of(width, slots)
    part = (rows[1], width)
    held = [(chips,) + part]
    message = (max(rows[1], 2 * slots + rows[0]), width)
    operands = [same, term, came]
    half, *first = call_parts(
        functools.partial(first_kernel, slots, rows), "first", operands, part, message, many
    )
    first = [exchange(m, 0, i + 1, j) for i, (m, j) in enumerate(zip(first, steps))]
    relaid = store(0, same, came, first, n_section, slots)
    message = (2 * slots + rows[1], width)
    second = functools.partial(second_kernel, slots, rows, n_rep, many)
    operands = [same, came, half, *first]
    half, *second = call_parts(second, "second", operands, part, message, many, held)
    second = [exchange(m, 1, i + 1, j) for i, (m, j) in enumerate(zip(second, steps))]
    third = functools.partial(third_kernel, slots, rows, n_rep)
    (half,) = call_parts(third, "third", [half, *second], part, part, 0, held)
    relaid = store(1, same, came, second, n_section, slots, relaid)
    half, relaid = lax.optimization_barrier((half, relaid))
    weight_grad = finish(half, swap(half, "section", 1), rows)
    return (relaid.reshape(1, 1, n_section, slots, width), weight_grad)


def solution(mesh):
    placed = (
        P(("section", "rep"), None),
        P("section", "rep", None, None, None),
        P("section", "rep", None),
        P(("section", "rep"), None),
        P(),
        P(("section", "rep"), None),
    )
    return jax.shard_map(
        per_device,
        mesh=mesh,
        in_specs=placed,
        out_specs=(P("section", "rep", None, None, None), P()),
        check_vma=False,
    )
```

```python
import functools

import jax
import jax.numpy as jnp
from jax import lax
from jax.experimental import pallas as pl
from jax.experimental.pallas import tpu as pltpu
from jax.sharding import PartitionSpec as P

VMEM = pl.BlockSpec(memory_space=pltpu.VMEM)
LIMIT = pltpu.CompilerParams(vmem_limit_bytes=32 * 1024 * 1024)
HBM = pl.BlockSpec(memory_space=pltpu.HBM)


def across(n):
    return list(range(n - 1, 0, -1))


def place_of_chip():
    return lax.axis_index("section") >> 1, lax.axis_size("section") // 2


def prepare_kernel(slots, tiles_ref, own_ref, target_ref, wide_ref, held_ref, placing_ref):
    many, depth = tiles_ref.shape[:2]
    for g in range(many):
        wide_ref[g] = jnp.concatenate([tiles_ref[g, k] for k in range(depth)], axis=1)
    held_ref[...] = own_ref[...]
    places, rows = placing_ref.shape
    n_section = places // slots
    target = target_ref[...]
    hits = lax.broadcasted_iota(jnp.int32, (n_section, rows), 0) == target
    hits = jnp.where(hits, 1.0, 0.0)
    earlier = lax.broadcasted_iota(jnp.int32, (rows, rows), 0) < lax.broadcasted_iota(
        jnp.int32, (rows, rows), 1
    )
    earlier = jnp.where(earlier, 1.0, 0.0).astype(jnp.bfloat16)
    before = jnp.dot(hits.astype(jnp.bfloat16), earlier, preferred_element_type=jnp.float32)
    slot = jnp.sum(before * hits, axis=0, keepdims=True).astype(jnp.int32)
    chip, chips = place_of_chip()
    apart = (target >> 1) - chip
    apart = jnp.where(apart < 0, apart + chips, apart)
    other_core = (target ^ lax.axis_index("section")) & 1
    position = (other_core * chips + apart) * slots + slot
    placing = lax.broadcasted_iota(jnp.int32, (places, rows), 0) == position
    placing_ref[...] = jnp.where(placing, 1.0, 0.0).astype(jnp.bfloat16)


def prepare(tiles, own, target, places, slots):
    many, depth, tile, _ = tiles.shape
    return pl.pallas_call(
        functools.partial(prepare_kernel, slots),
        out_shape=(
            jax.ShapeDtypeStruct((many, tile, depth * tile), jnp.bfloat16),
            jax.ShapeDtypeStruct(own.shape, jnp.bfloat16),
            jax.ShapeDtypeStruct((places, target.shape[1]), jnp.bfloat16),
        ),
        in_specs=[VMEM] * 3,
        out_specs=(VMEM,) * 3,
        compiler_params=LIMIT,
        cost_estimate=pl.CostEstimate(flops=0, bytes_accessed=2 * tiles.size * 2, transcendentals=0),
        name="prepare",
    )(tiles, own, target)


def partials_kernel(count, src_ref, wide_ref, *refs):
    block_refs, out_refs, held = refs[:count], refs[count:-1], refs[-1]
    depth = src_ref.shape[1]
    section, rep = lax.axis_index("section"), lax.axis_index("rep")
    for j in range(count):
        held[j] = block_refs[j][...]
    for j, out_ref in zip([0] + across(len(out_refs)), out_refs):
        g = rep ^ j
        right = jnp.concatenate([held[src_ref[g, k] ^ section] for k in range(depth)], axis=0)
        out_ref[...] = jnp.dot(wide_ref[g], right, preferred_element_type=jnp.float32).astype(
            jnp.bfloat16
        )


def partials(sources, wide, blocks):
    many = wide.shape[0]
    tile, width = blocks[0].shape
    return pl.pallas_call(
        functools.partial(partials_kernel, len(blocks)),
        out_shape=[jax.ShapeDtypeStruct((tile, width), jnp.bfloat16)] * many,
        in_specs=[VMEM] * (2 + len(blocks)),
        out_specs=[VMEM] * many,
        scratch_shapes=[pltpu.VMEM((len(blocks), tile, width), jnp.bfloat16)],
        compiler_params=LIMIT,
        name="partials",
    )(sources, wide, *blocks)


def swap(value, axis, j):
    return lax.ppermute(value, axis, [(i, i ^ j) for i in range(lax.axis_size(axis))])


def tree_sum(terms):
    while len(terms) > 1:
        terms = [terms[i] + terms[i + 1] for i in range(0, len(terms), 2)]
    return terms[0]


def parts_of(width, slots):
    low = (width - 2 * slots) // 2 // 16 * 16
    return low, width - low


def dense_kernel(n_part, slots, weight_ref, cot_ref, placing_ref, *refs):
    part_refs, (same_ref, term_ref, sent_ref) = refs[:n_part], refs[n_part:]
    core = lax.axis_index("section") & 1
    agg_b = tree_sum([ref[...].astype(jnp.float32) for ref in part_refs]).astype(jnp.bfloat16)
    pre = jnp.dot(agg_b, weight_ref[...], preferred_element_type=jnp.float32)
    sig = jax.nn.sigmoid(pre)
    factor = sig * (1.0 + pre * (1.0 - sig))
    grad_pre = (cot_ref[...].astype(jnp.float32) * factor).astype(jnp.bfloat16)
    term = lax.dot_general(
        agg_b, grad_pre, (((0,), (0,)), ((), ())), preferred_element_type=jnp.float32
    )
    term_ref[...] = term
    output = (pre * sig).astype(jnp.bfloat16)
    packed = jnp.dot(placing_ref[...], output, preferred_element_type=jnp.float32)
    half = packed.shape[0] // 2
    same_ref[...] = packed[:half].astype(jnp.bfloat16)
    sent_ref[:half] = packed[half:].astype(jnp.bfloat16)
    low, high = parts_of(term.shape[0], slots)

    @pl.when(core == 0)
    def _():
        sent_ref[half:] = term[low:].astype(jnp.bfloat16)

    @pl.when(core == 1)
    def _():
        sent_ref[half : half + low] = term[:low].astype(jnp.bfloat16)


def dense(parts, weight, cotangent, placing, slots):
    places, width = placing.shape[0], weight.shape[0]
    return pl.pallas_call(
        functools.partial(dense_kernel, len(parts), slots),
        out_shape=(
            jax.ShapeDtypeStruct((places // 2, width), jnp.bfloat16),
            jax.ShapeDtypeStruct((width, width), jnp.float32),
            jax.ShapeDtypeStruct((places // 2 + parts_of(width, slots)[1], width), jnp.bfloat16),
        ),
        in_specs=[VMEM] * (3 + len(parts)),
        out_specs=(VMEM,) * 3,
        compiler_params=LIMIT,
        name="dense",
    )(weight, cotangent, placing, *parts)


def write_messages(core_along, slots, rows, same_ref, came_ref, half_ref, out_refs):
    core = lax.axis_index("section") & 1

    @pl.when(core == core_along)
    def _():
        for i, ref in enumerate(out_refs):
            start = (i + 1) * slots % same_ref.shape[0]
            ref[:slots] = same_ref[start : start + slots]
            ref[slots : 2 * slots] = came_ref[start : start + slots]
            ref[2 * slots : 2 * slots + rows[core_along]] = half_ref[: rows[core_along]]

    @pl.when(core != core_along)
    def _():
        for ref in out_refs:
            ref[: rows[1 - core_along]] = half_ref[: rows[1 - core_along]]


def sum_parts(core_along, slots, rows, half_ref, held, own_ref, message_refs, n_rep):
    chip, chips = place_of_chip()
    core = lax.axis_index("section") & 1

    @pl.when(core == core_along)
    def _():
        many = rows[core_along]
        held[chip, :many] = own_ref[:many]
        for i, ref in enumerate(message_refs[: chips - 1]):
            held[(chip + chips - i - 1) % chips, :many] = ref[2 * slots : 2 * slots + many]
        total = tree_sum([held[c, :many].astype(jnp.float32) for c in range(chips)])
        half_ref[:many] = total.astype(jnp.bfloat16)

    @pl.when(core != core_along)
    def _():
        many = rows[1 - core_along]
        by_xor = [ref[:many].astype(jnp.float32) for ref in [own_ref] + list(message_refs[::-1])]
        half_ref[:many] = tree_sum(by_xor[:n_rep]).astype(jnp.bfloat16)


def first_kernel(slots, rows, same_ref, term_ref, came_ref, half_ref, *out_refs):
    core = lax.axis_index("section") & 1
    start = same_ref.shape[0]

    @pl.when(core == 0)
    def _():
        other = came_ref[start : start + rows[0]].astype(jnp.float32)
        half_ref[: rows[0]] = (term_ref[: rows[0]] + other).astype(jnp.bfloat16)

    @pl.when(core == 1)
    def _():
        other = came_ref[start:].astype(jnp.float32)
        half_ref[...] = (term_ref[rows[0] :] + other).astype(jnp.bfloat16)

    write_messages(0, slots, rows, same_ref, came_ref, half_ref, out_refs)


def second_kernel(slots, rows, n_rep, many, same_ref, came_ref, own_ref, *refs):
    message_refs, half_ref, out_refs, held = refs[:many], refs[many], refs[many + 1 : -1], refs[-1]
    sum_parts(0, slots, rows, half_ref, held, own_ref, message_refs, n_rep)
    write_messages(1, slots, rows, same_ref, came_ref, half_ref, out_refs)


def third_kernel(slots, rows, n_rep, own_ref, *refs):
    sum_parts(1, slots, rows, refs[-2], refs[-1], own_ref, refs[:-2], n_rep)


def call_parts(kernel, name, operands, half, message, many, held=()):
    shapes = [jax.ShapeDtypeStruct(half, jnp.bfloat16)]
    shapes += [jax.ShapeDtypeStruct(message, jnp.bfloat16)] * many
    return pl.pallas_call(
        kernel,
        out_shape=shapes,
        in_specs=[VMEM] * len(operands),
        out_specs=[VMEM] * len(shapes),
        scratch_shapes=[pltpu.VMEM(shape, jnp.bfloat16) for shape in held],
        compiler_params=LIMIT,
        name=name,
    )(*operands)


def store_kernel(core, slots, same_ref, came_ref, *refs):
    message_refs, (out_ref, rows, sem) = refs[:-3], refs[-3:]
    section = lax.axis_index("section")
    chip, chips = place_of_chip()

    @pl.when(section & 1 == core)
    def _():
        rows[section] = same_ref[:slots]
        rows[section ^ 1] = came_ref[:slots]
        for i, ref in enumerate(message_refs[: chips - 1]):
            source = 2 * ((chip + chips - i - 1) % chips)
            rows[source + core] = ref[:slots]
            rows[source + 1 - core] = ref[slots : 2 * slots]
        copy = pltpu.make_async_copy(rows, out_ref, sem)
        copy.start()
        copy.wait()


def store(core, same, came, messages, n_section, slots, base=None):
    shape = (n_section, slots, same.shape[1])
    operands = [same, came, *messages]
    kernel, first, specs = functools.partial(store_kernel, core, slots), [], []
    if base is not None:
        kernel, first, specs = lambda _, *refs: store_kernel(core, slots, *refs), [base], [HBM]
    return pl.pallas_call(
        kernel,
        out_shape=jax.ShapeDtypeStruct(shape, jnp.bfloat16),
        in_specs=specs + [VMEM] * len(operands),
        out_specs=HBM,
        scratch_shapes=[pltpu.VMEM(shape, jnp.bfloat16), pltpu.SemaphoreType.DMA],
        input_output_aliases={0: 0} if first else {},
        compiler_params=LIMIT,
        name="store",
    )(*first, *operands)


def finish_kernel(rows, own_ref, came_ref, out_ref):
    core = lax.axis_index("section") & 1
    low, high = rows

    @pl.when(core == 0)
    def _():
        out_ref[:low] = own_ref[:low].astype(jnp.float32)
        out_ref[low:] = came_ref[...].astype(jnp.float32)

    @pl.when(core == 1)
    def _():
        out_ref[:low] = came_ref[:low].astype(jnp.float32)
        out_ref[low:] = own_ref[...].astype(jnp.float32)


def finish(own, came, rows):
    width = own.shape[1]
    return pl.pallas_call(
        functools.partial(finish_kernel, rows),
        out_shape=jax.ShapeDtypeStruct((width, width), jnp.float32),
        in_specs=[VMEM] * 2,
        out_specs=VMEM,
        compiler_params=LIMIT,
        name="finish",
    )(own, came)


def exchange(value, core_along, shift, j):
    n_section, n_rep = lax.axis_size("section"), lax.axis_size("rep")
    pairs = []
    for s in range(n_section):
        along = s & 1 == core_along
        to = (s + 2 * shift) % n_section if along else s
        for r in range(n_rep):
            pairs.append((s * n_rep + r, to * n_rep + (r if along else r ^ j % n_rep)))
    return lax.ppermute(value, ("section", "rep"), pairs)


def gather_blocks(features, axis, ready):
    n = lax.axis_size(axis)
    blocks = [None] * n
    blocks[0] = features
    far = n // 2 & -2
    for j in sorted(range(2, n, 2), key=lambda j: (j & 4, -(j & 2))):
        blocks[j] = swap(features, axis, j)
    blocks[1] = swap(features, axis, 1)
    blocks[far], ready = lax.optimization_barrier((blocks[far], ready))
    for j in sorted(range(2, n, 2), key=lambda j: -j):
        blocks[j + 1] = swap(blocks[j], axis, 1)
    return blocks, ready


def per_device(features, adj_tiles, adj_src, cotangent, weight, destination):
    n_section, n_rep = lax.axis_size("section"), lax.axis_size("rep")
    rows_here, width = features.shape
    tile = adj_tiles.shape[3]
    slots = max(2, 2 * rows_here // n_section)
    target = destination.reshape(1, rows_here)
    wide, own, placing = prepare(adj_tiles[:, 0], features, target, n_section * slots, slots)
    blocks, (wide, own, placing) = gather_blocks(features, "section", (wide, own, placing))
    parts = list(partials(adj_src[:, 0], wide, [own] + blocks[1:]))
    others = across(n_rep)
    parts = parts[:1] + [swap(part, "rep", j) for part, j in zip(parts[1:], others)]
    same, term, sent = dense(parts, weight, cotangent, placing, slots)
    came = swap(sent, "section", 1)
    chips = n_section // 2
    steps = across(max(n_rep, chips))
    many = len(steps)
    rows = parts_of(width, slots)
    part = (rows[1], width)
    held = [(chips,) + part]
    message = (max(rows[1], 2 * slots + rows[0]), width)
    operands = [same, term, came]
    half, *first = call_parts(
        functools.partial(first_kernel, slots, rows), "first", operands, part, message, many
    )
    first = [exchange(m, 0, i + 1, j) for i, (m, j) in enumerate(zip(first, steps))]
    relaid = store(0, same, came, first, n_section, slots)
    message = (2 * slots + rows[1], width)
    second = functools.partial(second_kernel, slots, rows, n_rep, many)
    operands = [same, came, half, *first]
    half, *second = call_parts(second, "second", operands, part, message, many, held)
    second = [exchange(m, 1, i + 1, j) for i, (m, j) in enumerate(zip(second, steps))]
    third = functools.partial(third_kernel, slots, rows, n_rep)
    (half,) = call_parts(third, "third", [half, *second], part, part, 0, held)
    relaid = store(1, same, came, second, n_section, slots, relaid)
    weight_grad = finish(half, swap(half, "section", 1), rows)
    return (relaid.reshape(1, 1, n_section, slots, width), weight_grad)


def solution(mesh):
    placed = (
        P(("section", "rep"), None),
        P("section", "rep", None, None, None),
        P("section", "rep", None),
        P(("section", "rep"), None),
        P(),
        P(("section", "rep"), None),
    )
    return jax.shard_map(
        per_device,
        mesh=mesh,
        in_specs=placed,
        out_specs=(P("section", "rep", None, None, None), P()),
        check_vma=False,
    )
```
